32 devices in a mesh: dp: 8 (over z, y), section: 2 (over x), tensor: 2 (over core).
Axes of the slice: x: 2, y: 2, z: 4, core: 2. Of those that a mesh axis runs over, the one named last changes fastest.
Arguments:
- layer_input: bfloat16 [2, 8, 1024, 1024], P(None, 'dp', 'tensor'), may hold values from -6 to 6
- segment_ids: int32 [2, 8, 1024], P(None, 'dp'), may hold values from 0 to 127, never falling along the last dimension, each value on 1 to 256 neighbouring positions
- buckets: int32 [2047], replicated, may hold values from 0 to 31, as said below
- attn_in: bfloat16 [2, 1024, 3, 1024], P('section', None, None, 'tensor'), may hold values from -0.1875 to 0.1875
- attn_out: bfloat16 [2, 1024, 1024], P('section', 'tensor'), may hold values from -0.75 to 0.75
- ffn_in: bfloat16 [2, 1024, 4096], P('section', None, 'tensor'), may hold values from -0.1875 to 0.1875
- ffn_out: bfloat16 [2, 4096, 1024], P('section', 'tensor'), may hold values from -0.09375 to 0.09375
- norm_gain: float32 [2, 2, 1024], replicated, may hold values from 0.5 to 1.5
- bert_shift: float32 [4, 1024], replicated, may hold values from -2 to 2
- head_bias: float32 [2, 1024], P(None, 'tensor'), may hold values from -3 to 3
- ffn_bias: float32 [4096], P('tensor'), may hold values from -2 to 2
- position_bias: float32 [16, 32], P('tensor'), may hold values from -4 to 4
- decoder_grads: bfloat16 [2, 2, 8, 1024, 1024], P('section', None, 'dp', 'tensor'), may hold values from -6 to 6
Outputs:
- delivered: bfloat16 [2, 2, 8, 1024, 1024], P('section', None, 'dp', 'tensor')
- input_grad: float32 [2, 8, 1024, 1024], P(None, 'dp', 'tensor', 'section')
- attn_in_grad: float32 [2, 1024, 3, 1024], P('section', 'dp', None, 'tensor')
- attn_out_grad: float32 [2, 1024, 1024], P('section', 'tensor', 'dp')
- ffn_in_grad: float32 [2, 1024, 4096], P('section', 'dp', 'tensor')
- ffn_out_grad: float32 [2, 4096, 1024], P('section', 'tensor', 'dp')
- norm_gain_grad: float32 [2, 2, 1024], replicated
- bert_shift_grad: float32 [4, 1024], replicated
- head_bias_grad: float32 [2, 1024], P(None, 'tensor')
- ffn_bias_grad: float32 [4096], P('tensor')
- position_bias_grad: float32 [16, 32], P('tensor')
The draws below stay inside these ranges and needn't reach their ends.
Inputs may be any that keep to these rules, and one draw needn't show every extreme that they name: `segment_ids`: segment numbers never fall along a packed row; a token attends to the keys of its own row and segment. Entry o + 1023 is the bucket of the offset o = key position minus query position; negative offsets take buckets below 16, the others the rest, and on either side buckets never fall as the distance grows.
All inputs are finite; a program needn't handle non-finite values.
Results may differ from the reference program's by a relative error of at most 0.025.
Values may be sent and summed in bfloat16 or wider, within the bound.
A program may use at most 448 MiB of HBM per device.

```python
import math
import jax
import jax.numpy as jnp
import numpy as np
from jax import lax

D = 1024
H = 16
DH = 64
FF = 4096
BUCKETS = 32
ROW_LEN = 1024
MICRO = 2
PACKS = 8
SECTIONS = 2


def draw_buckets(key, part):
    key = jax.random.fold_in(key, 7)
    half_count = BUCKETS // 2
    step_limit = max(2, ROW_LEN // (2 * half_count))
    step_sizes = jax.random.randint(key, (half_count - 1,), 1, step_limit)
    boundaries = jnp.cumsum(step_sizes)
    offsets = jnp.arange(2 * ROW_LEN - 1) - (ROW_LEN - 1)
    distance = jnp.abs(offsets)
    below = jnp.sum((boundaries[None, :] <= (distance - 1)[:, None]).astype(jnp.int32), axis=1)
    above = jnp.sum((boundaries[None, :] <= distance[:, None]).astype(jnp.int32), axis=1)
    return jnp.where(offsets < 0, below, half_count + above).astype(jnp.int32)


def levels(key, extent, shards, least, high):
    level, own = 1.0, jax.random.fold_in(key, 6)
    for axis_at, blocks in shards:
        heights = jnp.exp(jax.random.uniform(jax.random.fold_in(own, axis_at), (blocks,), jnp.float32, least / len(shards), high / len(shards)))
        level = level * jnp.repeat(heights, extent[axis_at] // blocks).reshape([-1 if axis == axis_at else 1 for axis in range(len(extent))])
    return level


def split_up(count, total, limit, lean):
    portions = [(1 << 20) // math.isqrt(rank ** lean) + 1 for rank in range(2, count + 1)]
    surplus, given = total - limit - (count - 1), [1] * (count - 1)
    while surplus > 0:
        candidates = [i for i in range(count - 1) if given[i] < limit]
        mass, remaining = sum([portions[i] for i in candidates]), surplus
        for i in candidates:
            more = min(limit - given[i], max(1, remaining * portions[i] // mass), surplus)
            given[i] = given[i] + more
            surplus = surplus - more
    return np.array([limit] + given)


def uneven_parts(own_key, count, total, reach, lean):
    if count == 2:
        one = jax.random.randint(own_key, (), max(1, total - reach), min(reach, total - 1) + 1)
        return jnp.stack([one, total - one])
    sizes = jnp.asarray(split_up(count, total, reach, lean), jnp.int32)
    pairs = (count - 1) // 2
    donor, taker = sizes[1:1 + 2 * pairs:2], sizes[2:2 + 2 * pairs:2]
    room = jnp.minimum(donor - 1, reach - taker)
    moved = jax.random.randint(jax.random.fold_in(own_key, 1), (pairs,), 0, 1 << 20) % (room + 1)
    sizes = sizes.at[1:1 + 2 * pairs:2].set(donor - moved).at[2:2 + 2 * pairs:2].set(taker + moved)
    return sizes[jax.random.permutation(jax.random.fold_in(own_key, 2), count)]


def bell_draw(stream_key, extent, deviation, most, cuts=(), held_as=jnp.bfloat16):
    drawn = deviation * jax.random.normal(stream_key, extent, jnp.float32)
    if cuts:
        drawn = drawn * levels(stream_key, extent, cuts, -0.22, 0.18)
    return jnp.clip(drawn, -most, most).astype(held_as)


def setup_inputs(seed: int = 0) -> dict:
    arg_keys = jax.random.split(jax.random.key(seed), 14)
    layer_input = bell_draw(arg_keys[0], (MICRO, PACKS, ROW_LEN, D), 1.0, 6.0, ((1, 8), (2, 2)))
    segment_ids = jax.vmap(lambda own: jnp.searchsorted(jnp.cumsum(uneven_parts(own, max(8, ROW_LEN // 8), ROW_LEN, ROW_LEN // 4, 2)), jnp.arange(ROW_LEN), side="right"))(jax.random.split(arg_keys[1], MICRO * PACKS)).reshape((MICRO, PACKS, ROW_LEN)).astype(jnp.int32)
    buckets = draw_buckets(jax.random.fold_in(arg_keys[13], 71), 0)
    attn_in = bell_draw(arg_keys[3], (2, D, 3, H * DH), D ** -0.5, 0.1875, ((0, 2), (3, 2)))
    attn_out = bell_draw(arg_keys[4], (2, H * DH, D), (max(16, H * DH // 16)) ** -0.5, 0.75, ((0, 2), (1, 2)))
    ffn_in = bell_draw(arg_keys[5], (2, D, FF), D ** -0.5, 0.1875, ((0, 2), (2, 2)))
    ffn_out = bell_draw(arg_keys[6], (2, FF, D), FF ** -0.5, 0.09375, ((0, 2), (1, 2)))
    norm_gain = jnp.clip(1.0 + 0.1 * jax.random.normal(arg_keys[7], (2, 2, D), jnp.float32), 0.5, 1.5)
    bert_shift = bell_draw(arg_keys[8], (4, D), 0.3, 2.0, (), jnp.float32)
    head_bias = bell_draw(arg_keys[9], (2, H * DH), 0.5, 3.0, ((1, 2),), jnp.float32)
    ffn_bias = bell_draw(arg_keys[10], (FF,), 0.3, 2.0, ((0, 2),), jnp.float32)
    position_bias = bell_draw(arg_keys[11], (H, BUCKETS), 1.0, 4.0, ((0, 2),), jnp.float32)
    decoder_grads = bell_draw(arg_keys[12], (SECTIONS, MICRO, PACKS, ROW_LEN, D), 1.0, 6.0, ((0, 2), (2, 8), (3, 2)))
    return dict(layer_input=layer_input, segment_ids=segment_ids, buckets=buckets, attn_in=attn_in, attn_out=attn_out, ffn_in=ffn_in, ffn_out=ffn_out, norm_gain=norm_gain, bert_shift=bert_shift, head_bias=head_bias, ffn_bias=ffn_bias, position_bias=position_bias, decoder_grads=decoder_grads)


@jax.custom_vjp
def low(v):
    return lax.optimization_barrier(v.astype(jnp.bfloat16)).astype(jnp.float32)

@jax.custom_vjp
def low_back(v):
    return v

def low_keep(v):
    return (low(v), None)

def low_pass(kept, grad):
    return (grad,)

def back_keep(v):
    return (v, None)

def back_low(kept, grad):
    return (low(grad),)
low.defvjp(low_keep, low_pass)
low_back.defvjp(back_keep, back_low)

def rounded(operand):
    return low_back(low(operand))

def product(left, right):
    return jnp.dot(left, right, precision=lax.Precision.HIGHEST, preferred_element_type=jnp.float32)

def layer_norm(operand, gain_row, shift_row):
    center = operand - lax.optimization_barrier(jnp.mean(operand, axis=-1, keepdims=True))
    variance = lax.optimization_barrier(jnp.mean(center * center, axis=-1, keepdims=True))
    return center * lax.rsqrt(variance + 1e-05) * gain_row + shift_row

def rms_norm(operand, gain_row):
    return operand * lax.rsqrt(lax.optimization_barrier(jnp.mean(operand * operand, axis=-1, keepdims=True)) + 1e-06) * gain_row

def gelu_act(operand):
    return jax.nn.gelu(operand, approximate=False)

def attention(queries, key_rows, values, allowed, score_bias):
    shaped_q = queries.reshape(ROW_LEN, H, DH)
    shaped_k = key_rows.reshape(ROW_LEN, H, DH)
    shaped_v = values.reshape(ROW_LEN, H, DH)
    scores = jnp.einsum('qhd,khd->hqk', shaped_q, shaped_k, precision=lax.Precision.HIGHEST) * DH ** (-0.5) + score_bias
    scores = low_back(scores)
    masked = jnp.where(allowed[None], scores, -jnp.inf)
    highest = lax.optimization_barrier(jnp.max(masked, axis=-1, keepdims=True))
    weights = jnp.exp(masked - highest)
    probs_all = weights / lax.optimization_barrier(jnp.sum(weights, axis=-1, keepdims=True))
    context = jnp.einsum('hqk,khd->qhd', low(probs_all), shaped_v, precision=lax.Precision.HIGHEST)
    return rounded(context.reshape(ROW_LEN, H * DH))

def bert_layer(sequence, allowed, bert_weights):
    qkv_weight, out_weight, up_weight, down_weight, gain_pair, shift_rows, head_shift, ffn_shift = bert_weights
    projected = product(sequence, qkv_weight.reshape(D, 3 * H * DH)).reshape(ROW_LEN, 3, H * DH)
    queries = rounded(projected[:, 0] + head_shift[0])
    key_rows = rounded(projected[:, 1])
    values = rounded(projected[:, 2] + head_shift[1])
    context = attention(queries, key_rows, values, allowed, 0.0)
    branch = low_back(product(context, out_weight))
    after_attention = layer_norm(sequence + branch + shift_rows[0], gain_pair[0], shift_rows[2])
    pre_act = low_back(product(low(after_attention), up_weight) + ffn_shift)
    hidden = low(gelu_act(pre_act))
    second = low_back(product(hidden, down_weight))
    return low(layer_norm(after_attention + second + shift_rows[1], gain_pair[1], shift_rows[3]))

def reader_layer(sequence, allowed, reader_weights, score_bias):
    qkv_weight, out_weight, up_weight, down_weight, gain_pair = reader_weights
    normed = low(rms_norm(sequence, gain_pair[0]))
    projected = product(normed, qkv_weight.reshape(D, 3 * H * DH)).reshape(ROW_LEN, 3, H * DH)
    queries = rounded(projected[:, 0])
    key_rows = rounded(projected[:, 1])
    values = rounded(projected[:, 2])
    context = attention(queries, key_rows, values, allowed, score_bias)
    branch = low_back(product(context, out_weight))
    after_attention = sequence + branch
    pre_act = low_back(product(low(rms_norm(after_attention, gain_pair[1])), up_weight))
    hidden = low(gelu_act(pre_act))
    second = low_back(product(hidden, down_weight))
    return after_attention + second

def reference(layer_input, segment_ids, buckets, attn_in, attn_out, ffn_in, ffn_out, norm_gain, bert_shift, head_bias, ffn_bias, position_bias, decoder_grads):
    sequences = layer_input.astype(jnp.float32).reshape(MICRO * PACKS, ROW_LEN, D)
    segment_rows = segment_ids.reshape(MICRO * PACKS, ROW_LEN)
    offsets = jnp.arange(ROW_LEN)[None, :] - jnp.arange(ROW_LEN)[:, None] + (ROW_LEN - 1)
    bucket_of = buckets[offsets]
    parameters = (attn_in.astype(jnp.float32), attn_out.astype(jnp.float32), ffn_in.astype(jnp.float32), ffn_out.astype(jnp.float32), norm_gain.astype(jnp.float32), bert_shift.astype(jnp.float32), head_bias.astype(jnp.float32), ffn_bias.astype(jnp.float32), position_bias.astype(jnp.float32))

    def network(sequences, parameters):
        qkv_weight, out_weight, up_weight, down_weight, gain_all, shift_rows, head_shift, ffn_shift, bias_table = parameters
        score_bias = bias_table[:, bucket_of]
        bert_weights = (qkv_weight[0], out_weight[0], up_weight[0], down_weight[0], gain_all[0], shift_rows, head_shift, ffn_shift)
        reader_weights = (qkv_weight[1], out_weight[1], up_weight[1], down_weight[1], gain_all[1])

        def single_row(row_pair):
            sequence, segment = row_pair
            allowed = segment[:, None] == segment[None, :]
            between = bert_layer(sequence, allowed, bert_weights)
            return reader_layer(between, allowed, reader_weights, score_bias)
        return lax.map(jax.checkpoint(single_row), (sequences, segment_rows))
    encoded, pull_back = jax.vjp(network, sequences, parameters)
    cotangent = lax.optimization_barrier(jnp.sum(decoder_grads.astype(jnp.float32), axis=0)).reshape(MICRO * PACKS, ROW_LEN, D)
    row_grad, grad_terms = pull_back(cotangent)
    encoded_low = encoded.astype(jnp.bfloat16).reshape(MICRO, PACKS, ROW_LEN, D)
    delivered = jnp.broadcast_to(encoded_low[None], (SECTIONS, MICRO, PACKS, ROW_LEN, D))
    return (delivered, row_grad.reshape(MICRO, PACKS, ROW_LEN, D), grad_terms[0], grad_terms[1], grad_terms[2], grad_terms[3], grad_terms[4], grad_terms[5], grad_terms[6], grad_terms[7], grad_terms[8])
```

```python
import jax
import jax.numpy as jnp
from jax import lax
from jax.experimental import pallas as pl
from jax.experimental.pallas import tpu as pltpu
from jax.sharding import PartitionSpec as P


def passed_along(value, axis, steps):
    count = lax.axis_size(axis)
    initial, last = (max(0, -steps), min(count, count - steps))
    return lax.ppermute(value, axis, [(source, source + steps) for source in range(initial, last)])


def spread(block, axis, source):
    block = jnp.where(lax.axis_index(axis) == source, block, jnp.zeros_like(block))
    return lax.psum(block, axis)


def layer_norm(operand, gain_row, shift_row):
    center = operand - jnp.mean(operand, axis=-1, keepdims=True)
    variance = jnp.mean(center * center, axis=-1, keepdims=True)
    return center * lax.rsqrt(variance + 1e-05) * gain_row + shift_row


def rms_norm(operand, gain_row):
    return (
        operand * lax.rsqrt(jnp.mean(operand * operand, axis=-1, keepdims=True) + 1e-06) * gain_row
    )


def gelu_act(operand):
    return jax.nn.gelu(operand, approximate=False)


def gelu_slope(operand):
    return (
        0.5 * (1.0 + jax.scipy.special.erf(operand * 0.7071067811865476))
        + operand * jnp.exp(-0.5 * operand * operand) * 0.3989422804014327
    )


def entry_norm(residual, gain_rows, leading):
    return jnp.where(leading, residual, rms_norm(residual, gain_rows[0]))


def middle(residual, branch, gain_rows, shift_rows, leading):
    joined = residual + branch
    bert_rows = layer_norm(joined + shift_rows[0], gain_rows[0], shift_rows[2])
    carried = jnp.where(leading, bert_rows, joined)
    normed = jnp.where(leading, bert_rows, rms_norm(joined, gain_rows[1]))
    return (carried, normed)


def final(carried, second, gain_rows, shift_rows, leading):
    joined = carried + second
    return jnp.where(
        leading, layer_norm(joined + shift_rows[1], gain_rows[1], shift_rows[3]), joined
    )


def contract_rows(left, right):
    return lax.dot_general(
        left, right, (((0,), (0,)), ((), ())), preferred_element_type=jnp.float32
    )


def contract_cols(left, right):
    return lax.dot_general(
        left, right, (((1,), (1,)), ((), ())), preferred_element_type=jnp.float32
    )


def gather_rows(operand, weight):
    return (
        jnp.dot(
            lax.all_gather(operand, "tensor", axis=0, tiled=True),
            weight,
            preferred_element_type=jnp.float32,
        ),
        None,
    )


def collect(full_rows, weight):
    return lax.psum_scatter(
        jnp.dot(full_rows, weight, preferred_element_type=jnp.float32),
        "tensor",
        scatter_dimension=0,
        tiled=True,
    )


def scatter_back(grad_rows, weight):
    return lax.psum_scatter(
        contract_cols(grad_rows, weight).astype(jnp.bfloat16),
        "tensor",
        scatter_dimension=0,
        tiled=True,
    ).astype(jnp.float32)


def fold_back(grad_share, weight, activations):
    fragment = lax.all_gather(grad_share, "tensor", axis=0, tiled=True)
    product_rows = contract_cols(fragment, weight)
    return (product_rows, contract_rows(activations, fragment))


def weight_grad(operand, grad_rows):
    return contract_rows(lax.all_gather(operand, "tensor", axis=0, tiled=True), grad_rows)


DH = 64
QB = 128
NARROW = 3
WIDE = 5
VMEM = 56 * 1024 * 1024


def dot_nt(left, right):
    return lax.dot_general(left, right, (((1,), (1,)), ((), ())), preferred_element_type=jnp.float32)


def dot_nn(left, right):
    return lax.dot_general(left, right, (((1,), (0,)), ((), ())), preferred_element_type=jnp.float32)


def toeplitz_kernel(w_ref, t_ref):
    width = w_ref.shape[2]
    half = []
    for head in range(2):
        rows = jnp.broadcast_to(w_ref[0, head : head + 1, :], (QB, width))
        rolled = pltpu.roll(rows, 0, 1, stride=1, stride_axis=0)
        half.append(rolled.T[QB:, :])
    t_ref[0] = jnp.concatenate(half, axis=1)


def toeplitz(offset_bias):
    heads, width = offset_bias.shape
    pairs = heads // 2
    return pl.pallas_call(
        toeplitz_kernel,
        grid=(pairs,),
        in_specs=[pl.BlockSpec((1, 2, width), lambda p: (p, 0, 0))],
        out_specs=pl.BlockSpec((1, width - QB, 2 * QB), lambda p: (p, 0, 0)),
        out_shape=jax.ShapeDtypeStruct((pairs, width - QB, 2 * QB), jnp.float32),
        compiler_params=pltpu.CompilerParams(vmem_limit_bytes=VMEM),
    )(offset_bias.reshape(pairs, 2, width))


def diagonal_kernel(a_ref, s_ref):
    total = a_ref[0, 0]
    for extra in range(1, a_ref.shape[0]):
        total = total + a_ref[extra, 0]
    total = jnp.concatenate([jnp.zeros((QB, 2 * QB), jnp.float32), total], axis=0)
    width = total.shape[0]
    row = lax.broadcasted_iota(jnp.int32, (QB, QB), 0)
    col = lax.broadcasted_iota(jnp.int32, (QB, QB), 1)
    mirror = jnp.where(row + col == QB - 1, 1.0, 0.0)
    for head in range(2):
        turned = lax.dot_general(
            mirror,
            total[:, head * QB : (head + 1) * QB],
            (((1,), (1,)), ((), ())),
            precision=lax.Precision.HIGHEST,
            preferred_element_type=jnp.float32,
        )
        aligned = pltpu.roll(turned, width - QB + 1, 1, stride=1, stride_axis=0)
        s_ref[0, head : head + 1, :] = jnp.sum(aligned, axis=0, keepdims=True)


def window(i, count, width):
    return jnp.clip(i - width // 2, 0, count - width)


def two_heads(block, first):
    zero = jnp.zeros_like(block)
    return jnp.concatenate([jnp.where(first, block, zero), jnp.where(first, zero, block)], axis=0)


def joined_heads(turned):
    return jnp.concatenate([turned[:DH, :QB], turned[DH:, QB:]], axis=0).T


def visit_blocks(seg_ref, count, block):
    narrow = min(NARROW, count)
    wide = min(WIDE, count)

    @pl.loop(0, count)
    def _(i):
        first = seg_ref[i * QB]
        last = seg_ref[i * QB + QB - 1]
        before = seg_ref[jnp.maximum((i - 1) * QB - 1, 0)]
        after = seg_ref[jnp.minimum((i + 2) * QB, count * QB - 1)]
        reach = ((i >= 2) & (before == first)) | ((i + 2 < count) & (after == last))

        @pl.when(reach)
        def _():
            block(i, wide)

        @pl.when(jnp.logical_not(reach))
        def _():
            block(i, narrow)


def attend_kernel(seg_ref, segk_ref, segq_ref, q_ref, k_ref, v_ref, t_ref, o_ref, lse_ref, vt_ref):
    length = q_ref.shape[0]
    count = length // QB
    pairs = q_ref.shape[1] // (2 * DH)
    first = lax.broadcasted_iota(jnp.int32, (QB, 2 * DH), 1) < DH
    vt_ref[...] = v_ref[...].T

    def block(i, width):
        start = window(i, count, width)
        keys = pl.ds(pl.multiple_of(start * QB, QB), width * QB)
        mine = pl.ds(pl.multiple_of(i * QB, QB), QB)
        shifted = pl.ds(pl.multiple_of((start - i + 4) * QB, QB), width * QB)
        allowed = segk_ref[keys, :] == segq_ref[pl.ds(i, 1), :]
        allowed = jnp.concatenate([allowed, allowed], axis=1)
        for pair in range(pairs):
            lanes = slice(pair * 2 * DH, (pair + 1) * 2 * DH)
            both = two_heads(q_ref[mine, lanes] * jnp.bfloat16(0.125), first)
            scores = dot_nt(k_ref[keys, lanes], both) + t_ref[pair, shifted, :]
            scores = jnp.where(allowed, scores, -jnp.inf)
            highest = jnp.max(scores, axis=0, keepdims=True)
            weights = jnp.exp(scores - highest)
            totals = jnp.sum(weights, axis=0, keepdims=True)
            probs = (weights * (1.0 / totals)).astype(jnp.bfloat16)
            turned = dot_nn(vt_ref[lanes, keys], probs)
            o_ref[mine, lanes] = joined_heads(turned).astype(jnp.bfloat16)
            lse_ref[pair, pl.ds(i, 1), :] = highest + jnp.log(totals)

    visit_blocks(seg_ref, count, block)


def attend(qkv, segments, bias):
    length, width = qkv.shape
    width = width // 3
    span = min(256, width)
    groups = width // span
    pairs = span // (2 * DH)
    count = length // QB
    seg_cols = jnp.broadcast_to(segments[:, None], (length, QB))
    seg_rows = segments.reshape(count, QB)
    whole = lambda g, s: (0, 0)
    return pl.pallas_call(
        attend_kernel,
        grid_spec=pltpu.PrefetchScalarGridSpec(
            num_scalar_prefetch=1,
            grid=(groups,),
            in_specs=[
                pl.BlockSpec((length, QB), whole),
                pl.BlockSpec((count, QB), whole),
                pl.BlockSpec((length, span), lambda g, s: (0, g)),
                pl.BlockSpec((length, span), lambda g, s: (0, g + groups)),
                pl.BlockSpec((length, span), lambda g, s: (0, g + 2 * groups)),
                pl.BlockSpec((pairs,) + bias.shape[1:], lambda g, s: (g, 0, 0)),
            ],
            out_specs=[
                pl.BlockSpec((length, span), lambda g, s: (0, g)),
                pl.BlockSpec((pairs, count, 2 * QB), lambda g, s: (g, 0, 0)),
            ],
            scratch_shapes=[pltpu.VMEM((span, length), jnp.bfloat16)],
        ),
        out_shape=[
            jax.ShapeDtypeStruct((length, width), jnp.bfloat16),
            jax.ShapeDtypeStruct((groups * pairs, count, 2 * QB), jnp.float32),
        ],
        compiler_params=pltpu.CompilerParams(vmem_limit_bytes=VMEM),
        name="attend",
    )(segments, seg_cols, seg_rows, qkv, qkv, qkv, bias)


def attend_back_kernel(
    seg_ref, segk_ref, segq_ref, q_ref, k_ref, v_ref, g_ref, t_ref, lse_ref,
    dq_ref, dk_ref, dv_ref, head_ref, diag_ref, kt_ref, dk_acc, dv_acc
):
    length = q_ref.shape[0]
    count = length // QB
    pairs = q_ref.shape[1] // (2 * DH)
    first = lax.broadcasted_iota(jnp.int32, (QB, 2 * DH), 1) < DH
    kt_ref[...] = k_ref[...].T
    dk_acc[...] = jnp.zeros_like(dk_acc)
    dv_acc[...] = jnp.zeros_like(dv_acc)
    diag_ref[...] = jnp.zeros_like(diag_ref)
    head_ref[...] = jnp.zeros_like(head_ref)

    def block(i, width):
        start = window(i, count, width)
        keys = pl.ds(pl.multiple_of(start * QB, QB), width * QB)
        mine = pl.ds(pl.multiple_of(i * QB, QB), QB)
        shifted = pl.ds(pl.multiple_of((start - i + 4) * QB, QB), width * QB)
        allowed = segk_ref[keys, :] == segq_ref[pl.ds(i, 1), :]
        allowed = jnp.concatenate([allowed, allowed], axis=1)
        for pair in range(pairs):
            lanes = slice(pair * 2 * DH, (pair + 1) * 2 * DH)
            both = two_heads(q_ref[mine, lanes] * jnp.bfloat16(0.125), first)
            grads = two_heads(g_ref[mine, lanes], first)
            scores = dot_nt(k_ref[keys, lanes], both) + t_ref[pair, shifted, :]
            scores = jnp.where(allowed, scores - lse_ref[pair, pl.ds(i, 1), :], -jnp.inf)
            probs = jnp.exp(scores)
            grad_probs = dot_nt(v_ref[keys, lanes], grads)
            dv_acc[keys, lanes] += dot_nn(probs.astype(jnp.bfloat16), grads)
            inner = jnp.sum(probs * grad_probs, axis=0, keepdims=True)
            rounded = (probs * (grad_probs - inner)).astype(jnp.bfloat16)
            dk_acc[keys, lanes] += dot_nn(rounded, both)
            diag_ref[pair, shifted, :] += rounded.astype(jnp.float32)
            turned = dot_nn(kt_ref[lanes, keys], rounded)
            low = (joined_heads(turned) * 0.125).astype(jnp.bfloat16)
            dq_ref[mine, lanes] = low
            head_ref[0, 0:1, lanes] += jnp.sum(low.astype(jnp.float32), axis=0, keepdims=True)

    visit_blocks(seg_ref, count, block)
    dk_ref[...] = dk_acc[...].astype(jnp.bfloat16)
    low_v = dv_acc[...].astype(jnp.bfloat16)
    dv_ref[...] = low_v
    head_ref[0, 1:2, :] = jnp.sum(low_v.astype(jnp.float32), axis=0, keepdims=True)


def attend_back(qkv, grad_context, segments, bias, lse):
    length, width = qkv.shape
    width = width // 3
    span = min(256, width)
    groups = width // span
    pairs = span // (2 * DH)
    count = length // QB
    seg_cols = jnp.broadcast_to(segments[:, None], (length, QB))
    seg_rows = segments.reshape(count, QB)
    whole = lambda g, s: (0, 0)
    column = pl.BlockSpec((length, span), lambda g, s: (0, g))
    table = pl.BlockSpec((pairs,) + bias.shape[1:], lambda g, s: (g, 0, 0))
    return pl.pallas_call(
        attend_back_kernel,
        grid_spec=pltpu.PrefetchScalarGridSpec(
            num_scalar_prefetch=1,
            grid=(groups,),
            in_specs=[
                pl.BlockSpec((length, QB), whole),
                pl.BlockSpec((count, QB), whole),
                column,
                pl.BlockSpec((length, span), lambda g, s: (0, g + groups)),
                pl.BlockSpec((length, span), lambda g, s: (0, g + 2 * groups)),
                column,
                table,
                pl.BlockSpec((pairs, count, 2 * QB), lambda g, s: (g, 0, 0)),
            ],
            out_specs=[
                column,
                column,
                column,
                pl.BlockSpec((1, 8, span), lambda g, s: (g, 0, 0)),
                table,
            ],
            scratch_shapes=[
                pltpu.VMEM((span, length), jnp.bfloat16),
                pltpu.VMEM((length, span), jnp.float32),
                pltpu.VMEM((length, span), jnp.float32),
            ],
        ),
        out_shape=[
            jax.ShapeDtypeStruct((length, width), jnp.bfloat16),
            jax.ShapeDtypeStruct((length, width), jnp.bfloat16),
            jax.ShapeDtypeStruct((length, width), jnp.bfloat16),
            jax.ShapeDtypeStruct((groups, 8, span), jnp.float32),
            jax.ShapeDtypeStruct(bias.shape, jnp.float32),
        ],
        compiler_params=pltpu.CompilerParams(vmem_limit_bytes=VMEM),
        name="attend_back",
    )(segments, seg_cols, seg_rows, qkv, qkv, qkv, grad_context, bias, lse)


def diagonals(tables):
    steps, pairs, rows, _ = tables.shape
    width = rows + QB
    out = pl.pallas_call(
        diagonal_kernel,
        grid=(pairs,),
        in_specs=[pl.BlockSpec((steps, 1, rows, 2 * QB), lambda p: (0, p, 0, 0))],
        out_specs=pl.BlockSpec((1, 2, width), lambda p: (p, 0, 0)),
        out_shape=jax.ShapeDtypeStruct((pairs, 2, width), jnp.float32),
        compiler_params=pltpu.CompilerParams(vmem_limit_bytes=VMEM),
    )(tables)
    return out.reshape(2 * pairs, width)


def body(
    layer_input,
    segment_ids,
    buckets,
    attn_in,
    attn_out,
    ffn_in,
    ffn_out,
    norm_gain,
    bert_shift,
    head_bias,
    ffn_bias,
    position_bias,
    decoder_grads,
):
    micro_count = layer_input.shape[0]
    shard_rows = layer_input.shape[2]
    model_width = layer_input.shape[3]
    length = segment_ids.shape[2]
    leading = lax.axis_index("section") == 0
    weighting = jnp.where(leading, 1.0, 0.0)
    qkv_weight = attn_in[0].reshape(model_width, -1)
    out_weight = attn_out[0]
    ffn_up = ffn_in[0]
    ffn_down = ffn_out[0]
    gain_rows = jnp.where(leading, norm_gain[0], norm_gain[1])
    head_shift = head_bias * weighting
    qkv_shift = jnp.concatenate([head_shift[0], jnp.zeros_like(head_shift[0]), head_shift[1]])
    ffn_shift = ffn_bias * weighting
    bias_table = position_bias * (1.0 - weighting)
    bucket_hits = (buckets[None, :] == jnp.arange(bias_table.shape[1])[:, None]).astype(jnp.float32)
    offset_bias = jnp.dot(bias_table, bucket_hits, precision=lax.Precision.HIGHEST)
    near = length - 1 - 5 * QB
    bias = toeplitz(offset_bias[:, near : near + 10 * QB])
    segment_rows = segment_ids[:, 0]

    def middle_part(residual_in, branch_in, gain_in, shift_in):
        return middle(residual_in, branch_in, gain_in, shift_in, leading)

    def final_part(carried_in, second_in, gain_in, shift_in):
        return final(carried_in, second_in, gain_in, shift_in, leading)

    def entry_part(residual_in, gain_in):
        return entry_norm(residual_in, gain_in, leading)

    received = jnp.zeros((shard_rows, model_width), jnp.bfloat16)
    saved_steps = []
    encoded = []
    for moment in range(micro_count + 1):
        own_rows = layer_input[min(moment, micro_count - 1), 0]
        if moment >= micro_count:
            own_rows = jnp.zeros_like(own_rows)
        segment_row = jnp.where(
            leading, segment_rows[min(moment, micro_count - 1)], segment_rows[max(moment - 1, 0)]
        )
        forward_incoming = jnp.where(leading, own_rows, received)
        forward_residual = forward_incoming.astype(jnp.float32)
        forward_entered = entry_norm(forward_residual, gain_rows, leading).astype(jnp.bfloat16)
        projected, forward_gathered_in = gather_rows(forward_entered, qkv_weight)
        forward_qkv = (projected + qkv_shift).astype(jnp.bfloat16)
        forward_context, forward_log_totals = attend(forward_qkv, segment_row, bias)
        forward_branch = collect(forward_context, out_weight)
        forward_carried, forward_normed = middle(
            forward_residual, forward_branch, gain_rows, bert_shift, leading
        )
        pre_full, forward_gathered_mid = gather_rows(forward_normed.astype(jnp.bfloat16), ffn_up)
        forward_pre_act = pre_full + ffn_shift
        forward_second = collect(gelu_act(forward_pre_act).astype(jnp.bfloat16), ffn_down)
        result = final(forward_carried, forward_second, gain_rows, bert_shift, leading).astype(
            jnp.bfloat16
        )
        result, saved = (
            result,
            (
                forward_incoming,
                segment_row,
                forward_branch,
                forward_second,
                forward_qkv,
                forward_context,
                forward_log_totals,
                forward_pre_act,
                forward_gathered_in,
                forward_gathered_mid,
            ),
        )
        saved_steps.append(saved)
        if moment >= 1:
            encoded.append(result)
        if moment < micro_count:
            received = passed_along(result, "section", 1)
    delivered = spread(jnp.stack(encoded), "section", 1)
    section_grads = lax.psum(
        decoder_grads[0, :, 0].astype(jnp.float32).astype(jnp.bfloat16), "section"
    ).astype(jnp.float32)
    grad_received = jnp.zeros((shard_rows, model_width), jnp.float32)
    running_terms = None
    input_rows = []
    for moment in range(micro_count + 1):
        own_grad = section_grads[min(moment, micro_count - 1)]
        if moment >= micro_count:
            own_grad = jnp.zeros_like(own_grad)
        earlier = saved_steps[max(moment - 1, 0)]
        later = saved_steps[min(moment + 1, micro_count)]
        chosen = jax.tree.map(
            lambda from_first, from_second: jnp.where(leading, from_first, from_second),
            earlier,
            later,
        )
        (
            incoming,
            backward_segment_row,
            branch,
            second,
            qkv,
            context,
            log_totals,
            pre_act,
            gathered_in,
            gathered_mid,
        ) = chosen
        residual = incoming.astype(jnp.float32)
        (carried, normed), pull_middle = jax.vjp(
            middle_part, residual, branch, gain_rows, bert_shift
        )
        finished, pull_final = jax.vjp(final_part, carried, second, gain_rows, bert_shift)
        grad_carried, grad_second, gain_end, shift_end = pull_final(
            jnp.where(leading, grad_received, own_grad)
        )
        hidden = gelu_act(pre_act).astype(jnp.bfloat16)
        grad_hidden, backward_grad_down = fold_back(
            grad_second.astype(jnp.bfloat16), ffn_down, hidden
        )
        grad_pre = (grad_hidden * gelu_slope(pre_act)).astype(jnp.bfloat16)
        grad_shift = jnp.sum(grad_pre.astype(jnp.float32), axis=0) * weighting
        backward_grad_up = weight_grad(normed.astype(jnp.bfloat16), grad_pre)
        grad_normed = scatter_back(grad_pre, ffn_up)
        grad_residual, grad_branch, gain_mid, shift_mid = pull_middle((grad_carried, grad_normed))
        grad_context, backward_grad_out_weight = fold_back(
            grad_branch.astype(jnp.bfloat16), out_weight, context
        )
        low_q, low_k, low_v, head_sums, grad_table = attend_back(
            qkv, grad_context.astype(jnp.bfloat16), backward_segment_row, bias, log_totals
        )
        grad_head = jnp.moveaxis(head_sums[:, :2], 1, 0).reshape(2, -1) * weighting
        grad_rows = jnp.concatenate([low_q, low_k, low_v], axis=1)
        entered, pull_entry = jax.vjp(entry_part, residual, gain_rows)
        backward_grad_qkv = weight_grad(entered.astype(jnp.bfloat16), grad_rows)
        grad_entered = scatter_back(grad_rows, qkv_weight)
        grad_from_entry, gain_entry = pull_entry(grad_entered)
        grad_terms = (
            backward_grad_qkv,
            backward_grad_out_weight,
            backward_grad_up,
            backward_grad_down,
            gain_end + gain_mid + gain_entry,
            shift_end + shift_mid,
            grad_head,
            grad_shift,
            grad_table,
        )
        grad_input, grad_terms = (grad_residual + grad_from_entry, grad_terms)
        if running_terms is None:
            running_terms = grad_terms
        else:
            running_terms = jax.tree.map(jnp.add, running_terms, grad_terms)
        if moment >= 1:
            input_rows.append(grad_input)
        if moment < micro_count:
            grad_received = passed_along(grad_input.astype(jnp.bfloat16), "section", -1).astype(
                grad_input.dtype
            )
    input_all = jnp.stack(input_rows)
    half_width = model_width // 2
    upper_half = passed_along(
        input_all[:, :, half_width:].astype(jnp.bfloat16), "section", 1
    ).astype(jnp.float32)
    input_grad = jnp.where(leading, input_all[:, :, :half_width], upper_half)[:, None]
    (
        grad_qkv,
        grad_out_weight,
        grad_up,
        grad_down,
        gain_sum,
        shift_sum,
        head_sum,
        shift_ffn_sum,
        table_sum,
    ) = running_terms
    near_hits = bucket_hits[:, near : near + 10 * QB]
    table_sum = jnp.dot(diagonals(table_sum[None]), near_hits.T, precision=lax.Precision.HIGHEST) * (
        1.0 - weighting
    )
    weights_out = (
        lax.psum_scatter(
            grad_qkv.reshape(1, model_width, 3, -1).astype(jnp.bfloat16),
            "dp",
            scatter_dimension=1,
            tiled=True,
        ).astype(jnp.float32),
        lax.psum_scatter(
            grad_out_weight[None].astype(jnp.bfloat16), "dp", scatter_dimension=2, tiled=True
        ).astype(jnp.float32),
        lax.psum_scatter(
            grad_up[None].astype(jnp.bfloat16), "dp", scatter_dimension=1, tiled=True
        ).astype(jnp.float32),
        lax.psum_scatter(
            grad_down[None].astype(jnp.bfloat16), "dp", scatter_dimension=2, tiled=True
        ).astype(jnp.float32),
    )
    gain_both = jnp.stack([gain_sum * weighting, gain_sum * (1.0 - weighting)])
    shared_out = lax.psum((gain_both, shift_sum), ("dp", "section", "tensor"))
    split_out = lax.psum((head_sum, shift_ffn_sum, table_sum), ("dp", "section"))
    return (
        delivered[None, :, None],
        input_grad,
        weights_out[0],
        weights_out[1],
        weights_out[2],
        weights_out[3],
        shared_out[0],
        shared_out[1],
        split_out[0],
        split_out[1],
        split_out[2],
    )


def solution(mesh):
    placed = (
        P(None, "dp", "tensor", None),
        P(None, "dp", None),
        P(),
        P("section", None, None, "tensor"),
        P("section", "tensor", None),
        P("section", None, "tensor"),
        P("section", "tensor", None),
        P(),
        P(),
        P(None, "tensor"),
        P("tensor"),
        P("tensor", None),
        P("section", None, "dp", "tensor", None),
    )
    return jax.shard_map(
        body,
        mesh=mesh,
        in_specs=placed,
        out_specs=(
            P("section", None, "dp", "tensor", None),
            P(None, "dp", "tensor", "section"),
            P("section", "dp", None, "tensor"),
            P("section", "tensor", "dp"),
            P("section", "dp", "tensor"),
            P("section", "tensor", "dp"),
            P(),
            P(),
            P(None, "tensor"),
            P("tensor"),
            P("tensor", None),
        ),
        check_vma=False,
    )
```

```python
import functools

import jax
import jax.numpy as jnp
from jax import lax
from jax.experimental import pallas as pl
from jax.experimental.pallas import tpu as pltpu
from jax.sharding import PartitionSpec as P

DH = 64
QB = 128
PAD = 2
REACH = 256
VMEM = 56 * 1024 * 1024
LOW = jnp.bfloat16
F32 = jnp.float32


def dot_nt(left, right):
    return lax.dot_general(left, right, (((1,), (1,)), ((), ())), preferred_element_type=F32)


def dot_nn(left, right):
    return lax.dot_general(left, right, (((1,), (0,)), ((), ())), preferred_element_type=F32)


def params():
    return pltpu.CompilerParams(vmem_limit_bytes=VMEM)


def slotted(shape, dtype):
    return jax.ShapeDtypeStruct((3,) + shape, dtype)


def call_with_slots(kernel, scalars, inputs, in_specs, outputs, out_specs, previous, grid, scratch, name):
    count = len(inputs)
    kept = [] if previous is None else [item for item in previous if item is not None]
    aliases = {}
    if previous is not None:
        at = len(scalars) + count
        for index, item in enumerate(previous):
            if item is not None:
                aliases[at] = index
                at += 1

    def run(*refs):
        front = len(scalars) + count
        kernel(*refs[:front], *refs[front + len(kept) :])

    return pl.pallas_call(
        run,
        grid_spec=pltpu.PrefetchScalarGridSpec(
            num_scalar_prefetch=len(scalars),
            grid=grid,
            in_specs=list(in_specs) + [pl.BlockSpec(memory_space=pl.ANY)] * len(kept),
            out_specs=out_specs,
            scratch_shapes=scratch,
        ),
        out_shape=outputs,
        input_output_aliases=aliases,
        compiler_params=params(),
        name=name,
    )(*scalars, *inputs, *kept)


def toeplitz_kernel(w_ref, t_ref):
    width = w_ref.shape[2]
    half = []
    for head in range(2):
        rows = jnp.broadcast_to(w_ref[0, head : head + 1, :], (QB, width))
        rolled = pltpu.roll(rows, 0, 1, stride=1, stride_axis=0)
        half.append(rolled.T[QB:, :])
    t_ref[0] = jnp.concatenate(half, axis=1)


def toeplitz(offset_bias):
    heads, width = offset_bias.shape
    pairs = heads // 2
    return pl.pallas_call(
        toeplitz_kernel,
        grid=(pairs,),
        in_specs=[pl.BlockSpec((1, 2, width), lambda p: (p, 0, 0))],
        out_specs=pl.BlockSpec((1, width - QB, 2 * QB), lambda p: (p, 0, 0)),
        out_shape=jax.ShapeDtypeStruct((pairs, width - QB, 2 * QB), F32),
        compiler_params=params(),
        name="toeplitz",
    )(offset_bias.reshape(pairs, 2, width))


def diagonal_kernel(a_ref, s_ref):
    total = a_ref[0, 0]
    for extra in range(1, a_ref.shape[0]):
        total = total + a_ref[extra, 0]
    total = jnp.concatenate([jnp.zeros((QB, 2 * QB), F32), total], axis=0)
    width = total.shape[0]
    row = lax.broadcasted_iota(jnp.int32, (QB, QB), 0)
    col = lax.broadcasted_iota(jnp.int32, (QB, QB), 1)
    mirror = jnp.where(row + col == QB - 1, 1.0, 0.0)
    for head in range(2):
        turned = lax.dot_general(
            mirror,
            total[:, head * QB : (head + 1) * QB],
            (((1,), (1,)), ((), ())),
            precision=lax.Precision.HIGHEST,
            preferred_element_type=F32,
        )
        aligned = pltpu.roll(turned, width - QB + 1, 1, stride=1, stride_axis=0)
        s_ref[0, head : head + 1, :] = jnp.sum(aligned, axis=0, keepdims=True)


def diagonals(tables, steps):
    _, pairs, rows, _ = tables.shape
    width = rows + QB
    out = pl.pallas_call(
        diagonal_kernel,
        grid=(pairs,),
        in_specs=[pl.BlockSpec((steps, 1, rows, 2 * QB), lambda p: (0, p, 0, 0))],
        out_specs=pl.BlockSpec((1, 2, width), lambda p: (p, 0, 0)),
        out_shape=jax.ShapeDtypeStruct((pairs, 2, width), F32),
        compiler_params=params(),
        name="diagonals",
    )(tables)
    return out.reshape(2 * pairs, width)


def two_heads(block, first):
    zero = jnp.zeros_like(block)
    return jnp.concatenate([jnp.where(first, block, zero), jnp.where(first, zero, block)], axis=0)


def joined_heads(turned):
    return jnp.concatenate([turned[:DH, :QB], turned[DH:, QB:]], axis=0).T


def fill_columns(segq_ref, segk_ref):
    for block in range(segq_ref.shape[0]):
        rows = jnp.broadcast_to(segq_ref[block : block + 1, :], (QB, QB))
        segk_ref[block * QB : (block + 1) * QB, :] = rows.T


def visit_blocks(seg_ref, origin, count, block):
    @pl.loop(0, count)
    def _(i):
        at = i + origin
        first = seg_ref[at * QB]
        last = seg_ref[at * QB + QB - 1]
        far = (seg_ref[(at - 1) * QB - 1] == first) | (seg_ref[(at + 2) * QB] == last)

        @pl.when(far)
        def _():
            block(i, at, 2)

        @pl.when(jnp.logical_not(far))
        def _():
            block(i, at, 1)


def placed_rows(info, source, halo, target, halo_count):
    edge = PAD * QB
    rows = source.shape[0]
    target[:edge, :] = jnp.zeros((edge, target.shape[1]), target.dtype)
    target[target.shape[0] - edge :, :] = jnp.zeros((edge, target.shape[1]), target.dtype)
    target[pl.ds(pl.multiple_of(info[2] * QB, QB), rows), :] = source[...]
    if halo_count:
        target[pl.ds(pl.multiple_of(info[3] * QB, QB), halo_count), :] = halo[...]


def attend_kernel(halo_count, info, seg_ref, *refs):
    if halo_count:
        segq_ref, q_ref, k_ref, v_ref, t_ref, kh_ref, vh_ref, o_ref, lse_ref, kk_ref, vk_ref = refs[:11]
        segk_ref, kp_ref, vp_ref, vt_ref = refs[11:]
        kk_ref[0] = kh_ref[...]
        vk_ref[0] = vh_ref[...]
    else:
        segq_ref, q_ref, k_ref, v_ref, t_ref, o_ref, lse_ref = refs[:7]
        segk_ref, kp_ref, vp_ref, vt_ref = refs[7:]
        kh_ref = vh_ref = None
    rows = q_ref.shape[1]
    pairs = q_ref.shape[2] // (2 * DH)
    first = lax.broadcasted_iota(jnp.int32, (QB, 2 * DH), 1) < DH

    @pl.when(pl.program_id(0) == 0)
    def _():
        fill_columns(segq_ref, segk_ref)

    placed_rows(info, k_ref.at[0], kh_ref, kp_ref, halo_count)
    placed_rows(info, v_ref.at[0], vh_ref, vp_ref, halo_count)
    vt_ref[...] = vp_ref[...].T

    def block(i, at, reach):
        span = (2 * reach + 1) * QB
        keys = pl.ds(pl.multiple_of((at - reach) * QB, QB), span)
        mine = pl.ds(pl.multiple_of(i * QB, QB), QB)
        shifted = pl.ds((2 - reach) * QB, span)
        allowed = segk_ref[keys, :] == segq_ref[pl.ds(at, 1), :]
        allowed = jnp.concatenate([allowed, allowed], axis=1)
        for pair in range(pairs):
            lanes = slice(pair * 2 * DH, (pair + 1) * 2 * DH)
            both = two_heads(q_ref[0, mine, lanes] * LOW(0.125), first)
            scores = dot_nt(kp_ref[keys, lanes], both) + t_ref[pair, shifted, :]
            scores = jnp.where(allowed, scores, -jnp.inf)
            highest = jnp.max(scores, axis=0, keepdims=True)
            weights = jnp.exp(scores - highest)
            totals = jnp.sum(weights, axis=0, keepdims=True)
            probs = (weights * (1.0 / totals)).astype(LOW)
            turned = dot_nn(vt_ref[lanes, keys], probs)
            o_ref[0, mine, lanes] = joined_heads(turned).astype(LOW)
            lse_ref[0, pair, pl.ds(i, 1), :] = highest + jnp.log(totals)

    visit_blocks(seg_ref, info[2], rows // QB, block)


def head_specs(rows, span, groups, halo_count):
    column = lambda part: pl.BlockSpec((1, rows, span), lambda g, s, t: (s[1], 0, g + part * groups))
    halo = lambda part: pl.BlockSpec((halo_count, span), lambda g, s, t: (0, g + part * groups))
    return column, halo


def attend(info, segments, qkv, halo, bias, previous):
    _, rows, width = qkv.shape
    width = width // 3
    span = min(256, width)
    groups = width // span
    pairs = span // (2 * DH)
    count = rows // QB
    blocks = segments.shape[0] // QB
    halo_count = 0 if halo is None else halo.shape[0]
    column, halo_spec = head_specs(rows, span, groups, halo_count)
    slot_pairs = pl.BlockSpec((1, pairs, count, 2 * QB), lambda g, s, t: (s[1], g, 0, 0))
    in_specs = [
        pl.BlockSpec((blocks, QB), lambda g, s, t: (0, 0)),
        column(0),
        column(1),
        column(2),
        pl.BlockSpec((pairs,) + bias.shape[1:], lambda g, s, t: (g, 0, 0)),
    ]
    inputs = [segments.reshape(blocks, QB), qkv, qkv, qkv, bias]
    outputs = [slotted((rows, width), LOW), slotted((groups * pairs, count, 2 * QB), F32)]
    out_specs = [column(0), slot_pairs]
    if halo_count:
        in_specs += [halo_spec(0), halo_spec(1)]
        inputs += [halo, halo]
        outputs += [slotted((halo_count, width), LOW)] * 2
        kept = pl.BlockSpec((1, halo_count, span), lambda g, s, t: (s[1], 0, g))
        out_specs += [kept, kept]
    return call_with_slots(
        functools.partial(attend_kernel, halo_count),
        [info, segments],
        inputs,
        in_specs,
        outputs,
        out_specs,
        previous,
        (groups,),
        [
            pltpu.VMEM((blocks * QB, QB), jnp.int32),
            pltpu.VMEM((blocks * QB, span), LOW),
            pltpu.VMEM((blocks * QB, span), LOW),
            pltpu.VMEM((span, blocks * QB), LOW),
        ],
        "attend",
    )


def attend_back_kernel(halo_count, info, seg_ref, *refs):
    if halo_count:
        segq_ref, q_ref, k_ref, v_ref, g_ref, t_ref, lse_ref, kh_ref, vh_ref = refs[:9]
        dq_ref, dk_ref, dv_ref, diag_ref, dh_ref = refs[9:14]
        segk_ref, kp_ref, vp_ref, kt_ref, dk_acc, dv_acc = refs[14:]
        kh_ref, vh_ref = kh_ref.at[0], vh_ref.at[0]
    else:
        segq_ref, q_ref, k_ref, v_ref, g_ref, t_ref, lse_ref = refs[:7]
        dq_ref, dk_ref, dv_ref, diag_ref = refs[7:11]
        segk_ref, kp_ref, vp_ref, kt_ref, dk_acc, dv_acc = refs[11:]
        kh_ref = vh_ref = None
    rows = q_ref.shape[1]
    pairs = q_ref.shape[2] // (2 * DH)
    first = lax.broadcasted_iota(jnp.int32, (QB, 2 * DH), 1) < DH

    @pl.when(pl.program_id(0) == 0)
    def _():
        fill_columns(segq_ref, segk_ref)

    placed_rows(info, k_ref.at[0], kh_ref, kp_ref, halo_count)
    placed_rows(info, v_ref.at[0], vh_ref, vp_ref, halo_count)
    kt_ref[...] = kp_ref[...].T
    dk_acc[...] = jnp.zeros_like(dk_acc)
    dv_acc[...] = jnp.zeros_like(dv_acc)
    diag_ref[...] = jnp.zeros_like(diag_ref)

    def block(i, at, reach):
        span = (2 * reach + 1) * QB
        keys = pl.ds(pl.multiple_of((at - reach) * QB, QB), span)
        mine = pl.ds(pl.multiple_of(i * QB, QB), QB)
        shifted = pl.ds((2 - reach) * QB, span)
        allowed = segk_ref[keys, :] == segq_ref[pl.ds(at, 1), :]
        allowed = jnp.concatenate([allowed, allowed], axis=1)
        for pair in range(pairs):
            lanes = slice(pair * 2 * DH, (pair + 1) * 2 * DH)
            both = two_heads(q_ref[0, mine, lanes] * LOW(0.125), first)
            grads = two_heads(g_ref[mine, lanes], first)
            scores = dot_nt(kp_ref[keys, lanes], both) + t_ref[pair, shifted, :]
            scores = jnp.where(allowed, scores - lse_ref[0, pair, pl.ds(i, 1), :], -jnp.inf)
            probs = jnp.exp(scores)
            grad_probs = dot_nt(vp_ref[keys, lanes], grads)
            dv_acc[keys, lanes] += dot_nn(probs.astype(LOW), grads)
            inner = jnp.sum(probs * grad_probs, axis=0, keepdims=True)
            rounded = (probs * (grad_probs - inner)).astype(LOW)
            dk_acc[keys, lanes] += dot_nn(rounded, both)
            diag_ref[0, pair, shifted, :] += rounded.astype(F32)
            turned = dot_nn(kt_ref[lanes, keys], rounded)
            dq_ref[mine, lanes] = (joined_heads(turned) * 0.125).astype(LOW)

    visit_blocks(seg_ref, info[2], rows // QB, block)
    own = pl.ds(pl.multiple_of(info[2] * QB, QB), rows)
    dk_ref[...] = dk_acc[own, :].astype(LOW)
    dv_ref[...] = dv_acc[own, :].astype(LOW)
    if halo_count:
        far = pl.ds(pl.multiple_of(info[3] * QB, QB), halo_count)
        dh_ref[0] = dk_acc[far, :].astype(LOW)
        dh_ref[1] = dv_acc[far, :].astype(LOW)


def attend_back(info, segments, qkv, halo_kept, grad_context, bias, lse, previous):
    _, rows, width = qkv.shape
    width = width // 3
    span = min(256, width)
    groups = width // span
    pairs = span // (2 * DH)
    count = rows // QB
    blocks = segments.shape[0] // QB
    halo_count = 0 if halo_kept is None else halo_kept[0].shape[1]
    column, _ = head_specs(rows, span, groups, halo_count)
    plain = pl.BlockSpec((rows, span), lambda g, s, t: (0, g))
    in_specs = [
        pl.BlockSpec((blocks, QB), lambda g, s, t: (0, 0)),
        column(0),
        column(1),
        column(2),
        plain,
        pl.BlockSpec((pairs,) + bias.shape[1:], lambda g, s, t: (g, 0, 0)),
        pl.BlockSpec((1, pairs, count, 2 * QB), lambda g, s, t: (s[1], g, 0, 0)),
    ]
    inputs = [segments.reshape(blocks, QB), qkv, qkv, qkv, grad_context, bias, lse]
    plain_shape = jax.ShapeDtypeStruct((rows, width), LOW)
    outputs = [plain_shape] * 3 + [slotted(bias.shape, F32)]
    out_specs = [plain] * 3 + [
        pl.BlockSpec((1, pairs) + bias.shape[1:], lambda g, s, t: (s[1], g, 0, 0))
    ]
    if halo_count:
        kept = pl.BlockSpec((1, halo_count, span), lambda g, s, t: (s[1], 0, g))
        in_specs += [kept, kept]
        inputs += list(halo_kept)
        outputs.append(jax.ShapeDtypeStruct((2, halo_count, width), LOW))
        out_specs.append(pl.BlockSpec((2, halo_count, span), lambda g, s, t: (0, 0, lax.rem(g + groups // 2, groups))))
    keep = None if previous is None else [None] * 3 + [previous] + [None] * (len(outputs) - 4)
    return call_with_slots(
        functools.partial(attend_back_kernel, halo_count),
        [info, segments],
        inputs,
        in_specs,
        outputs,
        out_specs,
        keep,
        (groups,),
        [
            pltpu.VMEM((blocks * QB, QB), jnp.int32),
            pltpu.VMEM((blocks * QB, span), LOW),
            pltpu.VMEM((blocks * QB, span), LOW),
            pltpu.VMEM((span, blocks * QB), LOW),
            pltpu.VMEM((blocks * QB, span), F32),
            pltpu.VMEM((blocks * QB, span), F32),
        ],
        "attend_back",
    )


def mean_of(block):
    return jnp.mean(block, axis=-1, keepdims=True)


def rms_scale(block):
    return lax.rsqrt(mean_of(block * block) + 1e-06)


def sum_rows(block):
    return jnp.sum(block, axis=0, keepdims=True)


def gelu_parts(u):
    depth = jnp.abs(u) * 0.7071067811865476
    divisor = 1.0 + 0.3275911 * depth
    t = pl.reciprocal(divisor, approx=True)
    t = t * (2.0 - divisor * t)
    series = ((((1.061405429 * t - 1.453152027) * t + 1.421413741) * t - 0.284496736) * t + 0.254829592) * t
    bell = jnp.exp(-0.5 * u * u)
    tail = 0.5 * series * bell
    below = jnp.where(u >= 0.0, 1.0 - tail, tail)
    return u * below, below + u * bell * 0.3989422804014327


def enter_kernel(info, first_ref, second_ref, gain_ref, shift_ref, own_ref, oth_ref, x_ref, e_ref, qkv_ref, halo_ref):
    m = pl.program_id(0)
    half = own_ref.shape[1]

    @pl.when((m == 0) & (info[0] == 1))
    def _():
        x_ref[0] = first_ref[...]
        e_ref[0] = first_ref[...]

    @pl.when((m == 0) & (info[0] == 0))
    def _():
        x_ref[0] = second_ref[...]
        x = second_ref[...].astype(F32)
        e_ref[0] = (x * rms_scale(x) * gain_ref[...]).astype(LOW)

    e = e_ref[0]
    for part, weight in enumerate((own_ref, oth_ref)):
        lanes = slice(part * half, (part + 1) * half)
        block = (dot_nn(e, weight[...]) + shift_ref[:, lanes]).astype(LOW)
        qkv_ref[0, :, lanes] = block
    start = pl.ds(pl.multiple_of(info[4], QB), halo_ref.shape[0])
    halo_ref[:, :half] = qkv_ref[0, start, half:]
    halo_ref[:, half:] = qkv_ref[0, start, :half]


def enter(info, first, second, gain, shift, own, oth, previous):
    rows, width = first.shape
    half = own.shape[1] // 3
    whole = pl.BlockSpec((rows, width), lambda m, s: (0, 0))
    weight = pl.BlockSpec((width, half), lambda m, s: (0, m))
    kept = pl.BlockSpec((1, rows, width), lambda m, s: (s[1], 0, 0))
    keep = None if previous is None else list(previous) + [None]
    return call_with_slots(
        enter_kernel,
        [info],
        [first, second, gain, shift, own, oth],
        [
            whole,
            whole,
            pl.BlockSpec((1, width), lambda m, s: (0, 0)),
            pl.BlockSpec((1, 2 * half), lambda m, s: (0, m)),
            weight,
            weight,
        ],
        [
            slotted((rows, width), LOW),
            slotted((rows, width), LOW),
            slotted((rows, 6 * half), LOW),
            jax.ShapeDtypeStruct((REACH, 4 * half), LOW),
        ],
        [
            kept,
            kept,
            pl.BlockSpec((1, rows, 2 * half), lambda m, s: (s[1], 0, m)),
            pl.BlockSpec((REACH, 2 * half), lambda m, s: (0, jnp.maximum(m - 1, 0))),
        ],
        keep,
        (3,),
        [],
        "enter",
    )


def feed_kernel(
    info, x_ref, c_ref, wo_own, wo_oth, up_own, up_oth, down_own, down_oth, bias_ref, gain_ref, shift_ref,
    f_ref, slope_ref, n_ref, one_ref, two_ref, out_ref, acc_ref, carry_ref
):
    j = pl.program_id(0)
    steps = pl.num_programs(0)
    half = wo_own.shape[0]
    rows = x_ref.shape[1]

    @pl.when(j == 0)
    def _():
        joined = (
            dot_nn(c_ref[0, :, :half], wo_own[...])
            + dot_nn(c_ref[0, :, half:], wo_oth[...])
            + x_ref[0].astype(F32)
        )

        @pl.when(info[0] == 1)
        def _():
            before = joined + shift_ref[0:1, :]
            one_ref[0] = before
            center = before - mean_of(before)
            normed = center * lax.rsqrt(mean_of(center * center) + 1e-05) * gain_ref[0:1, :] + shift_ref[2:3, :]
            carry_ref[...] = normed
            n_ref[0] = normed.astype(LOW)

        @pl.when(info[0] == 0)
        def _():
            one_ref[0] = joined
            carry_ref[...] = joined
            n_ref[0] = (joined * rms_scale(joined) * gain_ref[1:2, :]).astype(LOW)

        acc_ref[...] = jnp.zeros_like(acc_ref)

    def part(up, down):
        for at in range(0, rows, 256):
            piece = slice(at, at + 256)
            u = dot_nn(n_ref[0, piece, :], up[...]) + bias_ref[...]
            f, slope = gelu_parts(u)
            low = f.astype(LOW)
            f_ref[0, piece, :] = low
            slope_ref[0, piece, :] = slope.astype(LOW)
            acc_ref[piece, :] += dot_nn(low, down[...])

    @pl.when(j < steps // 2)
    def _():
        part(up_own, down_own)

    @pl.when(j >= steps // 2)
    def _():
        part(up_oth, down_oth)

    @pl.when(j == steps - 1)
    def _():
        joined = carry_ref[...] + acc_ref[...]

        @pl.when(info[0] == 1)
        def _():
            before = joined + shift_ref[1:2, :]
            two_ref[0] = before
            center = before - mean_of(before)
            normed = center * lax.rsqrt(mean_of(center * center) + 1e-05) * gain_ref[1:2, :] + shift_ref[3:4, :]
            out_ref[...] = normed.astype(LOW)

        @pl.when(info[0] == 0)
        def _():
            two_ref[0] = joined
            out_ref[...] = joined.astype(LOW)


def split_steps(hidden, chunk):
    each = hidden // chunk
    near = lambda j: jnp.minimum(j, each - 1)
    far = lambda j: jnp.maximum(j - each, 0)
    return 2 * each, near, far


def feed(info, x, context, wo, up, down, bias, gains, shifts, previous):
    _, rows, width = x.shape
    hidden = up[0].shape[1]
    chunk = min(512, hidden)
    steps, near, far = split_steps(hidden, chunk)
    kept = pl.BlockSpec((1, rows, width), lambda j, s: (s[1], 0, 0))
    fixed = lambda a: pl.BlockSpec(a.shape, lambda j, s: (0, 0))
    moving = pl.BlockSpec((1, rows, chunk), lambda j, s: (s[1], 0, j))
    keep = None if previous is None else list(previous) + [None]
    return call_with_slots(
        feed_kernel,
        [info],
        [x, context, wo[0], wo[1], up[0], up[1], down[0], down[1], bias, gains, shifts],
        [
            kept,
            kept,
            fixed(wo[0]),
            fixed(wo[1]),
            pl.BlockSpec((width, chunk), lambda j, s: (0, near(j))),
            pl.BlockSpec((width, chunk), lambda j, s: (0, far(j))),
            pl.BlockSpec((chunk, width), lambda j, s: (near(j), 0)),
            pl.BlockSpec((chunk, width), lambda j, s: (far(j), 0)),
            pl.BlockSpec((1, chunk), lambda j, s: (0, j)),
            fixed(gains),
            fixed(shifts),
        ],
        [
            slotted((rows, 2 * hidden), LOW),
            slotted((rows, 2 * hidden), LOW),
            slotted((rows, width), LOW),
            slotted((rows, width), F32),
            slotted((rows, width), F32),
            jax.ShapeDtypeStruct((rows, width), LOW),
        ],
        [moving, moving, kept, kept, kept, pl.BlockSpec((rows, width), lambda j, s: (0, 0))],
        keep,
        (steps,),
        [pltpu.VMEM((rows, width), F32), pltpu.VMEM((rows, width), F32)],
        "feed",
    )


def layer_norm_back(before, grad, gain_row):
    center = before - mean_of(before)
    scale = lax.rsqrt(mean_of(center * center) + 1e-05)
    unit = center * scale
    inner = grad * gain_row
    back = scale * (inner - mean_of(inner) - unit * mean_of(inner * unit))
    return back, sum_rows(grad * unit)


def rms_norm_back(before, grad, gain_row):
    scale = rms_scale(before)
    unit = before * scale
    inner = grad * gain_row
    back = scale * (inner - unit * mean_of(inner * unit))
    return back, sum_rows(grad * unit)


def feed_back_kernel(
    info, got_ref, mine_ref, other_ref, one_ref, two_ref, slope_ref, wo_own, wo_oth, up_own, up_oth, down_own, down_oth,
    gain_ref, dy_ref, du_ref, db_ref, stat_ref, bias_ref, dz_ref, dc_ref, acc_ref, carry_ref
):
    j = pl.program_id(0)
    steps = pl.num_programs(0)
    half = wo_own.shape[0]
    rows = got_ref.shape[0]

    @pl.when(j == 0)
    def _():
        stat_ref[...] = jnp.zeros_like(stat_ref)
        acc_ref[...] = jnp.zeros_like(acc_ref)

        @pl.when(info[0] == 1)
        def _():
            grad = got_ref[...].astype(F32)
            back, gain = layer_norm_back(two_ref[0], grad, gain_ref[1:2, :])
            stat_ref[0, 1:2, :] = gain
            stat_ref[0, 5:6, :] = sum_rows(grad)
            stat_ref[0, 3:4, :] = sum_rows(back)
            carry_ref[...] = back
            dy_ref[0] = back.astype(LOW)

        @pl.when(info[0] == 0)
        def _():
            grad = mine_ref[...].astype(F32) + other_ref[...].astype(F32)
            carry_ref[...] = grad
            dy_ref[0] = grad.astype(LOW)

    def part(up, down):
        for at in range(0, rows, 256):
            piece = slice(at, at + 256)
            grad = dot_nt(dy_ref[0, piece, :], down[...])
            low = (grad * slope_ref[0, piece, :].astype(F32)).astype(LOW)
            du_ref[0, piece, :] = low
            acc_ref[piece, :] += dot_nt(low, up[...])
        bias_ref[0] = sum_rows(du_ref[0].astype(F32))

    @pl.when(j < steps // 2)
    def _():
        part(up_own, down_own)

    @pl.when(j >= steps // 2)
    def _():
        part(up_oth, down_oth)

    @pl.when(j == steps - 1)
    def _():
        @pl.when(info[0] == 1)
        def _():
            grad = acc_ref[...] + carry_ref[...]
            back, gain = layer_norm_back(one_ref[0], grad, gain_ref[0:1, :])
            stat_ref[0, 0:1, :] = gain
            stat_ref[0, 4:5, :] = sum_rows(grad)
            stat_ref[0, 2:3, :] = sum_rows(back)
            dz_ref[...] = back

        @pl.when(info[0] == 0)
        def _():
            back, gain = rms_norm_back(one_ref[0], acc_ref[...], gain_ref[1:2, :])
            stat_ref[0, 1:2, :] = gain
            dz_ref[...] = carry_ref[...] + back

        low = dz_ref[...].astype(LOW)
        db_ref[0] = low
        dc_ref[:, :half] = dot_nt(low, wo_own[...]).astype(LOW)
        dc_ref[:, half:] = dot_nt(low, wo_oth[...]).astype(LOW)


def feed_back(info, got, mine, other, one, two, slope, wo, up, down, gains, previous):
    _, rows, width = one.shape
    hidden = up[0].shape[1]
    chunk = min(512, hidden)
    steps, near, far = split_steps(hidden, chunk)
    kept = pl.BlockSpec((1, rows, width), lambda j, s: (s[1], 0, 0))
    fixed = lambda a: pl.BlockSpec(a.shape, lambda j, s: (0, 0))
    plain = pl.BlockSpec((rows, width), lambda j, s: (0, 0))
    moving = pl.BlockSpec((1, rows, chunk), lambda j, s: (s[1], 0, j))
    keep = None if previous is None else list(previous) + [None, None]
    return call_with_slots(
        feed_back_kernel,
        [info],
        [got, mine, other, one, two, slope, wo[0], wo[1], up[0], up[1], down[0], down[1], gains],
        [
            plain,
            plain,
            plain,
            kept,
            kept,
            moving,
            fixed(wo[0]),
            fixed(wo[1]),
            pl.BlockSpec((width, chunk), lambda j, s: (0, near(j))),
            pl.BlockSpec((width, chunk), lambda j, s: (0, far(j))),
            pl.BlockSpec((chunk, width), lambda j, s: (near(j), 0)),
            pl.BlockSpec((chunk, width), lambda j, s: (far(j), 0)),
            fixed(gains),
        ],
        [
            slotted((rows, width), LOW),
            slotted((rows, 2 * hidden), LOW),
            slotted((rows, width), LOW),
            slotted((8, width), F32),
            slotted((1, 2 * hidden), F32),
            jax.ShapeDtypeStruct((rows, width), F32),
            jax.ShapeDtypeStruct((rows, width), LOW),
        ],
        [
            kept,
            moving,
            kept,
            pl.BlockSpec((1, 8, width), lambda j, s: (s[1], 0, 0)),
            pl.BlockSpec((1, 1, chunk), lambda j, s: (s[1], 0, j)),
            plain,
            plain,
        ],
        keep,
        (steps,),
        [pltpu.VMEM((rows, width), F32), pltpu.VMEM((rows, width), F32)],
        "feed_back",
    )


def enter_back_kernel(
    info, dq_ref, dk_ref, dv_ref, far_ref, x_ref, dz_ref, own_ref, oth_ref, gain_ref,
    d_ref, stat_ref, low_ref, lower_ref, acc_ref
):
    m = pl.program_id(0)
    half = own_ref.shape[1]
    start = pl.ds(pl.multiple_of(info[4], QB), far_ref.shape[1])

    @pl.when(m == 0)
    def _():
        stat_ref[...] = jnp.zeros_like(stat_ref)
        acc_ref[...] = jnp.zeros_like(acc_ref)
        d_ref[0] = dq_ref[...]
        stat_ref[0, 0:1, :] = sum_rows(dq_ref[...].astype(F32))

    def with_far(block_ref, part):
        d_ref[0] = block_ref[...]
        d_ref[0, start, :] = (block_ref[start, :].astype(F32) + far_ref[part].astype(F32)).astype(LOW)

    @pl.when(m == 1)
    def _():
        with_far(dk_ref, 0)

    @pl.when(m == 2)
    def _():
        with_far(dv_ref, 1)
        stat_ref[0, 1:2, :] = sum_rows(d_ref[0].astype(F32))

    acc_ref[...] += dot_nt(d_ref[0, :, :half], own_ref[...]) + dot_nt(d_ref[0, :, half:], oth_ref[...])

    @pl.when(m == 2)
    def _():
        split = lower_ref.shape[1]

        @pl.when(info[0] == 1)
        def _():
            total = dz_ref[...] + acc_ref[...]
            low_ref[...] = total.astype(LOW)
            lower_ref[...] = total[:, :split]

        @pl.when(info[0] == 0)
        def _():
            back, gain = rms_norm_back(x_ref[0].astype(F32), acc_ref[...], gain_ref[...])
            stat_ref[0, 2:3, :] = gain
            total = dz_ref[...] + back
            low_ref[...] = total.astype(LOW)
            lower_ref[...] = total[:, :split]


def enter_back(info, dq, dk, dv, far, x, dz, own, oth, gain, previous):
    _, rows, width = x.shape
    half = own.shape[1] // 3
    plain = pl.BlockSpec((rows, width), lambda m, s: (0, 0))
    kept = pl.BlockSpec((1, rows, width), lambda m, s: (s[1], 0, 0))
    weight = pl.BlockSpec((width, half), lambda m, s: (0, m))
    keep = None if previous is None else list(previous) + [None, None]
    return call_with_slots(
        enter_back_kernel,
        [info],
        [dq, dk, dv, far, x, dz, own, oth, gain],
        [
            plain,
            plain,
            plain,
            pl.BlockSpec(far.shape, lambda m, s: (0, 0, 0)),
            kept,
            plain,
            weight,
            weight,
            pl.BlockSpec((1, width), lambda m, s: (0, 0)),
        ],
        [
            slotted((rows, 6 * half), LOW),
            slotted((8, width), F32),
            jax.ShapeDtypeStruct((rows, width), LOW),
            jax.ShapeDtypeStruct((rows, width // 2), F32),
        ],
        [
            pl.BlockSpec((1, rows, 2 * half), lambda m, s: (s[1], 0, m)),
            pl.BlockSpec((1, 8, width), lambda m, s: (s[1], 0, 0)),
            plain,
            pl.BlockSpec((rows, width // 2), lambda m, s: (0, 0)),
        ],
        keep,
        (3,),
        [pltpu.VMEM((rows, width), F32)],
        "enter_back",
    )


def wide_kernel(left_ref, right_ref, own_ref, oth_ref, turned_ref):
    j = pl.program_id(0)
    rows = left_ref.shape[1]

    @pl.when(j == 0)
    def _():
        for slot in range(2):
            turned_ref[:, slot * rows : (slot + 1) * rows] = left_ref[slot].T

    both = jnp.concatenate([right_ref[0], right_ref[1]], axis=0)
    product = dot_nn(turned_ref[...], both).astype(LOW)

    @pl.when(lax.rem(j, 2) == 0)
    def _():
        own_ref[...] = product

    @pl.when(lax.rem(j, 2) == 1)
    def _():
        oth_ref[...] = product


def wide_grad(left, right, chunk, position, name):
    _, rows, width = left.shape
    total = right.shape[2]
    steps = total // chunk
    out = jax.ShapeDtypeStruct((width, total // 2), LOW)
    spec = pl.BlockSpec((width, chunk), lambda j: (0, j // 2))
    return pl.pallas_call(
        wide_kernel,
        grid=(steps,),
        in_specs=[
            pl.BlockSpec((2, rows, width), lambda j: (0, 0, 0)),
            pl.BlockSpec((2, rows, chunk), lambda j: (0, 0, position(j))),
        ],
        out_specs=[spec, spec],
        out_shape=[out, out],
        scratch_shapes=[pltpu.VMEM((width, 2 * rows), LOW)],
        compiler_params=params(),
        name=name,
    )(left, right)


def tall_kernel(left_ref, right_ref, own_ref, oth_ref):
    j = pl.program_id(0)
    piece = own_ref.shape[2]
    turned = jnp.concatenate([left_ref[0].T, left_ref[1].T], axis=1)
    both = jnp.concatenate([right_ref[0], right_ref[1]], axis=0)
    product = dot_nn(turned, both).astype(LOW)

    def store(ref):
        for at in range(ref.shape[0]):
            ref[at] = product[:, at * piece : (at + 1) * piece]

    @pl.when(lax.rem(j, 2) == 0)
    def _():
        store(own_ref)

    @pl.when(lax.rem(j, 2) == 1)
    def _():
        store(oth_ref)


def tall_grad(left, right, chunk, pieces, name):
    _, rows, total = left.shape
    width = right.shape[2]
    each = total // 2 // chunk
    out = jax.ShapeDtypeStruct((pieces, total // 2, width // pieces), LOW)
    spec = pl.BlockSpec((pieces, chunk, width // pieces), lambda j: (0, j // 2, 0))
    return pl.pallas_call(
        tall_kernel,
        grid=(2 * each,),
        in_specs=[
            pl.BlockSpec((2, rows, chunk), lambda j: (0, 0, lax.rem(j, 2) * each + j // 2)),
            pl.BlockSpec((2, rows, width), lambda j: (0, 0, 0)),
        ],
        out_specs=[spec, spec],
        out_shape=[out, out],
        compiler_params=params(),
        name=name,
    )(left, right)


def passed_along(value, axis, steps):
    count = lax.axis_size(axis)
    initial, last = (max(0, -steps), min(count, count - steps))
    return lax.ppermute(value, axis, [(source, source + steps) for source in range(initial, last)])


def spread(block, axis, source):
    block = jnp.where(lax.axis_index(axis) == source, block, jnp.zeros_like(block))
    return lax.psum(block, axis)


def layer_norm(operand, gain_row, shift_row):
    center = operand - jnp.mean(operand, axis=-1, keepdims=True)
    variance = jnp.mean(center * center, axis=-1, keepdims=True)
    return center * lax.rsqrt(variance + 1e-05) * gain_row + shift_row


def rms_norm(operand, gain_row):
    return (
        operand * lax.rsqrt(jnp.mean(operand * operand, axis=-1, keepdims=True) + 1e-06) * gain_row
    )


def gelu_act(operand):
    return jax.nn.gelu(operand, approximate=False)


def gelu_slope(operand):
    return (
        0.5 * (1.0 + jax.scipy.special.erf(operand * 0.7071067811865476))
        + operand * jnp.exp(-0.5 * operand * operand) * 0.3989422804014327
    )


def entry_norm(residual, gain_rows, leading):
    return jnp.where(leading, residual, rms_norm(residual, gain_rows[0]))


def middle(residual, branch, gain_rows, shift_rows, leading):
    joined = residual + branch
    bert_rows = layer_norm(joined + shift_rows[0], gain_rows[0], shift_rows[2])
    carried = jnp.where(leading, bert_rows, joined)
    normed = jnp.where(leading, bert_rows, rms_norm(joined, gain_rows[1]))
    return (carried, normed)


def final(carried, second, gain_rows, shift_rows, leading):
    joined = carried + second
    return jnp.where(
        leading, layer_norm(joined + shift_rows[1], gain_rows[1], shift_rows[3]), joined
    )


def contract_rows(left, right):
    return lax.dot_general(
        left, right, (((0,), (0,)), ((), ())), preferred_element_type=jnp.float32
    )


def contract_cols(left, right):
    return lax.dot_general(
        left, right, (((1,), (1,)), ((), ())), preferred_element_type=jnp.float32
    )


def gather_rows(operand, weight):
    return (
        jnp.dot(
            lax.all_gather(operand, "tensor", axis=0, tiled=True),
            weight,
            preferred_element_type=jnp.float32,
        ),
        None,
    )


def collect(full_rows, weight):
    return lax.psum_scatter(
        jnp.dot(full_rows, weight, preferred_element_type=jnp.float32),
        "tensor",
        scatter_dimension=0,
        tiled=True,
    )


def scatter_back(grad_rows, weight):
    return lax.psum_scatter(
        contract_cols(grad_rows, weight).astype(jnp.bfloat16),
        "tensor",
        scatter_dimension=0,
        tiled=True,
    ).astype(jnp.float32)


def fold_back(grad_share, weight, activations):
    fragment = lax.all_gather(grad_share, "tensor", axis=0, tiled=True)
    product_rows = contract_cols(fragment, weight)
    return (product_rows, contract_rows(activations, fragment))


def weight_grad(operand, grad_rows):
    return contract_rows(lax.all_gather(operand, "tensor", axis=0, tiled=True), grad_rows)


DH = 64
QB = 128
NARROW = 3
WIDE = 5
VMEM = 56 * 1024 * 1024


def padded(segments):
    return jnp.pad(segments, (PAD * QB, PAD * QB), constant_values=-1)


def general_body(
    layer_input,
    segment_ids,
    buckets,
    attn_in,
    attn_out,
    ffn_in,
    ffn_out,
    norm_gain,
    bert_shift,
    head_bias,
    ffn_bias,
    position_bias,
    decoder_grads,
):
    micro_count = layer_input.shape[0]
    shard_rows = layer_input.shape[2]
    model_width = layer_input.shape[3]
    length = segment_ids.shape[2]
    leading = lax.axis_index("section") == 0
    weighting = jnp.where(leading, 1.0, 0.0)
    qkv_weight = attn_in[0].reshape(model_width, -1)
    out_weight = attn_out[0]
    ffn_up = ffn_in[0]
    ffn_down = ffn_out[0]
    gain_rows = jnp.where(leading, norm_gain[0], norm_gain[1])
    head_shift = head_bias * weighting
    qkv_shift = jnp.concatenate([head_shift[0], jnp.zeros_like(head_shift[0]), head_shift[1]])
    ffn_shift = ffn_bias * weighting
    bias_table = position_bias * (1.0 - weighting)
    bucket_hits = (buckets[None, :] == jnp.arange(bias_table.shape[1])[:, None]).astype(jnp.float32)
    offset_bias = jnp.dot(bias_table, bucket_hits, precision=lax.Precision.HIGHEST)
    near = length - 1 - 3 * QB
    bias = toeplitz(offset_bias[:, near : near + 6 * QB])
    info = jnp.array([0, 0, PAD, 0, 0], jnp.int32)
    segment_rows = segment_ids[:, 0]

    def middle_part(residual_in, branch_in, gain_in, shift_in):
        return middle(residual_in, branch_in, gain_in, shift_in, leading)

    def final_part(carried_in, second_in, gain_in, shift_in):
        return final(carried_in, second_in, gain_in, shift_in, leading)

    def entry_part(residual_in, gain_in):
        return entry_norm(residual_in, gain_in, leading)

    received = jnp.zeros((shard_rows, model_width), jnp.bfloat16)
    saved_steps = []
    encoded = []
    for moment in range(micro_count + 1):
        own_rows = layer_input[min(moment, micro_count - 1), 0]
        if moment >= micro_count:
            own_rows = jnp.zeros_like(own_rows)
        segment_row = jnp.where(
            leading, segment_rows[min(moment, micro_count - 1)], segment_rows[max(moment - 1, 0)]
        )
        forward_incoming = jnp.where(leading, own_rows, received)
        forward_residual = forward_incoming.astype(jnp.float32)
        forward_entered = entry_norm(forward_residual, gain_rows, leading).astype(jnp.bfloat16)
        projected, forward_gathered_in = gather_rows(forward_entered, qkv_weight)
        forward_qkv = (projected + qkv_shift).astype(jnp.bfloat16)
        forward_context, forward_log_totals = attend(
            info, padded(segment_row), forward_qkv[None], None, bias, None
        )
        forward_context = forward_context[0]
        forward_branch = collect(forward_context, out_weight)
        forward_carried, forward_normed = middle(
            forward_residual, forward_branch, gain_rows, bert_shift, leading
        )
        pre_full, forward_gathered_mid = gather_rows(forward_normed.astype(jnp.bfloat16), ffn_up)
        forward_pre_act = pre_full + ffn_shift
        forward_second = collect(gelu_act(forward_pre_act).astype(jnp.bfloat16), ffn_down)
        result = final(forward_carried, forward_second, gain_rows, bert_shift, leading).astype(
            jnp.bfloat16
        )
        result, saved = (
            result,
            (
                forward_incoming,
                segment_row,
                forward_branch,
                forward_second,
                forward_qkv,
                forward_context,
                forward_log_totals,
                forward_pre_act,
                forward_gathered_in,
                forward_gathered_mid,
            ),
        )
        saved_steps.append(saved)
        if moment >= 1:
            encoded.append(result)
        if moment < micro_count:
            received = passed_along(result, "section", 1)
    delivered = spread(jnp.stack(encoded), "section", 1)
    section_grads = lax.psum(
        decoder_grads[0, :, 0].astype(jnp.float32).astype(jnp.bfloat16), "section"
    ).astype(jnp.float32)
    grad_received = jnp.zeros((shard_rows, model_width), jnp.float32)
    running_terms = None
    input_rows = []
    for moment in range(micro_count + 1):
        own_grad = section_grads[min(moment, micro_count - 1)]
        if moment >= micro_count:
            own_grad = jnp.zeros_like(own_grad)
        earlier = saved_steps[max(moment - 1, 0)]
        later = saved_steps[min(moment + 1, micro_count)]
        chosen = jax.tree.map(
            lambda from_first, from_second: jnp.where(leading, from_first, from_second),
            earlier,
            later,
        )
        (
            incoming,
            backward_segment_row,
            branch,
            second,
            qkv,
            context,
            log_totals,
            pre_act,
            gathered_in,
            gathered_mid,
        ) = chosen
        residual = incoming.astype(jnp.float32)
        (carried, normed), pull_middle = jax.vjp(
            middle_part, residual, branch, gain_rows, bert_shift
        )
        finished, pull_final = jax.vjp(final_part, carried, second, gain_rows, bert_shift)
        grad_carried, grad_second, gain_end, shift_end = pull_final(
            jnp.where(leading, grad_received, own_grad)
        )
        hidden = gelu_act(pre_act).astype(jnp.bfloat16)
        grad_hidden, backward_grad_down = fold_back(
            grad_second.astype(jnp.bfloat16), ffn_down, hidden
        )
        grad_pre = (grad_hidden * gelu_slope(pre_act)).astype(jnp.bfloat16)
        grad_shift = jnp.sum(grad_pre.astype(jnp.float32), axis=0) * weighting
        backward_grad_up = weight_grad(normed.astype(jnp.bfloat16), grad_pre)
        grad_normed = scatter_back(grad_pre, ffn_up)
        grad_residual, grad_branch, gain_mid, shift_mid = pull_middle((grad_carried, grad_normed))
        grad_context, backward_grad_out_weight = fold_back(
            grad_branch.astype(jnp.bfloat16), out_weight, context
        )
        low_q, low_k, low_v, grad_table = attend_back(
            info, padded(backward_segment_row), qkv[None], None, grad_context.astype(jnp.bfloat16), bias, log_totals, None
        )
        grad_table = grad_table[0]
        grad_head = (
            jnp.stack([jnp.sum(low.astype(jnp.float32), axis=0) for low in (low_q, low_v)]) * weighting
        )
        grad_rows = jnp.concatenate([low_q, low_k, low_v], axis=1)
        entered, pull_entry = jax.vjp(entry_part, residual, gain_rows)
        backward_grad_qkv = weight_grad(entered.astype(jnp.bfloat16), grad_rows)
        grad_entered = scatter_back(grad_rows, qkv_weight)
        grad_from_entry, gain_entry = pull_entry(grad_entered)
        grad_terms = (
            backward_grad_qkv,
            backward_grad_out_weight,
            backward_grad_up,
            backward_grad_down,
            gain_end + gain_mid + gain_entry,
            shift_end + shift_mid,
            grad_head,
            grad_shift,
            grad_table,
        )
        grad_input, grad_terms = (grad_residual + grad_from_entry, grad_terms)
        if running_terms is None:
            running_terms = grad_terms
        else:
            running_terms = jax.tree.map(jnp.add, running_terms, grad_terms)
        if moment >= 1:
            input_rows.append(grad_input)
        if moment < micro_count:
            grad_received = passed_along(grad_input.astype(jnp.bfloat16), "section", -1).astype(
                grad_input.dtype
            )
    input_all = jnp.stack(input_rows)
    half_width = model_width // 2
    upper_half = passed_along(
        input_all[:, :, half_width:].astype(jnp.bfloat16), "section", 1
    ).astype(jnp.float32)
    input_grad = jnp.where(leading, input_all[:, :, :half_width], upper_half)[:, None]
    (
        grad_qkv,
        grad_out_weight,
        grad_up,
        grad_down,
        gain_sum,
        shift_sum,
        head_sum,
        shift_ffn_sum,
        table_sum,
    ) = running_terms
    near_hits = bucket_hits[:, near : near + 6 * QB]
    table_sum = jnp.dot(diagonals(table_sum[None], 1), near_hits.T, precision=lax.Precision.HIGHEST) * (
        1.0 - weighting
    )
    weights_out = (
        lax.psum_scatter(
            grad_qkv.reshape(1, model_width, 3, -1).astype(jnp.bfloat16),
            "dp",
            scatter_dimension=1,
            tiled=True,
        ).astype(jnp.float32),
        lax.psum_scatter(
            grad_out_weight[None].astype(jnp.bfloat16), "dp", scatter_dimension=2, tiled=True
        ).astype(jnp.float32),
        lax.psum_scatter(
            grad_up[None].astype(jnp.bfloat16), "dp", scatter_dimension=1, tiled=True
        ).astype(jnp.float32),
        lax.psum_scatter(
            grad_down[None].astype(jnp.bfloat16), "dp", scatter_dimension=2, tiled=True
        ).astype(jnp.float32),
    )
    gain_both = jnp.stack([gain_sum * weighting, gain_sum * (1.0 - weighting)])
    shared_out = lax.psum((gain_both, shift_sum), ("dp", "section", "tensor"))
    split_out = lax.psum((head_sum, shift_ffn_sum, table_sum), ("dp", "section"))
    return (
        delivered[None, :, None],
        input_grad,
        weights_out[0],
        weights_out[1],
        weights_out[2],
        weights_out[3],
        shared_out[0],
        shared_out[1],
        split_out[0],
        split_out[1],
        split_out[2],
    )


def swapped(value, axis, bit):
    pairs = [(at, at ^ bit) for at in range(lax.axis_size(axis))]
    return lax.ppermute(value, axis, pairs)


def halves_summed(total, axis, bit):
    side = lax.rem(lax.axis_index(axis) // bit, 2)
    given = lax.dynamic_index_in_dim(total, 1 - side, 0, keepdims=False)
    kept = lax.dynamic_index_in_dim(total, side, 0, keepdims=False)
    got = swapped(given, axis, bit)
    return (kept.astype(F32) + got.astype(F32)).astype(LOW)


def scattered(own, got):
    total = (own.astype(F32) + got.astype(F32)).astype(LOW)
    rest = own.shape[1:]
    total = jnp.moveaxis(total.reshape((2, 2, 2) + rest), 2, 0)
    total = halves_summed(total, "dp", 1)
    total = jnp.moveaxis(total, 1, 0)
    total = halves_summed(total, "dp", 2)
    side = lax.rem(lax.axis_index("dp") // 4, 2)
    given = lax.dynamic_index_in_dim(total, 1 - side, 0, keepdims=False)
    kept = lax.dynamic_index_in_dim(total, side, 0, keepdims=False)
    return kept.astype(F32) + swapped(given, "dp", 4).astype(F32)


def paired_body(
    layer_input,
    segment_ids,
    buckets,
    attn_in,
    attn_out,
    ffn_in,
    ffn_out,
    norm_gain,
    bert_shift,
    head_bias,
    ffn_bias,
    position_bias,
    decoder_grads,
):
    micro_count, _, rows, width = layer_input.shape
    length = segment_ids.shape[2]
    heads, bucket_count = position_bias.shape
    section = lax.axis_index("section")
    core = lax.axis_index("tensor")
    leading = section == 0
    lead = jnp.where(leading, 1, 0).astype(jnp.int32)
    pieces = lax.axis_size("dp")

    remote_grads = [
        lax.ppermute(decoder_grads[0, micro, 0], "section", [(0, 1)]) for micro in range(micro_count)
    ]
    qkv_own = attn_in[0].reshape(width, -1)
    qkv_oth = swapped(qkv_own, "tensor", 1)
    wo = (attn_out[0], swapped(attn_out[0], "tensor", 1))
    up = (ffn_in[0], swapped(ffn_in[0], "tensor", 1))
    down = (ffn_out[0], swapped(ffn_out[0], "tensor", 1))
    small = jnp.concatenate([head_bias.reshape(-1), ffn_bias, position_bias.reshape(-1)])
    small_oth = swapped(small, "tensor", 1)
    near_heads = head_bias.size
    near_ffn = near_heads + ffn_bias.size
    both_small = jnp.stack([small, small_oth])
    head_both = both_small[:, :near_heads].reshape(2, 2, -1)
    ffn_both = jnp.where(leading, both_small[:, near_heads:near_ffn], 0.0).reshape(1, -1)
    table_both = jnp.where(leading, 0.0, both_small[:, near_ffn:]).reshape(2 * heads, bucket_count)
    q_shift = head_both[:, 0].reshape(1, -1)
    v_shift = head_both[:, 1].reshape(1, -1)
    qkv_shift = jnp.where(
        leading, jnp.concatenate([q_shift, jnp.zeros_like(q_shift), v_shift], axis=1), 0.0
    )
    gains = jnp.where(leading, norm_gain[0], norm_gain[1])
    entry_gain = gains[0:1]

    near = length - 1 - 3 * QB
    near_hits = (buckets[None, near : near + 6 * QB] == jnp.arange(bucket_count)[:, None]).astype(F32)
    bias = toeplitz(jnp.dot(table_both, near_hits, precision=lax.Precision.HIGHEST))

    window = rows + REACH
    base = core * (length - window)
    segments = jnp.pad(
        lax.dynamic_slice_in_dim(segment_ids[:, 0], base, window, axis=1),
        ((0, 0), (PAD * QB, PAD * QB)),
        constant_values=-1,
    )
    reach_blocks = REACH // QB
    own_block = PAD + core * reach_blocks
    halo_block = jnp.where(core == 0, PAD + rows // QB, PAD)
    edge = jnp.where(core == 0, rows - REACH, 0)

    def info_of(slot):
        return jnp.stack([lead, slot, own_block, halo_block, edge]).astype(jnp.int32)

    received = jnp.zeros((rows, width), LOW)
    entered = attended = fed = None
    delivered = []
    for moment in range(micro_count + 1):
        slot = jnp.where(leading, moment, (moment + micro_count) % (micro_count + 1))
        info = info_of(slot)
        micro = jnp.minimum(slot, micro_count - 1)
        own_rows = layer_input[min(moment, micro_count - 1), 0]
        row_segments = lax.dynamic_index_in_dim(segments, micro, 0, keepdims=False)
        *entered, halo = enter(info, own_rows, received, entry_gain, qkv_shift, qkv_own, qkv_oth, entered)
        halo = swapped(halo, "tensor", 1)
        attended = attend(info, row_segments, entered[2], halo, bias, attended)
        *fed, result = feed(
            info, entered[0], attended[0], wo, up, down, ffn_both, gains, bert_shift, fed
        )
        if moment < micro_count:
            received = lax.ppermute(result, "section", [(0, 1)])
        if moment >= 1:
            delivered.append(
                jnp.where(leading, lax.ppermute(result, "section", [(1, 0)]), result)
            )
    x_saved, e_saved, qkv_saved = entered
    context, lse, *halo_saved = attended
    f_saved, slope_saved, n_saved, one_saved, two_saved = fed

    received = jnp.zeros((rows, width), LOW)
    feed_kept = table_kept = entry_kept = None
    input_low = []
    input_lower = []
    for moment in range(micro_count + 1):
        slot = jnp.where(leading, (moment + micro_count) % (micro_count + 1), moment)
        info = info_of(slot)
        micro = jnp.minimum(slot, micro_count - 1)
        at = min(moment, micro_count - 1)
        row_segments = lax.dynamic_index_in_dim(segments, micro, 0, keepdims=False)
        *feed_kept, dz, grad_context = feed_back(
            info, received, decoder_grads[0, at, 0], remote_grads[at], one_saved, two_saved, slope_saved,
            wo, up, down, gains, feed_kept,
        )
        if moment == micro_count:
            dy_saved, du_saved, db_saved, stat_feed, stat_bias = feed_kept
            down_own, down_oth = tall_grad(f_saved, dy_saved, 512, pieces, "down_grad")
            ffn_each = du_saved.shape[2] // 2 // 512
            up_own, up_oth = wide_grad(
                n_saved, du_saved, 512, lambda j: lax.rem(j, 2) * ffn_each + j // 2, "up_grad"
            )
            grad_context, down_oth, up_oth = lax.optimization_barrier((grad_context, down_oth, up_oth))
            down_got = swapped(down_oth, "tensor", 1)
            up_got = swapped(up_oth, "tensor", 1)
            down_sum = scattered(down_own, down_got)
            up_sum = scattered(
                up_own.reshape(pieces, width // pieces, -1), up_got.reshape(pieces, width // pieces, -1)
            )
        dq, dk, dv, table_kept, far = attend_back(
            info, row_segments, qkv_saved, halo_saved, grad_context, bias, lse, table_kept
        )
        far = swapped(far, "tensor", 1)
        *entry_kept, low, lower = enter_back(
            info, dq, dk, dv, far, x_saved, dz, qkv_own, qkv_oth, entry_gain, entry_kept
        )
        if moment >= 1:
            input_low.append(low)
            input_lower.append(lower)
        if moment < micro_count:
            received = lax.ppermute(low, "section", [(1, 0)])
    dqkv_saved, stat_entry = entry_kept

    out_own, out_oth = tall_grad(context, db_saved, 512, pieces, "out_grad")
    qkv_sum_own, qkv_sum_oth = wide_grad(e_saved, dqkv_saved, 512, lambda j: j, "qkv_grad")
    out_sum = scattered(out_own, swapped(out_oth, "tensor", 1))
    shape = (pieces, width // pieces, -1)
    qkv_sum = scattered(qkv_sum_own.reshape(shape), swapped(qkv_sum_oth, "tensor", 1).reshape(shape))

    half = width // 2
    upper = lax.ppermute(jnp.stack(input_low)[:, :, half:], "section", [(0, 1)]).astype(F32)
    input_grad = jnp.where(leading, jnp.stack(input_lower), upper)[:, None]

    near_table = jnp.dot(diagonals(table_kept, micro_count), near_hits.T, precision=lax.Precision.HIGHEST)

    def placed(pair):
        return jnp.where(core == 0, pair, pair[::-1])

    stat_feed = stat_feed[0] + stat_feed[1]
    stat_entry = stat_entry[0] + stat_entry[1]
    gain_first = jnp.where(leading, stat_feed[0:1], stat_entry[2:3])
    gain_rows = jnp.concatenate([gain_first, stat_feed[1:2]])
    nothing = jnp.zeros_like(gain_rows)
    gain_all = jnp.where(leading, jnp.concatenate([gain_rows, nothing]), jnp.concatenate([nothing, gain_rows]))
    shift_all = jnp.where(leading, stat_feed[2:6], 0.0)
    head_all = jnp.where(leading, stat_entry[0:2], 0.0).reshape(2, 2, -1)
    head_all = placed(jnp.moveaxis(head_all, 1, 0))
    bias_all = placed(jnp.where(leading, stat_bias[0] + stat_bias[1], 0.0).reshape(2, -1))
    table_all = placed(jnp.where(leading, 0.0, near_table).reshape(2, heads, bucket_count))
    parts = [gain_all, shift_all, head_all, bias_all, table_all]
    packed = jnp.concatenate([part.reshape(-1) for part in parts])
    packed = packed + swapped(packed, "tensor", 1)
    packed = packed + swapped(packed, "dp", 1)
    packed = packed + swapped(packed, "section", 1)
    packed = packed + swapped(packed, "dp", 2)
    packed = packed + swapped(packed, "dp", 4)
    unpacked = []
    start = 0
    for part in parts:
        unpacked.append(packed[start : start + part.size].reshape(part.shape))
        start += part.size
    gain_all, shift_all, head_all, bias_all, table_all = unpacked
    mine = lambda value: lax.dynamic_index_in_dim(value, core, 0, keepdims=False)
    return (
        jnp.stack(delivered)[None, :, None],
        input_grad,
        qkv_sum.reshape(1, width // pieces, 3, -1),
        out_sum[None],
        up_sum[None],
        down_sum[None],
        gain_all.reshape(norm_gain.shape),
        shift_all,
        mine(head_all),
        mine(bias_all),
        mine(table_all),
    )


def solution(mesh):
    placed = (
        P(None, "dp", "tensor", None),
        P(None, "dp", None),
        P(),
        P("section", None, None, "tensor"),
        P("section", "tensor", None),
        P("section", None, "tensor"),
        P("section", "tensor", None),
        P(),
        P(),
        P(None, "tensor"),
        P("tensor"),
        P("tensor", None),
        P("section", None, "dp", "tensor", None),
    )
    paired = mesh.shape["tensor"] == 2 and mesh.shape["dp"] == 8
    return jax.shard_map(
        paired_body if paired else general_body,
        mesh=mesh,
        in_specs=placed,
        out_specs=(
            P("section", None, "dp", "tensor", None),
            P(None, "dp", "tensor", "section"),
            P("section", "dp", None, "tensor"),
            P("section", "tensor", "dp"),
            P("section", "dp", "tensor"),
            P("section", "tensor", "dp"),
            P(),
            P(),
            P(None, "tensor"),
            P("tensor"),
            P("tensor", None),
        ),
        check_vma=False,
    )
```

```python
import functools

import jax
import jax.numpy as jnp
from jax import lax
from jax.experimental import pallas as pl
from jax.experimental.pallas import tpu as pltpu
from jax.sharding import PartitionSpec as P

DH = 64
QB = 128
PAD = 2
REACH = 256
VMEM = 56 * 1024 * 1024
TAIL_VMEM = 60 * 1024 * 1024
LOW = jnp.bfloat16
F32 = jnp.float32


def dot_nt(left, right):
    return lax.dot_general(left, right, (((1,), (1,)), ((), ())), preferred_element_type=F32)


def dot_nn(left, right):
    return lax.dot_general(left, right, (((1,), (0,)), ((), ())), preferred_element_type=F32)


def params():
    return pltpu.CompilerParams(vmem_limit_bytes=VMEM)


def cost_of(micros):
    return pl.CostEstimate(flops=int(micros * 1e9), bytes_accessed=0, transcendentals=0)


def slotted(shape, dtype):
    return jax.ShapeDtypeStruct((3,) + shape, dtype)


def call_with_slots(
    kernel, scalars, inputs, in_specs, outputs, out_specs, previous, grid, scratch, name, micros
):
    count = len(inputs)
    kept = [] if previous is None else [item for item in previous if item is not None]
    aliases = {}
    if previous is not None:
        at = len(scalars) + count
        for index, item in enumerate(previous):
            if item is not None:
                aliases[at] = index
                at += 1

    def run(*refs):
        front = len(scalars) + count
        kernel(*refs[:front], *refs[front + len(kept) :])

    return pl.pallas_call(
        run,
        grid_spec=pltpu.PrefetchScalarGridSpec(
            num_scalar_prefetch=len(scalars),
            grid=grid,
            in_specs=list(in_specs) + [pl.BlockSpec(memory_space=pl.ANY)] * len(kept),
            out_specs=out_specs,
            scratch_shapes=scratch,
        ),
        out_shape=outputs,
        input_output_aliases=aliases,
        compiler_params=params(),
        cost_estimate=cost_of(micros),
        name=name,
    )(*scalars, *inputs, *kept)


def toeplitz_kernel(w_ref, t_ref):
    width = w_ref.shape[2]
    half = []
    for head in range(2):
        rows = jnp.broadcast_to(w_ref[0, head : head + 1, :], (QB, width))
        rolled = pltpu.roll(rows, 0, 1, stride=1, stride_axis=0)
        half.append(rolled.T[QB:, :])
    t_ref[0] = jnp.concatenate(half, axis=1)


def toeplitz(offset_bias):
    heads, width = offset_bias.shape
    pairs = heads // 2
    return pl.pallas_call(
        toeplitz_kernel,
        grid=(pairs,),
        in_specs=[pl.BlockSpec((1, 2, width), lambda p: (p, 0, 0))],
        out_specs=pl.BlockSpec((1, width - QB, 2 * QB), lambda p: (p, 0, 0)),
        out_shape=jax.ShapeDtypeStruct((pairs, width - QB, 2 * QB), F32),
        compiler_params=params(),
        cost_estimate=cost_of(6),
        name="toeplitz",
    )(offset_bias.reshape(pairs, 2, width))


def diagonal_kernel(a_ref, s_ref):
    total = a_ref[0, 0]
    for extra in range(1, a_ref.shape[0]):
        total = total + a_ref[extra, 0]
    total = jnp.concatenate([jnp.zeros((QB, 2 * QB), F32), total], axis=0)
    width = total.shape[0]
    row = lax.broadcasted_iota(jnp.int32, (QB, QB), 0)
    col = lax.broadcasted_iota(jnp.int32, (QB, QB), 1)
    mirror = jnp.where(row + col == QB - 1, 1.0, 0.0)
    for head in range(2):
        turned = lax.dot_general(
            mirror,
            total[:, head * QB : (head + 1) * QB],
            (((1,), (1,)), ((), ())),
            precision=lax.Precision.HIGHEST,
            preferred_element_type=F32,
        )
        aligned = pltpu.roll(turned, width - QB + 1, 1, stride=1, stride_axis=0)
        s_ref[0, head : head + 1, :] = jnp.sum(aligned, axis=0, keepdims=True)


def diagonals(tables, steps):
    _, pairs, rows, _ = tables.shape
    width = rows + QB
    out = pl.pallas_call(
        diagonal_kernel,
        grid=(pairs,),
        in_specs=[pl.BlockSpec((steps, 1, rows, 2 * QB), lambda p: (0, p, 0, 0))],
        out_specs=pl.BlockSpec((1, 2, width), lambda p: (p, 0, 0)),
        out_shape=jax.ShapeDtypeStruct((pairs, 2, width), F32),
        compiler_params=params(),
        cost_estimate=cost_of(10),
        name="diagonals",
    )(tables)
    return out.reshape(2 * pairs, width)


def two_heads(block, first):
    zero = jnp.zeros_like(block)
    return jnp.concatenate([jnp.where(first, block, zero), jnp.where(first, zero, block)], axis=0)


def joined_heads(turned):
    return jnp.concatenate([turned[:DH, :QB], turned[DH:, QB:]], axis=0).T


def fill_columns(segq_ref, segk_ref):
    for block in range(segq_ref.shape[0]):
        rows = jnp.broadcast_to(segq_ref[block : block + 1, :], (QB, QB))
        segk_ref[block * QB : (block + 1) * QB, :] = rows.T


def visit_blocks(seg_ref, origin, count, block):
    @pl.loop(0, count)
    def _(i):
        at = i + origin
        first = seg_ref[at * QB]
        last = seg_ref[at * QB + QB - 1]
        far = (seg_ref[(at - 1) * QB - 1] == first) | (seg_ref[(at + 2) * QB] == last)

        @pl.when(far)
        def _():
            block(i, at, 2)

        @pl.when(jnp.logical_not(far))
        def _():
            block(i, at, 1)


def placed_rows(info, source, halo, target, halo_count):
    edge = PAD * QB
    rows = source.shape[0]
    target[:edge, :] = jnp.zeros((edge, target.shape[1]), target.dtype)
    target[target.shape[0] - edge :, :] = jnp.zeros((edge, target.shape[1]), target.dtype)
    target[pl.ds(pl.multiple_of(info[2] * QB, QB), rows), :] = source[...]
    if halo_count:
        target[pl.ds(pl.multiple_of(info[3] * QB, QB), halo_count), :] = halo[...]


def attend_kernel(halo_count, info, seg_ref, *refs):
    if halo_count:
        segq_ref, q_ref, k_ref, v_ref, t_ref, kh_ref, vh_ref, o_ref, lse_ref, kk_ref, vk_ref = refs[:11]
        segk_ref, kp_ref, vp_ref, vt_ref = refs[11:]
        kk_ref[0] = kh_ref[...]
        vk_ref[0] = vh_ref[...]
    else:
        segq_ref, q_ref, k_ref, v_ref, t_ref, o_ref, lse_ref = refs[:7]
        segk_ref, kp_ref, vp_ref, vt_ref = refs[7:]
        kh_ref = vh_ref = None
    rows = q_ref.shape[1]
    pairs = q_ref.shape[2] // (2 * DH)
    first = lax.broadcasted_iota(jnp.int32, (QB, 2 * DH), 1) < DH

    @pl.when(pl.program_id(0) == 0)
    def _():
        fill_columns(segq_ref, segk_ref)

    placed_rows(info, k_ref.at[0], kh_ref, kp_ref, halo_count)
    placed_rows(info, v_ref.at[0], vh_ref, vp_ref, halo_count)
    vt_ref[...] = vp_ref[...].T

    def block(i, at, reach):
        span = (2 * reach + 1) * QB
        keys = pl.ds(pl.multiple_of((at - reach) * QB, QB), span)
        mine = pl.ds(pl.multiple_of(i * QB, QB), QB)
        shifted = pl.ds((2 - reach) * QB, span)
        allowed = segk_ref[keys, :] == segq_ref[pl.ds(at, 1), :]
        allowed = jnp.concatenate([allowed, allowed], axis=1)
        for pair in range(pairs):
            lanes = slice(pair * 2 * DH, (pair + 1) * 2 * DH)
            both = two_heads(q_ref[0, mine, lanes] * LOW(0.125), first)
            scores = dot_nt(kp_ref[keys, lanes], both) + t_ref[pair, shifted, :]
            scores = jnp.where(allowed, scores, -jnp.inf)
            highest = jnp.max(scores, axis=0, keepdims=True)
            weights = jnp.exp(scores - highest)
            totals = jnp.sum(weights, axis=0, keepdims=True)
            probs = (weights * (1.0 / totals)).astype(LOW)
            turned = dot_nn(vt_ref[lanes, keys], probs)
            o_ref[0, mine, lanes] = joined_heads(turned).astype(LOW)
            lse_ref[0, pair, pl.ds(i, 1), :] = highest + jnp.log(totals)

    visit_blocks(seg_ref, info[2], rows // QB, block)


def head_specs(rows, span, groups, halo_count):
    column = lambda part: pl.BlockSpec((1, rows, span), lambda g, s, t: (s[1], 0, g + part * groups))
    halo = lambda part: pl.BlockSpec((halo_count, span), lambda g, s, t: (0, g + part * groups))
    return column, halo


def attend(info, segments, qkv, halo, bias, previous):
    _, rows, width = qkv.shape
    width = width // 3
    span = min(256, width)
    groups = width // span
    pairs = span // (2 * DH)
    count = rows // QB
    blocks = segments.shape[0] // QB
    halo_count = 0 if halo is None else halo.shape[0]
    column, halo_spec = head_specs(rows, span, groups, halo_count)
    slot_pairs = pl.BlockSpec((1, pairs, count, 2 * QB), lambda g, s, t: (s[1], g, 0, 0))
    in_specs = [
        pl.BlockSpec((blocks, QB), lambda g, s, t: (0, 0)),
        column(0),
        column(1),
        column(2),
        pl.BlockSpec((pairs,) + bias.shape[1:], lambda g, s, t: (g, 0, 0)),
    ]
    inputs = [segments.reshape(blocks, QB), qkv, qkv, qkv, bias]
    outputs = [slotted((rows, width), LOW), slotted((groups * pairs, count, 2 * QB), F32)]
    out_specs = [column(0), slot_pairs]
    if halo_count:
        in_specs += [halo_spec(0), halo_spec(1)]
        inputs += [halo, halo]
        outputs += [slotted((halo_count, width), LOW)] * 2
        kept = pl.BlockSpec((1, halo_count, span), lambda g, s, t: (s[1], 0, g))
        out_specs += [kept, kept]
    return call_with_slots(
        functools.partial(attend_kernel, halo_count),
        [info, segments],
        inputs,
        in_specs,
        outputs,
        out_specs,
        previous,
        (groups,),
        [
            pltpu.VMEM((blocks * QB, QB), jnp.int32),
            pltpu.VMEM((blocks * QB, span), LOW),
            pltpu.VMEM((blocks * QB, span), LOW),
            pltpu.VMEM((span, blocks * QB), LOW),
        ],
        "attend",
        24,
    )


def attend_back_kernel(halo_count, info, seg_ref, *refs):
    if halo_count:
        segq_ref, q_ref, k_ref, v_ref, g_ref, t_ref, lse_ref, kh_ref, vh_ref = refs[:9]
        dq_ref, dk_ref, dv_ref, diag_ref, dh_ref = refs[9:14]
        segk_ref, kp_ref, vp_ref, kt_ref, dk_acc, dv_acc = refs[14:]
        kh_ref, vh_ref = kh_ref.at[0], vh_ref.at[0]
    else:
        segq_ref, q_ref, k_ref, v_ref, g_ref, t_ref, lse_ref = refs[:7]
        dq_ref, dk_ref, dv_ref, diag_ref = refs[7:11]
        segk_ref, kp_ref, vp_ref, kt_ref, dk_acc, dv_acc = refs[11:]
        kh_ref = vh_ref = None
    rows = q_ref.shape[1]
    pairs = q_ref.shape[2] // (2 * DH)
    first = lax.broadcasted_iota(jnp.int32, (QB, 2 * DH), 1) < DH

    @pl.when(pl.program_id(0) == 0)
    def _():
        fill_columns(segq_ref, segk_ref)

    placed_rows(info, k_ref.at[0], kh_ref, kp_ref, halo_count)
    placed_rows(info, v_ref.at[0], vh_ref, vp_ref, halo_count)
    kt_ref[...] = kp_ref[...].T
    dk_acc[...] = jnp.zeros_like(dk_acc)
    dv_acc[...] = jnp.zeros_like(dv_acc)
    diag_ref[...] = jnp.zeros_like(diag_ref)

    def block(i, at, reach):
        span = (2 * reach + 1) * QB
        keys = pl.ds(pl.multiple_of((at - reach) * QB, QB), span)
        mine = pl.ds(pl.multiple_of(i * QB, QB), QB)
        shifted = pl.ds((2 - reach) * QB, span)
        allowed = segk_ref[keys, :] == segq_ref[pl.ds(at, 1), :]
        allowed = jnp.concatenate([allowed, allowed], axis=1)
        for pair in range(pairs):
            lanes = slice(pair * 2 * DH, (pair + 1) * 2 * DH)
            both = two_heads(q_ref[0, mine, lanes] * LOW(0.125), first)
            grads = two_heads(g_ref[mine, lanes], first)
            scores = dot_nt(kp_ref[keys, lanes], both) + t_ref[pair, shifted, :]
            scores = jnp.where(allowed, scores - lse_ref[0, pair, pl.ds(i, 1), :], -jnp.inf)
            probs = jnp.exp(scores)
            grad_probs = dot_nt(vp_ref[keys, lanes], grads)
            dv_acc[keys, lanes] += dot_nn(probs.astype(LOW), grads)
            inner = jnp.sum(probs * grad_probs, axis=0, keepdims=True)
            rounded = (probs * (grad_probs - inner)).astype(LOW)
            dk_acc[keys, lanes] += dot_nn(rounded, both)
            diag_ref[0, pair, shifted, :] += rounded.astype(F32)
            turned = dot_nn(kt_ref[lanes, keys], rounded)
            dq_ref[mine, lanes] = (joined_heads(turned) * 0.125).astype(LOW)

    visit_blocks(seg_ref, info[2], rows // QB, block)
    own = pl.ds(pl.multiple_of(info[2] * QB, QB), rows)
    dk_ref[...] = dk_acc[own, :].astype(LOW)
    dv_ref[...] = dv_acc[own, :].astype(LOW)
    if halo_count:
        far = pl.ds(pl.multiple_of(info[3] * QB, QB), halo_count)
        dh_ref[0] = dk_acc[far, :].astype(LOW)
        dh_ref[1] = dv_acc[far, :].astype(LOW)


def attend_back(info, segments, qkv, halo_kept, grad_context, bias, lse, previous):
    _, rows, width = qkv.shape
    width = width // 3
    span = min(256, width)
    groups = width // span
    pairs = span // (2 * DH)
    count = rows // QB
    blocks = segments.shape[0] // QB
    halo_count = 0 if halo_kept is None else halo_kept[0].shape[1]
    column, _ = head_specs(rows, span, groups, halo_count)
    plain = pl.BlockSpec((rows, span), lambda g, s, t: (0, g))
    in_specs = [
        pl.BlockSpec((blocks, QB), lambda g, s, t: (0, 0)),
        column(0),
        column(1),
        column(2),
        plain,
        pl.BlockSpec((pairs,) + bias.shape[1:], lambda g, s, t: (g, 0, 0)),
        pl.BlockSpec((1, pairs, count, 2 * QB), lambda g, s, t: (s[1], g, 0, 0)),
    ]
    inputs = [segments.reshape(blocks, QB), qkv, qkv, qkv, grad_context, bias, lse]
    plain_shape = jax.ShapeDtypeStruct((rows, width), LOW)
    outputs = [plain_shape] * 3 + [slotted(bias.shape, F32)]
    out_specs = [plain] * 3 + [
        pl.BlockSpec((1, pairs) + bias.shape[1:], lambda g, s, t: (s[1], g, 0, 0))
    ]
    if halo_count:
        kept = pl.BlockSpec((1, halo_count, span), lambda g, s, t: (s[1], 0, g))
        in_specs += [kept, kept]
        inputs += list(halo_kept)
        outputs.append(jax.ShapeDtypeStruct((2, halo_count, width), LOW))
        out_specs.append(pl.BlockSpec((2, halo_count, span), lambda g, s, t: (0, 0, lax.rem(g + groups // 2, groups))))
    keep = None if previous is None else [None] * 3 + [previous] + [None] * (len(outputs) - 4)
    return call_with_slots(
        functools.partial(attend_back_kernel, halo_count),
        [info, segments],
        inputs,
        in_specs,
        outputs,
        out_specs,
        keep,
        (groups,),
        [
            pltpu.VMEM((blocks * QB, QB), jnp.int32),
            pltpu.VMEM((blocks * QB, span), LOW),
            pltpu.VMEM((blocks * QB, span), LOW),
            pltpu.VMEM((span, blocks * QB), LOW),
            pltpu.VMEM((blocks * QB, span), F32),
            pltpu.VMEM((blocks * QB, span), F32),
        ],
        "attend_back",
        26,
    )


def mean_of(block):
    return jnp.mean(block, axis=-1, keepdims=True)


def rms_scale(block):
    return lax.rsqrt(mean_of(block * block) + 1e-06)


def sum_rows(block):
    return jnp.sum(block, axis=0, keepdims=True)


def gelu_parts(u):
    depth = jnp.abs(u) * 0.7071067811865476
    divisor = 1.0 + 0.3275911 * depth
    t = pl.reciprocal(divisor, approx=True)
    t = t * (2.0 - divisor * t)
    series = ((((1.061405429 * t - 1.453152027) * t + 1.421413741) * t - 0.284496736) * t + 0.254829592) * t
    bell = jnp.exp(-0.5 * u * u)
    tail = 0.5 * series * bell
    below = jnp.where(u >= 0.0, 1.0 - tail, tail)
    return u * below, below + u * bell * 0.3989422804014327


def enter_kernel(info, first_ref, second_ref, gain_ref, shift_ref, own_ref, oth_ref, x_ref, e_ref, qkv_ref, halo_ref):
    m = pl.program_id(0)
    half = own_ref.shape[1]

    @pl.when((m == 0) & (info[0] == 1))
    def _():
        x_ref[0] = first_ref[...]
        e_ref[0] = first_ref[...]

    @pl.when((m == 0) & (info[0] == 0))
    def _():
        x_ref[0] = second_ref[...]
        x = second_ref[...].astype(F32)
        e_ref[0] = (x * rms_scale(x) * gain_ref[...]).astype(LOW)

    e = e_ref[0]
    for part, weight in enumerate((own_ref, oth_ref)):
        lanes = slice(part * half, (part + 1) * half)
        block = (dot_nn(e, weight[...]) + shift_ref[:, lanes]).astype(LOW)
        qkv_ref[0, :, lanes] = block
    start = pl.ds(pl.multiple_of(info[4], QB), halo_ref.shape[0])
    halo_ref[:, :half] = qkv_ref[0, start, half:]
    halo_ref[:, half:] = qkv_ref[0, start, :half]


def enter(info, first, second, gain, shift, own, oth, previous):
    rows, width = first.shape
    half = own.shape[1] // 3
    whole = pl.BlockSpec((rows, width), lambda m, s: (0, 0))
    weight = pl.BlockSpec((width, half), lambda m, s: (0, m))
    kept = pl.BlockSpec((1, rows, width), lambda m, s: (s[1], 0, 0))
    keep = None if previous is None else list(previous) + [None]
    return call_with_slots(
        enter_kernel,
        [info],
        [first, second, gain, shift, own, oth],
        [
            whole,
            whole,
            pl.BlockSpec((1, width), lambda m, s: (0, 0)),
            pl.BlockSpec((1, 2 * half), lambda m, s: (0, m)),
            weight,
            weight,
        ],
        [
            slotted((rows, width), LOW),
            slotted((rows, width), LOW),
            slotted((rows, 6 * half), LOW),
            jax.ShapeDtypeStruct((REACH, 4 * half), LOW),
        ],
        [
            kept,
            kept,
            pl.BlockSpec((1, rows, 2 * half), lambda m, s: (s[1], 0, m)),
            pl.BlockSpec((REACH, 2 * half), lambda m, s: (0, jnp.maximum(m - 1, 0))),
        ],
        keep,
        (3,),
        [],
        "enter",
        9,
    )


def feed_kernel(
    info, x_ref, c_ref, wo_own, wo_oth, up_own, up_oth, down_own, down_oth, bias_ref, gain_ref, shift_ref,
    f_ref, slope_ref, n_ref, one_ref, two_ref, out_ref, acc_ref, carry_ref
):
    j = pl.program_id(0)
    steps = pl.num_programs(0)
    half = wo_own.shape[0]
    rows = x_ref.shape[1]

    @pl.when(j == 0)
    def _():
        joined = (
            dot_nn(c_ref[0, :, :half], wo_own[...])
            + dot_nn(c_ref[0, :, half:], wo_oth[...])
            + x_ref[0].astype(F32)
        )

        @pl.when(info[0] == 1)
        def _():
            before = joined + shift_ref[0:1, :]
            one_ref[0] = before
            center = before - mean_of(before)
            normed = center * lax.rsqrt(mean_of(center * center) + 1e-05) * gain_ref[0:1, :] + shift_ref[2:3, :]
            carry_ref[...] = normed
            n_ref[0] = normed.astype(LOW)

        @pl.when(info[0] == 0)
        def _():
            one_ref[0] = joined
            carry_ref[...] = joined
            n_ref[0] = (joined * rms_scale(joined) * gain_ref[1:2, :]).astype(LOW)

        acc_ref[...] = jnp.zeros_like(acc_ref)

    def part(up, down):
        for at in range(0, rows, 256):
            piece = slice(at, at + 256)
            u = dot_nn(n_ref[0, piece, :], up[...]) + bias_ref[...]
            f, slope = gelu_parts(u)
            low = f.astype(LOW)
            f_ref[0, piece, :] = low
            slope_ref[0, piece, :] = slope.astype(LOW)
            acc_ref[piece, :] += dot_nn(low, down[...])

    @pl.when(j < steps // 2)
    def _():
        part(up_own, down_own)

    @pl.when(j >= steps // 2)
    def _():
        part(up_oth, down_oth)

    @pl.when(j == steps - 1)
    def _():
        joined = carry_ref[...] + acc_ref[...]

        @pl.when(info[0] == 1)
        def _():
            before = joined + shift_ref[1:2, :]
            two_ref[0] = before
            center = before - mean_of(before)
            normed = center * lax.rsqrt(mean_of(center * center) + 1e-05) * gain_ref[1:2, :] + shift_ref[3:4, :]
            out_ref[...] = normed.astype(LOW)

        @pl.when(info[0] == 0)
        def _():
            two_ref[0] = joined
            out_ref[...] = joined.astype(LOW)


def split_steps(hidden, chunk):
    each = hidden // chunk
    near = lambda j: jnp.minimum(j, each - 1)
    far = lambda j: jnp.maximum(j - each, 0)
    return 2 * each, near, far


def feed(info, x, context, wo, up, down, bias, gains, shifts, previous):
    _, rows, width = x.shape
    hidden = up[0].shape[1]
    chunk = min(512, hidden)
    steps, near, far = split_steps(hidden, chunk)
    kept = pl.BlockSpec((1, rows, width), lambda j, s: (s[1], 0, 0))
    fixed = lambda a: pl.BlockSpec(a.shape, lambda j, s: (0, 0))
    moving = pl.BlockSpec((1, rows, chunk), lambda j, s: (s[1], 0, j))
    keep = None if previous is None else list(previous) + [None]
    return call_with_slots(
        feed_kernel,
        [info],
        [x, context, wo[0], wo[1], up[0], up[1], down[0], down[1], bias, gains, shifts],
        [
            kept,
            kept,
            fixed(wo[0]),
            fixed(wo[1]),
            pl.BlockSpec((width, chunk), lambda j, s: (0, near(j))),
            pl.BlockSpec((width, chunk), lambda j, s: (0, far(j))),
            pl.BlockSpec((chunk, width), lambda j, s: (near(j), 0)),
            pl.BlockSpec((chunk, width), lambda j, s: (far(j), 0)),
            pl.BlockSpec((1, chunk), lambda j, s: (0, j)),
            fixed(gains),
            fixed(shifts),
        ],
        [
            slotted((rows, 2 * hidden), LOW),
            slotted((rows, 2 * hidden), LOW),
            slotted((rows, width), LOW),
            slotted((rows, width), F32),
            slotted((rows, width), F32),
            jax.ShapeDtypeStruct((rows, width), LOW),
        ],
        [moving, moving, kept, kept, kept, pl.BlockSpec((rows, width), lambda j, s: (0, 0))],
        keep,
        (steps,),
        [pltpu.VMEM((rows, width), F32), pltpu.VMEM((rows, width), F32)],
        "feed",
        29,
    )


def layer_norm_back(before, grad, gain_row):
    center = before - mean_of(before)
    scale = lax.rsqrt(mean_of(center * center) + 1e-05)
    unit = center * scale
    inner = grad * gain_row
    back = scale * (inner - mean_of(inner) - unit * mean_of(inner * unit))
    return back, sum_rows(grad * unit)


def rms_norm_back(before, grad, gain_row):
    scale = rms_scale(before)
    unit = before * scale
    inner = grad * gain_row
    back = scale * (inner - unit * mean_of(inner * unit))
    return back, sum_rows(grad * unit)


def feed_back_kernel(
    info, got_ref, mine_ref, other_ref, one_ref, two_ref, slope_ref, wo_own, wo_oth, up_own, up_oth, down_own, down_oth,
    gain_ref, dy_ref, du_ref, db_ref, stat_ref, bias_ref, dz_ref, dc_ref, acc_ref, carry_ref
):
    j = pl.program_id(0)
    steps = pl.num_programs(0)
    half = wo_own.shape[0]
    rows = got_ref.shape[0]

    @pl.when(j == 0)
    def _():
        stat_ref[...] = jnp.zeros_like(stat_ref)
        acc_ref[...] = jnp.zeros_like(acc_ref)

        @pl.when(info[0] == 1)
        def _():
            grad = got_ref[...].astype(F32)
            back, gain = layer_norm_back(two_ref[0], grad, gain_ref[1:2, :])
            stat_ref[0, 1:2, :] = gain
            stat_ref[0, 5:6, :] = sum_rows(grad)
            stat_ref[0, 3:4, :] = sum_rows(back)
            carry_ref[...] = back
            dy_ref[0] = back.astype(LOW)

        @pl.when(info[0] == 0)
        def _():
            grad = mine_ref[...].astype(F32) + other_ref[...].astype(F32)
            carry_ref[...] = grad
            dy_ref[0] = grad.astype(LOW)

    def part(up, down):
        for at in range(0, rows, 256):
            piece = slice(at, at + 256)
            grad = dot_nt(dy_ref[0, piece, :], down[...])
            low = (grad * slope_ref[0, piece, :].astype(F32)).astype(LOW)
            du_ref[0, piece, :] = low
            acc_ref[piece, :] += dot_nt(low, up[...])
        bias_ref[0] = sum_rows(du_ref[0].astype(F32))

    @pl.when(j < steps // 2)
    def _():
        part(up_own, down_own)

    @pl.when(j >= steps // 2)
    def _():
        part(up_oth, down_oth)

    @pl.when(j == steps - 1)
    def _():
        @pl.when(info[0] == 1)
        def _():
            grad = acc_ref[...] + carry_ref[...]
            back, gain = layer_norm_back(one_ref[0], grad, gain_ref[0:1, :])
            stat_ref[0, 0:1, :] = gain
            stat_ref[0, 4:5, :] = sum_rows(grad)
            stat_ref[0, 2:3, :] = sum_rows(back)
            dz_ref[...] = back

        @pl.when(info[0] == 0)
        def _():
            back, gain = rms_norm_back(one_ref[0], acc_ref[...], gain_ref[1:2, :])
            stat_ref[0, 1:2, :] = gain
            dz_ref[...] = carry_ref[...] + back

        low = dz_ref[...].astype(LOW)
        db_ref[0] = low
        dc_ref[:, :half] = dot_nt(low, wo_own[...]).astype(LOW)
        dc_ref[:, half:] = dot_nt(low, wo_oth[...]).astype(LOW)


def feed_back(info, got, mine, other, one, two, slope, wo, up, down, gains, previous):
    _, rows, width = one.shape
    hidden = up[0].shape[1]
    chunk = min(512, hidden)
    steps, near, far = split_steps(hidden, chunk)
    kept = pl.BlockSpec((1, rows, width), lambda j, s: (s[1], 0, 0))
    fixed = lambda a: pl.BlockSpec(a.shape, lambda j, s: (0, 0))
    plain = pl.BlockSpec((rows, width), lambda j, s: (0, 0))
    moving = pl.BlockSpec((1, rows, chunk), lambda j, s: (s[1], 0, j))
    keep = None if previous is None else list(previous) + [None, None]
    return call_with_slots(
        feed_back_kernel,
        [info],
        [got, mine, other, one, two, slope, wo[0], wo[1], up[0], up[1], down[0], down[1], gains],
        [
            plain,
            plain,
            plain,
            kept,
            kept,
            moving,
            fixed(wo[0]),
            fixed(wo[1]),
            pl.BlockSpec((width, chunk), lambda j, s: (0, near(j))),
            pl.BlockSpec((width, chunk), lambda j, s: (0, far(j))),
            pl.BlockSpec((chunk, width), lambda j, s: (near(j), 0)),
            pl.BlockSpec((chunk, width), lambda j, s: (far(j), 0)),
            fixed(gains),
        ],
        [
            slotted((rows, width), LOW),
            slotted((rows, 2 * hidden), LOW),
            slotted((rows, width), LOW),
            slotted((8, width), F32),
            slotted((1, 2 * hidden), F32),
            jax.ShapeDtypeStruct((rows, width), F32),
            jax.ShapeDtypeStruct((rows, width), LOW),
        ],
        [
            kept,
            moving,
            kept,
            pl.BlockSpec((1, 8, width), lambda j, s: (s[1], 0, 0)),
            pl.BlockSpec((1, 1, chunk), lambda j, s: (s[1], 0, j)),
            plain,
            plain,
        ],
        keep,
        (steps,),
        [pltpu.VMEM((rows, width), F32), pltpu.VMEM((rows, width), F32)],
        "feed_back",
        27,
    )


def enter_back_kernel(
    info, dq_ref, dk_ref, dv_ref, far_ref, x_ref, dz_ref, own_ref, oth_ref, gain_ref,
    d_ref, stat_ref, low_ref, lower_ref, acc_ref
):
    m = pl.program_id(0)
    half = own_ref.shape[1]
    start = pl.ds(pl.multiple_of(info[4], QB), far_ref.shape[1])

    @pl.when(m == 0)
    def _():
        stat_ref[...] = jnp.zeros_like(stat_ref)
        acc_ref[...] = jnp.zeros_like(acc_ref)
        d_ref[0] = dq_ref[...]
        stat_ref[0, 0:1, :] = sum_rows(dq_ref[...].astype(F32))

    def with_far(block_ref, part):
        d_ref[0] = block_ref[...]
        d_ref[0, start, :] = (block_ref[start, :].astype(F32) + far_ref[part].astype(F32)).astype(LOW)

    @pl.when(m == 1)
    def _():
        with_far(dk_ref, 0)

    @pl.when(m == 2)
    def _():
        with_far(dv_ref, 1)
        stat_ref[0, 1:2, :] = sum_rows(d_ref[0].astype(F32))

    acc_ref[...] += dot_nt(d_ref[0, :, :half], own_ref[...]) + dot_nt(d_ref[0, :, half:], oth_ref[...])

    @pl.when(m == 2)
    def _():
        split = lower_ref.shape[1]

        @pl.when(info[0] == 1)
        def _():
            total = dz_ref[...] + acc_ref[...]
            low_ref[...] = total.astype(LOW)
            lower_ref[...] = total[:, :split]

        @pl.when(info[0] == 0)
        def _():
            back, gain = rms_norm_back(x_ref[0].astype(F32), acc_ref[...], gain_ref[...])
            stat_ref[0, 2:3, :] = gain
            total = dz_ref[...] + back
            low_ref[...] = total.astype(LOW)
            lower_ref[...] = total[:, :split]


def enter_back(info, dq, dk, dv, far, x, dz, own, oth, gain, previous):
    _, rows, width = x.shape
    half = own.shape[1] // 3
    plain = pl.BlockSpec((rows, width), lambda m, s: (0, 0))
    kept = pl.BlockSpec((1, rows, width), lambda m, s: (s[1], 0, 0))
    weight = pl.BlockSpec((width, half), lambda m, s: (0, m))
    keep = None if previous is None else list(previous) + [None, None]
    return call_with_slots(
        enter_back_kernel,
        [info],
        [dq, dk, dv, far, x, dz, own, oth, gain],
        [
            plain,
            plain,
            plain,
            pl.BlockSpec(far.shape, lambda m, s: (0, 0, 0)),
            kept,
            plain,
            weight,
            weight,
            pl.BlockSpec((1, width), lambda m, s: (0, 0)),
        ],
        [
            slotted((rows, 6 * half), LOW),
            slotted((8, width), F32),
            jax.ShapeDtypeStruct((rows, width), LOW),
            jax.ShapeDtypeStruct((rows, width // 2), F32),
        ],
        [
            pl.BlockSpec((1, rows, 2 * half), lambda m, s: (s[1], 0, m)),
            pl.BlockSpec((1, 8, width), lambda m, s: (s[1], 0, 0)),
            plain,
            pl.BlockSpec((rows, width // 2), lambda m, s: (0, 0)),
        ],
        keep,
        (3,),
        [pltpu.VMEM((rows, width), F32)],
        "enter_back",
        12,
    )


def passed_along(value, axis, steps):
    count = lax.axis_size(axis)
    initial, last = (max(0, -steps), min(count, count - steps))
    return lax.ppermute(value, axis, [(source, source + steps) for source in range(initial, last)])


def spread(block, axis, source):
    block = jnp.where(lax.axis_index(axis) == source, block, jnp.zeros_like(block))
    return lax.psum(block, axis)


def layer_norm(operand, gain_row, shift_row):
    center = operand - jnp.mean(operand, axis=-1, keepdims=True)
    variance = jnp.mean(center * center, axis=-1, keepdims=True)
    return center * lax.rsqrt(variance + 1e-05) * gain_row + shift_row


def rms_norm(operand, gain_row):
    return (
        operand * lax.rsqrt(jnp.mean(operand * operand, axis=-1, keepdims=True) + 1e-06) * gain_row
    )


def gelu_act(operand):
    return jax.nn.gelu(operand, approximate=False)


def gelu_slope(operand):
    return (
        0.5 * (1.0 + jax.scipy.special.erf(operand * 0.7071067811865476))
        + operand * jnp.exp(-0.5 * operand * operand) * 0.3989422804014327
    )


def entry_norm(residual, gain_rows, leading):
    return jnp.where(leading, residual, rms_norm(residual, gain_rows[0]))


def middle(residual, branch, gain_rows, shift_rows, leading):
    joined = residual + branch
    bert_rows = layer_norm(joined + shift_rows[0], gain_rows[0], shift_rows[2])
    carried = jnp.where(leading, bert_rows, joined)
    normed = jnp.where(leading, bert_rows, rms_norm(joined, gain_rows[1]))
    return (carried, normed)


def final(carried, second, gain_rows, shift_rows, leading):
    joined = carried + second
    return jnp.where(
        leading, layer_norm(joined + shift_rows[1], gain_rows[1], shift_rows[3]), joined
    )


def contract_rows(left, right):
    return lax.dot_general(
        left, right, (((0,), (0,)), ((), ())), preferred_element_type=jnp.float32
    )


def contract_cols(left, right):
    return lax.dot_general(
        left, right, (((1,), (1,)), ((), ())), preferred_element_type=jnp.float32
    )


def gather_rows(operand, weight):
    return (
        jnp.dot(
            lax.all_gather(operand, "tensor", axis=0, tiled=True),
            weight,
            preferred_element_type=jnp.float32,
        ),
        None,
    )


def collect(full_rows, weight):
    return lax.psum_scatter(
        jnp.dot(full_rows, weight, preferred_element_type=jnp.float32),
        "tensor",
        scatter_dimension=0,
        tiled=True,
    )


def scatter_back(grad_rows, weight):
    return lax.psum_scatter(
        contract_cols(grad_rows, weight).astype(jnp.bfloat16),
        "tensor",
        scatter_dimension=0,
        tiled=True,
    ).astype(jnp.float32)


def fold_back(grad_share, weight, activations):
    fragment = lax.all_gather(grad_share, "tensor", axis=0, tiled=True)
    product_rows = contract_cols(fragment, weight)
    return (product_rows, contract_rows(activations, fragment))


def weight_grad(operand, grad_rows):
    return contract_rows(lax.all_gather(operand, "tensor", axis=0, tiled=True), grad_rows)


DH = 64
QB = 128
NARROW = 3
WIDE = 5
VMEM = 56 * 1024 * 1024


def padded(segments):
    return jnp.pad(segments, (PAD * QB, PAD * QB), constant_values=-1)


def general_body(
    layer_input,
    segment_ids,
    buckets,
    attn_in,
    attn_out,
    ffn_in,
    ffn_out,
    norm_gain,
    bert_shift,
    head_bias,
    ffn_bias,
    position_bias,
    decoder_grads,
):
    micro_count = layer_input.shape[0]
    shard_rows = layer_input.shape[2]
    model_width = layer_input.shape[3]
    length = segment_ids.shape[2]
    leading = lax.axis_index("section") == 0
    weighting = jnp.where(leading, 1.0, 0.0)
    qkv_weight = attn_in[0].reshape(model_width, -1)
    out_weight = attn_out[0]
    ffn_up = ffn_in[0]
    ffn_down = ffn_out[0]
    gain_rows = jnp.where(leading, norm_gain[0], norm_gain[1])
    head_shift = head_bias * weighting
    qkv_shift = jnp.concatenate([head_shift[0], jnp.zeros_like(head_shift[0]), head_shift[1]])
    ffn_shift = ffn_bias * weighting
    bias_table = position_bias * (1.0 - weighting)
    bucket_hits = (buckets[None, :] == jnp.arange(bias_table.shape[1])[:, None]).astype(jnp.float32)
    offset_bias = jnp.dot(bias_table, bucket_hits, precision=lax.Precision.HIGHEST)
    near = length - 1 - 3 * QB
    bias = toeplitz(offset_bias[:, near : near + 6 * QB])
    info = jnp.array([0, 0, PAD, 0, 0], jnp.int32)
    segment_rows = segment_ids[:, 0]

    def middle_part(residual_in, branch_in, gain_in, shift_in):
        return middle(residual_in, branch_in, gain_in, shift_in, leading)

    def final_part(carried_in, second_in, gain_in, shift_in):
        return final(carried_in, second_in, gain_in, shift_in, leading)

    def entry_part(residual_in, gain_in):
        return entry_norm(residual_in, gain_in, leading)

    received = jnp.zeros((shard_rows, model_width), jnp.bfloat16)
    saved_steps = []
    encoded = []
    for moment in range(micro_count + 1):
        own_rows = layer_input[min(moment, micro_count - 1), 0]
        if moment >= micro_count:
            own_rows = jnp.zeros_like(own_rows)
        segment_row = jnp.where(
            leading, segment_rows[min(moment, micro_count - 1)], segment_rows[max(moment - 1, 0)]
        )
        forward_incoming = jnp.where(leading, own_rows, received)
        forward_residual = forward_incoming.astype(jnp.float32)
        forward_entered = entry_norm(forward_residual, gain_rows, leading).astype(jnp.bfloat16)
        projected, forward_gathered_in = gather_rows(forward_entered, qkv_weight)
        forward_qkv = (projected + qkv_shift).astype(jnp.bfloat16)
        forward_context, forward_log_totals = attend(
            info, padded(segment_row), forward_qkv[None], None, bias, None
        )
        forward_context = forward_context[0]
        forward_branch = collect(forward_context, out_weight)
        forward_carried, forward_normed = middle(
            forward_residual, forward_branch, gain_rows, bert_shift, leading
        )
        pre_full, forward_gathered_mid = gather_rows(forward_normed.astype(jnp.bfloat16), ffn_up)
        forward_pre_act = pre_full + ffn_shift
        forward_second = collect(gelu_act(forward_pre_act).astype(jnp.bfloat16), ffn_down)
        result = final(forward_carried, forward_second, gain_rows, bert_shift, leading).astype(
            jnp.bfloat16
        )
        result, saved = (
            result,
            (
                forward_incoming,
                segment_row,
                forward_branch,
                forward_second,
                forward_qkv,
                forward_context,
                forward_log_totals,
                forward_pre_act,
                forward_gathered_in,
                forward_gathered_mid,
            ),
        )
        saved_steps.append(saved)
        if moment >= 1:
            encoded.append(result)
        if moment < micro_count:
            received = passed_along(result, "section", 1)
    delivered = spread(jnp.stack(encoded), "section", 1)
    section_grads = lax.psum(
        decoder_grads[0, :, 0].astype(jnp.float32).astype(jnp.bfloat16), "section"
    ).astype(jnp.float32)
    grad_received = jnp.zeros((shard_rows, model_width), jnp.float32)
    running_terms = None
    input_rows = []
    for moment in range(micro_count + 1):
        own_grad = section_grads[min(moment, micro_count - 1)]
        if moment >= micro_count:
            own_grad = jnp.zeros_like(own_grad)
        earlier = saved_steps[max(moment - 1, 0)]
        later = saved_steps[min(moment + 1, micro_count)]
        chosen = jax.tree.map(
            lambda from_first, from_second: jnp.where(leading, from_first, from_second),
            earlier,
            later,
        )
        (
            incoming,
            backward_segment_row,
            branch,
            second,
            qkv,
            context,
            log_totals,
            pre_act,
            gathered_in,
            gathered_mid,
        ) = chosen
        residual = incoming.astype(jnp.float32)
        (carried, normed), pull_middle = jax.vjp(
            middle_part, residual, branch, gain_rows, bert_shift
        )
        finished, pull_final = jax.vjp(final_part, carried, second, gain_rows, bert_shift)
        grad_carried, grad_second, gain_end, shift_end = pull_final(
            jnp.where(leading, grad_received, own_grad)
        )
        hidden = gelu_act(pre_act).astype(jnp.bfloat16)
        grad_hidden, backward_grad_down = fold_back(
            grad_second.astype(jnp.bfloat16), ffn_down, hidden
        )
        grad_pre = (grad_hidden * gelu_slope(pre_act)).astype(jnp.bfloat16)
        grad_shift = jnp.sum(grad_pre.astype(jnp.float32), axis=0) * weighting
        backward_grad_up = weight_grad(normed.astype(jnp.bfloat16), grad_pre)
        grad_normed = scatter_back(grad_pre, ffn_up)
        grad_residual, grad_branch, gain_mid, shift_mid = pull_middle((grad_carried, grad_normed))
        grad_context, backward_grad_out_weight = fold_back(
            grad_branch.astype(jnp.bfloat16), out_weight, context
        )
        low_q, low_k, low_v, grad_table = attend_back(
            info, padded(backward_segment_row), qkv[None], None, grad_context.astype(jnp.bfloat16), bias, log_totals, None
        )
        grad_table = grad_table[0]
        grad_head = (
            jnp.stack([jnp.sum(low.astype(jnp.float32), axis=0) for low in (low_q, low_v)]) * weighting
        )
        grad_rows = jnp.concatenate([low_q, low_k, low_v], axis=1)
        entered, pull_entry = jax.vjp(entry_part, residual, gain_rows)
        backward_grad_qkv = weight_grad(entered.astype(jnp.bfloat16), grad_rows)
        grad_entered = scatter_back(grad_rows, qkv_weight)
        grad_from_entry, gain_entry = pull_entry(grad_entered)
        grad_terms = (
            backward_grad_qkv,
            backward_grad_out_weight,
            backward_grad_up,
            backward_grad_down,
            gain_end + gain_mid + gain_entry,
            shift_end + shift_mid,
            grad_head,
            grad_shift,
            grad_table,
        )
        grad_input, grad_terms = (grad_residual + grad_from_entry, grad_terms)
        if running_terms is None:
            running_terms = grad_terms
        else:
            running_terms = jax.tree.map(jnp.add, running_terms, grad_terms)
        if moment >= 1:
            input_rows.append(grad_input)
        if moment < micro_count:
            grad_received = passed_along(grad_input.astype(jnp.bfloat16), "section", -1).astype(
                grad_input.dtype
            )
    input_all = jnp.stack(input_rows)
    half_width = model_width // 2
    upper_half = passed_along(
        input_all[:, :, half_width:].astype(jnp.bfloat16), "section", 1
    ).astype(jnp.float32)
    input_grad = jnp.where(leading, input_all[:, :, :half_width], upper_half)[:, None]
    (
        grad_qkv,
        grad_out_weight,
        grad_up,
        grad_down,
        gain_sum,
        shift_sum,
        head_sum,
        shift_ffn_sum,
        table_sum,
    ) = running_terms
    near_hits = bucket_hits[:, near : near + 6 * QB]
    table_sum = jnp.dot(diagonals(table_sum[None], 1), near_hits.T, precision=lax.Precision.HIGHEST) * (
        1.0 - weighting
    )
    weights_out = (
        lax.psum_scatter(
            grad_qkv.reshape(1, model_width, 3, -1).astype(jnp.bfloat16),
            "dp",
            scatter_dimension=1,
            tiled=True,
        ).astype(jnp.float32),
        lax.psum_scatter(
            grad_out_weight[None].astype(jnp.bfloat16), "dp", scatter_dimension=2, tiled=True
        ).astype(jnp.float32),
        lax.psum_scatter(
            grad_up[None].astype(jnp.bfloat16), "dp", scatter_dimension=1, tiled=True
        ).astype(jnp.float32),
        lax.psum_scatter(
            grad_down[None].astype(jnp.bfloat16), "dp", scatter_dimension=2, tiled=True
        ).astype(jnp.float32),
    )
    gain_both = jnp.stack([gain_sum * weighting, gain_sum * (1.0 - weighting)])
    shared_out = lax.psum((gain_both, shift_sum), ("dp", "section", "tensor"))
    split_out = lax.psum((head_sum, shift_ffn_sum, table_sum), ("dp", "section"))
    return (
        delivered[None, :, None],
        input_grad,
        weights_out[0],
        weights_out[1],
        weights_out[2],
        weights_out[3],
        shared_out[0],
        shared_out[1],
        split_out[0],
        split_out[1],
        split_out[2],
    )


def grads_kernel(
    f_hbm, dy_hbm, c_hbm, db_hbm, n_hbm, du_hbm, e_hbm, dqkv_hbm, packed_ref,
    out_ref, summed_ref,
    still, moving, turned, given, held, near_ref, y_ref, low_ref, high_ref, small_ref, small_got,
    still_sem, moving_sem, near_send, near_recv, y_send, y_recv, low_send, low_recv, high_send, high_recv,
    small_send, small_recv
):
    dp = lax.axis_index("dp")
    core = lax.axis_index("tensor")
    section = lax.axis_index("section")
    y_side = lax.rem(dp, 2)
    low_side = lax.rem(dp // 2, 2)
    high_side = dp // 4

    def across(bit, side):
        return {"dp": dp + bit * (1 - 2 * side)}

    core_peer = {"tensor": 1 - core}
    y_peer = across(1, y_side)
    low_peer = across(2, low_side)
    high_peer = across(4, high_side)
    peers = [core_peer, y_peer, low_peer, high_peer, {"section": 1 - section}]
    mesh_id = pl.DeviceIdType.MESH
    total = out_ref.shape[0]

    barrier = pltpu.get_barrier_semaphore()
    for peer in peers:
        pl.semaphore_signal(barrier, inc=1, device_id=peer, device_id_type=mesh_id)
    pl.semaphore_wait(barrier, len(peers))

    def send(source, target, out_sem, in_sem, peer):
        return pltpu.make_async_remote_copy(
            src_ref=source, dst_ref=target, send_sem=out_sem, recv_sem=in_sem,
            device_id=peer, device_id_type=mesh_id,
        )

    def near_copy(k, slot):
        return send(given.at[slot], near_ref.at[k], near_send.at[slot], near_recv.at[k], core_peer)

    def y_copy(k):
        return send(held.at[k, :, :, 1 - y_side], y_ref.at[k], y_send.at[k], y_recv.at[k], y_peer)

    def low_copy(k):
        return send(y_ref.at[k, :, 1 - low_side], low_ref.at[k], low_send.at[k], low_recv.at[k], low_peer)

    def high_copy(k):
        return send(low_ref.at[k, 1 - high_side], high_ref.at[k], high_send.at[k], high_recv.at[k], high_peer)

    def small_copy(s):
        return send(small_ref.at[s], small_got.at[s], small_send.at[s], small_recv.at[s], peers[s])

    def added(a, b):
        return (a.astype(F32) + b.astype(F32)).astype(LOW)

    def near_stage(k):
        near_copy(k, 0).wait_recv()
        for hi in range(2):
            for lo in range(2):
                for side in range(2):
                    held[k, hi, lo, side] = added(held[k, hi, lo, side], near_ref[k, hi, lo, side])
        y_copy(k).start()

    def y_stage(k):
        y_copy(k).wait_recv()
        for hi in range(2):
            for lo in range(2):
                y_ref[k, hi, lo] = added(y_ref[k, hi, lo], held[k, hi, lo, y_side])
        low_copy(k).start()

    def low_stage(k):
        low_copy(k).wait_recv()
        for hi in range(2):
            low_ref[k, hi] = added(low_ref[k, hi], y_ref[k, hi, low_side])
        high_copy(k).start()

    def high_stage(k):
        high_copy(k).wait_recv()
        out_ref[k] = high_ref[k].astype(F32) + low_ref[k, high_side].astype(F32)

    def small_stage(s):
        small_copy(s).wait_recv()
        small_ref[s + 1] = small_ref[s] + small_got[s]
        if s + 1 < len(peers):
            small_copy(s + 1).start()

    chunk = moving.shape[4]
    each = du_hbm.shape[2] // 2 // chunk
    phases = [
        (False, dy_hbm, f_hbm, each, lambda c: c * chunk, lambda c: (each + c) * chunk),
        (True, n_hbm, du_hbm, each, lambda c: c * chunk, lambda c: (each + c) * chunk),
        (False, db_hbm, c_hbm, 1, lambda c: 0 * c, lambda c: 0 * c + chunk),
        (True, e_hbm, dqkv_hbm, 3, lambda c: 2 * c * chunk, lambda c: (2 * c + 1) * chunk),
    ]

    def still_copy(p):
        return pltpu.make_async_copy(phases[p][1].at[0:2], still.at[p % 2], still_sem.at[p % 2])

    def moving_copies(p, c, slot):
        _, _, source, _, own_at, oth_at = phases[p]
        return [
            pltpu.make_async_copy(
                source.at[0:2, :, pl.ds(pl.multiple_of(at(c), chunk), chunk)],
                moving.at[slot, part],
                moving_sem.at[slot, part],
            )
            for part, at in enumerate((own_at, oth_at))
        ]

    still_copy(0).start()
    for copy in moving_copies(0, 0, 0):
        copy.start()
    still_copy(1).start()
    small_ref[0] = packed_ref[...]
    small_copy(0).start()

    tokens = 2 * still.shape[2]
    base = 0
    for p, (wide, _, _, count, _, _) in enumerate(phases):
        still_copy(p).wait()
        stay = still.at[p % 2]
        if wide:
            for micro in range(2):
                turned[:, micro * tokens // 2 : (micro + 1) * tokens // 2] = stay[micro].T

        @pl.loop(0, count)
        def _(c, p=p, wide=wide, count=count, base=base, stay=stay):
            k = base + c
            slot = lax.rem(k, 2)
            for copy in moving_copies(p, c, slot):
                copy.wait()

            @pl.when(c + 1 < count)
            def _():
                for copy in moving_copies(p, c + 1, 1 - slot):
                    copy.start()

            if p + 1 < len(phases):

                @pl.when(c + 1 == count)
                def _():
                    for copy in moving_copies(p + 1, 0, 1 - slot):
                        copy.start()

            @pl.when(k >= 2)
            def _():
                near_copy(k, slot).wait_send()

            def product(part, store):
                block = moving[slot, part].reshape(tokens, chunk)
                if wide:
                    result = dot_nn(turned[...], block).astype(LOW)
                    for z in range(4):
                        for side in range(2):
                            at = (2 * z + side) * QB
                            store(z, side, slice(None), result[at : at + QB, :])
                else:
                    result = dot_nn(block.T, stay[...].reshape(tokens, -1)).astype(LOW)
                    for z in range(4):
                        for side in range(2):
                            at = (2 * z + side) * QB
                            for q in range(chunk // QB):
                                lanes = slice(q * QB, (q + 1) * QB)
                                store(z, side, lanes, result[lanes, at : at + QB])

            def to_given(z, side, lanes, value):
                given[slot, z // 2, z % 2, side, :, lanes] = value

            def to_held(z, side, lanes, value):
                held[k, z // 2, z % 2, side, :, lanes] = value

            product(1, to_given)
            near_copy(k, slot).start()
            product(0, to_held)

            @pl.when(k >= 1)
            def _():
                near_stage(k - 1)

            for s in range(len(peers)):

                @pl.when(k == 2 * s + 1)
                def _(s=s):
                    small_stage(s)

            @pl.when((k >= 5) & (lax.rem(k, 3) == 2))
            def _():
                y_stage((k - 5) // 3)

        if p + 2 < len(phases):
            still_copy(p + 2).start()
        base += count

    near_stage(total - 1)
    early = (total - 1 - 5) // 3 + 1
    for k in range(early):
        low_stage(k)
    for k in range(early - 1):
        high_stage(k)

    @pl.loop(early, total)
    def _(k):
        y_stage(k)
        high_stage(k - 1)
        low_stage(k)

    high_stage(total - 1)
    summed_ref[...] = small_ref[len(peers)]
    near_copy(total - 2, (total - 2) % 2).wait_send()
    near_copy(total - 1, (total - 1) % 2).wait_send()

    @pl.loop(0, total)
    def _(k):
        y_copy(k).wait_send()
        low_copy(k).wait_send()
        high_copy(k).wait_send()

    for s in range(len(peers)):
        small_copy(s).wait_send()


def summed_grads(f, dy, context, db, n, du, e, dqkv, packed):
    rows, width = dy.shape[1:]
    chunk = 512
    total = du.shape[2] // chunk + 4
    dma = pltpu.SemaphoreType.DMA
    anywhere = pl.BlockSpec(memory_space=pl.ANY)
    local = pl.BlockSpec(memory_space=pltpu.VMEM)
    return pl.pallas_call(
        grads_kernel,
        in_specs=[anywhere] * 8 + [local],
        out_specs=[local, local],
        out_shape=[
            jax.ShapeDtypeStruct((total, QB, chunk), F32),
            jax.ShapeDtypeStruct(packed.shape, F32),
        ],
        scratch_shapes=[
            pltpu.VMEM((2, 2, rows, width), LOW),
            pltpu.VMEM((2, 2, 2, rows, chunk), LOW),
            pltpu.VMEM((width, 2 * rows), LOW),
            pltpu.VMEM((2, 2, 2, 2, QB, chunk), LOW),
            pltpu.VMEM((total, 2, 2, 2, QB, chunk), LOW),
            pltpu.VMEM((total, 2, 2, 2, QB, chunk), LOW),
            pltpu.VMEM((total, 2, 2, QB, chunk), LOW),
            pltpu.VMEM((total, 2, QB, chunk), LOW),
            pltpu.VMEM((total, QB, chunk), LOW),
            pltpu.VMEM((6,) + packed.shape, F32),
            pltpu.VMEM((5,) + packed.shape, F32),
            dma((2,)),
            dma((2, 2)),
            dma((2,)),
            dma((total,)),
            dma((total,)),
            dma((total,)),
            dma((total,)),
            dma((total,)),
            dma((total,)),
            dma((total,)),
            dma((5,)),
            dma((5,)),
        ],
        compiler_params=pltpu.CompilerParams(
            collective_id=0, has_side_effects=True, vmem_limit_bytes=TAIL_VMEM
        ),
        cost_estimate=cost_of(150),
        name="summed_grads",
    )(f, dy, context, db, n, du, e, dqkv, packed)


def swapped(value, axis, bit):
    pairs = [(at, at ^ bit) for at in range(lax.axis_size(axis))]
    return lax.ppermute(value, axis, pairs)


def paired_body(
    layer_input,
    segment_ids,
    buckets,
    attn_in,
    attn_out,
    ffn_in,
    ffn_out,
    norm_gain,
    bert_shift,
    head_bias,
    ffn_bias,
    position_bias,
    decoder_grads,
):
    micro_count, _, rows, width = layer_input.shape
    length = segment_ids.shape[2]
    heads, bucket_count = position_bias.shape
    section = lax.axis_index("section")
    core = lax.axis_index("tensor")
    leading = section == 0
    lead = jnp.where(leading, 1, 0).astype(jnp.int32)
    pieces = lax.axis_size("dp")

    remote_grads = [lax.ppermute(decoder_grads[0, 0, 0], "section", [(0, 1)])]
    qkv_own = attn_in[0].reshape(width, -1)
    qkv_oth = swapped(qkv_own, "tensor", 1)
    wo = (attn_out[0], swapped(attn_out[0], "tensor", 1))
    up = (ffn_in[0], swapped(ffn_in[0], "tensor", 1))
    down = (ffn_out[0], swapped(ffn_out[0], "tensor", 1))
    small = jnp.concatenate([head_bias.reshape(-1), ffn_bias, position_bias.reshape(-1)])
    small_oth = swapped(small, "tensor", 1)
    near_heads = head_bias.size
    near_ffn = near_heads + ffn_bias.size
    both_small = jnp.stack([small, small_oth])
    head_both = both_small[:, :near_heads].reshape(2, 2, -1)
    ffn_both = jnp.where(leading, both_small[:, near_heads:near_ffn], 0.0).reshape(1, -1)
    table_both = jnp.where(leading, 0.0, both_small[:, near_ffn:]).reshape(2 * heads, bucket_count)
    q_shift = head_both[:, 0].reshape(1, -1)
    v_shift = head_both[:, 1].reshape(1, -1)
    qkv_shift = jnp.where(
        leading, jnp.concatenate([q_shift, jnp.zeros_like(q_shift), v_shift], axis=1), 0.0
    )
    gains = jnp.where(leading, norm_gain[0], norm_gain[1])
    entry_gain = gains[0:1]

    near = length - 1 - 3 * QB
    near_hits = (buckets[None, near : near + 6 * QB] == jnp.arange(bucket_count)[:, None]).astype(F32)
    bias = toeplitz(jnp.dot(table_both, near_hits, precision=lax.Precision.HIGHEST))

    window = rows + REACH
    base = core * (length - window)
    segments = jnp.pad(
        lax.dynamic_slice_in_dim(segment_ids[:, 0], base, window, axis=1),
        ((0, 0), (PAD * QB, PAD * QB)),
        constant_values=-1,
    )
    reach_blocks = REACH // QB
    own_block = PAD + core * reach_blocks
    halo_block = jnp.where(core == 0, PAD + rows // QB, PAD)
    edge = jnp.where(core == 0, rows - REACH, 0)

    def info_of(slot):
        return jnp.stack([lead, slot, own_block, halo_block, edge]).astype(jnp.int32)

    received = jnp.zeros((rows, width), LOW)
    entered = attended = fed = None
    results = []
    finished = []
    for moment in range(micro_count + 1):
        slot = jnp.where(leading, moment, (moment + micro_count) % (micro_count + 1))
        info = info_of(slot)
        micro = jnp.minimum(slot, micro_count - 1)
        own_rows = layer_input[min(moment, micro_count - 1), 0]
        row_segments = lax.dynamic_index_in_dim(segments, micro, 0, keepdims=False)
        *entered, halo = enter(info, own_rows, received, entry_gain, qkv_shift, qkv_own, qkv_oth, entered)
        halo = swapped(halo, "tensor", 1)
        attended = attend(info, row_segments, entered[2], halo, bias, attended)
        if moment < micro_count:
            info, remote_grads[moment] = lax.optimization_barrier((info, remote_grads[moment]))
        *fed, result = feed(
            info, entered[0], attended[0], wo, up, down, ffn_both, gains, bert_shift, fed
        )
        results.append(result)
        if moment == 0:
            received = lax.ppermute(result, "section", [(0, 1)])
            later, received = lax.optimization_barrier((decoder_grads[0, 1, 0], received))
            remote_grads.append(lax.ppermute(later, "section", [(0, 1)]))
        elif moment < micro_count:
            received = lax.ppermute(result, "section", [(0, 1), (1, 0)])
            finished.append(received)
    finished.append(lax.ppermute(result, "section", [(1, 0)]))
    x_saved, e_saved, qkv_saved = entered
    context, lse, *halo_saved = attended
    f_saved, slope_saved, n_saved, one_saved, two_saved = fed

    received = jnp.zeros((rows, width), LOW)
    feed_kept = table_kept = entry_kept = None
    input_low = []
    input_lower = []
    for moment in range(micro_count + 1):
        slot = jnp.where(leading, (moment + micro_count) % (micro_count + 1), moment)
        info = info_of(slot)
        micro = jnp.minimum(slot, micro_count - 1)
        at = min(moment, micro_count - 1)
        row_segments = lax.dynamic_index_in_dim(segments, micro, 0, keepdims=False)
        *feed_kept, dz, grad_context = feed_back(
            info, received, decoder_grads[0, at, 0], remote_grads[at], one_saved, two_saved, slope_saved,
            wo, up, down, gains, feed_kept,
        )
        dq, dk, dv, table_kept, far = attend_back(
            info, row_segments, qkv_saved, halo_saved, grad_context, bias, lse, table_kept
        )
        far = swapped(far, "tensor", 1)
        if moment == 0:
            info, finished[-1] = lax.optimization_barrier((info, finished[-1]))
        *entry_kept, low, lower = enter_back(
            info, dq, dk, dv, far, x_saved, dz, qkv_own, qkv_oth, entry_gain, entry_kept
        )
        if moment >= 1:
            input_low.append(low)
            input_lower.append(lower)
        if moment < micro_count:
            received = lax.ppermute(low, "section", [(1, 0)])
    dqkv_saved, stat_entry = entry_kept

    dy_saved, du_saved, db_saved, stat_feed, stat_bias = feed_kept

    half = width // 2
    upper = lax.ppermute(jnp.stack(input_low)[:, :, half:], "section", [(0, 1)]).astype(F32)
    input_grad = jnp.where(leading, jnp.stack(input_lower), upper)[:, None]

    near_table = jnp.dot(diagonals(table_kept, micro_count), near_hits.T, precision=lax.Precision.HIGHEST)

    def placed(pair):
        return jnp.where(core == 0, pair, pair[::-1])

    stat_feed = stat_feed[0] + stat_feed[1]
    stat_entry = stat_entry[0] + stat_entry[1]
    gain_first = jnp.where(leading, stat_feed[0:1], stat_entry[2:3])
    gain_rows = jnp.concatenate([gain_first, stat_feed[1:2]])
    nothing = jnp.zeros_like(gain_rows)
    gain_all = jnp.where(leading, jnp.concatenate([gain_rows, nothing]), jnp.concatenate([nothing, gain_rows]))
    shift_all = jnp.where(leading, stat_feed[2:6], 0.0)
    head_all = jnp.where(leading, stat_entry[0:2], 0.0).reshape(2, 2, -1)
    head_all = placed(jnp.moveaxis(head_all, 1, 0))
    bias_all = placed(jnp.where(leading, stat_bias[0] + stat_bias[1], 0.0).reshape(2, -1))
    table_all = placed(jnp.where(leading, 0.0, near_table).reshape(2, heads, bucket_count))
    parts = [gain_all, shift_all, head_all, bias_all, table_all]
    packed = jnp.concatenate([part.reshape(-1) for part in parts])
    packed_rows = 8 * (-(-packed.size // (8 * width)))
    packed = jnp.pad(packed, (0, packed_rows * width - packed.size)).reshape(packed_rows, width)
    summed, packed = summed_grads(
        f_saved, dy_saved, context, db_saved, n_saved, du_saved, e_saved, dqkv_saved, packed
    )
    packed = packed.reshape(-1)
    quarters = ffn_in.shape[2] // summed.shape[2]
    piece = width // pieces
    down_sum = summed[:quarters].reshape(quarters, QB, -1, QB).transpose(0, 2, 1, 3).reshape(-1, piece)
    up_sum = summed[quarters : 2 * quarters].transpose(1, 0, 2).reshape(piece, -1)
    out_sum = summed[2 * quarters].reshape(QB, -1, QB).transpose(1, 0, 2).reshape(-1, piece)
    qkv_sum = summed[2 * quarters + 1 :].transpose(1, 0, 2)
    unpacked = []
    start = 0
    for part in parts:
        unpacked.append(packed[start : start + part.size].reshape(part.shape))
        start += part.size
    gain_all, shift_all, head_all, bias_all, table_all = unpacked
    mine = lambda value: lax.dynamic_index_in_dim(value, core, 0, keepdims=False)
    return (
        jnp.where(leading, jnp.stack(finished), jnp.stack(results[1:]))[None, :, None],
        input_grad,
        qkv_sum[None],
        out_sum[None],
        up_sum[None],
        down_sum[None],
        gain_all.reshape(norm_gain.shape),
        shift_all,
        mine(head_all),
        mine(bias_all),
        mine(table_all),
    )


def solution(mesh):
    placed = (
        P(None, "dp", "tensor", None),
        P(None, "dp", None),
        P(),
        P("section", None, None, "tensor"),
        P("section", "tensor", None),
        P("section", None, "tensor"),
        P("section", "tensor", None),
        P(),
        P(),
        P(None, "tensor"),
        P("tensor"),
        P("tensor", None),
        P("section", None, "dp", "tensor", None),
    )
    paired = mesh.shape["tensor"] == 2 and mesh.shape["dp"] == 8
    return jax.shard_map(
        paired_body if paired else general_body,
        mesh=mesh,
        in_specs=placed,
        out_specs=(
            P("section", None, "dp", "tensor", None),
            P(None, "dp", "tensor", "section"),
            P("section", "dp", None, "tensor"),
            P("section", "tensor", "dp"),
            P("section", "dp", "tensor"),
            P("section", "tensor", "dp"),
            P(),
            P(),
            P(None, "tensor"),
            P("tensor"),
            P("tensor", None),
        ),
        check_vma=False,
    )
```

```python
import functools

import jax
import jax.numpy as jnp
from jax import lax
from jax.experimental import pallas as pl
from jax.experimental.pallas import tpu as pltpu
from jax.sharding import PartitionSpec as P

DH = 64
QB = 128
PAD = 2
REACH = 256
STRIP = 64
HEAD_SPAN = 512
FEED_CHUNK = 1024
VMEM = 56 * 1024 * 1024
TAIL_VMEM = 60 * 1024 * 1024
LOW = jnp.bfloat16
F32 = jnp.float32


def dot_nt(left, right):
    return lax.dot_general(left, right, (((1,), (1,)), ((), ())), preferred_element_type=F32)


def dot_nn(left, right):
    return lax.dot_general(left, right, (((1,), (0,)), ((), ())), preferred_element_type=F32)


def params():
    return pltpu.CompilerParams(vmem_limit_bytes=VMEM)


def cost_of(micros):
    return pl.CostEstimate(flops=int(micros * 5e7), bytes_accessed=0, transcendentals=0)


def slotted(shape, dtype):
    return jax.ShapeDtypeStruct((3,) + shape, dtype)


def call_with_slots(
    kernel, scalars, inputs, in_specs, outputs, out_specs, previous, grid, scratch, name, micros
):
    count = len(inputs)
    kept = [] if previous is None else [item for item in previous if item is not None]
    aliases = {}
    if previous is not None:
        at = len(scalars) + count
        for index, item in enumerate(previous):
            if item is not None:
                aliases[at] = index
                at += 1

    def gated(spec):
        return pl.BlockSpec(spec.block_shape, lambda j, s, *rest: spec.index_map(j * s[5], s, *rest))

    in_specs = [gated(spec) for spec in in_specs]
    out_specs = [gated(spec) for spec in out_specs]

    def run(*refs):
        @pl.when(refs[0][5] == 1)
        def _():
            front = len(scalars) + count
            kernel(*refs[:front], *refs[front + len(kept) :])

    return pl.pallas_call(
        run,
        grid_spec=pltpu.PrefetchScalarGridSpec(
            num_scalar_prefetch=len(scalars),
            grid=grid,
            in_specs=list(in_specs) + [pl.BlockSpec(memory_space=pl.ANY)] * len(kept),
            out_specs=out_specs,
            scratch_shapes=scratch,
        ),
        out_shape=outputs,
        input_output_aliases=aliases,
        compiler_params=params(),
        cost_estimate=cost_of(micros),
        name=name,
    )(*scalars, *inputs, *kept)


def toeplitz_kernel(flag_ref, w_ref, t_ref):
    width = w_ref.shape[2]

    @pl.when(flag_ref[0] == 0)
    def _():
        t_ref[...] = jnp.zeros_like(t_ref)

    @pl.when(flag_ref[0] == 1)
    def _():
        half = []
        for head in range(2):
            rows = jnp.broadcast_to(w_ref[0, head : head + 1, :], (QB, width))
            rolled = pltpu.roll(rows, 0, 1, stride=1, stride_axis=0)
            half.append(rolled.T[QB:, :])
        t_ref[0] = jnp.concatenate(half, axis=1)


def toeplitz(flag, offset_bias):
    heads, width = offset_bias.shape
    pairs = heads // 2
    return pl.pallas_call(
        toeplitz_kernel,
        grid_spec=pltpu.PrefetchScalarGridSpec(
            num_scalar_prefetch=1,
            grid=(pairs,),
            in_specs=[pl.BlockSpec((1, 2, width), lambda p, s: (p, 0, 0))],
            out_specs=pl.BlockSpec((1, width - QB, 2 * QB), lambda p, s: (p, 0, 0)),
        ),
        out_shape=jax.ShapeDtypeStruct((pairs, width - QB, 2 * QB), F32),
        compiler_params=params(),
        cost_estimate=cost_of(6),
        name="toeplitz",
    )(flag, offset_bias.reshape(pairs, 2, width))


def diagonal_kernel(flag_ref, a_ref, s_ref):
    @pl.when(flag_ref[0] == 0)
    def _():
        s_ref[...] = jnp.zeros_like(s_ref)

    @pl.when(flag_ref[0] == 1)
    def _():
        sum_diagonals(a_ref, s_ref)


def sum_diagonals(a_ref, s_ref):
    total = a_ref[0, 0]
    for extra in range(1, a_ref.shape[0]):
        total = total + a_ref[extra, 0]
    total = jnp.concatenate([jnp.zeros((QB, 2 * QB), F32), total], axis=0)
    width = total.shape[0]
    row = lax.broadcasted_iota(jnp.int32, (QB, QB), 0)
    col = lax.broadcasted_iota(jnp.int32, (QB, QB), 1)
    mirror = jnp.where(row + col == QB - 1, 1.0, 0.0)
    for head in range(2):
        turned = lax.dot_general(
            mirror,
            total[:, head * QB : (head + 1) * QB],
            (((1,), (1,)), ((), ())),
            precision=lax.Precision.HIGHEST,
            preferred_element_type=F32,
        )
        aligned = pltpu.roll(turned, width - QB + 1, 1, stride=1, stride_axis=0)
        s_ref[0, head : head + 1, :] = jnp.sum(aligned, axis=0, keepdims=True)


def diagonals(flag, tables, steps):
    _, pairs, rows, _ = tables.shape
    width = rows + QB
    out = pl.pallas_call(
        diagonal_kernel,
        grid_spec=pltpu.PrefetchScalarGridSpec(
            num_scalar_prefetch=1,
            grid=(pairs,),
            in_specs=[pl.BlockSpec((steps, 1, rows, 2 * QB), lambda p, s: (0, p * s[0], 0, 0))],
            out_specs=pl.BlockSpec((1, 2, width), lambda p, s: (p, 0, 0)),
        ),
        out_shape=jax.ShapeDtypeStruct((pairs, 2, width), F32),
        compiler_params=params(),
        cost_estimate=cost_of(10),
        name="diagonals",
    )(flag, tables)
    return out.reshape(2 * pairs, width)


def two_heads(block, first):
    zero = jnp.zeros_like(block)
    return jnp.concatenate([jnp.where(first, block, zero), jnp.where(first, zero, block)], axis=0)


def joined_heads(turned):
    return jnp.concatenate([turned[:DH, :QB], turned[DH:, QB:]], axis=0).T


def fill_columns(segq_ref, segk_ref):
    for block in range(segq_ref.shape[0]):
        rows = jnp.broadcast_to(segq_ref[block : block + 1, :], (QB, QB))
        segk_ref[block * QB : (block + 1) * QB, :] = rows.T


def visit_blocks(seg_ref, origin, count, block):
    @pl.loop(0, count)
    def _(i):
        at = i + origin
        first = seg_ref[at * QB]
        last = seg_ref[at * QB + QB - 1]
        far = (seg_ref[(at - 1) * QB - 1] == first) | (seg_ref[(at + 2) * QB] == last)

        @pl.when(far)
        def _():
            block(i, at, 2)

        @pl.when(jnp.logical_not(far))
        def _():
            block(i, at, 1)


def placed_rows(info, source, halo, target, halo_count):
    edge = PAD * QB
    rows = source.shape[0]
    target[:edge, :] = jnp.zeros((edge, target.shape[1]), target.dtype)
    target[target.shape[0] - edge :, :] = jnp.zeros((edge, target.shape[1]), target.dtype)
    target[pl.ds(pl.multiple_of(info[2] * QB, QB), rows), :] = source[...]
    if halo_count:
        target[pl.ds(pl.multiple_of(info[3] * QB, QB), halo_count), :] = halo[...]


def attend_kernel(halo_count, info, seg_ref, *refs):
    if halo_count:
        segq_ref, q_ref, k_ref, v_ref, t_ref, kh_ref, vh_ref, o_ref, lse_ref, kk_ref, vk_ref = refs[:11]
        segk_ref, kp_ref, vp_ref, vt_ref, mask_ref, score_ref, prob_ref, stat_ref = refs[11:]
        kh_ref, vh_ref = kh_ref.at[0], vh_ref.at[0]
        kk_ref[0] = kh_ref[...]
        vk_ref[0] = vh_ref[...]
    else:
        segq_ref, q_ref, k_ref, v_ref, t_ref, o_ref, lse_ref = refs[:7]
        segk_ref, kp_ref, vp_ref, vt_ref, mask_ref, score_ref, prob_ref, stat_ref = refs[7:]
        kh_ref = vh_ref = None
    rows = q_ref.shape[1]
    pairs = q_ref.shape[2] // (2 * DH)
    first = lax.broadcasted_iota(jnp.int32, (QB, 2 * DH), 1) < DH

    @pl.when(pl.program_id(0) == 0)
    def _():
        fill_columns(segq_ref, segk_ref)

    placed_rows(info, k_ref.at[0], kh_ref, kp_ref, halo_count)
    placed_rows(info, v_ref.at[0], vh_ref, vp_ref, halo_count)
    vt_ref[...] = vp_ref[...].T

    def block(i, at, reach):
        span = (2 * reach + 1) * QB
        keys = pl.ds(pl.multiple_of((at - reach) * QB, QB), span)
        mine = pl.ds(pl.multiple_of(i * QB, QB), QB)
        shifted = pl.ds((2 - reach) * QB, span)
        allowed = segk_ref[keys, :] == segq_ref[pl.ds(at, 1), :]
        mask_ref[:span, :] = jnp.where(allowed, 0.0, -jnp.inf)
        for pair in range(pairs):
            lanes = slice(pair * 2 * DH, (pair + 1) * 2 * DH)
            both = two_heads(q_ref[0, mine, lanes] * LOW(0.125), first)
            score_ref[pair, :span, :] = dot_nt(kp_ref[keys, lanes], both) + t_ref[pair, shifted, :]
        for pair in range(pairs):
            lanes = slice(pair * 2 * DH, (pair + 1) * 2 * DH)
            stats = []
            for head in range(2):
                side = slice(head * QB, (head + 1) * QB)
                top = None
                for strip in range(0, span, STRIP):
                    piece = slice(strip, strip + STRIP)
                    masked = score_ref[pair, piece, side] + mask_ref[piece, :]
                    score_ref[pair, piece, side] = masked
                    peak = jnp.max(masked.reshape(STRIP // 8, 8, QB), axis=0)
                    top = peak if top is None else jnp.maximum(top, peak)
                highest = jnp.max(top, axis=0, keepdims=True)
                total = None
                for strip in range(0, span, STRIP):
                    piece = slice(strip, strip + STRIP)
                    weights = jnp.exp(score_ref[pair, piece, side] - highest)
                    prob_ref[pair, piece, side] = weights.astype(LOW)
                    mass = jnp.sum(weights.reshape(STRIP // 8, 8, QB), axis=0)
                    total = mass if total is None else total + mass
                totals = jnp.sum(total, axis=0, keepdims=True)
                stat_ref[2 * pair + head : 2 * pair + head + 1, :] = 1.0 / totals
                stats.append(highest + jnp.log(totals))
            lse_ref[0, pair, pl.ds(i, 1), :] = jnp.concatenate(stats, axis=1)
        for pair in range(pairs):
            lanes = slice(pair * 2 * DH, (pair + 1) * 2 * DH)
            turned = dot_nn(vt_ref[lanes, keys], prob_ref[pair, :span, :])
            upper = turned[:DH, :QB] * stat_ref[2 * pair : 2 * pair + 1, :]
            lower = turned[DH:, QB:] * stat_ref[2 * pair + 1 : 2 * pair + 2, :]
            o_ref[0, mine, lanes] = jnp.concatenate([upper, lower], axis=0).T.astype(LOW)

    visit_blocks(seg_ref, info[2], rows // QB, block)


def head_specs(rows, span, groups, halo_count):
    column = lambda part: pl.BlockSpec((1, rows, span), lambda g, s, t: (s[1], 0, g + part * groups))
    halo = lambda part: pl.BlockSpec((1, halo_count, span), lambda g, s, t: (part, 0, g))
    return column, halo


def attend(info, segments, qkv, halo, bias, previous):
    _, rows, width = qkv.shape
    width = width // 3
    span = min(HEAD_SPAN, width)
    groups = width // span
    pairs = span // (2 * DH)
    count = rows // QB
    blocks = segments.shape[0] // QB
    halo_count = 0 if halo is None else halo.shape[1]
    column, halo_spec = head_specs(rows, span, groups, halo_count)
    slot_pairs = pl.BlockSpec((1, pairs, count, 2 * QB), lambda g, s, t: (s[1], g, 0, 0))
    in_specs = [
        pl.BlockSpec((blocks, QB), lambda g, s, t: (0, 0)),
        column(0),
        column(1),
        column(2),
        pl.BlockSpec((pairs,) + bias.shape[1:], lambda g, s, t: (g, 0, 0)),
    ]
    inputs = [segments.reshape(blocks, QB), qkv, qkv, qkv, bias]
    outputs = [slotted((rows, width), LOW), slotted((groups * pairs, count, 2 * QB), F32)]
    out_specs = [column(0), slot_pairs]
    if halo_count:
        in_specs += [halo_spec(0), halo_spec(1)]
        inputs += [halo, halo]
        outputs += [slotted((halo_count, width), LOW)] * 2
        kept = pl.BlockSpec((1, halo_count, span), lambda g, s, t: (s[1], 0, g))
        out_specs += [kept, kept]
    return call_with_slots(
        functools.partial(attend_kernel, halo_count),
        [info, segments],
        inputs,
        in_specs,
        outputs,
        out_specs,
        previous,
        (groups,),
        [
            pltpu.VMEM((blocks * QB, QB), jnp.int32),
            pltpu.VMEM((blocks * QB, span), LOW),
            pltpu.VMEM((blocks * QB, span), LOW),
            pltpu.VMEM((span, blocks * QB), LOW),
            pltpu.VMEM((5 * QB, QB), F32),
            pltpu.VMEM((pairs, 5 * QB, 2 * QB), F32),
            pltpu.VMEM((pairs, 5 * QB, 2 * QB), LOW),
            pltpu.VMEM((8, QB), F32),
        ],
        "attend",
        24,
    )


def attend_back_kernel(halo_count, info, seg_ref, *refs):
    if halo_count:
        segq_ref, q_ref, k_ref, v_ref, g_ref, t_ref, lse_ref, kh_ref, vh_ref = refs[:9]
        dq_ref, dk_ref, dv_ref, diag_ref, dh_ref = refs[9:14]
        segk_ref, kp_ref, vp_ref, kt_ref, dk_acc, dv_acc = refs[14:]
        kh_ref, vh_ref = kh_ref.at[0], vh_ref.at[0]
    else:
        segq_ref, q_ref, k_ref, v_ref, g_ref, t_ref, lse_ref = refs[:7]
        dq_ref, dk_ref, dv_ref, diag_ref = refs[7:11]
        segk_ref, kp_ref, vp_ref, kt_ref, dk_acc, dv_acc = refs[11:]
        kh_ref = vh_ref = None
    rows = q_ref.shape[1]
    pairs = q_ref.shape[2] // (2 * DH)
    first = lax.broadcasted_iota(jnp.int32, (QB, 2 * DH), 1) < DH

    @pl.when(pl.program_id(0) == 0)
    def _():
        fill_columns(segq_ref, segk_ref)

    placed_rows(info, k_ref.at[0], kh_ref, kp_ref, halo_count)
    placed_rows(info, v_ref.at[0], vh_ref, vp_ref, halo_count)
    kt_ref[...] = kp_ref[...].T
    dk_acc[...] = jnp.zeros_like(dk_acc)
    dv_acc[...] = jnp.zeros_like(dv_acc)
    diag_ref[...] = jnp.zeros_like(diag_ref)

    def block(i, at, reach):
        span = (2 * reach + 1) * QB
        keys = pl.ds(pl.multiple_of((at - reach) * QB, QB), span)
        mine = pl.ds(pl.multiple_of(i * QB, QB), QB)
        shifted = pl.ds((2 - reach) * QB, span)
        allowed = segk_ref[keys, :] == segq_ref[pl.ds(at, 1), :]
        allowed = jnp.concatenate([allowed, allowed], axis=1)
        for pair in range(pairs):
            lanes = slice(pair * 2 * DH, (pair + 1) * 2 * DH)
            both = two_heads(q_ref[0, mine, lanes] * LOW(0.125), first)
            grads = two_heads(g_ref[mine, lanes], first)
            scores = dot_nt(kp_ref[keys, lanes], both) + t_ref[pair, shifted, :]
            scores = jnp.where(allowed, scores - lse_ref[0, pair, pl.ds(i, 1), :], -jnp.inf)
            probs = jnp.exp(scores)
            grad_probs = dot_nt(vp_ref[keys, lanes], grads)
            dv_acc[keys, lanes] += dot_nn(probs.astype(LOW), grads)
            inner = jnp.sum(probs * grad_probs, axis=0, keepdims=True)
            rounded = (probs * (grad_probs - inner)).astype(LOW)
            dk_acc[keys, lanes] += dot_nn(rounded, both)
            diag_ref[0, pair, shifted, :] += rounded.astype(F32)
            turned = dot_nn(kt_ref[lanes, keys], rounded)
            dq_ref[mine, lanes] = (joined_heads(turned) * 0.125).astype(LOW)

    visit_blocks(seg_ref, info[2], rows // QB, block)
    own = pl.ds(pl.multiple_of(info[2] * QB, QB), rows)
    dk_ref[...] = dk_acc[own, :].astype(LOW)
    dv_ref[...] = dv_acc[own, :].astype(LOW)
    if halo_count:
        far = pl.ds(pl.multiple_of(info[3] * QB, QB), halo_count)
        dh_ref[0] = dk_acc[far, :].astype(LOW)
        dh_ref[1] = dv_acc[far, :].astype(LOW)


def attend_back(info, segments, qkv, halo_kept, grad_context, bias, lse, previous):
    _, rows, width = qkv.shape
    width = width // 3
    span = min(HEAD_SPAN, width)
    groups = width // span
    pairs = span // (2 * DH)
    count = rows // QB
    blocks = segments.shape[0] // QB
    halo_count = 0 if halo_kept is None else halo_kept[0].shape[1]
    column, _ = head_specs(rows, span, groups, halo_count)
    plain = pl.BlockSpec((rows, span), lambda g, s, t: (0, g))
    in_specs = [
        pl.BlockSpec((blocks, QB), lambda g, s, t: (0, 0)),
        column(0),
        column(1),
        column(2),
        plain,
        pl.BlockSpec((pairs,) + bias.shape[1:], lambda g, s, t: (g, 0, 0)),
        pl.BlockSpec((1, pairs, count, 2 * QB), lambda g, s, t: (s[1], g, 0, 0)),
    ]
    inputs = [segments.reshape(blocks, QB), qkv, qkv, qkv, grad_context, bias, lse]
    plain_shape = jax.ShapeDtypeStruct((rows, width), LOW)
    outputs = [plain_shape] * 3 + [slotted(bias.shape, F32)]
    out_specs = [plain] * 3 + [
        pl.BlockSpec((1, pairs) + bias.shape[1:], lambda g, s, t: (s[1], g, 0, 0))
    ]
    if halo_count:
        kept = pl.BlockSpec((1, halo_count, span), lambda g, s, t: (s[1], 0, g))
        in_specs += [kept, kept]
        inputs += list(halo_kept)
        outputs.append(jax.ShapeDtypeStruct((2, halo_count, width), LOW))
        out_specs.append(pl.BlockSpec((2, halo_count, span), lambda g, s, t: (0, 0, lax.rem(g + groups // 2, groups))))
    keep = None if previous is None else [None] * 3 + [previous] + [None] * (len(outputs) - 4)
    return call_with_slots(
        functools.partial(attend_back_kernel, halo_count),
        [info, segments],
        inputs,
        in_specs,
        outputs,
        out_specs,
        keep,
        (groups,),
        [
            pltpu.VMEM((blocks * QB, QB), jnp.int32),
            pltpu.VMEM((blocks * QB, span), LOW),
            pltpu.VMEM((blocks * QB, span), LOW),
            pltpu.VMEM((span, blocks * QB), LOW),
            pltpu.VMEM((blocks * QB, span), F32),
            pltpu.VMEM((blocks * QB, span), F32),
        ],
        "attend_back",
        26,
    )


def exchange_kernel(give_ref, get_ref, send_sem, recv_sem):
    peer = {"tensor": 1 - lax.axis_index("tensor")}
    barrier = pltpu.get_barrier_semaphore()
    pl.semaphore_signal(barrier, inc=1, device_id=peer, device_id_type=pl.DeviceIdType.MESH)
    pl.semaphore_wait(barrier, 1)
    copy = pltpu.make_async_remote_copy(
        src_ref=give_ref, dst_ref=get_ref, send_sem=send_sem, recv_sem=recv_sem,
        device_id=peer, device_id_type=pl.DeviceIdType.MESH,
    )
    copy.start()
    copy.wait()


def exchanged(value):
    return pl.pallas_call(
        exchange_kernel,
        in_specs=[pl.BlockSpec(memory_space=pl.ANY)],
        out_specs=pl.BlockSpec(memory_space=pl.ANY),
        out_shape=jax.ShapeDtypeStruct(value.shape, value.dtype),
        scratch_shapes=[pltpu.SemaphoreType.DMA, pltpu.SemaphoreType.DMA],
        compiler_params=pltpu.CompilerParams(collective_id=1, has_side_effects=True),
        cost_estimate=cost_of(3),
        name="exchange",
    )(value)


def mean_of(block):
    return jnp.mean(block, axis=-1, keepdims=True)


def rms_scale(block):
    return lax.rsqrt(mean_of(block * block) + 1e-06)


def sum_rows(block):
    return jnp.sum(block, axis=0, keepdims=True)


def gelu_parts(u):
    bell = jnp.exp(u * u * -0.5)
    below = 0.5 + 0.5 * lax.erf(u * 0.7071067811865476)
    return u * below, below + u * (bell * 0.3989422804014327)


def enter_kernel(info, first_ref, second_ref, gain_ref, shift_ref, own_ref, oth_ref, x_ref, e_ref, qkv_ref, halo_ref):
    m = pl.program_id(0)
    half = own_ref.shape[1]

    @pl.when((m == 0) & (info[0] == 1))
    def _():
        x_ref[0] = first_ref[...]
        e_ref[0] = first_ref[...]

    @pl.when((m == 0) & (info[0] == 0))
    def _():
        x_ref[0] = second_ref[...]
        x = second_ref[...].astype(F32)
        e_ref[0] = (x * rms_scale(x) * gain_ref[...]).astype(LOW)

    e = e_ref[0]
    for part, weight in enumerate((own_ref, oth_ref)):
        lanes = slice(part * half, (part + 1) * half)
        block = (dot_nn(e, weight[...]) + shift_ref[:, lanes]).astype(LOW)
        qkv_ref[0, :, lanes] = block
    start = pl.ds(pl.multiple_of(info[4], QB), halo_ref.shape[1])
    halo_ref[0, :, :half] = qkv_ref[0, start, half:]
    halo_ref[0, :, half:] = qkv_ref[0, start, :half]


def enter(info, first, second, gain, shift, own, oth, previous):
    rows, width = first.shape
    half = own.shape[1] // 3
    whole = pl.BlockSpec((rows, width), lambda m, s: (0, 0))
    weight = pl.BlockSpec((width, half), lambda m, s: (0, m))
    kept = pl.BlockSpec((1, rows, width), lambda m, s: (s[1], 0, 0))
    keep = None if previous is None else list(previous) + [None]
    return call_with_slots(
        enter_kernel,
        [info],
        [first, second, gain, shift, own, oth],
        [
            whole,
            whole,
            pl.BlockSpec((1, width), lambda m, s: (0, 0)),
            pl.BlockSpec((1, 2 * half), lambda m, s: (0, m)),
            weight,
            weight,
        ],
        [
            slotted((rows, width), LOW),
            slotted((rows, width), LOW),
            slotted((rows, 6 * half), LOW),
            jax.ShapeDtypeStruct((2, REACH, 2 * half), LOW),
        ],
        [
            kept,
            kept,
            pl.BlockSpec((1, rows, 2 * half), lambda m, s: (s[1], 0, m)),
            pl.BlockSpec((1, REACH, 2 * half), lambda m, s: (jnp.maximum(m - 1, 0), 0, 0)),
        ],
        keep,
        (3,),
        [],
        "enter",
        9,
    )


def feed_kernel(
    info, x_ref, c_ref, wo_own, wo_oth, up_own, up_oth, down_own, down_oth, bias_ref, gain_ref, shift_ref,
    f_ref, slope_ref, n_ref, one_ref, two_ref, out_ref, acc_ref, carry_ref, hidden_ref
):
    j = pl.program_id(0)
    steps = pl.num_programs(0)
    half = wo_own.shape[0]
    rows = x_ref.shape[1]

    @pl.when(j == 0)
    def _():
        joined = (
            dot_nn(c_ref[0, :, :half], wo_own[...])
            + dot_nn(c_ref[0, :, half:], wo_oth[...])
            + x_ref[0].astype(F32)
        )

        @pl.when(info[0] == 1)
        def _():
            before = joined + shift_ref[0:1, :]
            one_ref[0] = before.astype(LOW)
            center = before - mean_of(before)
            normed = center * lax.rsqrt(mean_of(center * center) + 1e-05) * gain_ref[0:1, :] + shift_ref[2:3, :]
            carry_ref[...] = normed
            n_ref[0] = normed.astype(LOW)

        @pl.when(info[0] == 0)
        def _():
            one_ref[0] = joined.astype(LOW)
            carry_ref[...] = joined
            n_ref[0] = (joined * rms_scale(joined) * gain_ref[1:2, :]).astype(LOW)

        acc_ref[...] = jnp.zeros_like(acc_ref)

    each = (steps - 1) // 2
    now = lax.rem(j, 2)

    def rise(up):
        u = dot_nn(n_ref[0], up[...]) + bias_ref[...]
        f, slope = gelu_parts(u)
        low = f.astype(LOW)
        f_ref[0] = low
        hidden_ref[now] = low
        slope_ref[0] = slope.astype(LOW)

    def fall(down):
        acc_ref[...] += dot_nn(hidden_ref[1 - now], down[...])

    @pl.when(j == 0)
    def _():
        rise(up_own)

    @pl.when((j > 0) & (j < each))
    def _():
        rise(up_own)
        fall(down_own)

    @pl.when(j == each)
    def _():
        rise(up_oth)
        fall(down_own)

    @pl.when((j > each) & (j < steps - 1))
    def _():
        rise(up_oth)
        fall(down_oth)

    @pl.when(j == steps - 1)
    def _():
        fall(down_oth)

    @pl.when(j == steps - 1)
    def _():
        joined = carry_ref[...] + acc_ref[...]

        @pl.when(info[0] == 1)
        def _():
            before = joined + shift_ref[1:2, :]
            two_ref[0] = before.astype(LOW)
            center = before - mean_of(before)
            normed = center * lax.rsqrt(mean_of(center * center) + 1e-05) * gain_ref[1:2, :] + shift_ref[3:4, :]
            out_ref[...] = normed.astype(LOW)

        @pl.when(info[0] == 0)
        def _():
            two_ref[0] = joined.astype(LOW)
            out_ref[...] = joined.astype(LOW)


def split_steps(hidden, chunk):
    each = hidden // chunk
    near = lambda j: jnp.minimum(j, each - 1)
    far = lambda j: jnp.maximum(j - each, 0)
    return 2 * each, near, far


def feed(info, x, context, wo, up, down, bias, gains, shifts, previous):
    _, rows, width = x.shape
    hidden = up[0].shape[1]
    chunk = min(FEED_CHUNK, hidden)
    each = hidden // chunk
    steps = 2 * each + 1
    rise = lambda j: jnp.minimum(j, 2 * each - 1)
    fall = lambda j: jnp.maximum(j - 1, 0)
    near = lambda j: jnp.minimum(j, each - 1)
    far = lambda j: jnp.maximum(j - each, 0)
    kept = pl.BlockSpec((1, rows, width), lambda j, s: (s[1], 0, 0))
    fixed = lambda a: pl.BlockSpec(a.shape, lambda j, s: (0, 0))
    moving = pl.BlockSpec((1, rows, chunk), lambda j, s: (s[1], 0, rise(j)))
    keep = None if previous is None else list(previous) + [None]
    return call_with_slots(
        feed_kernel,
        [info],
        [x, context, wo[0], wo[1], up[0], up[1], down[0], down[1], bias, gains, shifts],
        [
            kept,
            kept,
            fixed(wo[0]),
            fixed(wo[1]),
            pl.BlockSpec((width, chunk), lambda j, s: (0, near(rise(j)))),
            pl.BlockSpec((width, chunk), lambda j, s: (0, far(rise(j)))),
            pl.BlockSpec((chunk, width), lambda j, s: (near(fall(j)), 0)),
            pl.BlockSpec((chunk, width), lambda j, s: (far(fall(j)), 0)),
            pl.BlockSpec((1, chunk), lambda j, s: (0, rise(j))),
            fixed(gains),
            fixed(shifts),
        ],
        [
            slotted((rows, 2 * hidden), LOW),
            slotted((rows, 2 * hidden), LOW),
            slotted((rows, width), LOW),
            slotted((rows, width), LOW),
            slotted((rows, width), LOW),
            jax.ShapeDtypeStruct((rows, width), LOW),
        ],
        [moving, moving, kept, kept, kept, pl.BlockSpec((rows, width), lambda j, s: (0, 0))],
        keep,
        (steps,),
        [
            pltpu.VMEM((rows, width), F32),
            pltpu.VMEM((rows, width), F32),
            pltpu.VMEM((2, rows, chunk), LOW),
        ],
        "feed",
        29,
    )


def layer_norm_back(before, grad, gain_row):
    center = before - mean_of(before)
    scale = lax.rsqrt(mean_of(center * center) + 1e-05)
    unit = center * scale
    inner = grad * gain_row
    back = scale * (inner - mean_of(inner) - unit * mean_of(inner * unit))
    return back, sum_rows(grad * unit)


def rms_norm_back(before, grad, gain_row):
    scale = rms_scale(before)
    unit = before * scale
    inner = grad * gain_row
    back = scale * (inner - unit * mean_of(inner * unit))
    return back, sum_rows(grad * unit)


def feed_back_kernel(
    info, got_ref, mine_ref, other_ref, one_ref, two_ref, slope_ref, wo_own, wo_oth, up_own, up_oth, down_own, down_oth,
    gain_ref, dy_ref, du_ref, db_ref, stat_ref, bias_ref, dz_ref, dc_ref, acc_ref, carry_ref
):
    j = pl.program_id(0)
    steps = pl.num_programs(0)
    half = wo_own.shape[0]
    rows = got_ref.shape[0]

    @pl.when(j == 0)
    def _():
        stat_ref[...] = jnp.zeros_like(stat_ref)
        acc_ref[...] = jnp.zeros_like(acc_ref)

        @pl.when(info[0] == 1)
        def _():
            grad = got_ref[...].astype(F32)
            back, gain = layer_norm_back(two_ref[0].astype(F32), grad, gain_ref[1:2, :])
            stat_ref[0, 1:2, :] = gain
            stat_ref[0, 5:6, :] = sum_rows(grad)
            stat_ref[0, 3:4, :] = sum_rows(back)
            carry_ref[...] = back
            dy_ref[0] = back.astype(LOW)

        @pl.when(info[0] == 0)
        def _():
            grad = mine_ref[...].astype(F32) + other_ref[...].astype(F32)
            carry_ref[...] = grad
            dy_ref[0] = grad.astype(LOW)

    def part(up, down):
        grad = dot_nt(dy_ref[0], down[...])
        du_ref[0] = (grad * slope_ref[0].astype(F32)).astype(LOW)
        acc_ref[...] += dot_nt(du_ref[0], up[...])
        bias_ref[0] = sum_rows(du_ref[0].astype(F32))

    @pl.when(j < steps // 2)
    def _():
        part(up_own, down_own)

    @pl.when(j >= steps // 2)
    def _():
        part(up_oth, down_oth)

    @pl.when(j == steps - 1)
    def _():
        @pl.when(info[0] == 1)
        def _():
            grad = acc_ref[...] + carry_ref[...]
            back, gain = layer_norm_back(one_ref[0].astype(F32), grad, gain_ref[0:1, :])
            stat_ref[0, 0:1, :] = gain
            stat_ref[0, 4:5, :] = sum_rows(grad)
            stat_ref[0, 2:3, :] = sum_rows(back)
            dz_ref[...] = back

        @pl.when(info[0] == 0)
        def _():
            back, gain = rms_norm_back(one_ref[0].astype(F32), acc_ref[...], gain_ref[1:2, :])
            stat_ref[0, 1:2, :] = gain
            dz_ref[...] = carry_ref[...] + back

        low = dz_ref[...].astype(LOW)
        db_ref[0] = low
        dc_ref[:, :half] = dot_nt(low, wo_own[...]).astype(LOW)
        dc_ref[:, half:] = dot_nt(low, wo_oth[...]).astype(LOW)


def feed_back(info, got, mine, other, one, two, slope, wo, up, down, gains, previous):
    _, rows, width = one.shape
    hidden = up[0].shape[1]
    chunk = min(FEED_CHUNK, hidden)
    steps, near, far = split_steps(hidden, chunk)
    kept = pl.BlockSpec((1, rows, width), lambda j, s: (s[1], 0, 0))
    fixed = lambda a: pl.BlockSpec(a.shape, lambda j, s: (0, 0))
    plain = pl.BlockSpec((rows, width), lambda j, s: (0, 0))
    moving = pl.BlockSpec((1, rows, chunk), lambda j, s: (s[1], 0, j))
    keep = None if previous is None else list(previous) + [None, None]
    return call_with_slots(
        feed_back_kernel,
        [info],
        [got, mine, other, one, two, slope, wo[0], wo[1], up[0], up[1], down[0], down[1], gains],
        [
            plain,
            plain,
            plain,
            kept,
            kept,
            moving,
            fixed(wo[0]),
            fixed(wo[1]),
            pl.BlockSpec((width, chunk), lambda j, s: (0, near(j))),
            pl.BlockSpec((width, chunk), lambda j, s: (0, far(j))),
            pl.BlockSpec((chunk, width), lambda j, s: (near(j), 0)),
            pl.BlockSpec((chunk, width), lambda j, s: (far(j), 0)),
            fixed(gains),
        ],
        [
            slotted((rows, width), LOW),
            slotted((rows, 2 * hidden), LOW),
            slotted((rows, width), LOW),
            slotted((8, width), F32),
            slotted((1, 2 * hidden), F32),
            jax.ShapeDtypeStruct((rows, width), F32),
            jax.ShapeDtypeStruct((rows, width), LOW),
        ],
        [
            kept,
            moving,
            kept,
            pl.BlockSpec((1, 8, width), lambda j, s: (s[1], 0, 0)),
            pl.BlockSpec((1, 1, chunk), lambda j, s: (s[1], 0, j)),
            plain,
            plain,
        ],
        keep,
        (steps,),
        [pltpu.VMEM((rows, width), F32), pltpu.VMEM((rows, width), F32)],
        "feed_back",
        27,
    )


def enter_back_kernel(
    info, dq_ref, dk_ref, dv_ref, far_ref, x_ref, dz_ref, own_ref, oth_ref, gain_ref,
    d_ref, stat_ref, low_ref, lower_ref, acc_ref
):
    m = pl.program_id(0)
    half = own_ref.shape[1]
    start = pl.ds(pl.multiple_of(info[4], QB), far_ref.shape[1])

    @pl.when(m == 0)
    def _():
        stat_ref[...] = jnp.zeros_like(stat_ref)
        acc_ref[...] = jnp.zeros_like(acc_ref)
        d_ref[0] = dq_ref[...]
        stat_ref[0, 0:1, :] = sum_rows(dq_ref[...].astype(F32))

    def with_far(block_ref, part):
        d_ref[0] = block_ref[...]
        d_ref[0, start, :] = (block_ref[start, :].astype(F32) + far_ref[part].astype(F32)).astype(LOW)

    @pl.when(m == 1)
    def _():
        with_far(dk_ref, 0)

    @pl.when(m == 2)
    def _():
        with_far(dv_ref, 1)
        stat_ref[0, 1:2, :] = sum_rows(d_ref[0].astype(F32))

    acc_ref[...] += dot_nt(d_ref[0, :, :half], own_ref[...]) + dot_nt(d_ref[0, :, half:], oth_ref[...])

    @pl.when(m == 2)
    def _():
        split = lower_ref.shape[1]

        @pl.when(info[0] == 1)
        def _():
            total = dz_ref[...] + acc_ref[...]
            low_ref[...] = total.astype(LOW)
            lower_ref[...] = total[:, :split]

        @pl.when(info[0] == 0)
        def _():
            back, gain = rms_norm_back(x_ref[0].astype(F32), acc_ref[...], gain_ref[...])
            stat_ref[0, 2:3, :] = gain
            total = dz_ref[...] + back
            low_ref[...] = total.astype(LOW)
            lower_ref[...] = total[:, :split]


def enter_back(info, dq, dk, dv, far, x, dz, own, oth, gain, previous):
    _, rows, width = x.shape
    half = own.shape[1] // 3
    plain = pl.BlockSpec((rows, width), lambda m, s: (0, 0))
    kept = pl.BlockSpec((1, rows, width), lambda m, s: (s[1], 0, 0))
    weight = pl.BlockSpec((width, half), lambda m, s: (0, m))
    keep = None if previous is None else list(previous) + [None, None]
    return call_with_slots(
        enter_back_kernel,
        [info],
        [dq, dk, dv, far, x, dz, own, oth, gain],
        [
            plain,
            plain,
            plain,
            pl.BlockSpec(far.shape, lambda m, s: (0, 0, 0)),
            kept,
            plain,
            weight,
            weight,
            pl.BlockSpec((1, width), lambda m, s: (0, 0)),
        ],
        [
            slotted((rows, 6 * half), LOW),
            slotted((8, width), F32),
            jax.ShapeDtypeStruct((rows, width), LOW),
            jax.ShapeDtypeStruct((rows, width // 2), F32),
        ],
        [
            pl.BlockSpec((1, rows, 2 * half), lambda m, s: (s[1], 0, m)),
            pl.BlockSpec((1, 8, width), lambda m, s: (s[1], 0, 0)),
            plain,
            pl.BlockSpec((rows, width // 2), lambda m, s: (0, 0)),
        ],
        keep,
        (3,),
        [pltpu.VMEM((rows, width), F32)],
        "enter_back",
        12,
    )


def passed_along(value, axis, steps):
    count = lax.axis_size(axis)
    initial, last = (max(0, -steps), min(count, count - steps))
    return lax.ppermute(value, axis, [(source, source + steps) for source in range(initial, last)])


def spread(block, axis, source):
    block = jnp.where(lax.axis_index(axis) == source, block, jnp.zeros_like(block))
    return lax.psum(block, axis)


def layer_norm(operand, gain_row, shift_row):
    center = operand - jnp.mean(operand, axis=-1, keepdims=True)
    variance = jnp.mean(center * center, axis=-1, keepdims=True)
    return center * lax.rsqrt(variance + 1e-05) * gain_row + shift_row


def rms_norm(operand, gain_row):
    return (
        operand * lax.rsqrt(jnp.mean(operand * operand, axis=-1, keepdims=True) + 1e-06) * gain_row
    )


def gelu_act(operand):
    return jax.nn.gelu(operand, approximate=False)


def gelu_slope(operand):
    return (
        0.5 * (1.0 + jax.scipy.special.erf(operand * 0.7071067811865476))
        + operand * jnp.exp(-0.5 * operand * operand) * 0.3989422804014327
    )


def entry_norm(residual, gain_rows, leading):
    return jnp.where(leading, residual, rms_norm(residual, gain_rows[0]))


def middle(residual, branch, gain_rows, shift_rows, leading):
    joined = residual + branch
    bert_rows = layer_norm(joined + shift_rows[0], gain_rows[0], shift_rows[2])
    carried = jnp.where(leading, bert_rows, joined)
    normed = jnp.where(leading, bert_rows, rms_norm(joined, gain_rows[1]))
    return (carried, normed)


def final(carried, second, gain_rows, shift_rows, leading):
    joined = carried + second
    return jnp.where(
        leading, layer_norm(joined + shift_rows[1], gain_rows[1], shift_rows[3]), joined
    )


def contract_rows(left, right):
    return lax.dot_general(
        left, right, (((0,), (0,)), ((), ())), preferred_element_type=jnp.float32
    )


def contract_cols(left, right):
    return lax.dot_general(
        left, right, (((1,), (1,)), ((), ())), preferred_element_type=jnp.float32
    )


def gather_rows(operand, weight):
    return (
        jnp.dot(
            lax.all_gather(operand, "tensor", axis=0, tiled=True),
            weight,
            preferred_element_type=jnp.float32,
        ),
        None,
    )


def collect(full_rows, weight):
    return lax.psum_scatter(
        jnp.dot(full_rows, weight, preferred_element_type=jnp.float32),
        "tensor",
        scatter_dimension=0,
        tiled=True,
    )


def scatter_back(grad_rows, weight):
    return lax.psum_scatter(
        contract_cols(grad_rows, weight).astype(jnp.bfloat16),
        "tensor",
        scatter_dimension=0,
        tiled=True,
    ).astype(jnp.float32)


def fold_back(grad_share, weight, activations):
    fragment = lax.all_gather(grad_share, "tensor", axis=0, tiled=True)
    product_rows = contract_cols(fragment, weight)
    return (product_rows, contract_rows(activations, fragment))


def weight_grad(operand, grad_rows):
    return contract_rows(lax.all_gather(operand, "tensor", axis=0, tiled=True), grad_rows)


DH = 64
QB = 128
NARROW = 3
WIDE = 5
VMEM = 56 * 1024 * 1024


def padded(segments):
    return jnp.pad(segments, (PAD * QB, PAD * QB), constant_values=-1)


def general_body(
    layer_input,
    segment_ids,
    buckets,
    attn_in,
    attn_out,
    ffn_in,
    ffn_out,
    norm_gain,
    bert_shift,
    head_bias,
    ffn_bias,
    position_bias,
    decoder_grads,
):
    micro_count = layer_input.shape[0]
    shard_rows = layer_input.shape[2]
    model_width = layer_input.shape[3]
    length = segment_ids.shape[2]
    leading = lax.axis_index("section") == 0
    weighting = jnp.where(leading, 1.0, 0.0)
    qkv_weight = attn_in[0].reshape(model_width, -1)
    out_weight = attn_out[0]
    ffn_up = ffn_in[0]
    ffn_down = ffn_out[0]
    gain_rows = jnp.where(leading, norm_gain[0], norm_gain[1])
    head_shift = head_bias * weighting
    qkv_shift = jnp.concatenate([head_shift[0], jnp.zeros_like(head_shift[0]), head_shift[1]])
    ffn_shift = ffn_bias * weighting
    bias_table = position_bias * (1.0 - weighting)
    bucket_hits = (buckets[None, :] == jnp.arange(bias_table.shape[1])[:, None]).astype(jnp.float32)
    offset_bias = jnp.dot(bias_table, bucket_hits, precision=lax.Precision.HIGHEST)
    near = length - 1 - 3 * QB
    bias = toeplitz(jnp.ones((1,), jnp.int32), offset_bias[:, near : near + 6 * QB])
    info = jnp.array([0, 0, PAD, 0, 0, 1], jnp.int32)
    segment_rows = segment_ids[:, 0]

    def middle_part(residual_in, branch_in, gain_in, shift_in):
        return middle(residual_in, branch_in, gain_in, shift_in, leading)

    def final_part(carried_in, second_in, gain_in, shift_in):
        return final(carried_in, second_in, gain_in, shift_in, leading)

    def entry_part(residual_in, gain_in):
        return entry_norm(residual_in, gain_in, leading)

    received = jnp.zeros((shard_rows, model_width), jnp.bfloat16)
    saved_steps = []
    encoded = []
    for moment in range(micro_count + 1):
        own_rows = layer_input[min(moment, micro_count - 1), 0]
        if moment >= micro_count:
            own_rows = jnp.zeros_like(own_rows)
        segment_row = jnp.where(
            leading, segment_rows[min(moment, micro_count - 1)], segment_rows[max(moment - 1, 0)]
        )
        forward_incoming = jnp.where(leading, own_rows, received)
        forward_residual = forward_incoming.astype(jnp.float32)
        forward_entered = entry_norm(forward_residual, gain_rows, leading).astype(jnp.bfloat16)
        projected, forward_gathered_in = gather_rows(forward_entered, qkv_weight)
        forward_qkv = (projected + qkv_shift).astype(jnp.bfloat16)
        forward_context, forward_log_totals = attend(
            info, padded(segment_row), forward_qkv[None], None, bias, None
        )
        forward_context = forward_context[0]
        forward_branch = collect(forward_context, out_weight)
        forward_carried, forward_normed = middle(
            forward_residual, forward_branch, gain_rows, bert_shift, leading
        )
        pre_full, forward_gathered_mid = gather_rows(forward_normed.astype(jnp.bfloat16), ffn_up)
        forward_pre_act = pre_full + ffn_shift
        forward_second = collect(gelu_act(forward_pre_act).astype(jnp.bfloat16), ffn_down)
        result = final(forward_carried, forward_second, gain_rows, bert_shift, leading).astype(
            jnp.bfloat16
        )
        result, saved = (
            result,
            (
                forward_incoming,
                segment_row,
                forward_branch,
                forward_second,
                forward_qkv,
                forward_context,
                forward_log_totals,
                forward_pre_act,
                forward_gathered_in,
                forward_gathered_mid,
            ),
        )
        saved_steps.append(saved)
        if moment >= 1:
            encoded.append(result)
        if moment < micro_count:
            received = passed_along(result, "section", 1)
    delivered = spread(jnp.stack(encoded), "section", 1)
    section_grads = lax.psum(
        decoder_grads[0, :, 0].astype(jnp.float32).astype(jnp.bfloat16), "section"
    ).astype(jnp.float32)
    grad_received = jnp.zeros((shard_rows, model_width), jnp.float32)
    running_terms = None
    input_rows = []
    for moment in range(micro_count + 1):
        own_grad = section_grads[min(moment, micro_count - 1)]
        if moment >= micro_count:
            own_grad = jnp.zeros_like(own_grad)
        earlier = saved_steps[max(moment - 1, 0)]
        later = saved_steps[min(moment + 1, micro_count)]
        chosen = jax.tree.map(
            lambda from_first, from_second: jnp.where(leading, from_first, from_second),
            earlier,
            later,
        )
        (
            incoming,
            backward_segment_row,
            branch,
            second,
            qkv,
            context,
            log_totals,
            pre_act,
            gathered_in,
            gathered_mid,
        ) = chosen
        residual = incoming.astype(jnp.float32)
        (carried, normed), pull_middle = jax.vjp(
            middle_part, residual, branch, gain_rows, bert_shift
        )
        finished, pull_final = jax.vjp(final_part, carried, second, gain_rows, bert_shift)
        grad_carried, grad_second, gain_end, shift_end = pull_final(
            jnp.where(leading, grad_received, own_grad)
        )
        hidden = gelu_act(pre_act).astype(jnp.bfloat16)
        grad_hidden, backward_grad_down = fold_back(
            grad_second.astype(jnp.bfloat16), ffn_down, hidden
        )
        grad_pre = (grad_hidden * gelu_slope(pre_act)).astype(jnp.bfloat16)
        grad_shift = jnp.sum(grad_pre.astype(jnp.float32), axis=0) * weighting
        backward_grad_up = weight_grad(normed.astype(jnp.bfloat16), grad_pre)
        grad_normed = scatter_back(grad_pre, ffn_up)
        grad_residual, grad_branch, gain_mid, shift_mid = pull_middle((grad_carried, grad_normed))
        grad_context, backward_grad_out_weight = fold_back(
            grad_branch.astype(jnp.bfloat16), out_weight, context
        )
        low_q, low_k, low_v, grad_table = attend_back(
            info, padded(backward_segment_row), qkv[None], None, grad_context.astype(jnp.bfloat16), bias, log_totals, None
        )
        grad_table = grad_table[0]
        grad_head = (
            jnp.stack([jnp.sum(low.astype(jnp.float32), axis=0) for low in (low_q, low_v)]) * weighting
        )
        grad_rows = jnp.concatenate([low_q, low_k, low_v], axis=1)
        entered, pull_entry = jax.vjp(entry_part, residual, gain_rows)
        backward_grad_qkv = weight_grad(entered.astype(jnp.bfloat16), grad_rows)
        grad_entered = scatter_back(grad_rows, qkv_weight)
        grad_from_entry, gain_entry = pull_entry(grad_entered)
        grad_terms = (
            backward_grad_qkv,
            backward_grad_out_weight,
            backward_grad_up,
            backward_grad_down,
            gain_end + gain_mid + gain_entry,
            shift_end + shift_mid,
            grad_head,
            grad_shift,
            grad_table,
        )
        grad_input, grad_terms = (grad_residual + grad_from_entry, grad_terms)
        if running_terms is None:
            running_terms = grad_terms
        else:
            running_terms = jax.tree.map(jnp.add, running_terms, grad_terms)
        if moment >= 1:
            input_rows.append(grad_input)
        if moment < micro_count:
            grad_received = passed_along(grad_input.astype(jnp.bfloat16), "section", -1).astype(
                grad_input.dtype
            )
    input_all = jnp.stack(input_rows)
    half_width = model_width // 2
    upper_half = passed_along(
        input_all[:, :, half_width:].astype(jnp.bfloat16), "section", 1
    ).astype(jnp.float32)
    input_grad = jnp.where(leading, input_all[:, :, :half_width], upper_half)[:, None]
    (
        grad_qkv,
        grad_out_weight,
        grad_up,
        grad_down,
        gain_sum,
        shift_sum,
        head_sum,
        shift_ffn_sum,
        table_sum,
    ) = running_terms
    near_hits = bucket_hits[:, near : near + 6 * QB]
    table_sum = jnp.dot(diagonals(jnp.ones((1,), jnp.int32), table_sum[None], 1), near_hits.T, precision=lax.Precision.HIGHEST) * (
        1.0 - weighting
    )
    weights_out = (
        lax.psum_scatter(
            grad_qkv.reshape(1, model_width, 3, -1).astype(jnp.bfloat16),
            "dp",
            scatter_dimension=1,
            tiled=True,
        ).astype(jnp.float32),
        lax.psum_scatter(
            grad_out_weight[None].astype(jnp.bfloat16), "dp", scatter_dimension=2, tiled=True
        ).astype(jnp.float32),
        lax.psum_scatter(
            grad_up[None].astype(jnp.bfloat16), "dp", scatter_dimension=1, tiled=True
        ).astype(jnp.float32),
        lax.psum_scatter(
            grad_down[None].astype(jnp.bfloat16), "dp", scatter_dimension=2, tiled=True
        ).astype(jnp.float32),
    )
    gain_both = jnp.stack([gain_sum * weighting, gain_sum * (1.0 - weighting)])
    shared_out = lax.psum((gain_both, shift_sum), ("dp", "section", "tensor"))
    split_out = lax.psum((head_sum, shift_ffn_sum, table_sum), ("dp", "section"))
    return (
        delivered[None, :, None],
        input_grad,
        weights_out[0],
        weights_out[1],
        weights_out[2],
        weights_out[3],
        shared_out[0],
        shared_out[1],
        split_out[0],
        split_out[1],
        split_out[2],
    )


def grads_kernel(
    f_hbm, dy_hbm, c_hbm, db_hbm, n_hbm, du_hbm, e_hbm, dqkv_hbm, packed_ref,
    out_ref, summed_ref,
    still, moving, turned, given, held, near_ref, y_ref, low_ref, high_ref, small_ref, small_got,
    still_sem, moving_sem, near_send, near_recv, y_send, y_recv, low_send, low_recv, high_send, high_recv,
    small_send, small_recv
):
    dp = lax.axis_index("dp")
    core = lax.axis_index("tensor")
    section = lax.axis_index("section")
    y_side = lax.rem(dp, 2)
    low_side = lax.rem(dp // 2, 2)
    high_side = dp // 4

    def across(bit, side):
        return {"dp": dp + bit * (1 - 2 * side)}

    core_peer = {"tensor": 1 - core}
    y_peer = across(1, y_side)
    low_peer = across(2, low_side)
    high_peer = across(4, high_side)
    peers = [core_peer, y_peer, low_peer, high_peer, {"section": 1 - section}]
    mesh_id = pl.DeviceIdType.MESH
    total = out_ref.shape[0]

    barrier = pltpu.get_barrier_semaphore()
    for peer in peers:
        pl.semaphore_signal(barrier, inc=1, device_id=peer, device_id_type=mesh_id)
    pl.semaphore_wait(barrier, len(peers))

    def send(source, target, out_sem, in_sem, peer):
        return pltpu.make_async_remote_copy(
            src_ref=source, dst_ref=target, send_sem=out_sem, recv_sem=in_sem,
            device_id=peer, device_id_type=mesh_id,
        )

    def near_copy(k, slot):
        return send(given.at[slot], near_ref.at[k], near_send.at[slot], near_recv.at[k], core_peer)

    def y_copy(k):
        return send(held.at[k, :, :, 1 - y_side], y_ref.at[k], y_send.at[k], y_recv.at[k], y_peer)

    def low_copy(k):
        return send(y_ref.at[k, :, 1 - low_side], low_ref.at[k], low_send.at[k], low_recv.at[k], low_peer)

    def high_copy(k):
        return send(low_ref.at[k, 1 - high_side], high_ref.at[k], high_send.at[k], high_recv.at[k], high_peer)

    def small_copy(s):
        return send(small_ref.at[s], small_got.at[s], small_send.at[s], small_recv.at[s], peers[s])

    def added(a, b):
        return (a.astype(F32) + b.astype(F32)).astype(LOW)

    def near_stage(k):
        near_copy(k, 0).wait_recv()
        for hi in range(2):
            for lo in range(2):
                for side in range(2):
                    held[k, hi, lo, side] = added(held[k, hi, lo, side], near_ref[k, hi, lo, side])
        y_copy(k).start()

    def y_stage(k):
        y_copy(k).wait_recv()
        for hi in range(2):
            for lo in range(2):
                y_ref[k, hi, lo] = added(y_ref[k, hi, lo], held[k, hi, lo, y_side])
        low_copy(k).start()

    def low_stage(k):
        low_copy(k).wait_recv()
        for hi in range(2):
            low_ref[k, hi] = added(low_ref[k, hi], y_ref[k, hi, low_side])
        high_copy(k).start()

    def high_stage(k):
        high_copy(k).wait_recv()
        out_ref[k] = high_ref[k].astype(F32) + low_ref[k, high_side].astype(F32)

    def small_stage(s):
        small_copy(s).wait_recv()
        small_ref[s + 1] = small_ref[s] + small_got[s]
        if s + 1 < len(peers):
            small_copy(s + 1).start()

    chunk = moving.shape[4]
    each = du_hbm.shape[2] // 2 // chunk
    phases = [
        (False, dy_hbm, f_hbm, each, lambda c: c * chunk, lambda c: (each + c) * chunk),
        (True, n_hbm, du_hbm, each, lambda c: c * chunk, lambda c: (each + c) * chunk),
        (False, db_hbm, c_hbm, 1, lambda c: 0 * c, lambda c: 0 * c + chunk),
        (True, e_hbm, dqkv_hbm, 3, lambda c: 2 * c * chunk, lambda c: (2 * c + 1) * chunk),
    ]

    def still_copy(p):
        return pltpu.make_async_copy(phases[p][1].at[0:2], still.at[p % 2], still_sem.at[p % 2])

    def moving_copies(p, c, slot):
        _, _, source, _, own_at, oth_at = phases[p]
        return [
            pltpu.make_async_copy(
                source.at[0:2, :, pl.ds(pl.multiple_of(at(c), chunk), chunk)],
                moving.at[slot, part],
                moving_sem.at[slot, part],
            )
            for part, at in enumerate((own_at, oth_at))
        ]

    still_copy(0).start()
    for copy in moving_copies(0, 0, 0):
        copy.start()
    still_copy(1).start()
    small_ref[0] = packed_ref[...]
    small_copy(0).start()

    tokens = 2 * still.shape[2]
    base = 0
    for p, (wide, _, _, count, _, _) in enumerate(phases):
        still_copy(p).wait()
        stay = still.at[p % 2]
        if wide:
            for micro in range(2):
                turned[:, micro * tokens // 2 : (micro + 1) * tokens // 2] = stay[micro].T

        @pl.loop(0, count)
        def _(c, p=p, wide=wide, count=count, base=base, stay=stay):
            k = base + c
            slot = lax.rem(k, 2)
            for copy in moving_copies(p, c, slot):
                copy.wait()

            @pl.when(c + 1 < count)
            def _():
                for copy in moving_copies(p, c + 1, 1 - slot):
                    copy.start()

            if p + 1 < len(phases):

                @pl.when(c + 1 == count)
                def _():
                    for copy in moving_copies(p + 1, 0, 1 - slot):
                        copy.start()

            @pl.when(k >= 2)
            def _():
                near_copy(k, slot).wait_send()

            def product(part, store):
                block = moving[slot, part].reshape(tokens, chunk)
                if wide:
                    result = dot_nn(turned[...], block).astype(LOW)
                    for z in range(4):
                        for side in range(2):
                            at = (2 * z + side) * QB
                            store(z, side, slice(None), result[at : at + QB, :])
                else:
                    result = dot_nn(block.T, stay[...].reshape(tokens, -1)).astype(LOW)
                    for z in range(4):
                        for side in range(2):
                            at = (2 * z + side) * QB
                            for q in range(chunk // QB):
                                lanes = slice(q * QB, (q + 1) * QB)
                                store(z, side, lanes, result[lanes, at : at + QB])

            def to_given(z, side, lanes, value):
                given[slot, z // 2, z % 2, side, :, lanes] = value

            def to_held(z, side, lanes, value):
                held[k, z // 2, z % 2, side, :, lanes] = value

            product(1, to_given)
            near_copy(k, slot).start()
            product(0, to_held)

            @pl.when(k >= 1)
            def _():
                near_stage(k - 1)

            for s in range(len(peers)):

                @pl.when(k == 2 * s + 1)
                def _(s=s):
                    small_stage(s)

            @pl.when((k >= 5) & (lax.rem(k, 3) == 2))
            def _():
                y_stage((k - 5) // 3)

        if p + 2 < len(phases):
            still_copy(p + 2).start()
        base += count

    near_stage(total - 1)
    early = (total - 1 - 5) // 3 + 1
    for k in range(early):
        low_stage(k)
    for k in range(early - 1):
        high_stage(k)

    @pl.loop(early, total)
    def _(k):
        y_stage(k)
        high_stage(k - 1)
        low_stage(k)

    high_stage(total - 1)
    summed_ref[...] = small_ref[len(peers)]
    near_copy(total - 2, (total - 2) % 2).wait_send()
    near_copy(total - 1, (total - 1) % 2).wait_send()

    @pl.loop(0, total)
    def _(k):
        y_copy(k).wait_send()
        low_copy(k).wait_send()
        high_copy(k).wait_send()

    for s in range(len(peers)):
        small_copy(s).wait_send()


def summed_grads(f, dy, context, db, n, du, e, dqkv, packed):
    rows, width = dy.shape[1:]
    chunk = 512
    total = du.shape[2] // chunk + 4
    dma = pltpu.SemaphoreType.DMA
    anywhere = pl.BlockSpec(memory_space=pl.ANY)
    local = pl.BlockSpec(memory_space=pltpu.VMEM)
    return pl.pallas_call(
        grads_kernel,
        in_specs=[anywhere] * 8 + [local],
        out_specs=[local, local],
        out_shape=[
            jax.ShapeDtypeStruct((total, QB, chunk), F32),
            jax.ShapeDtypeStruct(packed.shape, F32),
        ],
        scratch_shapes=[
            pltpu.VMEM((2, 2, rows, width), LOW),
            pltpu.VMEM((2, 2, 2, rows, chunk), LOW),
            pltpu.VMEM((width, 2 * rows), LOW),
            pltpu.VMEM((2, 2, 2, 2, QB, chunk), LOW),
            pltpu.VMEM((total, 2, 2, 2, QB, chunk), LOW),
            pltpu.VMEM((total, 2, 2, 2, QB, chunk), LOW),
            pltpu.VMEM((total, 2, 2, QB, chunk), LOW),
            pltpu.VMEM((total, 2, QB, chunk), LOW),
            pltpu.VMEM((total, QB, chunk), LOW),
            pltpu.VMEM((6,) + packed.shape, F32),
            pltpu.VMEM((5,) + packed.shape, F32),
            dma((2,)),
            dma((2, 2)),
            dma((2,)),
            dma((total,)),
            dma((total,)),
            dma((total,)),
            dma((total,)),
            dma((total,)),
            dma((total,)),
            dma((total,)),
            dma((5,)),
            dma((5,)),
        ],
        compiler_params=pltpu.CompilerParams(
            collective_id=0, has_side_effects=True, vmem_limit_bytes=TAIL_VMEM
        ),
        cost_estimate=cost_of(150),
        name="summed_grads",
    )(f, dy, context, db, n, du, e, dqkv, packed)


def swapped(value, axis, bit):
    pairs = [(at, at ^ bit) for at in range(lax.axis_size(axis))]
    return lax.ppermute(value, axis, pairs)


def paired_body(
    layer_input,
    segment_ids,
    buckets,
    attn_in,
    attn_out,
    ffn_in,
    ffn_out,
    norm_gain,
    bert_shift,
    head_bias,
    ffn_bias,
    position_bias,
    decoder_grads,
):
    micro_count, _, rows, width = layer_input.shape
    length = segment_ids.shape[2]
    heads, bucket_count = position_bias.shape
    section = lax.axis_index("section")
    core = lax.axis_index("tensor")
    leading = section == 0
    lead = jnp.where(leading, 1, 0).astype(jnp.int32)
    pieces = lax.axis_size("dp")

    remote_grads = [lax.ppermute(decoder_grads[0, 0, 0], "section", [(0, 1)])]
    qkv_own = attn_in[0].reshape(width, -1)
    qkv_oth = swapped(qkv_own, "tensor", 1)
    wo = (attn_out[0], swapped(attn_out[0], "tensor", 1))
    up = (ffn_in[0], swapped(ffn_in[0], "tensor", 1))
    down = (ffn_out[0], swapped(ffn_out[0], "tensor", 1))
    small = jnp.concatenate([head_bias.reshape(-1), ffn_bias, position_bias.reshape(-1)])
    small_oth = swapped(small, "tensor", 1)
    near_heads = head_bias.size
    near_ffn = near_heads + ffn_bias.size
    both_small = jnp.stack([small, small_oth])
    head_both = both_small[:, :near_heads].reshape(2, 2, -1)
    ffn_both = jnp.where(leading, both_small[:, near_heads:near_ffn], 0.0).reshape(1, -1)
    table_both = jnp.where(leading, 0.0, both_small[:, near_ffn:]).reshape(2 * heads, bucket_count)
    q_shift = head_both[:, 0].reshape(1, -1)
    v_shift = head_both[:, 1].reshape(1, -1)
    qkv_shift = jnp.where(
        leading, jnp.concatenate([q_shift, jnp.zeros_like(q_shift), v_shift], axis=1), 0.0
    )
    gains = jnp.where(leading, norm_gain[0], norm_gain[1])
    entry_gain = gains[0:1]

    near = length - 1 - 3 * QB
    near_hits = (buckets[None, near : near + 6 * QB] == jnp.arange(bucket_count)[:, None]).astype(F32)
    trailing = jnp.reshape(1 - lead, (1,))
    bias = toeplitz(trailing, jnp.dot(table_both, near_hits, precision=lax.Precision.HIGHEST))

    window = rows + REACH
    base = core * (length - window)
    segments = jnp.pad(
        lax.dynamic_slice_in_dim(segment_ids[:, 0], base, window, axis=1),
        ((0, 0), (PAD * QB, PAD * QB)),
        constant_values=-1,
    )
    reach_blocks = REACH // QB
    own_block = PAD + core * reach_blocks
    halo_block = jnp.where(core == 0, PAD + rows // QB, PAD)
    edge = jnp.where(core == 0, rows - REACH, 0)

    def info_of(turn, micro):
        active = jnp.where(section == turn, 1, 0)
        slot = jnp.where(active == 1, micro, micro_count)
        return jnp.stack([lead, slot, own_block, halo_block, edge, active]).astype(jnp.int32)

    turns = [(turn, micro) for turn in range(2) for micro in range(micro_count)]
    received = [jnp.zeros((rows, width), LOW)] * micro_count
    entered = attended = fed = None
    results = []
    finished = []
    for turn, micro in turns:
        info = info_of(turn, micro)
        if turn + micro > 0:
            info, _ = lax.optimization_barrier((info, result))
        *entered, halo = enter(
            info, layer_input[micro, 0], received[micro], entry_gain, qkv_shift, qkv_own, qkv_oth, entered
        )
        halo = exchanged(halo)
        if turn == 0 and micro == 0:
            later, _ = lax.optimization_barrier((decoder_grads[0, 1, 0], (remote_grads[0], halo)))
            remote_grads.append(lax.ppermute(later, "section", [(0, 1)]))
        attended = attend(info, segments[micro], entered[2], halo, bias, attended)
        if turn == 0 and micro == 0:
            info, remote_grads[1] = lax.optimization_barrier((info, remote_grads[1]))
        *fed, result = feed(
            info, entered[0], attended[0], wo, up, down, ffn_both, gains, bert_shift, fed
        )
        if turn == 0:
            received = list(received)
            received[micro] = lax.ppermute(result, "section", [(0, 1)])
        else:
            results.append(result)
            finished.append(lax.ppermute(result, "section", [(1, 0)]))
    x_saved, e_saved, qkv_saved = entered
    context, lse, *halo_saved = attended
    f_saved, slope_saved, n_saved, one_saved, two_saved = fed

    received = [jnp.zeros((rows, width), LOW)] * micro_count
    feed_kept = table_kept = entry_kept = None
    input_low = []
    input_lower = []
    for step, (turn, micro) in enumerate([(1 - turn, micro) for turn, micro in turns]):
        info = info_of(turn, micro)
        if step > 0:
            info, _ = lax.optimization_barrier((info, low))
        *feed_kept, dz, grad_context = feed_back(
            info, received[micro], decoder_grads[0, micro, 0], remote_grads[micro], one_saved, two_saved,
            slope_saved, wo, up, down, gains, feed_kept,
        )
        dq, dk, dv, table_kept, far = attend_back(
            info, segments[micro], qkv_saved, halo_saved, grad_context, bias, lse, table_kept
        )
        far = exchanged(far)
        if turn == 1 and micro == 0:
            info, *finished = lax.optimization_barrier((info, *finished))
        *entry_kept, low, lower = enter_back(
            info, dq, dk, dv, far, x_saved, dz, qkv_own, qkv_oth, entry_gain, entry_kept
        )
        if turn == 1:
            received = list(received)
            received[micro] = lax.ppermute(low, "section", [(1, 0)])
        else:
            input_low.append(low)
            input_lower.append(lower)
    dy_saved, du_saved, db_saved, stat_feed, stat_bias = feed_kept
    dqkv_saved, stat_entry = entry_kept

    half = width // 2
    upper = lax.ppermute(jnp.stack(input_low)[:, :, half:], "section", [(0, 1)]).astype(F32)
    input_grad = jnp.where(leading, jnp.stack(input_lower), upper)[:, None]

    near_table = jnp.dot(diagonals(trailing, table_kept, micro_count), near_hits.T, precision=lax.Precision.HIGHEST)

    def placed(pair):
        return jnp.where(core == 0, pair, pair[::-1])

    stat_feed = stat_feed[0] + stat_feed[1]
    stat_entry = stat_entry[0] + stat_entry[1]
    gain_first = jnp.where(leading, stat_feed[0:1], stat_entry[2:3])
    gain_rows = jnp.concatenate([gain_first, stat_feed[1:2]])
    nothing = jnp.zeros_like(gain_rows)
    gain_all = jnp.where(leading, jnp.concatenate([gain_rows, nothing]), jnp.concatenate([nothing, gain_rows]))
    shift_all = jnp.where(leading, stat_feed[2:6], 0.0)
    head_all = jnp.where(leading, stat_entry[0:2], 0.0).reshape(2, 2, -1)
    head_all = placed(jnp.moveaxis(head_all, 1, 0))
    bias_all = placed(jnp.where(leading, stat_bias[0] + stat_bias[1], 0.0).reshape(2, -1))
    table_all = placed(jnp.where(leading, 0.0, near_table).reshape(2, heads, bucket_count))
    parts = [gain_all, shift_all, head_all, bias_all, table_all]
    packed = jnp.concatenate([part.reshape(-1) for part in parts])
    packed_rows = 8 * (-(-packed.size // (8 * width)))
    packed = jnp.pad(packed, (0, packed_rows * width - packed.size)).reshape(packed_rows, width)
    summed, packed = summed_grads(
        f_saved, dy_saved, context, db_saved, n_saved, du_saved, e_saved, dqkv_saved, packed
    )
    packed = packed.reshape(-1)
    quarters = ffn_in.shape[2] // summed.shape[2]
    piece = width // pieces
    down_sum = summed[:quarters].reshape(quarters, QB, -1, QB).transpose(0, 2, 1, 3).reshape(-1, piece)
    up_sum = summed[quarters : 2 * quarters].transpose(1, 0, 2).reshape(piece, -1)
    out_sum = summed[2 * quarters].reshape(QB, -1, QB).transpose(1, 0, 2).reshape(-1, piece)
    qkv_sum = summed[2 * quarters + 1 :].transpose(1, 0, 2)
    unpacked = []
    start = 0
    for part in parts:
        unpacked.append(packed[start : start + part.size].reshape(part.shape))
        start += part.size
    gain_all, shift_all, head_all, bias_all, table_all = unpacked
    mine = lambda value: lax.dynamic_index_in_dim(value, core, 0, keepdims=False)
    return (
        jnp.where(leading, jnp.stack(finished), jnp.stack(results))[None, :, None],
        input_grad,
        qkv_sum[None],
        out_sum[None],
        up_sum[None],
        down_sum[None],
        gain_all.reshape(norm_gain.shape),
        shift_all,
        mine(head_all),
        mine(bias_all),
        mine(table_all),
    )


def solution(mesh):
    placed = (
        P(None, "dp", "tensor", None),
        P(None, "dp", None),
        P(),
        P("section", None, None, "tensor"),
        P("section", "tensor", None),
        P("section", None, "tensor"),
        P("section", "tensor", None),
        P(),
        P(),
        P(None, "tensor"),
        P("tensor"),
        P("tensor", None),
        P("section", None, "dp", "tensor", None),
    )
    paired = mesh.shape["tensor"] == 2 and mesh.shape["dp"] == 8
    return jax.shard_map(
        paired_body if paired else general_body,
        mesh=mesh,
        in_specs=placed,
        out_specs=(
            P("section", None, "dp", "tensor", None),
            P(None, "dp", "tensor", "section"),
            P("section", "dp", None, "tensor"),
            P("section", "tensor", "dp"),
            P("section", "dp", "tensor"),
            P("section", "tensor", "dp"),
            P(),
            P(),
            P(None, "tensor"),
            P("tensor"),
            P("tensor", None),
        ),
        check_vma=False,
    )
```

```python
import functools

import jax
import jax.numpy as jnp
from jax import lax
from jax.experimental import pallas as pl
from jax.experimental.pallas import tpu as pltpu
from jax.sharding import PartitionSpec as P

DH = 64
QB = 128
PAD = 2
REACH = 256
STRIP = 64
HEAD_SPAN = 512
FEED_CHUNK = 1024
VMEM = 56 * 1024 * 1024
TAIL_VMEM = 60 * 1024 * 1024
LOW = jnp.bfloat16
F32 = jnp.float32


def dot_nt(left, right):
    return lax.dot_general(left, right, (((1,), (1,)), ((), ())), preferred_element_type=F32)


def dot_nn(left, right):
    return lax.dot_general(left, right, (((1,), (0,)), ((), ())), preferred_element_type=F32)


def params():
    return pltpu.CompilerParams(vmem_limit_bytes=VMEM)


def cost_of(micros):
    return pl.CostEstimate(flops=int(micros * 5e7), bytes_accessed=0, transcendentals=0)


def when(condition):
    return (lambda body: body()) if condition else (lambda body: None)


def slotted(shape, dtype):
    return jax.ShapeDtypeStruct((3,) + shape, dtype)


def call_with_slots(
    kernel, scalars, inputs, in_specs, outputs, out_specs, previous, grid, scratch, name, micros
):
    count = len(inputs)
    kept = [] if previous is None else [item for item in previous if item is not None]
    aliases = {}
    if previous is not None:
        at = len(scalars) + count
        for index, item in enumerate(previous):
            if item is not None:
                aliases[at] = index
                at += 1

    def gated(spec):
        return pl.BlockSpec(spec.block_shape, lambda j, s, *rest: spec.index_map(j * s[5], s, *rest))

    in_specs = [gated(spec) for spec in in_specs]
    out_specs = [gated(spec) for spec in out_specs]

    def run(*refs):
        @pl.when(refs[0][5] == 1)
        def _():
            front = len(scalars) + count
            kernel(*refs[:front], *refs[front + len(kept) :])

    return pl.pallas_call(
        run,
        grid_spec=pltpu.PrefetchScalarGridSpec(
            num_scalar_prefetch=len(scalars),
            grid=grid,
            in_specs=list(in_specs) + [pl.BlockSpec(memory_space=pl.ANY)] * len(kept),
            out_specs=out_specs,
            scratch_shapes=scratch,
        ),
        out_shape=outputs,
        input_output_aliases=aliases,
        compiler_params=params(),
        cost_estimate=cost_of(micros),
        name=name,
    )(*scalars, *inputs, *kept)


def toeplitz_kernel(flag_ref, w_ref, t_ref):
    width = w_ref.shape[2]

    @pl.when(flag_ref[0] == 0)
    def _():
        t_ref[...] = jnp.zeros_like(t_ref)

    @pl.when(flag_ref[0] == 1)
    def _():
        half = []
        for head in range(2):
            rows = jnp.broadcast_to(w_ref[0, head : head + 1, :], (QB, width))
            rolled = pltpu.roll(rows, 0, 1, stride=1, stride_axis=0)
            half.append(rolled.T[QB:, :])
        t_ref[0] = jnp.concatenate(half, axis=1)


def toeplitz(flag, offset_bias):
    heads, width = offset_bias.shape
    pairs = heads // 2
    return pl.pallas_call(
        toeplitz_kernel,
        grid_spec=pltpu.PrefetchScalarGridSpec(
            num_scalar_prefetch=1,
            grid=(pairs,),
            in_specs=[pl.BlockSpec((1, 2, width), lambda p, s: (p, 0, 0))],
            out_specs=pl.BlockSpec((1, width - QB, 2 * QB), lambda p, s: (p, 0, 0)),
        ),
        out_shape=jax.ShapeDtypeStruct((pairs, width - QB, 2 * QB), F32),
        compiler_params=params(),
        cost_estimate=cost_of(6),
        name="toeplitz",
    )(flag, offset_bias.reshape(pairs, 2, width))


def diagonal_kernel(flag_ref, a_ref, s_ref):
    @pl.when(flag_ref[0] == 0)
    def _():
        s_ref[...] = jnp.zeros_like(s_ref)

    @pl.when(flag_ref[0] == 1)
    def _():
        sum_diagonals(a_ref, s_ref)


def sum_diagonals(a_ref, s_ref):
    total = a_ref[0, 0]
    for extra in range(1, a_ref.shape[0]):
        total = total + a_ref[extra, 0]
    total = jnp.concatenate([jnp.zeros((QB, 2 * QB), F32), total], axis=0)
    width = total.shape[0]
    row = lax.broadcasted_iota(jnp.int32, (QB, QB), 0)
    col = lax.broadcasted_iota(jnp.int32, (QB, QB), 1)
    mirror = jnp.where(row + col == QB - 1, 1.0, 0.0)
    for head in range(2):
        turned = lax.dot_general(
            mirror,
            total[:, head * QB : (head + 1) * QB],
            (((1,), (1,)), ((), ())),
            precision=lax.Precision.HIGHEST,
            preferred_element_type=F32,
        )
        aligned = pltpu.roll(turned, width - QB + 1, 1, stride=1, stride_axis=0)
        s_ref[0, head : head + 1, :] = jnp.sum(aligned, axis=0, keepdims=True)


def diagonals(flag, tables, steps):
    _, pairs, rows, _ = tables.shape
    width = rows + QB
    out = pl.pallas_call(
        diagonal_kernel,
        grid_spec=pltpu.PrefetchScalarGridSpec(
            num_scalar_prefetch=1,
            grid=(pairs,),
            in_specs=[pl.BlockSpec((steps, 1, rows, 2 * QB), lambda p, s: (0, p * s[0], 0, 0))],
            out_specs=pl.BlockSpec((1, 2, width), lambda p, s: (p, 0, 0)),
        ),
        out_shape=jax.ShapeDtypeStruct((pairs, 2, width), F32),
        compiler_params=params(),
        cost_estimate=cost_of(10),
        name="diagonals",
    )(flag, tables)
    return out.reshape(2 * pairs, width)


def two_heads(block, first):
    zero = jnp.zeros_like(block)
    return jnp.concatenate([jnp.where(first, block, zero), jnp.where(first, zero, block)], axis=0)


def joined_heads(turned):
    return jnp.concatenate([turned[:DH, :QB], turned[DH:, QB:]], axis=0).T


def fill_columns(segq_ref, segk_ref):
    for block in range(segq_ref.shape[0]):
        rows = jnp.broadcast_to(segq_ref[block : block + 1, :], (QB, QB))
        segk_ref[block * QB : (block + 1) * QB, :] = rows.T


def visit_blocks(seg_ref, origin, count, block):
    @pl.loop(0, count)
    def _(i):
        at = i + origin
        first = seg_ref[at * QB]
        last = seg_ref[at * QB + QB - 1]
        far = (seg_ref[(at - 1) * QB - 1] == first) | (seg_ref[(at + 2) * QB] == last)

        @pl.when(far)
        def _():
            block(i, at, 2)

        @pl.when(jnp.logical_not(far))
        def _():
            block(i, at, 1)


def placed_rows(info, source, halo, target, halo_count):
    edge = PAD * QB
    rows = source.shape[0]
    target[:edge, :] = jnp.zeros((edge, target.shape[1]), target.dtype)
    target[target.shape[0] - edge :, :] = jnp.zeros((edge, target.shape[1]), target.dtype)
    target[pl.ds(pl.multiple_of(info[2] * QB, QB), rows), :] = source[...]
    if halo_count:
        target[pl.ds(pl.multiple_of(info[3] * QB, QB), halo_count), :] = halo[...]


def attend_kernel(halo_count, with_bias, info, seg_ref, *refs):
    refs = list(refs)
    segq_ref, q_ref, k_ref, v_ref = refs[:4]
    t_ref = refs.pop(4) if with_bias else None
    kh_ref = vh_ref = None
    if halo_count:
        kh_ref, vh_ref = refs.pop(4).at[0], refs.pop(4).at[0]
    o_ref, lse_ref = refs[4:6]
    if halo_count:
        refs.pop(6)[0] = kh_ref[...]
        refs.pop(6)[0] = vh_ref[...]
    segk_ref, kp_ref, vp_ref, vt_ref, mask_ref, score_ref, prob_ref = refs[6:]
    rows = q_ref.shape[1]
    pairs = q_ref.shape[2] // (2 * DH)
    first = lax.broadcasted_iota(jnp.int32, (QB, 2 * DH), 1) < DH

    @pl.when(pl.program_id(0) == 0)
    def _():
        fill_columns(segq_ref, segk_ref)

    placed_rows(info, k_ref.at[0], kh_ref, kp_ref, halo_count)
    placed_rows(info, v_ref.at[0], vh_ref, vp_ref, halo_count)
    vt_ref[...] = vp_ref[...].T

    def block(i, at, reach):
        span = (2 * reach + 1) * QB
        keys = pl.ds(pl.multiple_of((at - reach) * QB, QB), span)
        mine = pl.ds(pl.multiple_of(i * QB, QB), QB)
        shifted = pl.ds((2 - reach) * QB, span)
        allowed = segk_ref[keys, :] == segq_ref[pl.ds(at, 1), :]
        mask_ref[:span, :] = jnp.where(allowed, 0.0, -jnp.inf)
        for pair in range(pairs):
            lanes = slice(pair * 2 * DH, (pair + 1) * 2 * DH)
            both = two_heads(q_ref[0, mine, lanes] * LOW(0.125), first)
            scores = dot_nt(kp_ref[keys, lanes], both)
            score_ref[pair, :span, :] = scores + t_ref[pair, shifted, :] if with_bias else scores
        for pair in range(pairs):
            lanes = slice(pair * 2 * DH, (pair + 1) * 2 * DH)
            stats = []
            for head in range(2):
                side = slice(head * QB, (head + 1) * QB)
                top = None
                for strip in range(0, span, STRIP):
                    piece = slice(strip, strip + STRIP)
                    masked = score_ref[pair, piece, side] + mask_ref[piece, :]
                    score_ref[pair, piece, side] = masked
                    peak = jnp.max(masked.reshape(STRIP // 8, 8, QB), axis=0)
                    top = peak if top is None else jnp.maximum(top, peak)
                highest = jnp.max(top, axis=0, keepdims=True)
                total = None
                for strip in range(0, span, STRIP):
                    piece = slice(strip, strip + STRIP)
                    weights = jnp.exp(score_ref[pair, piece, side] - highest)
                    score_ref[pair, piece, side] = weights
                    mass = jnp.sum(weights.reshape(STRIP // 8, 8, QB), axis=0)
                    total = mass if total is None else total + mass
                totals = jnp.sum(total, axis=0, keepdims=True)
                inverse = 1.0 / totals
                for strip in range(0, span, STRIP):
                    piece = slice(strip, strip + STRIP)
                    prob_ref[pair, piece, side] = (score_ref[pair, piece, side] * inverse).astype(LOW)
                stats.append(highest + jnp.log(totals))
            lse_ref[0, pair, pl.ds(i, 1), :] = jnp.concatenate(stats, axis=1)
        for pair in range(pairs):
            lanes = slice(pair * 2 * DH, (pair + 1) * 2 * DH)
            turned = dot_nn(vt_ref[lanes, keys], prob_ref[pair, :span, :])
            o_ref[0, mine, lanes] = joined_heads(turned).astype(LOW)

    visit_blocks(seg_ref, info[2], rows // QB, block)


def head_specs(rows, span, groups, halo_count):
    column = lambda part: pl.BlockSpec((1, rows, span), lambda g, s, t: (s[1], 0, g + part * groups))
    halo = lambda part: pl.BlockSpec((1, halo_count, span), lambda g, s, t: (part, 0, g))
    return column, halo


def attend(info, segments, qkv, halo, bias, previous):
    _, rows, width = qkv.shape
    width = width // 3
    span = min(HEAD_SPAN, width)
    groups = width // span
    pairs = span // (2 * DH)
    count = rows // QB
    blocks = segments.shape[0] // QB
    halo_count = 0 if halo is None else halo.shape[1]
    column, halo_spec = head_specs(rows, span, groups, halo_count)
    slot_pairs = pl.BlockSpec((1, pairs, count, 2 * QB), lambda g, s, t: (s[1], g, 0, 0))
    in_specs = [
        pl.BlockSpec((blocks, QB), lambda g, s, t: (0, 0)),
        column(0),
        column(1),
        column(2),
    ]
    inputs = [segments.reshape(blocks, QB), qkv, qkv, qkv]
    if bias is not None:
        in_specs.append(pl.BlockSpec((pairs,) + bias.shape[1:], lambda g, s, t: (g, 0, 0)))
        inputs.append(bias)
    outputs = [slotted((rows, width), LOW), slotted((groups * pairs, count, 2 * QB), F32)]
    out_specs = [column(0), slot_pairs]
    if halo_count:
        in_specs += [halo_spec(0), halo_spec(1)]
        inputs += [halo, halo]
        outputs += [slotted((halo_count, width), LOW)] * 2
        kept = pl.BlockSpec((1, halo_count, span), lambda g, s, t: (s[1], 0, g))
        out_specs += [kept, kept]
    return call_with_slots(
        functools.partial(attend_kernel, halo_count, bias is not None),
        [info, segments],
        inputs,
        in_specs,
        outputs,
        out_specs,
        previous,
        (groups,),
        [
            pltpu.VMEM((blocks * QB, QB), jnp.int32),
            pltpu.VMEM((blocks * QB, span), LOW),
            pltpu.VMEM((blocks * QB, span), LOW),
            pltpu.VMEM((span, blocks * QB), LOW),
            pltpu.VMEM((5 * QB, QB), F32),
            pltpu.VMEM((pairs, 5 * QB, 2 * QB), F32),
            pltpu.VMEM((pairs, 5 * QB, 2 * QB), LOW),
        ],
        "attend",
        24,
    )


def attend_back_kernel(halo_count, with_bias, info, seg_ref, *refs):
    refs = list(refs)
    segq_ref, q_ref, k_ref, v_ref, g_ref, lse_ref = refs[:6]
    t_ref = refs.pop(6) if with_bias else None
    kh_ref = vh_ref = dh_ref = diag_ref = None
    if halo_count:
        kh_ref, vh_ref = refs.pop(6).at[0], refs.pop(6).at[0]
    dq_ref, dk_ref, dv_ref = refs[6:9]
    if with_bias:
        diag_ref = refs.pop(9)
        diag_ref[...] = jnp.zeros_like(diag_ref)
    if halo_count:
        dh_ref = refs.pop(9)
    segk_ref, kp_ref, vp_ref, kt_ref, dk_acc, dv_acc = refs[9:]
    rows = q_ref.shape[1]
    pairs = q_ref.shape[2] // (2 * DH)
    first = lax.broadcasted_iota(jnp.int32, (QB, 2 * DH), 1) < DH

    @pl.when(pl.program_id(0) == 0)
    def _():
        fill_columns(segq_ref, segk_ref)

    placed_rows(info, k_ref.at[0], kh_ref, kp_ref, halo_count)
    placed_rows(info, v_ref.at[0], vh_ref, vp_ref, halo_count)
    kt_ref[...] = kp_ref[...].T
    dk_acc[...] = jnp.zeros_like(dk_acc)
    dv_acc[...] = jnp.zeros_like(dv_acc)

    def block(i, at, reach):
        span = (2 * reach + 1) * QB
        keys = pl.ds(pl.multiple_of((at - reach) * QB, QB), span)
        mine = pl.ds(pl.multiple_of(i * QB, QB), QB)
        shifted = pl.ds((2 - reach) * QB, span)
        allowed = segk_ref[keys, :] == segq_ref[pl.ds(at, 1), :]
        allowed = jnp.concatenate([allowed, allowed], axis=1)
        for pair in range(pairs):
            lanes = slice(pair * 2 * DH, (pair + 1) * 2 * DH)
            both = two_heads(q_ref[0, mine, lanes] * LOW(0.125), first)
            grads = two_heads(g_ref[mine, lanes], first)
            scores = dot_nt(kp_ref[keys, lanes], both)
            if with_bias:
                scores = scores + t_ref[pair, shifted, :]
            scores = jnp.where(allowed, scores - lse_ref[0, pair, pl.ds(i, 1), :], -jnp.inf)
            probs = jnp.exp(scores)
            grad_probs = dot_nt(vp_ref[keys, lanes], grads)
            dv_acc[keys, lanes] += dot_nn(probs.astype(LOW), grads)
            inner = jnp.sum(probs * grad_probs, axis=0, keepdims=True)
            rounded = (probs * (grad_probs - inner)).astype(LOW)
            dk_acc[keys, lanes] += dot_nn(rounded, both)
            if with_bias:
                diag_ref[0, pair, shifted, :] += rounded.astype(F32)
            turned = dot_nn(kt_ref[lanes, keys], rounded)
            dq_ref[mine, lanes] = (joined_heads(turned) * 0.125).astype(LOW)

    visit_blocks(seg_ref, info[2], rows // QB, block)
    own = pl.ds(pl.multiple_of(info[2] * QB, QB), rows)
    dk_ref[...] = dk_acc[own, :].astype(LOW)
    dv_ref[...] = dv_acc[own, :].astype(LOW)
    if halo_count:
        far = pl.ds(pl.multiple_of(info[3] * QB, QB), halo_count)
        dh_ref[0] = dk_acc[far, :].astype(LOW)
        dh_ref[1] = dv_acc[far, :].astype(LOW)


def attend_back(info, segments, qkv, halo_kept, grad_context, bias, lse, previous):
    _, rows, width = qkv.shape
    width = width // 3
    span = min(HEAD_SPAN, width)
    groups = width // span
    pairs = span // (2 * DH)
    count = rows // QB
    blocks = segments.shape[0] // QB
    halo_count = 0 if halo_kept is None else halo_kept[0].shape[1]
    column, _ = head_specs(rows, span, groups, halo_count)
    plain = pl.BlockSpec((rows, span), lambda g, s, t: (0, g))
    in_specs = [
        pl.BlockSpec((blocks, QB), lambda g, s, t: (0, 0)),
        column(0),
        column(1),
        column(2),
        plain,
        pl.BlockSpec((1, pairs, count, 2 * QB), lambda g, s, t: (s[1], g, 0, 0)),
    ]
    inputs = [segments.reshape(blocks, QB), qkv, qkv, qkv, grad_context, lse]
    if bias is not None:
        in_specs.append(pl.BlockSpec((pairs,) + bias.shape[1:], lambda g, s, t: (g, 0, 0)))
        inputs.append(bias)
    plain_shape = jax.ShapeDtypeStruct((rows, width), LOW)
    outputs = [plain_shape] * 3
    out_specs = [plain] * 3
    if bias is not None:
        outputs.append(slotted(bias.shape, F32))
        out_specs.append(pl.BlockSpec((1, pairs) + bias.shape[1:], lambda g, s, t: (s[1], g, 0, 0)))
    if halo_count:
        kept = pl.BlockSpec((1, halo_count, span), lambda g, s, t: (s[1], 0, g))
        in_specs += [kept, kept]
        inputs += list(halo_kept)
        outputs.append(jax.ShapeDtypeStruct((2, halo_count, width), LOW))
        out_specs.append(pl.BlockSpec((2, halo_count, span), lambda g, s, t: (0, 0, lax.rem(g + groups // 2, groups))))
    keep = None if previous is None else [None] * 3 + [previous] + [None] * (len(outputs) - 4)
    return call_with_slots(
        functools.partial(attend_back_kernel, halo_count, bias is not None),
        [info, segments],
        inputs,
        in_specs,
        outputs,
        out_specs,
        keep,
        (groups,),
        [
            pltpu.VMEM((blocks * QB, QB), jnp.int32),
            pltpu.VMEM((blocks * QB, span), LOW),
            pltpu.VMEM((blocks * QB, span), LOW),
            pltpu.VMEM((span, blocks * QB), LOW),
            pltpu.VMEM((blocks * QB, span), F32),
            pltpu.VMEM((blocks * QB, span), F32),
        ],
        "attend_back",
        26,
    )


def exchange_kernel(give_ref, get_ref, send_sem, recv_sem):
    peer = {"tensor": 1 - lax.axis_index("tensor")}
    barrier = pltpu.get_barrier_semaphore()
    pl.semaphore_signal(barrier, inc=1, device_id=peer, device_id_type=pl.DeviceIdType.MESH)
    pl.semaphore_wait(barrier, 1)
    copy = pltpu.make_async_remote_copy(
        src_ref=give_ref, dst_ref=get_ref, send_sem=send_sem, recv_sem=recv_sem,
        device_id=peer, device_id_type=pl.DeviceIdType.MESH,
    )
    copy.start()
    copy.wait()


def exchanged(value):
    return pl.pallas_call(
        exchange_kernel,
        in_specs=[pl.BlockSpec(memory_space=pl.ANY)],
        out_specs=pl.BlockSpec(memory_space=pl.ANY),
        out_shape=jax.ShapeDtypeStruct(value.shape, value.dtype),
        scratch_shapes=[pltpu.SemaphoreType.DMA, pltpu.SemaphoreType.DMA],
        compiler_params=pltpu.CompilerParams(collective_id=1, has_side_effects=True),
        cost_estimate=cost_of(3),
        name="exchange",
    )(value)


def mean_of(block):
    return jnp.mean(block, axis=-1, keepdims=True)


def rms_scale(block):
    return lax.rsqrt(mean_of(block * block) + 1e-06)


def sum_rows(block):
    return jnp.sum(block, axis=0, keepdims=True)


def gelu_parts(u):
    bell = jnp.exp(u * u * -0.5)
    below = 0.5 + 0.5 * lax.erf(u * 0.7071067811865476)
    return u * below, below + u * (bell * 0.3989422804014327)


def enter_kernel(lead, info, given_ref, gain_ref, shift_ref, own_ref, oth_ref, x_ref, e_ref, qkv_ref, halo_ref):
    m = pl.program_id(0)
    half = own_ref.shape[1]

    @pl.when(m == 0)
    def _():
        x_ref[0] = given_ref[0]
        if lead:
            e_ref[0] = given_ref[0]
        else:
            x = given_ref[0].astype(F32)
            e_ref[0] = (x * rms_scale(x) * gain_ref[...]).astype(LOW)

    e = e_ref[0]
    for part, weight in enumerate((own_ref, oth_ref)):
        lanes = slice(part * half, (part + 1) * half)
        block = (dot_nn(e, weight[...]) + shift_ref[:, lanes]).astype(LOW)
        qkv_ref[0, :, lanes] = block
    start = pl.ds(pl.multiple_of(info[4], QB), halo_ref.shape[1])
    halo_ref[0, :, :half] = qkv_ref[0, start, half:]
    halo_ref[0, :, half:] = qkv_ref[0, start, :half]


def enter(lead, info, given, at, gain, shift, own, oth, previous):
    _, rows, width = given.shape
    half = own.shape[1] // 3
    whole = pl.BlockSpec((1, rows, width), lambda m, s: (at, 0, 0))
    weight = pl.BlockSpec((width, half), lambda m, s: (0, m))
    kept = pl.BlockSpec((1, rows, width), lambda m, s: (s[1], 0, 0))
    keep = None if previous is None else list(previous) + [None]
    return call_with_slots(
        functools.partial(enter_kernel, lead),
        [info],
        [given, gain, shift, own, oth],
        [
            whole,
            pl.BlockSpec((1, width), lambda m, s: (0, 0)),
            pl.BlockSpec((1, 2 * half), lambda m, s: (0, m)),
            weight,
            weight,
        ],
        [
            slotted((rows, width), LOW),
            slotted((rows, width), LOW),
            slotted((rows, 6 * half), LOW),
            jax.ShapeDtypeStruct((2, REACH, 2 * half), LOW),
        ],
        [
            kept,
            kept,
            pl.BlockSpec((1, rows, 2 * half), lambda m, s: (s[1], 0, m)),
            pl.BlockSpec((1, REACH, 2 * half), lambda m, s: (jnp.maximum(m - 1, 0), 0, 0)),
        ],
        keep,
        (3,),
        [],
        "enter",
        9,
    )


def feed_kernel(
    lead, info, x_ref, c_ref, wo_own, wo_oth, up_own, up_oth, down_own, down_oth, bias_ref, gain_ref, shift_ref,
    f_ref, slope_ref, n_ref, one_ref, two_ref, out_ref, acc_ref, carry_ref, hidden_ref
):
    j = pl.program_id(0)
    steps = pl.num_programs(0)
    half = wo_own.shape[0]
    rows = x_ref.shape[1]

    @pl.when(j == 0)
    def _():
        joined = (
            dot_nn(c_ref[0, :, :half], wo_own[...])
            + dot_nn(c_ref[0, :, half:], wo_oth[...])
            + x_ref[0].astype(F32)
        )

        @when(lead)
        def _():
            before = joined + shift_ref[0:1, :]
            one_ref[0] = before.astype(LOW)
            center = before - mean_of(before)
            normed = center * lax.rsqrt(mean_of(center * center) + 1e-05) * gain_ref[0:1, :] + shift_ref[2:3, :]
            carry_ref[...] = normed
            n_ref[0] = normed.astype(LOW)

        @when(not lead)
        def _():
            one_ref[0] = joined.astype(LOW)
            carry_ref[...] = joined
            n_ref[0] = (joined * rms_scale(joined) * gain_ref[1:2, :]).astype(LOW)

        acc_ref[...] = jnp.zeros_like(acc_ref)

    each = (steps - 1) // 2
    now = lax.rem(j, 2)

    def rise(up):
        u = dot_nn(n_ref[0], up[...]) + bias_ref[...]
        f, slope = gelu_parts(u)
        low = f.astype(LOW)
        f_ref[0] = low
        hidden_ref[now] = low
        slope_ref[0] = slope.astype(LOW)

    def fall(down):
        acc_ref[...] += dot_nn(hidden_ref[1 - now], down[...])

    @pl.when(j == 0)
    def _():
        rise(up_own)

    @pl.when((j > 0) & (j < each))
    def _():
        rise(up_own)
        fall(down_own)

    @pl.when(j == each)
    def _():
        rise(up_oth)
        fall(down_own)

    @pl.when((j > each) & (j < steps - 1))
    def _():
        rise(up_oth)
        fall(down_oth)

    @pl.when(j == steps - 1)
    def _():
        fall(down_oth)

    @pl.when(j == steps - 1)
    def _():
        joined = carry_ref[...] + acc_ref[...]

        @when(lead)
        def _():
            before = joined + shift_ref[1:2, :]
            two_ref[0] = before.astype(LOW)
            center = before - mean_of(before)
            normed = center * lax.rsqrt(mean_of(center * center) + 1e-05) * gain_ref[1:2, :] + shift_ref[3:4, :]
            out_ref[...] = normed.astype(LOW)

        @when(not lead)
        def _():
            two_ref[0] = joined.astype(LOW)
            out_ref[...] = joined.astype(LOW)


def split_steps(hidden, chunk):
    each = hidden // chunk
    near = lambda j: jnp.minimum(j, each - 1)
    far = lambda j: jnp.maximum(j - each, 0)
    return 2 * each, near, far


def feed(lead, info, x, context, wo, up, down, bias, gains, shifts, previous):
    _, rows, width = x.shape
    hidden = up[0].shape[1]
    chunk = min(FEED_CHUNK, hidden)
    each = hidden // chunk
    steps = 2 * each + 1
    rise = lambda j: jnp.minimum(j, 2 * each - 1)
    fall = lambda j: jnp.maximum(j - 1, 0)
    near = lambda j: jnp.minimum(j, each - 1)
    far = lambda j: jnp.maximum(j - each, 0)
    kept = pl.BlockSpec((1, rows, width), lambda j, s: (s[1], 0, 0))
    fixed = lambda a: pl.BlockSpec(a.shape, lambda j, s: (0, 0))
    moving = pl.BlockSpec((1, rows, chunk), lambda j, s: (s[1], 0, rise(j)))
    keep = None if previous is None else list(previous) + [None]
    return call_with_slots(
        functools.partial(feed_kernel, lead),
        [info],
        [x, context, wo[0], wo[1], up[0], up[1], down[0], down[1], bias, gains, shifts],
        [
            kept,
            kept,
            fixed(wo[0]),
            fixed(wo[1]),
            pl.BlockSpec((width, chunk), lambda j, s: (0, near(rise(j)))),
            pl.BlockSpec((width, chunk), lambda j, s: (0, far(rise(j)))),
            pl.BlockSpec((chunk, width), lambda j, s: (near(fall(j)), 0)),
            pl.BlockSpec((chunk, width), lambda j, s: (far(fall(j)), 0)),
            pl.BlockSpec((1, chunk), lambda j, s: (0, rise(j))),
            fixed(gains),
            fixed(shifts),
        ],
        [
            slotted((rows, 2 * hidden), LOW),
            slotted((rows, 2 * hidden), LOW),
            slotted((rows, width), LOW),
            slotted((rows, width), LOW),
            slotted((rows, width), LOW),
            jax.ShapeDtypeStruct((rows, width), LOW),
        ],
        [moving, moving, kept, kept, kept, pl.BlockSpec((rows, width), lambda j, s: (0, 0))],
        keep,
        (steps,),
        [
            pltpu.VMEM((rows, width), F32),
            pltpu.VMEM((rows, width), F32),
            pltpu.VMEM((2, rows, chunk), LOW),
        ],
        "feed",
        29,
    )


def layer_norm_back(before, grad, gain_row):
    center = before - mean_of(before)
    scale = lax.rsqrt(mean_of(center * center) + 1e-05)
    unit = center * scale
    inner = grad * gain_row
    back = scale * (inner - mean_of(inner) - unit * mean_of(inner * unit))
    return back, sum_rows(grad * unit)


def rms_norm_back(before, grad, gain_row):
    scale = rms_scale(before)
    unit = before * scale
    inner = grad * gain_row
    back = scale * (inner - unit * mean_of(inner * unit))
    return back, sum_rows(grad * unit)


def feed_back_kernel(
    lead, info, *refs
):
    refs = list(refs)
    got_refs = [refs.pop(0) for _ in range(2 - lead)]
    feed_back_steps(lead, got_refs, *refs)


def feed_back_steps(
    lead, got_refs, one_ref, two_ref, slope_ref, wo_own, wo_oth, up_own, up_oth, down_own, down_oth,
    gain_ref, dy_ref, du_ref, db_ref, stat_ref, bias_ref, dz_ref, dc_ref, acc_ref, carry_ref
):
    j = pl.program_id(0)
    steps = pl.num_programs(0)
    half = wo_own.shape[0]
    rows = dy_ref.shape[1]

    @pl.when(j == 0)
    def _():
        stat_ref[...] = jnp.zeros_like(stat_ref)
        acc_ref[...] = jnp.zeros_like(acc_ref)

        @when(lead)
        def _():
            grad = got_refs[0][0].astype(F32)
            back, gain = layer_norm_back(two_ref[0].astype(F32), grad, gain_ref[1:2, :])
            stat_ref[0, 1:2, :] = gain
            stat_ref[0, 5:6, :] = sum_rows(grad)
            stat_ref[0, 3:4, :] = sum_rows(back)
            carry_ref[...] = back
            dy_ref[0] = back.astype(LOW)

        @when(not lead)
        def _():
            grad = got_refs[0][0].astype(F32) + got_refs[1][0].astype(F32)
            carry_ref[...] = grad
            dy_ref[0] = grad.astype(LOW)

    def part(up, down):
        grad = dot_nt(dy_ref[0], down[...])
        du_ref[0] = (grad * slope_ref[0].astype(F32)).astype(LOW)
        acc_ref[...] += dot_nt(du_ref[0], up[...])
        bias_ref[0] = sum_rows(du_ref[0].astype(F32))

    @pl.when(j < steps // 2)
    def _():
        part(up_own, down_own)

    @pl.when(j >= steps // 2)
    def _():
        part(up_oth, down_oth)

    @pl.when(j == steps - 1)
    def _():
        @when(lead)
        def _():
            grad = acc_ref[...] + carry_ref[...]
            back, gain = layer_norm_back(one_ref[0].astype(F32), grad, gain_ref[0:1, :])
            stat_ref[0, 0:1, :] = gain
            stat_ref[0, 4:5, :] = sum_rows(grad)
            stat_ref[0, 2:3, :] = sum_rows(back)
            dz_ref[...] = back

        @when(not lead)
        def _():
            back, gain = rms_norm_back(one_ref[0].astype(F32), acc_ref[...], gain_ref[1:2, :])
            stat_ref[0, 1:2, :] = gain
            dz_ref[...] = carry_ref[...] + back

        low = dz_ref[...].astype(LOW)
        db_ref[0] = low
        dc_ref[:, :half] = dot_nt(low, wo_own[...]).astype(LOW)
        dc_ref[:, half:] = dot_nt(low, wo_oth[...]).astype(LOW)


def feed_back(lead, info, got, at, one, two, slope, wo, up, down, gains, previous):
    _, rows, width = one.shape
    hidden = up[0].shape[1]
    chunk = min(FEED_CHUNK, hidden)
    steps, near, far = split_steps(hidden, chunk)
    kept = pl.BlockSpec((1, rows, width), lambda j, s: (s[1], 0, 0))
    fixed = lambda a: pl.BlockSpec(a.shape, lambda j, s: (0, 0))
    plain = pl.BlockSpec((rows, width), lambda j, s: (0, 0))
    moving = pl.BlockSpec((1, rows, chunk), lambda j, s: (s[1], 0, j))
    keep = None if previous is None else list(previous) + [None, None]
    return call_with_slots(
        functools.partial(feed_back_kernel, lead),
        [info],
        [*got, one, two, slope, wo[0], wo[1], up[0], up[1], down[0], down[1], gains],
        [pl.BlockSpec((1, rows, width), lambda j, s: (at, 0, 0))] * len(got)
        + [
            kept,
            kept,
            moving,
            fixed(wo[0]),
            fixed(wo[1]),
            pl.BlockSpec((width, chunk), lambda j, s: (0, near(j))),
            pl.BlockSpec((width, chunk), lambda j, s: (0, far(j))),
            pl.BlockSpec((chunk, width), lambda j, s: (near(j), 0)),
            pl.BlockSpec((chunk, width), lambda j, s: (far(j), 0)),
            fixed(gains),
        ],
        [
            slotted((rows, width), LOW),
            slotted((rows, 2 * hidden), LOW),
            slotted((rows, width), LOW),
            slotted((8, width), F32),
            slotted((1, 2 * hidden), F32),
            jax.ShapeDtypeStruct((rows, width), F32),
            jax.ShapeDtypeStruct((rows, width), LOW),
        ],
        [
            kept,
            moving,
            kept,
            pl.BlockSpec((1, 8, width), lambda j, s: (s[1], 0, 0)),
            pl.BlockSpec((1, 1, chunk), lambda j, s: (s[1], 0, j)),
            plain,
            plain,
        ],
        keep,
        (steps,),
        [pltpu.VMEM((rows, width), F32), pltpu.VMEM((rows, width), F32)],
        "feed_back",
        27,
    )


def enter_back_kernel(
    lead, info, dq_ref, dk_ref, dv_ref, far_ref, x_ref, dz_ref, own_ref, oth_ref, gain_ref,
    d_ref, stat_ref, lower_ref, upper_ref, low_ref, acc_ref
):
    m = pl.program_id(0)
    half = own_ref.shape[1]
    start = pl.ds(pl.multiple_of(info[4], QB), far_ref.shape[1])

    @pl.when(m == 0)
    def _():
        stat_ref[...] = jnp.zeros_like(stat_ref)
        acc_ref[...] = jnp.zeros_like(acc_ref)
        d_ref[0] = dq_ref[...]
        stat_ref[0, 0:1, :] = sum_rows(dq_ref[...].astype(F32))

    def with_far(block_ref, part):
        d_ref[0] = block_ref[...]
        d_ref[0, start, :] = (block_ref[start, :].astype(F32) + far_ref[part].astype(F32)).astype(LOW)

    @pl.when(m == 1)
    def _():
        with_far(dk_ref, 0)

    @pl.when(m == 2)
    def _():
        with_far(dv_ref, 1)
        stat_ref[0, 1:2, :] = sum_rows(d_ref[0].astype(F32))

    acc_ref[...] += dot_nt(d_ref[0, :, :half], own_ref[...]) + dot_nt(d_ref[0, :, half:], oth_ref[...])

    @pl.when(m == 2)
    def _():
        split = lower_ref.shape[2]

        @when(lead)
        def _():
            total = dz_ref[...] + acc_ref[...]
            low_ref[...] = total.astype(LOW)
            lower_ref[0] = total[:, :split]
            upper_ref[0] = total[:, split:].astype(LOW)

        @when(not lead)
        def _():
            back, gain = rms_norm_back(x_ref[0].astype(F32), acc_ref[...], gain_ref[...])
            stat_ref[0, 2:3, :] = gain
            total = dz_ref[...] + back
            low_ref[...] = total.astype(LOW)
            lower_ref[0] = total[:, :split]
            upper_ref[0] = total[:, split:].astype(LOW)


def enter_back(lead, info, dq, dk, dv, far, x, dz, own, oth, gain, previous):
    _, rows, width = x.shape
    half = own.shape[1] // 3
    plain = pl.BlockSpec((rows, width), lambda m, s: (0, 0))
    kept = pl.BlockSpec((1, rows, width), lambda m, s: (s[1], 0, 0))
    weight = pl.BlockSpec((width, half), lambda m, s: (0, m))
    keep = None if previous is None else list(previous) + [None]
    return call_with_slots(
        functools.partial(enter_back_kernel, lead),
        [info],
        [dq, dk, dv, far, x, dz, own, oth, gain],
        [
            plain,
            plain,
            plain,
            pl.BlockSpec(far.shape, lambda m, s: (0, 0, 0)),
            kept,
            plain,
            weight,
            weight,
            pl.BlockSpec((1, width), lambda m, s: (0, 0)),
        ],
        [
            slotted((rows, 6 * half), LOW),
            slotted((8, width), F32),
            slotted((rows, width // 2), F32),
            slotted((rows, width // 2), LOW),
            jax.ShapeDtypeStruct((rows, width), LOW),
        ],
        [
            pl.BlockSpec((1, rows, 2 * half), lambda m, s: (s[1], 0, m)),
            pl.BlockSpec((1, 8, width), lambda m, s: (s[1], 0, 0)),
            pl.BlockSpec((1, rows, width // 2), lambda m, s: (s[1], 0, 0)),
            pl.BlockSpec((1, rows, width // 2), lambda m, s: (s[1], 0, 0)),
            plain,
        ],
        keep,
        (3,),
        [pltpu.VMEM((rows, width), F32)],
        "enter_back",
        12,
    )


def passed_along(value, axis, steps):
    count = lax.axis_size(axis)
    initial, last = (max(0, -steps), min(count, count - steps))
    return lax.ppermute(value, axis, [(source, source + steps) for source in range(initial, last)])


def spread(block, axis, source):
    block = jnp.where(lax.axis_index(axis) == source, block, jnp.zeros_like(block))
    return lax.psum(block, axis)


def layer_norm(operand, gain_row, shift_row):
    center = operand - jnp.mean(operand, axis=-1, keepdims=True)
    variance = jnp.mean(center * center, axis=-1, keepdims=True)
    return center * lax.rsqrt(variance + 1e-05) * gain_row + shift_row


def rms_norm(operand, gain_row):
    return (
        operand * lax.rsqrt(jnp.mean(operand * operand, axis=-1, keepdims=True) + 1e-06) * gain_row
    )


def gelu_act(operand):
    return jax.nn.gelu(operand, approximate=False)


def gelu_slope(operand):
    return (
        0.5 * (1.0 + jax.scipy.special.erf(operand * 0.7071067811865476))
        + operand * jnp.exp(-0.5 * operand * operand) * 0.3989422804014327
    )


def entry_norm(residual, gain_rows, leading):
    return jnp.where(leading, residual, rms_norm(residual, gain_rows[0]))


def middle(residual, branch, gain_rows, shift_rows, leading):
    joined = residual + branch
    bert_rows = layer_norm(joined + shift_rows[0], gain_rows[0], shift_rows[2])
    carried = jnp.where(leading, bert_rows, joined)
    normed = jnp.where(leading, bert_rows, rms_norm(joined, gain_rows[1]))
    return (carried, normed)


def final(carried, second, gain_rows, shift_rows, leading):
    joined = carried + second
    return jnp.where(
        leading, layer_norm(joined + shift_rows[1], gain_rows[1], shift_rows[3]), joined
    )


def contract_rows(left, right):
    return lax.dot_general(
        left, right, (((0,), (0,)), ((), ())), preferred_element_type=jnp.float32
    )


def contract_cols(left, right):
    return lax.dot_general(
        left, right, (((1,), (1,)), ((), ())), preferred_element_type=jnp.float32
    )


def gather_rows(operand, weight):
    return (
        jnp.dot(
            lax.all_gather(operand, "tensor", axis=0, tiled=True),
            weight,
            preferred_element_type=jnp.float32,
        ),
        None,
    )


def collect(full_rows, weight):
    return lax.psum_scatter(
        jnp.dot(full_rows, weight, preferred_element_type=jnp.float32),
        "tensor",
        scatter_dimension=0,
        tiled=True,
    )


def scatter_back(grad_rows, weight):
    return lax.psum_scatter(
        contract_cols(grad_rows, weight).astype(jnp.bfloat16),
        "tensor",
        scatter_dimension=0,
        tiled=True,
    ).astype(jnp.float32)


def fold_back(grad_share, weight, activations):
    fragment = lax.all_gather(grad_share, "tensor", axis=0, tiled=True)
    product_rows = contract_cols(fragment, weight)
    return (product_rows, contract_rows(activations, fragment))


def weight_grad(operand, grad_rows):
    return contract_rows(lax.all_gather(operand, "tensor", axis=0, tiled=True), grad_rows)


DH = 64
QB = 128
NARROW = 3
WIDE = 5
VMEM = 56 * 1024 * 1024


def padded(segments):
    return jnp.pad(segments, (PAD * QB, PAD * QB), constant_values=-1)


def general_body(
    layer_input,
    segment_ids,
    buckets,
    attn_in,
    attn_out,
    ffn_in,
    ffn_out,
    norm_gain,
    bert_shift,
    head_bias,
    ffn_bias,
    position_bias,
    decoder_grads,
):
    micro_count = layer_input.shape[0]
    shard_rows = layer_input.shape[2]
    model_width = layer_input.shape[3]
    length = segment_ids.shape[2]
    leading = lax.axis_index("section") == 0
    weighting = jnp.where(leading, 1.0, 0.0)
    qkv_weight = attn_in[0].reshape(model_width, -1)
    out_weight = attn_out[0]
    ffn_up = ffn_in[0]
    ffn_down = ffn_out[0]
    gain_rows = jnp.where(leading, norm_gain[0], norm_gain[1])
    head_shift = head_bias * weighting
    qkv_shift = jnp.concatenate([head_shift[0], jnp.zeros_like(head_shift[0]), head_shift[1]])
    ffn_shift = ffn_bias * weighting
    bias_table = position_bias * (1.0 - weighting)
    bucket_hits = (buckets[None, :] == jnp.arange(bias_table.shape[1])[:, None]).astype(jnp.float32)
    offset_bias = jnp.dot(bias_table, bucket_hits, precision=lax.Precision.HIGHEST)
    near = length - 1 - 3 * QB
    bias = toeplitz(jnp.ones((1,), jnp.int32), offset_bias[:, near : near + 6 * QB])
    info = jnp.array([0, 0, PAD, 0, 0, 1], jnp.int32)
    segment_rows = segment_ids[:, 0]

    def middle_part(residual_in, branch_in, gain_in, shift_in):
        return middle(residual_in, branch_in, gain_in, shift_in, leading)

    def final_part(carried_in, second_in, gain_in, shift_in):
        return final(carried_in, second_in, gain_in, shift_in, leading)

    def entry_part(residual_in, gain_in):
        return entry_norm(residual_in, gain_in, leading)

    received = jnp.zeros((shard_rows, model_width), jnp.bfloat16)
    saved_steps = []
    encoded = []
    for moment in range(micro_count + 1):
        own_rows = layer_input[min(moment, micro_count - 1), 0]
        if moment >= micro_count:
            own_rows = jnp.zeros_like(own_rows)
        segment_row = jnp.where(
            leading, segment_rows[min(moment, micro_count - 1)], segment_rows[max(moment - 1, 0)]
        )
        forward_incoming = jnp.where(leading, own_rows, received)
        forward_residual = forward_incoming.astype(jnp.float32)
        forward_entered = entry_norm(forward_residual, gain_rows, leading).astype(jnp.bfloat16)
        projected, forward_gathered_in = gather_rows(forward_entered, qkv_weight)
        forward_qkv = (projected + qkv_shift).astype(jnp.bfloat16)
        forward_context, forward_log_totals = attend(
            info, padded(segment_row), forward_qkv[None], None, bias, None
        )
        forward_context = forward_context[0]
        forward_branch = collect(forward_context, out_weight)
        forward_carried, forward_normed = middle(
            forward_residual, forward_branch, gain_rows, bert_shift, leading
        )
        pre_full, forward_gathered_mid = gather_rows(forward_normed.astype(jnp.bfloat16), ffn_up)
        forward_pre_act = pre_full + ffn_shift
        forward_second = collect(gelu_act(forward_pre_act).astype(jnp.bfloat16), ffn_down)
        result = final(forward_carried, forward_second, gain_rows, bert_shift, leading).astype(
            jnp.bfloat16
        )
        result, saved = (
            result,
            (
                forward_incoming,
                segment_row,
                forward_branch,
                forward_second,
                forward_qkv,
                forward_context,
                forward_log_totals,
                forward_pre_act,
                forward_gathered_in,
                forward_gathered_mid,
            ),
        )
        saved_steps.append(saved)
        if moment >= 1:
            encoded.append(result)
        if moment < micro_count:
            received = passed_along(result, "section", 1)
    delivered = spread(jnp.stack(encoded), "section", 1)
    section_grads = lax.psum(
        decoder_grads[0, :, 0].astype(jnp.float32).astype(jnp.bfloat16), "section"
    ).astype(jnp.float32)
    grad_received = jnp.zeros((shard_rows, model_width), jnp.float32)
    running_terms = None
    input_rows = []
    for moment in range(micro_count + 1):
        own_grad = section_grads[min(moment, micro_count - 1)]
        if moment >= micro_count:
            own_grad = jnp.zeros_like(own_grad)
        earlier = saved_steps[max(moment - 1, 0)]
        later = saved_steps[min(moment + 1, micro_count)]
        chosen = jax.tree.map(
            lambda from_first, from_second: jnp.where(leading, from_first, from_second),
            earlier,
            later,
        )
        (
            incoming,
            backward_segment_row,
            branch,
            second,
            qkv,
            context,
            log_totals,
            pre_act,
            gathered_in,
            gathered_mid,
        ) = chosen
        residual = incoming.astype(jnp.float32)
        (carried, normed), pull_middle = jax.vjp(
            middle_part, residual, branch, gain_rows, bert_shift
        )
        finished, pull_final = jax.vjp(final_part, carried, second, gain_rows, bert_shift)
        grad_carried, grad_second, gain_end, shift_end = pull_final(
            jnp.where(leading, grad_received, own_grad)
        )
        hidden = gelu_act(pre_act).astype(jnp.bfloat16)
        grad_hidden, backward_grad_down = fold_back(
            grad_second.astype(jnp.bfloat16), ffn_down, hidden
        )
        grad_pre = (grad_hidden * gelu_slope(pre_act)).astype(jnp.bfloat16)
        grad_shift = jnp.sum(grad_pre.astype(jnp.float32), axis=0) * weighting
        backward_grad_up = weight_grad(normed.astype(jnp.bfloat16), grad_pre)
        grad_normed = scatter_back(grad_pre, ffn_up)
        grad_residual, grad_branch, gain_mid, shift_mid = pull_middle((grad_carried, grad_normed))
        grad_context, backward_grad_out_weight = fold_back(
            grad_branch.astype(jnp.bfloat16), out_weight, context
        )
        low_q, low_k, low_v, grad_table = attend_back(
            info, padded(backward_segment_row), qkv[None], None, grad_context.astype(jnp.bfloat16), bias, log_totals, None
        )
        grad_table = grad_table[0]
        grad_head = (
            jnp.stack([jnp.sum(low.astype(jnp.float32), axis=0) for low in (low_q, low_v)]) * weighting
        )
        grad_rows = jnp.concatenate([low_q, low_k, low_v], axis=1)
        entered, pull_entry = jax.vjp(entry_part, residual, gain_rows)
        backward_grad_qkv = weight_grad(entered.astype(jnp.bfloat16), grad_rows)
        grad_entered = scatter_back(grad_rows, qkv_weight)
        grad_from_entry, gain_entry = pull_entry(grad_entered)
        grad_terms = (
            backward_grad_qkv,
            backward_grad_out_weight,
            backward_grad_up,
            backward_grad_down,
            gain_end + gain_mid + gain_entry,
            shift_end + shift_mid,
            grad_head,
            grad_shift,
            grad_table,
        )
        grad_input, grad_terms = (grad_residual + grad_from_entry, grad_terms)
        if running_terms is None:
            running_terms = grad_terms
        else:
            running_terms = jax.tree.map(jnp.add, running_terms, grad_terms)
        if moment >= 1:
            input_rows.append(grad_input)
        if moment < micro_count:
            grad_received = passed_along(grad_input.astype(jnp.bfloat16), "section", -1).astype(
                grad_input.dtype
            )
    input_all = jnp.stack(input_rows)
    half_width = model_width // 2
    upper_half = passed_along(
        input_all[:, :, half_width:].astype(jnp.bfloat16), "section", 1
    ).astype(jnp.float32)
    input_grad = jnp.where(leading, input_all[:, :, :half_width], upper_half)[:, None]
    (
        grad_qkv,
        grad_out_weight,
        grad_up,
        grad_down,
        gain_sum,
        shift_sum,
        head_sum,
        shift_ffn_sum,
        table_sum,
    ) = running_terms
    near_hits = bucket_hits[:, near : near + 6 * QB]
    table_sum = jnp.dot(diagonals(jnp.ones((1,), jnp.int32), table_sum[None], 1), near_hits.T, precision=lax.Precision.HIGHEST) * (
        1.0 - weighting
    )
    weights_out = (
        lax.psum_scatter(
            grad_qkv.reshape(1, model_width, 3, -1).astype(jnp.bfloat16),
            "dp",
            scatter_dimension=1,
            tiled=True,
        ).astype(jnp.float32),
        lax.psum_scatter(
            grad_out_weight[None].astype(jnp.bfloat16), "dp", scatter_dimension=2, tiled=True
        ).astype(jnp.float32),
        lax.psum_scatter(
            grad_up[None].astype(jnp.bfloat16), "dp", scatter_dimension=1, tiled=True
        ).astype(jnp.float32),
        lax.psum_scatter(
            grad_down[None].astype(jnp.bfloat16), "dp", scatter_dimension=2, tiled=True
        ).astype(jnp.float32),
    )
    gain_both = jnp.stack([gain_sum * weighting, gain_sum * (1.0 - weighting)])
    shared_out = lax.psum((gain_both, shift_sum), ("dp", "section", "tensor"))
    split_out = lax.psum((head_sum, shift_ffn_sum, table_sum), ("dp", "section"))
    return (
        delivered[None, :, None],
        input_grad,
        weights_out[0],
        weights_out[1],
        weights_out[2],
        weights_out[3],
        shared_out[0],
        shared_out[1],
        split_out[0],
        split_out[1],
        split_out[2],
    )


def grads_kernel(
    f_hbm, dy_hbm, c_hbm, db_hbm, n_hbm, du_hbm, e_hbm, dqkv_hbm, upper_hbm, packed_ref,
    down_ref, up_ref, row_ref, qkv_ref, summed_ref, upper_got,
    still, moving, turned, given, held, near_ref, y_ref, low_ref, high_ref, small_ref, small_got,
    still_sem, moving_sem, near_send, near_recv, y_send, y_recv, low_send, low_recv, high_send, high_recv,
    small_send, small_recv, upper_send, upper_recv
):
    dp = lax.axis_index("dp")
    core = lax.axis_index("tensor")
    section = lax.axis_index("section")
    y_side = lax.rem(dp, 2)
    low_side = lax.rem(dp // 2, 2)
    high_side = dp // 4

    def across(bit, side):
        return {"dp": dp + bit * (1 - 2 * side)}

    core_peer = {"tensor": 1 - core}
    y_peer = across(1, y_side)
    low_peer = across(2, low_side)
    high_peer = across(4, high_side)
    peers = [core_peer, y_peer, low_peer, high_peer, {"section": 1 - section}]
    mesh_id = pl.DeviceIdType.MESH
    total = held.shape[0]
    chunk = moving.shape[4]
    each = du_hbm.shape[2] // 2 // chunk

    barrier = pltpu.get_barrier_semaphore()
    for peer in peers:
        pl.semaphore_signal(barrier, inc=1, device_id=peer, device_id_type=mesh_id)
    pl.semaphore_wait(barrier, len(peers))

    def send(source, target, out_sem, in_sem, peer):
        return pltpu.make_async_remote_copy(
            src_ref=source, dst_ref=target, send_sem=out_sem, recv_sem=in_sem,
            device_id=peer, device_id_type=mesh_id,
        )

    def near_copy(k, slot):
        return send(given.at[slot], near_ref.at[k], near_send.at[slot], near_recv.at[k], core_peer)

    def y_copy(k):
        return send(held.at[k, :, :, 1 - y_side], y_ref.at[k], y_send.at[k], y_recv.at[k], y_peer)

    def low_copy(k):
        return send(y_ref.at[k, :, 1 - low_side], low_ref.at[k], low_send.at[k], low_recv.at[k], low_peer)

    def high_copy(k):
        return send(low_ref.at[k, 1 - high_side], high_ref.at[k], high_send.at[k], high_recv.at[k], high_peer)

    def small_copy(s):
        return send(small_ref.at[s], small_got.at[s], small_send.at[s], small_recv.at[s], peers[s])

    def added(a, b):
        return (a.astype(F32) + b.astype(F32)).astype(LOW)

    def near_stage(k):
        near_copy(k, 0).wait_recv()
        for hi in range(2):
            for lo in range(2):
                for side in range(2):
                    held[k, hi, lo, side] = added(held[k, hi, lo, side], near_ref[k, hi, lo, side])
        y_copy(k).start()

    def y_stage(k):
        y_copy(k).wait_recv()
        for hi in range(2):
            for lo in range(2):
                y_ref[k, hi, lo] = added(y_ref[k, hi, lo], held[k, hi, lo, y_side])
        low_copy(k).start()

    def low_stage(k):
        low_copy(k).wait_recv()
        for hi in range(2):
            low_ref[k, hi] = added(low_ref[k, hi], y_ref[k, hi, low_side])
        high_copy(k).start()

    def high_stage(k):
        high_copy(k).wait_recv()
        value = high_ref[k].astype(F32) + low_ref[k, high_side].astype(F32)

        def cut(ref, first):
            for q in range(chunk // QB):
                ref[pl.ds(first + q * QB, QB), :] = value[:, q * QB : (q + 1) * QB]

        def lay(ref, at):
            ref[:, pl.ds(pl.multiple_of(at * chunk, chunk), chunk)] = value

        pl.when(k < each)(lambda: cut(down_ref, pl.multiple_of(k * chunk, chunk)))
        pl.when((k >= each) & (k < 2 * each))(lambda: lay(up_ref, k - each))
        pl.when(k == 2 * each)(lambda: cut(row_ref, 0))
        pl.when(k > 2 * each)(lambda: lay(qkv_ref, k - 2 * each - 1))

    def small_stage(s):
        small_copy(s).wait_recv()
        small_ref[s + 1] = small_ref[s] + small_got[s]
        if s + 1 < len(peers):
            small_copy(s + 1).start()

    phases = [
        (False, dy_hbm, f_hbm, each, lambda c: c * chunk, lambda c: (each + c) * chunk),
        (True, n_hbm, du_hbm, each, lambda c: c * chunk, lambda c: (each + c) * chunk),
        (False, db_hbm, c_hbm, 1, lambda c: 0 * c, lambda c: 0 * c + chunk),
        (True, e_hbm, dqkv_hbm, 3, lambda c: 2 * c * chunk, lambda c: (2 * c + 1) * chunk),
    ]

    def still_copy(p):
        return pltpu.make_async_copy(phases[p][1].at[0:2], still.at[p % 2], still_sem.at[p % 2])

    def moving_copies(p, c, slot):
        _, _, source, _, own_at, oth_at = phases[p]
        return [
            pltpu.make_async_copy(
                source.at[0:2, :, pl.ds(pl.multiple_of(at(c), chunk), chunk)],
                moving.at[slot, part],
                moving_sem.at[slot, part],
            )
            for part, at in enumerate((own_at, oth_at))
        ]

    still_copy(0).start()
    for copy in moving_copies(0, 0, 0):
        copy.start()
    still_copy(1).start()
    upper_copy = send(upper_hbm.at[0:2], upper_got, upper_send, upper_recv, peers[4])
    upper_copy.start()
    small_ref[0] = packed_ref[...]
    small_copy(0).start()

    tokens = 2 * still.shape[2]
    base = 0
    for p, (wide, _, _, count, _, _) in enumerate(phases):
        still_copy(p).wait()
        stay = still.at[p % 2]
        if wide:
            for micro in range(2):
                turned[:, micro * tokens // 2 : (micro + 1) * tokens // 2] = stay[micro].T

        @pl.loop(0, count)
        def _(c, p=p, wide=wide, count=count, base=base, stay=stay):
            k = base + c
            slot = lax.rem(k, 2)
            for copy in moving_copies(p, c, slot):
                copy.wait()

            @pl.when(c + 1 < count)
            def _():
                for copy in moving_copies(p, c + 1, 1 - slot):
                    copy.start()

            if p + 1 < len(phases):

                @pl.when(c + 1 == count)
                def _():
                    for copy in moving_copies(p + 1, 0, 1 - slot):
                        copy.start()

            @pl.when(k >= 2)
            def _():
                near_copy(k, slot).wait_send()

            def product(part, store):
                block = moving[slot, part].reshape(tokens, chunk)
                if wide:
                    result = dot_nn(turned[...], block).astype(LOW)
                    for z in range(4):
                        for side in range(2):
                            at = (2 * z + side) * QB
                            store(z, side, slice(None), result[at : at + QB, :])
                else:
                    result = dot_nn(block.T, stay[...].reshape(tokens, -1)).astype(LOW)
                    for z in range(4):
                        for side in range(2):
                            at = (2 * z + side) * QB
                            for q in range(chunk // QB):
                                lanes = slice(q * QB, (q + 1) * QB)
                                store(z, side, lanes, result[lanes, at : at + QB])

            def to_given(z, side, lanes, value):
                given[slot, z // 2, z % 2, side, :, lanes] = value

            def to_held(z, side, lanes, value):
                held[k, z // 2, z % 2, side, :, lanes] = value

            product(1, to_given)
            near_copy(k, slot).start()
            product(0, to_held)

            @pl.when(k >= 1)
            def _():
                near_stage(k - 1)

            for s in range(len(peers)):

                @pl.when(k == 2 * s + 1)
                def _(s=s):
                    small_stage(s)

            @pl.when((k >= 5) & (lax.rem(k, 3) == 2))
            def _():
                y_stage((k - 5) // 3)

        if p + 2 < len(phases):
            still_copy(p + 2).start()
        base += count

    near_stage(total - 1)
    early = (total - 1 - 5) // 3 + 1
    @pl.loop(0, early)
    def _(k):
        low_stage(k)

    @pl.loop(0, early - 1)
    def _(k):
        high_stage(k)

    @pl.loop(early, total)
    def _(k):
        y_stage(k)
        high_stage(k - 1)
        low_stage(k)

    @pl.loop(total - 1, total)
    def _(k):
        high_stage(k)

    summed_ref[...] = small_ref[len(peers)]
    near_copy(total - 2, (total - 2) % 2).wait_send()
    near_copy(total - 1, (total - 1) % 2).wait_send()

    @pl.loop(0, total)
    def _(k):
        y_copy(k).wait_send()
        low_copy(k).wait_send()
        high_copy(k).wait_send()

    for s in range(len(peers)):
        small_copy(s).wait_send()
    upper_copy.wait()


def summed_grads(f, dy, context, db, n, du, e, dqkv, upper, packed):
    rows, width = dy.shape[1:]
    chunk = 512
    total = du.shape[2] // chunk + 4
    dma = pltpu.SemaphoreType.DMA
    anywhere = pl.BlockSpec(memory_space=pl.ANY)
    local = pl.BlockSpec(memory_space=pltpu.VMEM)
    return pl.pallas_call(
        grads_kernel,
        in_specs=[anywhere] * 9 + [local],
        out_specs=[local] * 5 + [anywhere],
        out_shape=[
            jax.ShapeDtypeStruct((du.shape[2] // 2, QB), F32),
            jax.ShapeDtypeStruct((QB, du.shape[2] // 2), F32),
            jax.ShapeDtypeStruct((width // 2, QB), F32),
            jax.ShapeDtypeStruct((QB, dqkv.shape[2] // 2), F32),
            jax.ShapeDtypeStruct(packed.shape, F32),
            jax.ShapeDtypeStruct((2,) + upper.shape[1:], LOW),
        ],
        scratch_shapes=[
            pltpu.VMEM((2, 2, rows, width), LOW),
            pltpu.VMEM((2, 2, 2, rows, chunk), LOW),
            pltpu.VMEM((width, 2 * rows), LOW),
            pltpu.VMEM((2, 2, 2, 2, QB, chunk), LOW),
            pltpu.VMEM((total, 2, 2, 2, QB, chunk), LOW),
            pltpu.VMEM((total, 2, 2, 2, QB, chunk), LOW),
            pltpu.VMEM((total, 2, 2, QB, chunk), LOW),
            pltpu.VMEM((total, 2, QB, chunk), LOW),
            pltpu.VMEM((total, QB, chunk), LOW),
            pltpu.VMEM((6,) + packed.shape, F32),
            pltpu.VMEM((5,) + packed.shape, F32),
            dma((2,)),
            dma((2, 2)),
            dma((2,)),
            dma((total,)),
            dma((total,)),
            dma((total,)),
            dma((total,)),
            dma((total,)),
            dma((total,)),
            dma((total,)),
            dma((5,)),
            dma((5,)),
            dma,
            dma,
        ],
        compiler_params=pltpu.CompilerParams(
            collective_id=0, has_side_effects=True, vmem_limit_bytes=TAIL_VMEM
        ),
        cost_estimate=cost_of(5000),
        name="summed_grads",
    )(f, dy, context, db, n, du, e, dqkv, upper, packed)


def swapped(value, axis, bit):
    pairs = [(at, at ^ bit) for at in range(lax.axis_size(axis))]
    return lax.ppermute(value, axis, pairs)


def paired_body(
    layer_input,
    segment_ids,
    buckets,
    attn_in,
    attn_out,
    ffn_in,
    ffn_out,
    norm_gain,
    bert_shift,
    head_bias,
    ffn_bias,
    position_bias,
    decoder_grads,
):
    micro_count, _, rows, width = layer_input.shape
    length = segment_ids.shape[2]
    heads, bucket_count = position_bias.shape
    section = lax.axis_index("section")
    core = lax.axis_index("tensor")
    leading = section == 0
    lead = jnp.where(leading, 1, 0).astype(jnp.int32)
    pieces = lax.axis_size("dp")

    own_grads = decoder_grads[0, :, 0]
    remote_grads = lax.ppermute(own_grads, "section", [(0, 1)])
    given_rows = layer_input[:, 0]
    qkv_own = jnp.concatenate([attn_in[0, :, part] for part in range(3)], axis=1)
    qkv_oth = swapped(qkv_own, "tensor", 1)
    wo = (attn_out[0], swapped(attn_out[0], "tensor", 1))
    up = (ffn_in[0], swapped(ffn_in[0], "tensor", 1))
    down = (ffn_out[0], swapped(ffn_out[0], "tensor", 1))
    small = jnp.concatenate([head_bias.reshape(-1), ffn_bias, position_bias.reshape(-1)])
    small_oth = swapped(small, "tensor", 1)
    near_heads = head_bias.size
    near_ffn = near_heads + ffn_bias.size
    both_small = jnp.stack([small, small_oth])
    head_both = both_small[:, :near_heads].reshape(2, 2, -1)
    ffn_both = jnp.where(leading, both_small[:, near_heads:near_ffn], 0.0).reshape(1, -1)
    table_both = jnp.where(leading, 0.0, both_small[:, near_ffn:]).reshape(2 * heads, bucket_count)
    q_shift = head_both[:, 0].reshape(1, -1)
    v_shift = head_both[:, 1].reshape(1, -1)
    qkv_shift = jnp.where(
        leading, jnp.concatenate([q_shift, jnp.zeros_like(q_shift), v_shift], axis=1), 0.0
    )
    gains = jnp.where(leading, norm_gain[0], norm_gain[1])
    entry_gain = gains[0:1]

    near = length - 1 - 3 * QB
    near_hits = (buckets[None, near : near + 6 * QB] == jnp.arange(bucket_count)[:, None]).astype(F32)
    trailing = jnp.reshape(1 - lead, (1,))
    bias = toeplitz(trailing, jnp.dot(table_both, near_hits, precision=lax.Precision.HIGHEST))

    window = rows + REACH
    base = core * (length - window)
    segments = jnp.pad(
        lax.dynamic_slice_in_dim(segment_ids[:, 0], base, window, axis=1),
        ((0, 0), (PAD * QB, PAD * QB)),
        constant_values=-1,
    )
    reach_blocks = REACH // QB
    own_block = PAD + core * reach_blocks
    halo_block = jnp.where(core == 0, PAD + rows // QB, PAD)
    edge = jnp.where(core == 0, rows - REACH, 0)

    def info_of(turn, micro):
        active = jnp.where(section == turn, 1, 0)
        slot = jnp.where(active == 1, micro, micro_count)
        return jnp.stack([lead, slot, own_block, halo_block, edge, active]).astype(jnp.int32)

    turns = [(turn, micro) for turn in range(2) for micro in range(micro_count)]
    received = [None] * micro_count
    entered = attended = fed = None
    results = []
    finished = []
    for turn, micro in turns:
        info = info_of(turn, micro)
        if turn + micro > 0:
            info, _ = lax.optimization_barrier((info, result))
        if turn == 1 and micro == 0:
            info, remote_grads = lax.optimization_barrier((info, remote_grads))
        lead_turn = turn == 0
        given, at = (given_rows, micro) if lead_turn else (received[micro][None], 0)
        *entered, halo = enter(
            lead_turn, info, given, at, entry_gain, qkv_shift, qkv_own, qkv_oth, entered
        )
        halo = exchanged(halo)
        attended = attend(
            info, segments[micro], entered[2], halo, None if lead_turn else bias, attended
        )
        *fed, result = feed(
            lead_turn, info, entered[0], attended[0], wo, up, down, ffn_both, gains, bert_shift, fed
        )
        if turn == 0:
            received = list(received)
            received[micro] = lax.ppermute(result, "section", [(0, 1)])
        else:
            results.append(result)
            finished.append(lax.ppermute(result, "section", [(1, 0)]))
    x_saved, e_saved, qkv_saved = entered
    context, lse, *halo_saved = attended
    f_saved, slope_saved, n_saved, one_saved, two_saved = fed

    received = [None] * micro_count
    feed_kept = table_kept = entry_kept = None
    for step, (turn, micro) in enumerate([(1 - turn, micro) for turn, micro in turns]):
        info = info_of(turn, micro)
        if step > 0:
            info, _ = lax.optimization_barrier((info, low if step < 3 else entry_kept[1]))
        lead_turn = turn == 0
        got, at = ([received[micro][None]], 0) if lead_turn else ([own_grads, remote_grads], micro)
        *feed_kept, dz, grad_context = feed_back(
            lead_turn, info, got, at, one_saved, two_saved, slope_saved, wo, up, down, gains, feed_kept
        )
        dq, dk, dv, *tables, far = attend_back(
            info, segments[micro], qkv_saved, halo_saved, grad_context, None if lead_turn else bias, lse,
            None if lead_turn else table_kept,
        )
        if not lead_turn:
            table_kept = tables[0]
        far = exchanged(far)
        if turn == 1 and micro == 0:
            info, *finished = lax.optimization_barrier((info, *finished))
        *entry_kept, low = enter_back(
            lead_turn, info, dq, dk, dv, far, x_saved, dz, qkv_own, qkv_oth, entry_gain, entry_kept
        )
        if turn == 1:
            received = list(received)
            received[micro] = lax.ppermute(low, "section", [(1, 0)])
    dy_saved, du_saved, db_saved, stat_feed, stat_bias = feed_kept
    dqkv_saved, stat_entry, lower_kept, upper_kept = entry_kept

    near_table = jnp.dot(diagonals(trailing, table_kept, micro_count), near_hits.T, precision=lax.Precision.HIGHEST)

    def placed(pair):
        return jnp.where(core == 0, pair, pair[::-1])

    stat_feed = stat_feed[0] + stat_feed[1]
    stat_entry = stat_entry[0] + stat_entry[1]
    gain_first = jnp.where(leading, stat_feed[0:1], stat_entry[2:3])
    gain_rows = jnp.concatenate([gain_first, stat_feed[1:2]])
    nothing = jnp.zeros_like(gain_rows)
    gain_all = jnp.where(leading, jnp.concatenate([gain_rows, nothing]), jnp.concatenate([nothing, gain_rows]))
    shift_all = jnp.where(leading, stat_feed[2:6], 0.0)
    head_all = jnp.where(leading, stat_entry[0:2], 0.0).reshape(2, 2, -1)
    head_all = placed(jnp.moveaxis(head_all, 1, 0))
    bias_all = placed(jnp.where(leading, stat_bias[0] + stat_bias[1], 0.0).reshape(2, -1))
    table_all = placed(jnp.where(leading, 0.0, near_table).reshape(2, heads, bucket_count))
    parts = [gain_all, shift_all, head_all, bias_all, table_all]
    packed = jnp.concatenate([part.reshape(-1) for part in parts])
    packed_rows = 8 * (-(-packed.size // (8 * width)))
    packed = jnp.pad(packed, (0, packed_rows * width - packed.size)).reshape(packed_rows, width)
    down_sum, up_sum, out_sum, qkv_sum, packed, upper = summed_grads(
        f_saved, dy_saved, context, db_saved, n_saved, du_saved, e_saved, dqkv_saved, upper_kept, packed
    )
    packed = packed.reshape(-1)
    input_grad = jnp.where(leading, lower_kept[:micro_count], upper.astype(F32))[:, None]
    unpacked = []
    start = 0
    for part in parts:
        unpacked.append(packed[start : start + part.size].reshape(part.shape))
        start += part.size
    gain_all, shift_all, head_all, bias_all, table_all = unpacked
    mine = lambda value: lax.dynamic_index_in_dim(value, core, 0, keepdims=False)
    return (
        jnp.where(leading, jnp.stack(finished), jnp.stack(results))[None, :, None],
        input_grad,
        qkv_sum.reshape(1, width // pieces, 3, -1),
        out_sum[None],
        up_sum[None],
        down_sum[None],
        gain_all.reshape(norm_gain.shape),
        shift_all,
        mine(head_all),
        mine(bias_all),
        mine(table_all),
    )


def solution(mesh):
    placed = (
        P(None, "dp", "tensor", None),
        P(None, "dp", None),
        P(),
        P("section", None, None, "tensor"),
        P("section", "tensor", None),
        P("section", None, "tensor"),
        P("section", "tensor", None),
        P(),
        P(),
        P(None, "tensor"),
        P("tensor"),
        P("tensor", None),
        P("section", None, "dp", "tensor", None),
    )
    paired = mesh.shape["tensor"] == 2 and mesh.shape["dp"] == 8
    return jax.shard_map(
        paired_body if paired else general_body,
        mesh=mesh,
        in_specs=placed,
        out_specs=(
            P("section", None, "dp", "tensor", None),
            P(None, "dp", "tensor", "section"),
            P("section", "dp", None, "tensor"),
            P("section", "tensor", "dp"),
            P("section", "dp", "tensor"),
            P("section", "tensor", "dp"),
            P(),
            P(),
            P(None, "tensor"),
            P("tensor"),
            P("tensor", None),
        ),
        check_vma=False,
    )
```

```python
import functools

import jax
import jax.numpy as jnp
from jax import lax
from jax.experimental import pallas as pl
from jax.experimental.pallas import tpu as pltpu
from jax.sharding import PartitionSpec as P

DH = 64
QB = 128
PAD = 2
REACH = 256
STRIP = 64
HEAD_SPAN = 512
FEED_CHUNK = 1024
VMEM = 56 * 1024 * 1024
TAIL_VMEM = 60 * 1024 * 1024
LOW = jnp.bfloat16
F32 = jnp.float32


def dot_nt(left, right):
    return lax.dot_general(left, right, (((1,), (1,)), ((), ())), preferred_element_type=F32)


def dot_nn(left, right):
    return lax.dot_general(left, right, (((1,), (0,)), ((), ())), preferred_element_type=F32)


def params():
    return pltpu.CompilerParams(vmem_limit_bytes=VMEM)


def cost_of(micros):
    return pl.CostEstimate(flops=int(micros * 5e7), bytes_accessed=0, transcendentals=0)


def when(condition):
    return (lambda body: body()) if condition else (lambda body: None)


def slotted(shape, dtype):
    return jax.ShapeDtypeStruct((3,) + shape, dtype)


def call_with_slots(
    kernel, scalars, inputs, in_specs, outputs, out_specs, previous, grid, scratch, name, micros
):
    count = len(inputs)
    kept = [] if previous is None else [item for item in previous if item is not None]
    aliases = {}
    if previous is not None:
        at = len(scalars) + count
        for index, item in enumerate(previous):
            if item is not None:
                aliases[at] = index
                at += 1

    def gated(spec):
        if spec.index_map is None:
            return spec
        return pl.BlockSpec(spec.block_shape, lambda j, s, *rest: spec.index_map(j * s[5], s, *rest))

    in_specs = [gated(spec) for spec in in_specs]
    out_specs = [gated(spec) for spec in out_specs]

    def run(*refs):
        @pl.when(refs[0][5] == 1)
        def _():
            front = len(scalars) + count
            kernel(*refs[:front], *refs[front + len(kept) :])

    return pl.pallas_call(
        run,
        grid_spec=pltpu.PrefetchScalarGridSpec(
            num_scalar_prefetch=len(scalars),
            grid=grid,
            in_specs=list(in_specs) + [pl.BlockSpec(memory_space=pl.ANY)] * len(kept),
            out_specs=out_specs,
            scratch_shapes=scratch,
        ),
        out_shape=outputs,
        input_output_aliases=aliases,
        compiler_params=params(),
        cost_estimate=cost_of(micros),
        name=name,
    )(*scalars, *inputs, *kept)


def toeplitz_kernel(flag_ref, w_ref, t_ref):
    width = w_ref.shape[2]

    @pl.when(flag_ref[0] == 0)
    def _():
        t_ref[...] = jnp.zeros_like(t_ref)

    @pl.when(flag_ref[0] == 1)
    def _():
        half = []
        for head in range(2):
            rows = jnp.broadcast_to(w_ref[0, head : head + 1, :], (QB, width))
            rolled = pltpu.roll(rows, 0, 1, stride=1, stride_axis=0)
            half.append(rolled.T[QB:, :])
        t_ref[0] = jnp.concatenate(half, axis=1)


def toeplitz(flag, offset_bias):
    heads, width = offset_bias.shape
    pairs = heads // 2
    return pl.pallas_call(
        toeplitz_kernel,
        grid_spec=pltpu.PrefetchScalarGridSpec(
            num_scalar_prefetch=1,
            grid=(pairs,),
            in_specs=[pl.BlockSpec((1, 2, width), lambda p, s: (p, 0, 0))],
            out_specs=pl.BlockSpec((1, width - QB, 2 * QB), lambda p, s: (p, 0, 0)),
        ),
        out_shape=jax.ShapeDtypeStruct((pairs, width - QB, 2 * QB), F32),
        compiler_params=params(),
        cost_estimate=cost_of(6),
        name="toeplitz",
    )(flag, offset_bias.reshape(pairs, 2, width))


def diagonal_kernel(flag_ref, a_ref, s_ref):
    @pl.when(flag_ref[0] == 0)
    def _():
        s_ref[...] = jnp.zeros_like(s_ref)

    @pl.when(flag_ref[0] == 1)
    def _():
        sum_diagonals(a_ref, s_ref)


def sum_diagonals(a_ref, s_ref):
    total = a_ref[0, 0]
    for extra in range(1, a_ref.shape[0]):
        total = total + a_ref[extra, 0]
    total = jnp.concatenate([jnp.zeros((QB, 2 * QB), F32), total], axis=0)
    width = total.shape[0]
    row = lax.broadcasted_iota(jnp.int32, (QB, QB), 0)
    col = lax.broadcasted_iota(jnp.int32, (QB, QB), 1)
    mirror = jnp.where(row + col == QB - 1, 1.0, 0.0)
    for head in range(2):
        turned = lax.dot_general(
            mirror,
            total[:, head * QB : (head + 1) * QB],
            (((1,), (1,)), ((), ())),
            precision=lax.Precision.HIGHEST,
            preferred_element_type=F32,
        )
        aligned = pltpu.roll(turned, width - QB + 1, 1, stride=1, stride_axis=0)
        s_ref[0, head : head + 1, :] = jnp.sum(aligned, axis=0, keepdims=True)


def diagonals(flag, tables, steps):
    _, pairs, rows, _ = tables.shape
    width = rows + QB
    out = pl.pallas_call(
        diagonal_kernel,
        grid_spec=pltpu.PrefetchScalarGridSpec(
            num_scalar_prefetch=1,
            grid=(pairs,),
            in_specs=[pl.BlockSpec((steps, 1, rows, 2 * QB), lambda p, s: (0, p * s[0], 0, 0))],
            out_specs=pl.BlockSpec((1, 2, width), lambda p, s: (p, 0, 0)),
        ),
        out_shape=jax.ShapeDtypeStruct((pairs, 2, width), F32),
        compiler_params=params(),
        cost_estimate=cost_of(10),
        name="diagonals",
    )(flag, tables)
    return out.reshape(2 * pairs, width)


def two_heads(block, first):
    zero = jnp.zeros_like(block)
    return jnp.concatenate([jnp.where(first, block, zero), jnp.where(first, zero, block)], axis=0)


def joined_heads(turned):
    return jnp.concatenate([turned[:DH, :QB], turned[DH:, QB:]], axis=0).T


def fill_columns(segq_ref, segk_ref):
    for block in range(segq_ref.shape[0]):
        rows = jnp.broadcast_to(segq_ref[block : block + 1, :], (QB, QB))
        segk_ref[block * QB : (block + 1) * QB, :] = rows.T


def visit_blocks(seg_ref, origin, count, block):
    @pl.loop(0, count)
    def _(i):
        at = i + origin
        first = seg_ref[at * QB]
        last = seg_ref[at * QB + QB - 1]
        far = (seg_ref[(at - 1) * QB - 1] == first) | (seg_ref[(at + 2) * QB] == last)

        @pl.when(far)
        def _():
            block(i, at, 2)

        @pl.when(jnp.logical_not(far))
        def _():
            block(i, at, 1)


def placed_rows(info, source, halo, target, halo_count):
    edge = PAD * QB
    rows = source.shape[0]
    target[:edge, :] = jnp.zeros((edge, target.shape[1]), target.dtype)
    target[target.shape[0] - edge :, :] = jnp.zeros((edge, target.shape[1]), target.dtype)
    target[pl.ds(pl.multiple_of(info[2] * QB, QB), rows), :] = source[...]
    if halo_count:
        target[pl.ds(pl.multiple_of(info[3] * QB, QB), halo_count), :] = halo[...]


def turned_rows(info, source, halo, target, halo_count):
    edge = PAD * QB
    rows = source.shape[0]
    target[:, :edge] = jnp.zeros((target.shape[0], edge), target.dtype)
    target[:, target.shape[1] - edge :] = jnp.zeros((target.shape[0], edge), target.dtype)
    target[:, pl.ds(pl.multiple_of(info[2] * QB, QB), rows)] = source[...].T
    if halo_count:
        target[:, pl.ds(pl.multiple_of(info[3] * QB, QB), halo_count)] = halo[...].T


def attend_kernel(halo_count, with_bias, info, seg_ref, *refs):
    refs = list(refs)
    segq_ref, q_ref, k_ref, v_ref = refs[:4]
    t_ref = refs.pop(4) if with_bias else None
    kh_ref = vh_ref = None
    if halo_count:
        kh_ref, vh_ref = refs.pop(4).at[0], refs.pop(4).at[0]
    o_ref, lse_ref = refs[4:6]
    if halo_count:
        refs.pop(6)[0] = kh_ref[...]
        refs.pop(6)[0] = vh_ref[...]
    segk_ref, kp_ref, vt_ref, mask_ref, score_ref, prob_ref = refs[6:]
    rows = q_ref.shape[1]
    pairs = q_ref.shape[2] // (2 * DH)
    first = lax.broadcasted_iota(jnp.int32, (QB, 2 * DH), 1) < DH

    @pl.when(pl.program_id(0) == 0)
    def _():
        fill_columns(segq_ref, segk_ref)

    placed_rows(info, k_ref.at[0], kh_ref, kp_ref, halo_count)
    turned_rows(info, v_ref.at[0], vh_ref, vt_ref, halo_count)

    def block(i, at, reach):
        span = (2 * reach + 1) * QB
        keys = pl.ds(pl.multiple_of((at - reach) * QB, QB), span)
        mine = pl.ds(pl.multiple_of(i * QB, QB), QB)
        shifted = pl.ds((2 - reach) * QB, span)
        allowed = segk_ref[keys, :] == segq_ref[pl.ds(at, 1), :]
        mask_ref[:span, :] = jnp.where(allowed, 0.0, -jnp.inf)
        for pair in range(pairs):
            lanes = slice(pair * 2 * DH, (pair + 1) * 2 * DH)
            both = two_heads(q_ref[0, mine, lanes] * LOW(0.125), first)
            scores = dot_nt(kp_ref[keys, lanes], both)
            score_ref[pair, :span, :] = scores + t_ref[pair, shifted, :] if with_bias else scores
        for pair in range(pairs):
            lanes = slice(pair * 2 * DH, (pair + 1) * 2 * DH)
            stats = []
            for head in range(2):
                side = slice(head * QB, (head + 1) * QB)
                top = None
                for strip in range(0, span, STRIP):
                    piece = slice(strip, strip + STRIP)
                    masked = score_ref[pair, piece, side] + mask_ref[piece, :]
                    score_ref[pair, piece, side] = masked
                    peak = jnp.max(masked.reshape(STRIP // 8, 8, QB), axis=0)
                    top = peak if top is None else jnp.maximum(top, peak)
                highest = jnp.max(top, axis=0, keepdims=True)
                total = None
                for strip in range(0, span, STRIP):
                    piece = slice(strip, strip + STRIP)
                    weights = jnp.exp(score_ref[pair, piece, side] - highest)
                    score_ref[pair, piece, side] = weights
                    mass = jnp.sum(weights.reshape(STRIP // 8, 8, QB), axis=0)
                    total = mass if total is None else total + mass
                totals = jnp.sum(total, axis=0, keepdims=True)
                inverse = 1.0 / totals
                for strip in range(0, span, STRIP):
                    piece = slice(strip, strip + STRIP)
                    prob_ref[pair, piece, side] = (score_ref[pair, piece, side] * inverse).astype(LOW)
                stats.append(highest + jnp.log(totals))
            lse_ref[0, pair, pl.ds(i, 1), :] = jnp.concatenate(stats, axis=1)
        for pair in range(pairs):
            lanes = slice(pair * 2 * DH, (pair + 1) * 2 * DH)
            turned = dot_nn(vt_ref[lanes, keys], prob_ref[pair, :span, :])
            o_ref[0, mine, lanes] = joined_heads(turned).astype(LOW)

    visit_blocks(seg_ref, info[2], rows // QB, block)


def head_specs(rows, span, groups, halo_count):
    column = lambda part: pl.BlockSpec((1, rows, span), lambda g, s, t: (s[1], 0, g + part * groups))
    halo = lambda part: pl.BlockSpec((1, halo_count, span), lambda g, s, t: (part, 0, g))
    return column, halo


def attend(info, segments, qkv, halo, bias, previous):
    _, rows, width = qkv.shape
    width = width // 3
    span = min(HEAD_SPAN, width)
    groups = width // span
    pairs = span // (2 * DH)
    count = rows // QB
    blocks = segments.shape[0] // QB
    halo_count = 0 if halo is None else halo.shape[1]
    column, halo_spec = head_specs(rows, span, groups, halo_count)
    slot_pairs = pl.BlockSpec((1, pairs, count, 2 * QB), lambda g, s, t: (s[1], g, 0, 0))
    in_specs = [
        pl.BlockSpec((blocks, QB), lambda g, s, t: (0, 0)),
        column(0),
        column(1),
        column(2),
    ]
    inputs = [segments.reshape(blocks, QB), qkv, qkv, qkv]
    if bias is not None:
        in_specs.append(pl.BlockSpec((pairs,) + bias.shape[1:], lambda g, s, t: (g, 0, 0)))
        inputs.append(bias)
    outputs = [slotted((rows, width), LOW), slotted((groups * pairs, count, 2 * QB), F32)]
    out_specs = [column(0), slot_pairs]
    if halo_count:
        in_specs += [halo_spec(0), halo_spec(1)]
        inputs += [halo, halo]
        outputs += [slotted((halo_count, width), LOW)] * 2
        kept = pl.BlockSpec((1, halo_count, span), lambda g, s, t: (s[1], 0, g))
        out_specs += [kept, kept]
    return call_with_slots(
        functools.partial(attend_kernel, halo_count, bias is not None),
        [info, segments],
        inputs,
        in_specs,
        outputs,
        out_specs,
        previous,
        (groups,),
        [
            pltpu.VMEM((blocks * QB, QB), jnp.int32),
            pltpu.VMEM((blocks * QB, span), LOW),
            pltpu.VMEM((span, blocks * QB), LOW),
            pltpu.VMEM((5 * QB, QB), F32),
            pltpu.VMEM((pairs, 5 * QB, 2 * QB), F32),
            pltpu.VMEM((pairs, 5 * QB, 2 * QB), LOW),
        ],
        "attend",
        24,
    )


def attend_back_kernel(halo_count, with_bias, info, seg_ref, *refs):
    refs = list(refs)
    segq_ref, q_ref, k_ref, v_ref, g_ref, lse_ref = refs[:6]
    t_ref = refs.pop(6) if with_bias else None
    kh_ref = vh_ref = dh_ref = diag_ref = None
    if halo_count:
        kh_ref, vh_ref = refs.pop(6).at[0], refs.pop(6).at[0]
    dq_ref, dk_ref, dv_ref = refs[6:9]
    if with_bias:
        diag_ref = refs.pop(9)
        diag_ref[...] = jnp.zeros_like(diag_ref)
    if halo_count:
        dh_ref = refs.pop(9)
    segk_ref, kp_ref, vp_ref, kt_ref, dk_acc, dv_acc = refs[9:]
    rows = q_ref.shape[1]
    pairs = q_ref.shape[2] // (2 * DH)
    first = lax.broadcasted_iota(jnp.int32, (QB, 2 * DH), 1) < DH

    @pl.when(pl.program_id(0) == 0)
    def _():
        fill_columns(segq_ref, segk_ref)

    placed_rows(info, k_ref.at[0], kh_ref, kp_ref, halo_count)
    placed_rows(info, v_ref.at[0], vh_ref, vp_ref, halo_count)
    turned_rows(info, k_ref.at[0], kh_ref, kt_ref, halo_count)
    dk_acc[...] = jnp.zeros_like(dk_acc)
    dv_acc[...] = jnp.zeros_like(dv_acc)

    def block(i, at, reach):
        span = (2 * reach + 1) * QB
        keys = pl.ds(pl.multiple_of((at - reach) * QB, QB), span)
        mine = pl.ds(pl.multiple_of(i * QB, QB), QB)
        shifted = pl.ds((2 - reach) * QB, span)
        allowed = segk_ref[keys, :] == segq_ref[pl.ds(at, 1), :]
        allowed = jnp.concatenate([allowed, allowed], axis=1)
        for pair in range(pairs):
            lanes = slice(pair * 2 * DH, (pair + 1) * 2 * DH)
            both = two_heads(q_ref[0, mine, lanes] * LOW(0.125), first)
            grads = two_heads(g_ref[mine, lanes], first)
            scores = dot_nt(kp_ref[keys, lanes], both)
            if with_bias:
                scores = scores + t_ref[pair, shifted, :]
            scores = jnp.where(allowed, scores - lse_ref[0, pair, pl.ds(i, 1), :], -jnp.inf)
            probs = jnp.exp(scores)
            grad_probs = dot_nt(vp_ref[keys, lanes], grads)
            dv_acc[keys, lanes] += dot_nn(probs.astype(LOW), grads)
            inner = jnp.sum(probs * grad_probs, axis=0, keepdims=True)
            rounded = (probs * (grad_probs - inner)).astype(LOW)
            dk_acc[keys, lanes] += dot_nn(rounded, both)
            if with_bias:
                diag_ref[0, pair, shifted, :] += rounded.astype(F32)
            turned = dot_nn(kt_ref[lanes, keys], rounded)
            dq_ref[mine, lanes] = (joined_heads(turned) * 0.125).astype(LOW)

    visit_blocks(seg_ref, info[2], rows // QB, block)
    own = pl.ds(pl.multiple_of(info[2] * QB, QB), rows)
    dk_ref[...] = dk_acc[own, :].astype(LOW)
    dv_ref[...] = dv_acc[own, :].astype(LOW)
    if halo_count:
        far = pl.ds(pl.multiple_of(info[3] * QB, QB), halo_count)
        dh_ref[0] = dk_acc[far, :].astype(LOW)
        dh_ref[1] = dv_acc[far, :].astype(LOW)


def attend_back(info, segments, qkv, halo_kept, grad_context, bias, lse, previous):
    _, rows, width = qkv.shape
    width = width // 3
    span = min(HEAD_SPAN, width)
    groups = width // span
    pairs = span // (2 * DH)
    count = rows // QB
    blocks = segments.shape[0] // QB
    halo_count = 0 if halo_kept is None else halo_kept[0].shape[1]
    column, _ = head_specs(rows, span, groups, halo_count)
    plain = pl.BlockSpec((rows, span), lambda g, s, t: (0, g))
    in_specs = [
        pl.BlockSpec((blocks, QB), lambda g, s, t: (0, 0)),
        column(0),
        column(1),
        column(2),
        plain,
        pl.BlockSpec((1, pairs, count, 2 * QB), lambda g, s, t: (s[1], g, 0, 0)),
    ]
    inputs = [segments.reshape(blocks, QB), qkv, qkv, qkv, grad_context, lse]
    if bias is not None:
        in_specs.append(pl.BlockSpec((pairs,) + bias.shape[1:], lambda g, s, t: (g, 0, 0)))
        inputs.append(bias)
    plain_shape = jax.ShapeDtypeStruct((rows, width), LOW)
    outputs = [plain_shape] * 3
    out_specs = [plain] * 3
    if bias is not None:
        outputs.append(slotted(bias.shape, F32))
        out_specs.append(pl.BlockSpec((1, pairs) + bias.shape[1:], lambda g, s, t: (s[1], g, 0, 0)))
    if halo_count:
        kept = pl.BlockSpec((1, halo_count, span), lambda g, s, t: (s[1], 0, g))
        in_specs += [kept, kept]
        inputs += list(halo_kept)
        outputs.append(jax.ShapeDtypeStruct((2, halo_count, width), LOW))
        out_specs.append(pl.BlockSpec((2, halo_count, span), lambda g, s, t: (0, 0, lax.rem(g + groups // 2, groups))))
    keep = None if previous is None else [None] * 3 + [previous] + [None] * (len(outputs) - 4)
    return call_with_slots(
        functools.partial(attend_back_kernel, halo_count, bias is not None),
        [info, segments],
        inputs,
        in_specs,
        outputs,
        out_specs,
        keep,
        (groups,),
        [
            pltpu.VMEM((blocks * QB, QB), jnp.int32),
            pltpu.VMEM((blocks * QB, span), LOW),
            pltpu.VMEM((blocks * QB, span), LOW),
            pltpu.VMEM((span, blocks * QB), LOW),
            pltpu.VMEM((blocks * QB, span), F32),
            pltpu.VMEM((blocks * QB, span), F32),
        ],
        "attend_back",
        26,
    )


def exchange_kernel(give_ref, get_ref, send_sem, recv_sem):
    peer = {"tensor": 1 - lax.axis_index("tensor")}
    barrier = pltpu.get_barrier_semaphore()
    pl.semaphore_signal(barrier, inc=1, device_id=peer, device_id_type=pl.DeviceIdType.MESH)
    pl.semaphore_wait(barrier, 1)
    copy = pltpu.make_async_remote_copy(
        src_ref=give_ref, dst_ref=get_ref, send_sem=send_sem, recv_sem=recv_sem,
        device_id=peer, device_id_type=pl.DeviceIdType.MESH,
    )
    copy.start()
    copy.wait()


def exchanged(value):
    return pl.pallas_call(
        exchange_kernel,
        in_specs=[pl.BlockSpec(memory_space=pl.ANY)],
        out_specs=pl.BlockSpec(memory_space=pl.ANY),
        out_shape=jax.ShapeDtypeStruct(value.shape, value.dtype),
        scratch_shapes=[pltpu.SemaphoreType.DMA, pltpu.SemaphoreType.DMA],
        compiler_params=pltpu.CompilerParams(collective_id=1, has_side_effects=True),
        cost_estimate=cost_of(3),
        name="exchange",
    )(value)


def mean_of(block):
    return jnp.mean(block, axis=-1, keepdims=True)


def rms_scale(block):
    return lax.rsqrt(mean_of(block * block) + 1e-06)


def sum_rows(block):
    return jnp.sum(block, axis=0, keepdims=True)


def gelu_parts(u):
    bell = jnp.exp(u * u * -0.5)
    below = 0.5 + 0.5 * lax.erf(u * 0.7071067811865476)
    return u * below, below + u * (bell * 0.3989422804014327)


def enter_kernel(lead, info, given_ref, gain_ref, shift_ref, own_ref, oth_ref, x_ref, e_ref, qkv_ref, halo_ref):
    m = pl.program_id(0)
    half = own_ref.shape[1]

    @pl.when(m == 0)
    def _():
        x_ref[0] = given_ref[0]
        if lead:
            e_ref[0] = given_ref[0]
        else:
            x = given_ref[0].astype(F32)
            e_ref[0] = (x * rms_scale(x) * gain_ref[...]).astype(LOW)

    e = e_ref[0]
    for part, weight in enumerate((own_ref, oth_ref)):
        lanes = slice(part * half, (part + 1) * half)
        block = (dot_nn(e, weight[...]) + shift_ref[:, lanes]).astype(LOW)
        qkv_ref[0, :, lanes] = block
    start = pl.ds(pl.multiple_of(info[4], QB), halo_ref.shape[1])
    halo_ref[0, :, :half] = qkv_ref[0, start, half:]
    halo_ref[0, :, half:] = qkv_ref[0, start, :half]


def enter(lead, info, given, at, gain, shift, own, oth, previous):
    _, rows, width = given.shape
    half = own.shape[1] // 3
    whole = pl.BlockSpec((1, rows, width), lambda m, s: (at, 0, 0))
    weight = pl.BlockSpec((width, half), lambda m, s: (0, m))
    kept = pl.BlockSpec((1, rows, width), lambda m, s: (s[1], 0, 0))
    keep = None if previous is None else list(previous) + [None]
    return call_with_slots(
        functools.partial(enter_kernel, lead),
        [info],
        [given, gain, shift, own, oth],
        [
            whole,
            pl.BlockSpec((1, width), lambda m, s: (0, 0)),
            pl.BlockSpec((1, 2 * half), lambda m, s: (0, m)),
            weight,
            weight,
        ],
        [
            slotted((rows, width), LOW),
            slotted((rows, width), LOW),
            slotted((rows, 6 * half), LOW),
            jax.ShapeDtypeStruct((2, REACH, 2 * half), LOW),
        ],
        [
            kept,
            kept,
            pl.BlockSpec((1, rows, 2 * half), lambda m, s: (s[1], 0, m)),
            pl.BlockSpec((1, REACH, 2 * half), lambda m, s: (jnp.maximum(m - 1, 0), 0, 0)),
        ],
        keep,
        (3,),
        [],
        "enter",
        9,
    )


def weight_stream(up, down, up_ref, down_ref, sem, steps):
    chunk = up_ref.shape[2]

    def copies(part, c, slot):
        at = pl.ds(pl.multiple_of(c * chunk, chunk), chunk)
        return [
            pltpu.make_async_copy(up[part].at[:, at], up_ref.at[slot], sem.at[slot, 0]),
            pltpu.make_async_copy(down[part].at[at, :], down_ref.at[slot], sem.at[slot, 1]),
        ]

    def start(j):
        slot = lax.rem(j, 2)
        for part in range(2):

            @pl.when((j >= part * (steps // 2)) & (j < (part + 1) * (steps // 2)))
            def _(part=part):
                for copy in copies(part, j - part * (steps // 2), slot):
                    copy.start()

    def wait(j):
        for copy in copies(0, 0, lax.rem(j, 2)):
            copy.wait()

    return start, wait


def feed_kernel(
    lead, info, x_ref, c_ref, wo_own, wo_oth, up_own, up_oth, down_own, down_oth, bias_ref, gain_ref, shift_ref,
    f_ref, slope_ref, n_ref, one_ref, two_ref, out_ref, acc_ref, carry_ref, up_ref, down_ref, sem
):
    j = pl.program_id(0)
    steps = 2 * up_own.shape[1] // up_ref.shape[2]
    half = wo_own.shape[0]
    rows = x_ref.shape[1]

    start, wait = weight_stream((up_own, up_oth), (down_own, down_oth), up_ref, down_ref, sem, steps)

    @pl.when(j == 0)
    def _():
        start(j)
        start(j + 1)
        joined = (
            dot_nn(c_ref[0, :, :half], wo_own[...])
            + dot_nn(c_ref[0, :, half:], wo_oth[...])
            + x_ref[0].astype(F32)
        )

        @when(lead)
        def _():
            before = joined + shift_ref[0:1, :]
            one_ref[0] = before.astype(LOW)
            center = before - mean_of(before)
            normed = center * lax.rsqrt(mean_of(center * center) + 1e-05) * gain_ref[0:1, :] + shift_ref[2:3, :]
            carry_ref[...] = normed
            n_ref[0] = normed.astype(LOW)

        @when(not lead)
        def _():
            one_ref[0] = joined.astype(LOW)
            carry_ref[...] = joined
            n_ref[0] = (joined * rms_scale(joined) * gain_ref[1:2, :]).astype(LOW)

        acc_ref[...] = jnp.zeros_like(acc_ref)

    wait(j)

    @pl.when((j > 0) & (j + 1 < steps))
    def _():
        start(j + 1)

    slot = lax.rem(j, 2)
    u = dot_nn(n_ref[0], up_ref[slot]) + bias_ref[...]
    f, slope = gelu_parts(u)
    f_ref[0] = f.astype(LOW)
    slope_ref[0] = slope.astype(LOW)
    acc_ref[...] += dot_nn(f_ref[0], down_ref[slot])

    @pl.when(j == steps - 1)
    def _():
        joined = carry_ref[...] + acc_ref[...]

        @when(lead)
        def _():
            before = joined + shift_ref[1:2, :]
            two_ref[0] = before.astype(LOW)
            center = before - mean_of(before)
            normed = center * lax.rsqrt(mean_of(center * center) + 1e-05) * gain_ref[1:2, :] + shift_ref[3:4, :]
            out_ref[...] = normed.astype(LOW)

        @when(not lead)
        def _():
            two_ref[0] = joined.astype(LOW)
            out_ref[...] = joined.astype(LOW)


def feed(lead, info, x, context, wo, up, down, bias, gains, shifts, previous):
    _, rows, width = x.shape
    hidden = up[0].shape[1]
    chunk = min(FEED_CHUNK, hidden)
    steps = 2 * hidden // chunk
    anywhere = pl.BlockSpec(memory_space=pl.ANY)
    kept = pl.BlockSpec((1, rows, width), lambda j, s: (s[1], 0, 0))
    fixed = lambda a: pl.BlockSpec(a.shape, lambda j, s: (0, 0))
    moving = pl.BlockSpec((1, rows, chunk), lambda j, s: (s[1], 0, j))
    keep = None if previous is None else list(previous) + [None]
    return call_with_slots(
        functools.partial(feed_kernel, lead),
        [info],
        [x, context, wo[0], wo[1], up[0], up[1], down[0], down[1], bias, gains, shifts],
        [
            kept,
            kept,
            fixed(wo[0]),
            fixed(wo[1]),
            anywhere,
            anywhere,
            anywhere,
            anywhere,
            pl.BlockSpec((1, chunk), lambda j, s: (0, j)),
            fixed(gains),
            fixed(shifts),
        ],
        [
            slotted((rows, 2 * hidden), LOW),
            slotted((rows, 2 * hidden), LOW),
            slotted((rows, width), LOW),
            slotted((rows, width), LOW),
            slotted((rows, width), LOW),
            jax.ShapeDtypeStruct((rows, width), LOW),
        ],
        [moving, moving, kept, kept, kept, pl.BlockSpec((rows, width), lambda j, s: (0, 0))],
        keep,
        (steps,),
        [
            pltpu.VMEM((rows, width), F32),
            pltpu.VMEM((rows, width), F32),
            pltpu.VMEM((2, width, chunk), LOW),
            pltpu.VMEM((2, chunk, width), LOW),
            pltpu.SemaphoreType.DMA((2, 2)),
        ],
        "feed",
        29,
    )


def layer_norm_back(before, grad, gain_row):
    center = before - mean_of(before)
    scale = lax.rsqrt(mean_of(center * center) + 1e-05)
    unit = center * scale
    inner = grad * gain_row
    back = scale * (inner - mean_of(inner) - unit * mean_of(inner * unit))
    return back, sum_rows(grad * unit)


def rms_norm_back(before, grad, gain_row):
    scale = rms_scale(before)
    unit = before * scale
    inner = grad * gain_row
    back = scale * (inner - unit * mean_of(inner * unit))
    return back, sum_rows(grad * unit)


def feed_back_kernel(
    lead, info, *refs
):
    refs = list(refs)
    got_refs = [refs.pop(0) for _ in range(2 - lead)]
    feed_back_steps(lead, got_refs, *refs)


def feed_back_steps(
    lead, got_refs, one_ref, two_ref, slope_ref, wo_own, wo_oth, up_own, up_oth, down_own, down_oth,
    gain_ref, dy_ref, du_ref, db_ref, stat_ref, bias_ref, dz_ref, dc_ref, acc_ref, carry_ref, up_ref, down_ref, wo_ref, sem, wo_sem
):
    j = pl.program_id(0)
    steps = 2 * up_own.shape[1] // up_ref.shape[2]
    start, wait = weight_stream((up_own, up_oth), (down_own, down_oth), up_ref, down_ref, sem, steps)
    wo_copies = [
        pltpu.make_async_copy(source, wo_ref.at[part], wo_sem.at[part]) for part, source in enumerate((wo_own, wo_oth))
    ]
    half = wo_own.shape[0]
    rows = dy_ref.shape[1]

    @pl.when(j == 0)
    def _():
        start(j)
        start(j + 1)
        for copy in wo_copies:
            copy.start()
        stat_ref[...] = jnp.zeros_like(stat_ref)
        acc_ref[...] = jnp.zeros_like(acc_ref)

        @when(lead)
        def _():
            grad = got_refs[0][0].astype(F32)
            back, gain = layer_norm_back(two_ref[0].astype(F32), grad, gain_ref[1:2, :])
            stat_ref[0, 1:2, :] = gain
            stat_ref[0, 5:6, :] = sum_rows(grad)
            stat_ref[0, 3:4, :] = sum_rows(back)
            carry_ref[...] = back
            dy_ref[0] = back.astype(LOW)

        @when(not lead)
        def _():
            grad = got_refs[0][0].astype(F32) + got_refs[1][0].astype(F32)
            carry_ref[...] = grad
            dy_ref[0] = grad.astype(LOW)

    wait(j)

    @pl.when((j > 0) & (j + 1 < steps))
    def _():
        start(j + 1)

    slot = lax.rem(j, 2)
    grad = dot_nt(dy_ref[0], down_ref[slot])
    du_ref[0] = (grad * slope_ref[0].astype(F32)).astype(LOW)
    acc_ref[...] += dot_nt(du_ref[0], up_ref[slot])
    bias_ref[0] = sum_rows(du_ref[0].astype(F32))

    @pl.when(j == steps - 1)
    def _():
        @when(lead)
        def _():
            grad = acc_ref[...] + carry_ref[...]
            back, gain = layer_norm_back(one_ref[0].astype(F32), grad, gain_ref[0:1, :])
            stat_ref[0, 0:1, :] = gain
            stat_ref[0, 4:5, :] = sum_rows(grad)
            stat_ref[0, 2:3, :] = sum_rows(back)
            dz_ref[...] = back

        @when(not lead)
        def _():
            back, gain = rms_norm_back(one_ref[0].astype(F32), acc_ref[...], gain_ref[1:2, :])
            stat_ref[0, 1:2, :] = gain
            dz_ref[...] = carry_ref[...] + back

        for copy in wo_copies:
            copy.wait()
        low = dz_ref[...].astype(LOW)
        db_ref[0] = low
        dc_ref[:, :half] = dot_nt(low, wo_ref[0]).astype(LOW)
        dc_ref[:, half:] = dot_nt(low, wo_ref[1]).astype(LOW)


def feed_back(lead, info, got, at, one, two, slope, wo, up, down, gains, previous):
    _, rows, width = one.shape
    hidden = up[0].shape[1]
    chunk = min(FEED_CHUNK, hidden)
    steps = 2 * hidden // chunk
    anywhere = pl.BlockSpec(memory_space=pl.ANY)
    kept = pl.BlockSpec((1, rows, width), lambda j, s: (s[1], 0, 0))
    fixed = lambda a: pl.BlockSpec(a.shape, lambda j, s: (0, 0))
    plain = pl.BlockSpec((rows, width), lambda j, s: (0, 0))
    moving = pl.BlockSpec((1, rows, chunk), lambda j, s: (s[1], 0, j))
    keep = None if previous is None else list(previous) + [None, None]
    return call_with_slots(
        functools.partial(feed_back_kernel, lead),
        [info],
        [*got, one, two, slope, wo[0], wo[1], up[0], up[1], down[0], down[1], gains],
        [pl.BlockSpec((1, rows, width), lambda j, s: (at, 0, 0))] * len(got)
        + [
            kept,
            kept,
            moving,
            anywhere,
            anywhere,
            anywhere,
            anywhere,
            anywhere,
            anywhere,
            fixed(gains),
        ],
        [
            slotted((rows, width), LOW),
            slotted((rows, 2 * hidden), LOW),
            slotted((rows, width), LOW),
            slotted((8, width), F32),
            slotted((1, 2 * hidden), F32),
            jax.ShapeDtypeStruct((rows, width), F32),
            jax.ShapeDtypeStruct((rows, width), LOW),
        ],
        [
            kept,
            moving,
            kept,
            pl.BlockSpec((1, 8, width), lambda j, s: (s[1], 0, 0)),
            pl.BlockSpec((1, 1, chunk), lambda j, s: (s[1], 0, j)),
            plain,
            plain,
        ],
        keep,
        (steps,),
        [
            pltpu.VMEM((rows, width), F32),
            pltpu.VMEM((rows, width), F32),
            pltpu.VMEM((2, width, chunk), LOW),
            pltpu.VMEM((2, chunk, width), LOW),
            pltpu.VMEM((2,) + wo[0].shape, LOW),
            pltpu.SemaphoreType.DMA((2, 2)),
            pltpu.SemaphoreType.DMA((2,)),
        ],
        "feed_back",
        27,
    )


def enter_back_kernel(
    lead, info, dq_ref, dk_ref, dv_ref, far_ref, x_ref, dz_ref, own_ref, oth_ref, gain_ref,
    d_ref, stat_ref, lower_ref, upper_ref, low_ref, acc_ref
):
    m = pl.program_id(0)
    half = own_ref.shape[1]
    start = pl.ds(pl.multiple_of(info[4], QB), far_ref.shape[1])

    @pl.when(m == 0)
    def _():
        stat_ref[...] = jnp.zeros_like(stat_ref)
        acc_ref[...] = jnp.zeros_like(acc_ref)
        d_ref[0] = dq_ref[...]
        stat_ref[0, 0:1, :] = sum_rows(dq_ref[...].astype(F32))

    def with_far(block_ref, part):
        d_ref[0] = block_ref[...]
        d_ref[0, start, :] = (block_ref[start, :].astype(F32) + far_ref[part].astype(F32)).astype(LOW)

    @pl.when(m == 1)
    def _():
        with_far(dk_ref, 0)

    @pl.when(m == 2)
    def _():
        with_far(dv_ref, 1)
        stat_ref[0, 1:2, :] = sum_rows(d_ref[0].astype(F32))

    acc_ref[...] += dot_nt(d_ref[0, :, :half], own_ref[...]) + dot_nt(d_ref[0, :, half:], oth_ref[...])

    @pl.when(m == 2)
    def _():
        split = lower_ref.shape[2]

        @when(lead)
        def _():
            total = dz_ref[...] + acc_ref[...]
            low_ref[...] = total.astype(LOW)
            lower_ref[0] = total[:, :split]
            upper_ref[0] = total[:, split:].astype(LOW)

        @when(not lead)
        def _():
            back, gain = rms_norm_back(x_ref[0].astype(F32), acc_ref[...], gain_ref[...])
            stat_ref[0, 2:3, :] = gain
            total = dz_ref[...] + back
            low_ref[...] = total.astype(LOW)
            lower_ref[0] = total[:, :split]
            upper_ref[0] = total[:, split:].astype(LOW)


def enter_back(lead, info, dq, dk, dv, far, x, dz, own, oth, gain, previous):
    _, rows, width = x.shape
    half = own.shape[1] // 3
    plain = pl.BlockSpec((rows, width), lambda m, s: (0, 0))
    kept = pl.BlockSpec((1, rows, width), lambda m, s: (s[1], 0, 0))
    weight = pl.BlockSpec((width, half), lambda m, s: (0, m))
    keep = None if previous is None else list(previous) + [None]
    return call_with_slots(
        functools.partial(enter_back_kernel, lead),
        [info],
        [dq, dk, dv, far, x, dz, own, oth, gain],
        [
            plain,
            plain,
            plain,
            pl.BlockSpec(far.shape, lambda m, s: (0, 0, 0)),
            kept,
            plain,
            weight,
            weight,
            pl.BlockSpec((1, width), lambda m, s: (0, 0)),
        ],
        [
            slotted((rows, 6 * half), LOW),
            slotted((8, width), F32),
            slotted((rows, width // 2), F32),
            slotted((rows, width // 2), LOW),
            jax.ShapeDtypeStruct((rows, width), LOW),
        ],
        [
            pl.BlockSpec((1, rows, 2 * half), lambda m, s: (s[1], 0, m)),
            pl.BlockSpec((1, 8, width), lambda m, s: (s[1], 0, 0)),
            pl.BlockSpec((1, rows, width // 2), lambda m, s: (s[1], 0, 0)),
            pl.BlockSpec((1, rows, width // 2), lambda m, s: (s[1], 0, 0)),
            plain,
        ],
        keep,
        (3,),
        [pltpu.VMEM((rows, width), F32)],
        "enter_back",
        12,
    )


def passed_along(value, axis, steps):
    count = lax.axis_size(axis)
    initial, last = (max(0, -steps), min(count, count - steps))
    return lax.ppermute(value, axis, [(source, source + steps) for source in range(initial, last)])


def spread(block, axis, source):
    block = jnp.where(lax.axis_index(axis) == source, block, jnp.zeros_like(block))
    return lax.psum(block, axis)


def layer_norm(operand, gain_row, shift_row):
    center = operand - jnp.mean(operand, axis=-1, keepdims=True)
    variance = jnp.mean(center * center, axis=-1, keepdims=True)
    return center * lax.rsqrt(variance + 1e-05) * gain_row + shift_row


def rms_norm(operand, gain_row):
    return (
        operand * lax.rsqrt(jnp.mean(operand * operand, axis=-1, keepdims=True) + 1e-06) * gain_row
    )


def gelu_act(operand):
    return jax.nn.gelu(operand, approximate=False)


def gelu_slope(operand):
    return (
        0.5 * (1.0 + jax.scipy.special.erf(operand * 0.7071067811865476))
        + operand * jnp.exp(-0.5 * operand * operand) * 0.3989422804014327
    )


def entry_norm(residual, gain_rows, leading):
    return jnp.where(leading, residual, rms_norm(residual, gain_rows[0]))


def middle(residual, branch, gain_rows, shift_rows, leading):
    joined = residual + branch
    bert_rows = layer_norm(joined + shift_rows[0], gain_rows[0], shift_rows[2])
    carried = jnp.where(leading, bert_rows, joined)
    normed = jnp.where(leading, bert_rows, rms_norm(joined, gain_rows[1]))
    return (carried, normed)


def final(carried, second, gain_rows, shift_rows, leading):
    joined = carried + second
    return jnp.where(
        leading, layer_norm(joined + shift_rows[1], gain_rows[1], shift_rows[3]), joined
    )


def contract_rows(left, right):
    return lax.dot_general(
        left, right, (((0,), (0,)), ((), ())), preferred_element_type=jnp.float32
    )


def contract_cols(left, right):
    return lax.dot_general(
        left, right, (((1,), (1,)), ((), ())), preferred_element_type=jnp.float32
    )


def gather_rows(operand, weight):
    return (
        jnp.dot(
            lax.all_gather(operand, "tensor", axis=0, tiled=True),
            weight,
            preferred_element_type=jnp.float32,
        ),
        None,
    )


def collect(full_rows, weight):
    return lax.psum_scatter(
        jnp.dot(full_rows, weight, preferred_element_type=jnp.float32),
        "tensor",
        scatter_dimension=0,
        tiled=True,
    )


def scatter_back(grad_rows, weight):
    return lax.psum_scatter(
        contract_cols(grad_rows, weight).astype(jnp.bfloat16),
        "tensor",
        scatter_dimension=0,
        tiled=True,
    ).astype(jnp.float32)


def fold_back(grad_share, weight, activations):
    fragment = lax.all_gather(grad_share, "tensor", axis=0, tiled=True)
    product_rows = contract_cols(fragment, weight)
    return (product_rows, contract_rows(activations, fragment))


def weight_grad(operand, grad_rows):
    return contract_rows(lax.all_gather(operand, "tensor", axis=0, tiled=True), grad_rows)


DH = 64
QB = 128
NARROW = 3
WIDE = 5
VMEM = 56 * 1024 * 1024


def padded(segments):
    return jnp.pad(segments, (PAD * QB, PAD * QB), constant_values=-1)


def general_body(
    layer_input,
    segment_ids,
    buckets,
    attn_in,
    attn_out,
    ffn_in,
    ffn_out,
    norm_gain,
    bert_shift,
    head_bias,
    ffn_bias,
    position_bias,
    decoder_grads,
):
    micro_count = layer_input.shape[0]
    shard_rows = layer_input.shape[2]
    model_width = layer_input.shape[3]
    length = segment_ids.shape[2]
    leading = lax.axis_index("section") == 0
    weighting = jnp.where(leading, 1.0, 0.0)
    qkv_weight = attn_in[0].reshape(model_width, -1)
    out_weight = attn_out[0]
    ffn_up = ffn_in[0]
    ffn_down = ffn_out[0]
    gain_rows = jnp.where(leading, norm_gain[0], norm_gain[1])
    head_shift = head_bias * weighting
    qkv_shift = jnp.concatenate([head_shift[0], jnp.zeros_like(head_shift[0]), head_shift[1]])
    ffn_shift = ffn_bias * weighting
    bias_table = position_bias * (1.0 - weighting)
    bucket_hits = (buckets[None, :] == jnp.arange(bias_table.shape[1])[:, None]).astype(jnp.float32)
    offset_bias = jnp.dot(bias_table, bucket_hits, precision=lax.Precision.HIGHEST)
    near = length - 1 - 3 * QB
    bias = toeplitz(jnp.ones((1,), jnp.int32), offset_bias[:, near : near + 6 * QB])
    info = jnp.array([0, 0, PAD, 0, 0, 1], jnp.int32)
    segment_rows = segment_ids[:, 0]

    def middle_part(residual_in, branch_in, gain_in, shift_in):
        return middle(residual_in, branch_in, gain_in, shift_in, leading)

    def final_part(carried_in, second_in, gain_in, shift_in):
        return final(carried_in, second_in, gain_in, shift_in, leading)

    def entry_part(residual_in, gain_in):
        return entry_norm(residual_in, gain_in, leading)

    received = jnp.zeros((shard_rows, model_width), jnp.bfloat16)
    saved_steps = []
    encoded = []
    for moment in range(micro_count + 1):
        own_rows = layer_input[min(moment, micro_count - 1), 0]
        if moment >= micro_count:
            own_rows = jnp.zeros_like(own_rows)
        segment_row = jnp.where(
            leading, segment_rows[min(moment, micro_count - 1)], segment_rows[max(moment - 1, 0)]
        )
        forward_incoming = jnp.where(leading, own_rows, received)
        forward_residual = forward_incoming.astype(jnp.float32)
        forward_entered = entry_norm(forward_residual, gain_rows, leading).astype(jnp.bfloat16)
        projected, forward_gathered_in = gather_rows(forward_entered, qkv_weight)
        forward_qkv = (projected + qkv_shift).astype(jnp.bfloat16)
        forward_context, forward_log_totals = attend(
            info, padded(segment_row), forward_qkv[None], None, bias, None
        )
        forward_context = forward_context[0]
        forward_branch = collect(forward_context, out_weight)
        forward_carried, forward_normed = middle(
            forward_residual, forward_branch, gain_rows, bert_shift, leading
        )
        pre_full, forward_gathered_mid = gather_rows(forward_normed.astype(jnp.bfloat16), ffn_up)
        forward_pre_act = pre_full + ffn_shift
        forward_second = collect(gelu_act(forward_pre_act).astype(jnp.bfloat16), ffn_down)
        result = final(forward_carried, forward_second, gain_rows, bert_shift, leading).astype(
            jnp.bfloat16
        )
        result, saved = (
            result,
            (
                forward_incoming,
                segment_row,
                forward_branch,
                forward_second,
                forward_qkv,
                forward_context,
                forward_log_totals,
                forward_pre_act,
                forward_gathered_in,
                forward_gathered_mid,
            ),
        )
        saved_steps.append(saved)
        if moment >= 1:
            encoded.append(result)
        if moment < micro_count:
            received = passed_along(result, "section", 1)
    delivered = spread(jnp.stack(encoded), "section", 1)
    section_grads = lax.psum(
        decoder_grads[0, :, 0].astype(jnp.float32).astype(jnp.bfloat16), "section"
    ).astype(jnp.float32)
    grad_received = jnp.zeros((shard_rows, model_width), jnp.float32)
    running_terms = None
    input_rows = []
    for moment in range(micro_count + 1):
        own_grad = section_grads[min(moment, micro_count - 1)]
        if moment >= micro_count:
            own_grad = jnp.zeros_like(own_grad)
        earlier = saved_steps[max(moment - 1, 0)]
        later = saved_steps[min(moment + 1, micro_count)]
        chosen = jax.tree.map(
            lambda from_first, from_second: jnp.where(leading, from_first, from_second),
            earlier,
            later,
        )
        (
            incoming,
            backward_segment_row,
            branch,
            second,
            qkv,
            context,
            log_totals,
            pre_act,
            gathered_in,
            gathered_mid,
        ) = chosen
        residual = incoming.astype(jnp.float32)
        (carried, normed), pull_middle = jax.vjp(
            middle_part, residual, branch, gain_rows, bert_shift
        )
        finished, pull_final = jax.vjp(final_part, carried, second, gain_rows, bert_shift)
        grad_carried, grad_second, gain_end, shift_end = pull_final(
            jnp.where(leading, grad_received, own_grad)
        )
        hidden = gelu_act(pre_act).astype(jnp.bfloat16)
        grad_hidden, backward_grad_down = fold_back(
            grad_second.astype(jnp.bfloat16), ffn_down, hidden
        )
        grad_pre = (grad_hidden * gelu_slope(pre_act)).astype(jnp.bfloat16)
        grad_shift = jnp.sum(grad_pre.astype(jnp.float32), axis=0) * weighting
        backward_grad_up = weight_grad(normed.astype(jnp.bfloat16), grad_pre)
        grad_normed = scatter_back(grad_pre, ffn_up)
        grad_residual, grad_branch, gain_mid, shift_mid = pull_middle((grad_carried, grad_normed))
        grad_context, backward_grad_out_weight = fold_back(
            grad_branch.astype(jnp.bfloat16), out_weight, context
        )
        low_q, low_k, low_v, grad_table = attend_back(
            info, padded(backward_segment_row), qkv[None], None, grad_context.astype(jnp.bfloat16), bias, log_totals, None
        )
        grad_table = grad_table[0]
        grad_head = (
            jnp.stack([jnp.sum(low.astype(jnp.float32), axis=0) for low in (low_q, low_v)]) * weighting
        )
        grad_rows = jnp.concatenate([low_q, low_k, low_v], axis=1)
        entered, pull_entry = jax.vjp(entry_part, residual, gain_rows)
        backward_grad_qkv = weight_grad(entered.astype(jnp.bfloat16), grad_rows)
        grad_entered = scatter_back(grad_rows, qkv_weight)
        grad_from_entry, gain_entry = pull_entry(grad_entered)
        grad_terms = (
            backward_grad_qkv,
            backward_grad_out_weight,
            backward_grad_up,
            backward_grad_down,
            gain_end + gain_mid + gain_entry,
            shift_end + shift_mid,
            grad_head,
            grad_shift,
            grad_table,
        )
        grad_input, grad_terms = (grad_residual + grad_from_entry, grad_terms)
        if running_terms is None:
            running_terms = grad_terms
        else:
            running_terms = jax.tree.map(jnp.add, running_terms, grad_terms)
        if moment >= 1:
            input_rows.append(grad_input)
        if moment < micro_count:
            grad_received = passed_along(grad_input.astype(jnp.bfloat16), "section", -1).astype(
                grad_input.dtype
            )
    input_all = jnp.stack(input_rows)
    half_width = model_width // 2
    upper_half = passed_along(
        input_all[:, :, half_width:].astype(jnp.bfloat16), "section", 1
    ).astype(jnp.float32)
    input_grad = jnp.where(leading, input_all[:, :, :half_width], upper_half)[:, None]
    (
        grad_qkv,
        grad_out_weight,
        grad_up,
        grad_down,
        gain_sum,
        shift_sum,
        head_sum,
        shift_ffn_sum,
        table_sum,
    ) = running_terms
    near_hits = bucket_hits[:, near : near + 6 * QB]
    table_sum = jnp.dot(diagonals(jnp.ones((1,), jnp.int32), table_sum[None], 1), near_hits.T, precision=lax.Precision.HIGHEST) * (
        1.0 - weighting
    )
    weights_out = (
        lax.psum_scatter(
            grad_qkv.reshape(1, model_width, 3, -1).astype(jnp.bfloat16),
            "dp",
            scatter_dimension=1,
            tiled=True,
        ).astype(jnp.float32),
        lax.psum_scatter(
            grad_out_weight[None].astype(jnp.bfloat16), "dp", scatter_dimension=2, tiled=True
        ).astype(jnp.float32),
        lax.psum_scatter(
            grad_up[None].astype(jnp.bfloat16), "dp", scatter_dimension=1, tiled=True
        ).astype(jnp.float32),
        lax.psum_scatter(
            grad_down[None].astype(jnp.bfloat16), "dp", scatter_dimension=2, tiled=True
        ).astype(jnp.float32),
    )
    gain_both = jnp.stack([gain_sum * weighting, gain_sum * (1.0 - weighting)])
    shared_out = lax.psum((gain_both, shift_sum), ("dp", "section", "tensor"))
    split_out = lax.psum((head_sum, shift_ffn_sum, table_sum), ("dp", "section"))
    return (
        delivered[None, :, None],
        input_grad,
        weights_out[0],
        weights_out[1],
        weights_out[2],
        weights_out[3],
        shared_out[0],
        shared_out[1],
        split_out[0],
        split_out[1],
        split_out[2],
    )


def grads_kernel(
    f_hbm, dy_hbm, c_hbm, db_hbm, n_hbm, du_hbm, e_hbm, dqkv_hbm, upper_hbm, packed_ref,
    down_ref, up_ref, row_ref, qkv_ref, summed_ref, upper_got,
    still, moving, turned, given, held, near_ref, y_ref, low_ref, high_ref, small_ref, small_got,
    still_sem, moving_sem, near_send, near_recv, y_send, y_recv, low_send, low_recv, high_send, high_recv,
    small_send, small_recv, upper_send, upper_recv
):
    dp = lax.axis_index("dp")
    core = lax.axis_index("tensor")
    section = lax.axis_index("section")
    y_side = lax.rem(dp, 2)
    low_side = lax.rem(dp // 2, 2)
    high_side = dp // 4

    def across(bit, side):
        return {"dp": dp + bit * (1 - 2 * side)}

    core_peer = {"tensor": 1 - core}
    y_peer = across(1, y_side)
    low_peer = across(2, low_side)
    high_peer = across(4, high_side)
    peers = [core_peer, y_peer, low_peer, high_peer, {"section": 1 - section}]
    mesh_id = pl.DeviceIdType.MESH
    total = held.shape[0]
    chunk = moving.shape[4]
    each = du_hbm.shape[2] // 2 // chunk

    barrier = pltpu.get_barrier_semaphore()
    for peer in peers:
        pl.semaphore_signal(barrier, inc=1, device_id=peer, device_id_type=mesh_id)
    pl.semaphore_wait(barrier, len(peers))

    def send(source, target, out_sem, in_sem, peer):
        return pltpu.make_async_remote_copy(
            src_ref=source, dst_ref=target, send_sem=out_sem, recv_sem=in_sem,
            device_id=peer, device_id_type=mesh_id,
        )

    def near_copy(k, slot):
        return send(given.at[slot], near_ref.at[k], near_send.at[slot], near_recv.at[k], core_peer)

    def y_copy(k):
        return send(held.at[k, :, :, 1 - y_side], y_ref.at[k], y_send.at[k], y_recv.at[k], y_peer)

    def low_copy(k):
        return send(y_ref.at[k, :, 1 - low_side], low_ref.at[k], low_send.at[k], low_recv.at[k], low_peer)

    def high_copy(k):
        return send(low_ref.at[k, 1 - high_side], high_ref.at[k], high_send.at[k], high_recv.at[k], high_peer)

    def small_copy(s):
        return send(small_ref.at[s], small_got.at[s], small_send.at[s], small_recv.at[s], peers[s])

    def added(a, b):
        return (a.astype(F32) + b.astype(F32)).astype(LOW)

    def near_stage(k):
        near_copy(k, 0).wait_recv()
        for hi in range(2):
            for lo in range(2):
                for side in range(2):
                    held[k, hi, lo, side] = added(held[k, hi, lo, side], near_ref[k, hi, lo, side])
        y_copy(k).start()

    def y_stage(k):
        y_copy(k).wait_recv()
        for hi in range(2):
            for lo in range(2):
                y_ref[k, hi, lo] = added(y_ref[k, hi, lo], held[k, hi, lo, y_side])
        low_copy(k).start()

    def low_stage(k):
        low_copy(k).wait_recv()
        for hi in range(2):
            low_ref[k, hi] = added(low_ref[k, hi], y_ref[k, hi, low_side])
        high_copy(k).start()

    def high_stage(k):
        high_copy(k).wait_recv()
        value = high_ref[k].astype(F32) + low_ref[k, high_side].astype(F32)

        def cut(ref, first):
            for q in range(chunk // QB):
                ref[pl.ds(first + q * QB, QB), :] = value[:, q * QB : (q + 1) * QB]

        def lay(ref, at):
            ref[:, pl.ds(pl.multiple_of(at * chunk, chunk), chunk)] = value

        pl.when(k < each)(lambda: cut(down_ref, pl.multiple_of(k * chunk, chunk)))
        pl.when((k >= each) & (k < 2 * each))(lambda: lay(up_ref, k - each))
        pl.when(k == 2 * each)(lambda: cut(row_ref, 0))
        pl.when(k > 2 * each)(lambda: lay(qkv_ref, k - 2 * each - 1))

    def small_stage(s):
        small_copy(s).wait_recv()
        small_ref[s + 1] = small_ref[s] + small_got[s]
        if s + 1 < len(peers):
            small_copy(s + 1).start()

    phases = [
        (False, dy_hbm, f_hbm, each, lambda c: c * chunk, lambda c: (each + c) * chunk),
        (True, n_hbm, du_hbm, each, lambda c: c * chunk, lambda c: (each + c) * chunk),
        (False, db_hbm, c_hbm, 1, lambda c: 0 * c, lambda c: 0 * c + chunk),
        (True, e_hbm, dqkv_hbm, 3, lambda c: 2 * c * chunk, lambda c: (2 * c + 1) * chunk),
    ]

    def still_copy(p):
        return pltpu.make_async_copy(phases[p][1].at[0:2], still.at[p % 2], still_sem.at[p % 2])

    def moving_copies(p, c, slot):
        _, _, source, _, own_at, oth_at = phases[p]
        return [
            pltpu.make_async_copy(
                source.at[0:2, :, pl.ds(pl.multiple_of(at(c), chunk), chunk)],
                moving.at[slot, part],
                moving_sem.at[slot, part],
            )
            for part, at in enumerate((own_at, oth_at))
        ]

    still_copy(0).start()
    for copy in moving_copies(0, 0, 0):
        copy.start()
    still_copy(1).start()
    upper_copy = send(upper_hbm.at[0:2], upper_got, upper_send, upper_recv, peers[4])
    upper_copy.start()
    small_ref[0] = packed_ref[...]
    small_copy(0).start()

    tokens = 2 * still.shape[2]
    base = 0
    for p, (wide, _, _, count, _, _) in enumerate(phases):
        still_copy(p).wait()
        stay = still.at[p % 2]
        if wide:
            for micro in range(2):
                turned[:, micro * tokens // 2 : (micro + 1) * tokens // 2] = stay[micro].T

        @pl.loop(0, count)
        def _(c, p=p, wide=wide, count=count, base=base, stay=stay):
            k = base + c
            slot = lax.rem(k, 2)
            for copy in moving_copies(p, c, slot):
                copy.wait()

            @pl.when(c + 1 < count)
            def _():
                for copy in moving_copies(p, c + 1, 1 - slot):
                    copy.start()

            if p + 1 < len(phases):

                @pl.when(c + 1 == count)
                def _():
                    for copy in moving_copies(p + 1, 0, 1 - slot):
                        copy.start()

            @pl.when(k >= 2)
            def _():
                near_copy(k, slot).wait_send()

            def product(part, store):
                block = moving[slot, part].reshape(tokens, chunk)
                if wide:
                    result = dot_nn(turned[...], block).astype(LOW)
                    for z in range(4):
                        for side in range(2):
                            at = (2 * z + side) * QB
                            store(z, side, slice(None), result[at : at + QB, :])
                else:
                    result = dot_nn(block.T, stay[...].reshape(tokens, -1)).astype(LOW)
                    for z in range(4):
                        for side in range(2):
                            at = (2 * z + side) * QB
                            for q in range(chunk // QB):
                                lanes = slice(q * QB, (q + 1) * QB)
                                store(z, side, lanes, result[lanes, at : at + QB])

            def to_given(z, side, lanes, value):
                given[slot, z // 2, z % 2, side, :, lanes] = value

            def to_held(z, side, lanes, value):
                held[k, z // 2, z % 2, side, :, lanes] = value

            product(1, to_given)
            near_copy(k, slot).start()
            product(0, to_held)

            @pl.when(k >= 1)
            def _():
                near_stage(k - 1)

            for s in range(len(peers)):

                @pl.when(k == 2 * s + 1)
                def _(s=s):
                    small_stage(s)

            @pl.when((k >= 5) & (lax.rem(k, 3) == 2))
            def _():
                y_stage((k - 5) // 3)

        if p + 2 < len(phases):
            still_copy(p + 2).start()
        base += count

    near_stage(total - 1)
    early = (total - 1 - 5) // 3 + 1
    @pl.loop(0, early)
    def _(k):
        low_stage(k)

    @pl.loop(0, early - 1)
    def _(k):
        high_stage(k)

    @pl.loop(early, total)
    def _(k):
        y_stage(k)
        high_stage(k - 1)
        low_stage(k)

    @pl.loop(total - 1, total)
    def _(k):
        high_stage(k)

    summed_ref[...] = small_ref[len(peers)]
    near_copy(total - 2, (total - 2) % 2).wait_send()
    near_copy(total - 1, (total - 1) % 2).wait_send()

    @pl.loop(0, total)
    def _(k):
        y_copy(k).wait_send()
        low_copy(k).wait_send()
        high_copy(k).wait_send()

    for s in range(len(peers)):
        small_copy(s).wait_send()
    upper_copy.wait()


def summed_grads(f, dy, context, db, n, du, e, dqkv, upper, packed):
    rows, width = dy.shape[1:]
    chunk = 512
    total = du.shape[2] // chunk + 4
    dma = pltpu.SemaphoreType.DMA
    anywhere = pl.BlockSpec(memory_space=pl.ANY)
    local = pl.BlockSpec(memory_space=pltpu.VMEM)
    return pl.pallas_call(
        grads_kernel,
        in_specs=[anywhere] * 9 + [local],
        out_specs=[local] * 5 + [anywhere],
        out_shape=[
            jax.ShapeDtypeStruct((du.shape[2] // 2, QB), F32),
            jax.ShapeDtypeStruct((QB, du.shape[2] // 2), F32),
            jax.ShapeDtypeStruct((width // 2, QB), F32),
            jax.ShapeDtypeStruct((QB, dqkv.shape[2] // 2), F32),
            jax.ShapeDtypeStruct(packed.shape, F32),
            jax.ShapeDtypeStruct((2,) + upper.shape[1:], LOW),
        ],
        scratch_shapes=[
            pltpu.VMEM((2, 2, rows, width), LOW),
            pltpu.VMEM((2, 2, 2, rows, chunk), LOW),
            pltpu.VMEM((width, 2 * rows), LOW),
            pltpu.VMEM((2, 2, 2, 2, QB, chunk), LOW),
            pltpu.VMEM((total, 2, 2, 2, QB, chunk), LOW),
            pltpu.VMEM((total, 2, 2, 2, QB, chunk), LOW),
            pltpu.VMEM((total, 2, 2, QB, chunk), LOW),
            pltpu.VMEM((total, 2, QB, chunk), LOW),
            pltpu.VMEM((total, QB, chunk), LOW),
            pltpu.VMEM((6,) + packed.shape, F32),
            pltpu.VMEM((5,) + packed.shape, F32),
            dma((2,)),
            dma((2, 2)),
            dma((2,)),
            dma((total,)),
            dma((total,)),
            dma((total,)),
            dma((total,)),
            dma((total,)),
            dma((total,)),
            dma((total,)),
            dma((5,)),
            dma((5,)),
            dma,
            dma,
        ],
        compiler_params=pltpu.CompilerParams(
            collective_id=0, has_side_effects=True, vmem_limit_bytes=TAIL_VMEM
        ),
        cost_estimate=cost_of(5000),
        name="summed_grads",
    )(f, dy, context, db, n, du, e, dqkv, upper, packed)


def swapped(value, axis, bit):
    pairs = [(at, at ^ bit) for at in range(lax.axis_size(axis))]
    return lax.ppermute(value, axis, pairs)


def paired_body(
    layer_input,
    segment_ids,
    buckets,
    attn_in,
    attn_out,
    ffn_in,
    ffn_out,
    norm_gain,
    bert_shift,
    head_bias,
    ffn_bias,
    position_bias,
    decoder_grads,
):
    micro_count, _, rows, width = layer_input.shape
    length = segment_ids.shape[2]
    heads, bucket_count = position_bias.shape
    section = lax.axis_index("section")
    core = lax.axis_index("tensor")
    leading = section == 0
    lead = jnp.where(leading, 1, 0).astype(jnp.int32)
    pieces = lax.axis_size("dp")

    own_grads = decoder_grads[0, :, 0]
    given_rows = layer_input[:, 0]
    qkv_own = jnp.concatenate([attn_in[0, :, part] for part in range(3)], axis=1)
    qkv_oth = swapped(qkv_own, "tensor", 1)
    wo = (attn_out[0], swapped(attn_out[0], "tensor", 1))
    up = (ffn_in[0], swapped(ffn_in[0], "tensor", 1))
    down = (ffn_out[0], swapped(ffn_out[0], "tensor", 1))
    small = jnp.concatenate([head_bias.reshape(-1), ffn_bias, position_bias.reshape(-1)])
    small_oth = swapped(small, "tensor", 1)
    near_heads = head_bias.size
    near_ffn = near_heads + ffn_bias.size
    both_small = jnp.stack([small, small_oth])
    head_both = both_small[:, :near_heads].reshape(2, 2, -1)
    ffn_both = jnp.where(leading, both_small[:, near_heads:near_ffn], 0.0).reshape(1, -1)
    table_both = jnp.where(leading, 0.0, both_small[:, near_ffn:]).reshape(2 * heads, bucket_count)
    q_shift = head_both[:, 0].reshape(1, -1)
    v_shift = head_both[:, 1].reshape(1, -1)
    qkv_shift = jnp.where(
        leading, jnp.concatenate([q_shift, jnp.zeros_like(q_shift), v_shift], axis=1), 0.0
    )
    gains = jnp.where(leading, norm_gain[0], norm_gain[1])
    entry_gain = gains[0:1]

    near = length - 1 - 3 * QB
    near_hits = (buckets[None, near : near + 6 * QB] == jnp.arange(bucket_count)[:, None]).astype(F32)
    trailing = jnp.reshape(1 - lead, (1,))
    bias = toeplitz(trailing, jnp.dot(table_both, near_hits, precision=lax.Precision.HIGHEST))

    window = rows + REACH
    base = core * (length - window)
    segments = jnp.pad(
        lax.dynamic_slice_in_dim(segment_ids[:, 0], base, window, axis=1),
        ((0, 0), (PAD * QB, PAD * QB)),
        constant_values=-1,
    )
    reach_blocks = REACH // QB
    own_block = PAD + core * reach_blocks
    halo_block = jnp.where(core == 0, PAD + rows // QB, PAD)
    edge = jnp.where(core == 0, rows - REACH, 0)

    def info_of(turn, micro):
        active = jnp.where(section == turn, 1, 0)
        slot = jnp.where(active == 1, micro, micro_count)
        return jnp.stack([lead, slot, own_block, halo_block, edge, active]).astype(jnp.int32)

    turns = [(turn, micro) for turn in range(2) for micro in range(micro_count)]
    received = [None] * micro_count
    entered = attended = fed = None
    results = []
    finished = []
    for turn, micro in turns:
        info = info_of(turn, micro)
        if turn + micro > 0:
            info, _ = lax.optimization_barrier((info, result))
        if turn == 1 and micro == 0:
            info, remote_grads = lax.optimization_barrier((info, remote_grads))
        lead_turn = turn == 0
        given, at = (given_rows, micro) if lead_turn else (received[micro][None], 0)
        *entered, halo = enter(
            lead_turn, info, given, at, entry_gain, qkv_shift, qkv_own, qkv_oth, entered
        )
        halo = exchanged(halo)
        if turn + micro == 0:
            later, _ = lax.optimization_barrier((own_grads, halo))
            remote_grads = lax.ppermute(later, "section", [(0, 1)])
        attended = attend(
            info, segments[micro], entered[2], halo, None if lead_turn else bias, attended
        )
        *fed, result = feed(
            lead_turn, info, entered[0], attended[0], wo, up, down, ffn_both, gains, bert_shift, fed
        )
        if turn == 0:
            received = list(received)
            received[micro] = lax.ppermute(result, "section", [(0, 1)])
        else:
            results.append(result)
            finished.append(lax.ppermute(result, "section", [(1, 0)]))
    x_saved, e_saved, qkv_saved = entered
    context, lse, *halo_saved = attended
    f_saved, slope_saved, n_saved, one_saved, two_saved = fed

    received = [None] * micro_count
    feed_kept = table_kept = entry_kept = None
    for step, (turn, micro) in enumerate([(1 - turn, micro) for turn, micro in turns]):
        info = info_of(turn, micro)
        if step > 0:
            info, _ = lax.optimization_barrier((info, low if step < 3 else entry_kept[1]))
        lead_turn = turn == 0
        got, at = ([received[micro][None]], 0) if lead_turn else ([own_grads, remote_grads], micro)
        *feed_kept, dz, grad_context = feed_back(
            lead_turn, info, got, at, one_saved, two_saved, slope_saved, wo, up, down, gains, feed_kept
        )
        dq, dk, dv, *tables, far = attend_back(
            info, segments[micro], qkv_saved, halo_saved, grad_context, None if lead_turn else bias, lse,
            None if lead_turn else table_kept,
        )
        if not lead_turn:
            table_kept = tables[0]
        far = exchanged(far)
        if turn == 1 and micro == 0:
            info, *finished = lax.optimization_barrier((info, *finished))
        *entry_kept, low = enter_back(
            lead_turn, info, dq, dk, dv, far, x_saved, dz, qkv_own, qkv_oth, entry_gain, entry_kept
        )
        if turn == 1:
            received = list(received)
            received[micro] = lax.ppermute(low, "section", [(1, 0)])
    dy_saved, du_saved, db_saved, stat_feed, stat_bias = feed_kept
    dqkv_saved, stat_entry, lower_kept, upper_kept = entry_kept

    near_table = jnp.dot(diagonals(trailing, table_kept, micro_count), near_hits.T, precision=lax.Precision.HIGHEST)

    def placed(pair):
        return jnp.where(core == 0, pair, pair[::-1])

    stat_feed = stat_feed[0] + stat_feed[1]
    stat_entry = stat_entry[0] + stat_entry[1]
    gain_first = jnp.where(leading, stat_feed[0:1], stat_entry[2:3])
    gain_rows = jnp.concatenate([gain_first, stat_feed[1:2]])
    nothing = jnp.zeros_like(gain_rows)
    gain_all = jnp.where(leading, jnp.concatenate([gain_rows, nothing]), jnp.concatenate([nothing, gain_rows]))
    shift_all = jnp.where(leading, stat_feed[2:6], 0.0)
    head_all = jnp.where(leading, stat_entry[0:2], 0.0).reshape(2, 2, -1)
    head_all = placed(jnp.moveaxis(head_all, 1, 0))
    bias_all = placed(jnp.where(leading, stat_bias[0] + stat_bias[1], 0.0).reshape(2, -1))
    table_all = placed(jnp.where(leading, 0.0, near_table).reshape(2, heads, bucket_count))
    parts = [gain_all, shift_all, head_all, bias_all, table_all]
    packed = jnp.concatenate([part.reshape(-1) for part in parts])
    packed_rows = 8 * (-(-packed.size // (8 * width)))
    packed = jnp.pad(packed, (0, packed_rows * width - packed.size)).reshape(packed_rows, width)
    down_sum, up_sum, out_sum, qkv_sum, packed, upper = summed_grads(
        f_saved, dy_saved, context, db_saved, n_saved, du_saved, e_saved, dqkv_saved, upper_kept, packed
    )
    packed = packed.reshape(-1)
    input_grad = jnp.where(leading, lower_kept[:micro_count], upper.astype(F32))[:, None]
    unpacked = []
    start = 0
    for part in parts:
        unpacked.append(packed[start : start + part.size].reshape(part.shape))
        start += part.size
    gain_all, shift_all, head_all, bias_all, table_all = unpacked
    mine = lambda value: lax.dynamic_index_in_dim(value, core, 0, keepdims=False)
    return (
        jnp.where(leading, jnp.stack(finished), jnp.stack(results))[None, :, None],
        input_grad,
        qkv_sum.reshape(1, width // pieces, 3, -1),
        out_sum[None],
        up_sum[None],
        down_sum[None],
        gain_all.reshape(norm_gain.shape),
        shift_all,
        mine(head_all),
        mine(bias_all),
        mine(table_all),
    )


def solution(mesh):
    placed = (
        P(None, "dp", "tensor", None),
        P(None, "dp", None),
        P(),
        P("section", None, None, "tensor"),
        P("section", "tensor", None),
        P("section", None, "tensor"),
        P("section", "tensor", None),
        P(),
        P(),
        P(None, "tensor"),
        P("tensor"),
        P("tensor", None),
        P("section", None, "dp", "tensor", None),
    )
    paired = mesh.shape["tensor"] == 2 and mesh.shape["dp"] == 8
    return jax.shard_map(
        paired_body if paired else general_body,
        mesh=mesh,
        in_specs=placed,
        out_specs=(
            P("section", None, "dp", "tensor", None),
            P(None, "dp", "tensor", "section"),
            P("section", "dp", None, "tensor"),
            P("section", "tensor", "dp"),
            P("section", "dp", "tensor"),
            P("section", "tensor", "dp"),
            P(),
            P(),
            P(None, "tensor"),
            P("tensor"),
            P("tensor", None),
        ),
        check_vma=False,
    )
```

```python
import functools

import jax
import jax.numpy as jnp
from jax import lax
from jax.experimental import pallas as pl
from jax.experimental.pallas import tpu as pltpu
from jax.sharding import PartitionSpec as P

DH = 64
QB = 128
PAD = 2
REACH = 256
STRIP = 64
HEAD_SPAN = 512
FEED_CHUNK = 1024
VMEM = 56 * 1024 * 1024
TAIL_VMEM = 60 * 1024 * 1024
LOW = jnp.bfloat16
F32 = jnp.float32


def dot_nt(left, right):
    return lax.dot_general(left, right, (((1,), (1,)), ((), ())), preferred_element_type=F32)


def dot_nn(left, right):
    return lax.dot_general(left, right, (((1,), (0,)), ((), ())), preferred_element_type=F32)


def params():
    return pltpu.CompilerParams(vmem_limit_bytes=VMEM)


def cost_of(micros):
    return pl.CostEstimate(flops=int(micros * 5e7), bytes_accessed=0, transcendentals=0)


def when(condition):
    return (lambda body: body()) if condition else (lambda body: None)


def slotted(shape, dtype):
    return jax.ShapeDtypeStruct((3,) + shape, dtype)


def call_with_slots(
    kernel, scalars, inputs, in_specs, outputs, out_specs, previous, grid, scratch, name, micros
):
    count = len(inputs)
    kept = [] if previous is None else [item for item in previous if item is not None]
    aliases = {}
    if previous is not None:
        at = len(scalars) + count
        for index, item in enumerate(previous):
            if item is not None:
                aliases[at] = index
                at += 1

    def gated(spec):
        if spec.index_map is None:
            return spec
        return pl.BlockSpec(spec.block_shape, lambda j, s, *rest: spec.index_map(j * s[5], s, *rest))

    in_specs = [gated(spec) for spec in in_specs]
    out_specs = [gated(spec) for spec in out_specs]

    def run(*refs):
        @pl.when(refs[0][5] == 1)
        def _():
            front = len(scalars) + count
            kernel(*refs[:front], *refs[front + len(kept) :])

    return pl.pallas_call(
        run,
        grid_spec=pltpu.PrefetchScalarGridSpec(
            num_scalar_prefetch=len(scalars),
            grid=grid,
            in_specs=list(in_specs) + [pl.BlockSpec(memory_space=pl.ANY)] * len(kept),
            out_specs=out_specs,
            scratch_shapes=scratch,
        ),
        out_shape=outputs,
        input_output_aliases=aliases,
        compiler_params=params(),
        cost_estimate=cost_of(micros),
        name=name,
    )(*scalars, *inputs, *kept)


def toeplitz_kernel(flag_ref, w_ref, t_ref):
    width = w_ref.shape[2]

    @pl.when(flag_ref[0] == 0)
    def _():
        t_ref[...] = jnp.zeros_like(t_ref)

    @pl.when(flag_ref[0] == 1)
    def _():
        half = []
        for head in range(2):
            rows = jnp.broadcast_to(w_ref[0, head : head + 1, :], (QB, width))
            rolled = pltpu.roll(rows, 0, 1, stride=1, stride_axis=0)
            half.append(rolled.T[QB:, :])
        t_ref[0] = jnp.concatenate(half, axis=1)


def toeplitz(flag, offset_bias):
    heads, width = offset_bias.shape
    pairs = heads // 2
    return pl.pallas_call(
        toeplitz_kernel,
        grid_spec=pltpu.PrefetchScalarGridSpec(
            num_scalar_prefetch=1,
            grid=(pairs,),
            in_specs=[pl.BlockSpec((1, 2, width), lambda p, s: (p, 0, 0))],
            out_specs=pl.BlockSpec((1, width - QB, 2 * QB), lambda p, s: (p, 0, 0)),
        ),
        out_shape=jax.ShapeDtypeStruct((pairs, width - QB, 2 * QB), F32),
        compiler_params=params(),
        cost_estimate=cost_of(6),
        name="toeplitz",
    )(flag, offset_bias.reshape(pairs, 2, width))


def diagonal_kernel(flag_ref, a_ref, s_ref):
    @pl.when(flag_ref[0] == 0)
    def _():
        s_ref[...] = jnp.zeros_like(s_ref)

    @pl.when(flag_ref[0] == 1)
    def _():
        sum_diagonals(a_ref, s_ref)


def sum_diagonals(a_ref, s_ref):
    total = a_ref[0, 0]
    for extra in range(1, a_ref.shape[0]):
        total = total + a_ref[extra, 0]
    total = jnp.concatenate([jnp.zeros((QB, 2 * QB), F32), total], axis=0)
    width = total.shape[0]
    row = lax.broadcasted_iota(jnp.int32, (QB, QB), 0)
    col = lax.broadcasted_iota(jnp.int32, (QB, QB), 1)
    mirror = jnp.where(row + col == QB - 1, 1.0, 0.0)
    for head in range(2):
        turned = lax.dot_general(
            mirror,
            total[:, head * QB : (head + 1) * QB],
            (((1,), (1,)), ((), ())),
            precision=lax.Precision.HIGHEST,
            preferred_element_type=F32,
        )
        aligned = pltpu.roll(turned, width - QB + 1, 1, stride=1, stride_axis=0)
        s_ref[0, head : head + 1, :] = jnp.sum(aligned, axis=0, keepdims=True)


def diagonals(flag, tables, steps):
    _, pairs, rows, _ = tables.shape
    width = rows + QB
    out = pl.pallas_call(
        diagonal_kernel,
        grid_spec=pltpu.PrefetchScalarGridSpec(
            num_scalar_prefetch=1,
            grid=(pairs,),
            in_specs=[pl.BlockSpec((steps, 1, rows, 2 * QB), lambda p, s: (0, p * s[0], 0, 0))],
            out_specs=pl.BlockSpec((1, 2, width), lambda p, s: (p, 0, 0)),
        ),
        out_shape=jax.ShapeDtypeStruct((pairs, 2, width), F32),
        compiler_params=params(),
        cost_estimate=cost_of(10),
        name="diagonals",
    )(flag, tables)
    return out.reshape(2 * pairs, width)


def two_heads(block, first):
    zero = jnp.zeros_like(block)
    return jnp.concatenate([jnp.where(first, block, zero), jnp.where(first, zero, block)], axis=0)


def joined_heads(turned):
    return jnp.concatenate([turned[:DH, :QB], turned[DH:, QB:]], axis=0).T


def fill_columns(segq_ref, segk_ref):
    for block in range(segq_ref.shape[0]):
        rows = jnp.broadcast_to(segq_ref[block : block + 1, :], (QB, QB))
        segk_ref[block * QB : (block + 1) * QB, :] = rows.T


def visit_blocks(seg_ref, origin, count, block):
    @pl.loop(0, count)
    def _(i):
        at = i + origin
        first = seg_ref[at * QB]
        last = seg_ref[at * QB + QB - 1]
        far = (seg_ref[(at - 1) * QB - 1] == first) | (seg_ref[(at + 2) * QB] == last)

        @pl.when(far)
        def _():
            block(i, at, 2)

        @pl.when(jnp.logical_not(far))
        def _():
            block(i, at, 1)


def placed_rows(info, source, halo, target, halo_count):
    edge = PAD * QB
    rows = source.shape[0]
    target[:edge, :] = jnp.zeros((edge, target.shape[1]), target.dtype)
    target[target.shape[0] - edge :, :] = jnp.zeros((edge, target.shape[1]), target.dtype)
    target[pl.ds(pl.multiple_of(info[2] * QB, QB), rows), :] = source[...]
    if halo_count:
        target[pl.ds(pl.multiple_of(info[3] * QB, QB), halo_count), :] = halo[...]


def turned_rows(info, source, halo, target, halo_count):
    edge = PAD * QB
    rows = source.shape[0]
    target[:, :edge] = jnp.zeros((target.shape[0], edge), target.dtype)
    target[:, target.shape[1] - edge :] = jnp.zeros((target.shape[0], edge), target.dtype)
    target[:, pl.ds(pl.multiple_of(info[2] * QB, QB), rows)] = source[...].T
    if halo_count:
        target[:, pl.ds(pl.multiple_of(info[3] * QB, QB), halo_count)] = halo[...].T


def attend_kernel(halo_count, with_bias, info, seg_ref, *refs):
    refs = list(refs)
    segq_ref, q_ref, k_ref, v_ref = refs[:4]
    t_ref = refs.pop(4) if with_bias else None
    kh_ref = vh_ref = None
    if halo_count:
        kh_ref, vh_ref = refs.pop(4).at[0], refs.pop(4).at[0]
    o_ref, lse_ref = refs[4:6]
    if halo_count:
        refs.pop(6)[0] = kh_ref[...]
        refs.pop(6)[0] = vh_ref[...]
    segk_ref, kp_ref, vt_ref, mask_ref, score_ref, prob_ref = refs[6:]
    rows = q_ref.shape[1]
    pairs = q_ref.shape[2] // (2 * DH)
    first = lax.broadcasted_iota(jnp.int32, (QB, 2 * DH), 1) < DH

    @pl.when(pl.program_id(0) == 0)
    def _():
        fill_columns(segq_ref, segk_ref)

    placed_rows(info, k_ref.at[0], kh_ref, kp_ref, halo_count)
    turned_rows(info, v_ref.at[0], vh_ref, vt_ref, halo_count)

    def block(i, at, reach):
        span = (2 * reach + 1) * QB
        keys = pl.ds(pl.multiple_of((at - reach) * QB, QB), span)
        mine = pl.ds(pl.multiple_of(i * QB, QB), QB)
        shifted = pl.ds((2 - reach) * QB, span)
        allowed = segk_ref[keys, :] == segq_ref[pl.ds(at, 1), :]
        mask_ref[:span, :] = jnp.where(allowed, 0.0, -jnp.inf)
        for pair in range(pairs):
            lanes = slice(pair * 2 * DH, (pair + 1) * 2 * DH)
            both = two_heads(q_ref[0, mine, lanes] * LOW(0.125), first)
            scores = dot_nt(kp_ref[keys, lanes], both)
            score_ref[pair, :span, :] = scores + t_ref[pair, shifted, :] if with_bias else scores
        for pair in range(pairs):
            lanes = slice(pair * 2 * DH, (pair + 1) * 2 * DH)
            stats = []
            for head in range(2):
                side = slice(head * QB, (head + 1) * QB)
                top = None
                for strip in range(0, span, STRIP):
                    piece = slice(strip, strip + STRIP)
                    masked = score_ref[pair, piece, side] + mask_ref[piece, :]
                    score_ref[pair, piece, side] = masked
                    peak = jnp.max(masked.reshape(STRIP // 8, 8, QB), axis=0)
                    top = peak if top is None else jnp.maximum(top, peak)
                highest = jnp.max(top, axis=0, keepdims=True)
                total = None
                for strip in range(0, span, STRIP):
                    piece = slice(strip, strip + STRIP)
                    weights = jnp.exp(score_ref[pair, piece, side] - highest)
                    score_ref[pair, piece, side] = weights
                    mass = jnp.sum(weights.reshape(STRIP // 8, 8, QB), axis=0)
                    total = mass if total is None else total + mass
                totals = jnp.sum(total, axis=0, keepdims=True)
                inverse = 1.0 / totals
                for strip in range(0, span, STRIP):
                    piece = slice(strip, strip + STRIP)
                    prob_ref[pair, piece, side] = (score_ref[pair, piece, side] * inverse).astype(LOW)
                stats.append(highest + jnp.log(totals))
            lse_ref[0, pair, pl.ds(i, 1), :] = jnp.concatenate(stats, axis=1)
        for pair in range(pairs):
            lanes = slice(pair * 2 * DH, (pair + 1) * 2 * DH)
            turned = dot_nn(vt_ref[lanes, keys], prob_ref[pair, :span, :])
            o_ref[0, mine, lanes] = joined_heads(turned).astype(LOW)

    visit_blocks(seg_ref, info[2], rows // QB, block)


def head_specs(rows, span, groups, halo_count):
    column = lambda part: pl.BlockSpec((1, rows, span), lambda g, s, t: (s[1], 0, g + part * groups))
    halo = lambda part: pl.BlockSpec((1, halo_count, span), lambda g, s, t: (part, 0, g))
    return column, halo


def attend(info, segments, qkv, halo, bias, previous):
    _, rows, width = qkv.shape
    width = width // 3
    span = min(HEAD_SPAN, width)
    groups = width // span
    pairs = span // (2 * DH)
    count = rows // QB
    blocks = segments.shape[0] // QB
    halo_count = 0 if halo is None else halo.shape[1]
    column, halo_spec = head_specs(rows, span, groups, halo_count)
    slot_pairs = pl.BlockSpec((1, pairs, count, 2 * QB), lambda g, s, t: (s[1], g, 0, 0))
    in_specs = [
        pl.BlockSpec((blocks, QB), lambda g, s, t: (0, 0)),
        column(0),
        column(1),
        column(2),
    ]
    inputs = [segments.reshape(blocks, QB), qkv, qkv, qkv]
    if bias is not None:
        in_specs.append(pl.BlockSpec((pairs,) + bias.shape[1:], lambda g, s, t: (g, 0, 0)))
        inputs.append(bias)
    outputs = [slotted((rows, width), LOW), slotted((groups * pairs, count, 2 * QB), F32)]
    out_specs = [column(0), slot_pairs]
    if halo_count:
        in_specs += [halo_spec(0), halo_spec(1)]
        inputs += [halo, halo]
        outputs += [slotted((halo_count, width), LOW)] * 2
        kept = pl.BlockSpec((1, halo_count, span), lambda g, s, t: (s[1], 0, g))
        out_specs += [kept, kept]
    return call_with_slots(
        functools.partial(attend_kernel, halo_count, bias is not None),
        [info, segments],
        inputs,
        in_specs,
        outputs,
        out_specs,
        previous,
        (groups,),
        [
            pltpu.VMEM((blocks * QB, QB), jnp.int32),
            pltpu.VMEM((blocks * QB, span), LOW),
            pltpu.VMEM((span, blocks * QB), LOW),
            pltpu.VMEM((5 * QB, QB), F32),
            pltpu.VMEM((pairs, 5 * QB, 2 * QB), F32),
            pltpu.VMEM((pairs, 5 * QB, 2 * QB), LOW),
        ],
        "attend",
        24,
    )


def attend_back_kernel(halo_count, with_bias, info, seg_ref, *refs):
    refs = list(refs)
    segq_ref, q_ref, k_ref, v_ref, g_ref, lse_ref = refs[:6]
    t_ref = refs.pop(6) if with_bias else None
    kh_ref = vh_ref = dh_ref = diag_ref = None
    if halo_count:
        kh_ref, vh_ref = refs.pop(6).at[0], refs.pop(6).at[0]
    dq_ref, dk_ref, dv_ref = [refs[6].at[part] for part in range(3)]
    if with_bias:
        diag_ref = refs.pop(7)
        diag_ref[...] = jnp.zeros_like(diag_ref)
    if halo_count:
        dh_ref = refs.pop(7)
    segk_ref, kp_ref, vp_ref, kt_ref, dk_acc, dv_acc = refs[7:]
    rows = q_ref.shape[1]
    pairs = q_ref.shape[2] // (2 * DH)
    first = lax.broadcasted_iota(jnp.int32, (QB, 2 * DH), 1) < DH

    @pl.when(pl.program_id(0) == 0)
    def _():
        fill_columns(segq_ref, segk_ref)

    placed_rows(info, k_ref.at[0], kh_ref, kp_ref, halo_count)
    placed_rows(info, v_ref.at[0], vh_ref, vp_ref, halo_count)
    turned_rows(info, k_ref.at[0], kh_ref, kt_ref, halo_count)
    dk_acc[...] = jnp.zeros_like(dk_acc)
    dv_acc[...] = jnp.zeros_like(dv_acc)

    def block(i, at, reach):
        span = (2 * reach + 1) * QB
        keys = pl.ds(pl.multiple_of((at - reach) * QB, QB), span)
        mine = pl.ds(pl.multiple_of(i * QB, QB), QB)
        shifted = pl.ds((2 - reach) * QB, span)
        allowed = segk_ref[keys, :] == segq_ref[pl.ds(at, 1), :]
        allowed = jnp.concatenate([allowed, allowed], axis=1)
        for pair in range(pairs):
            lanes = slice(pair * 2 * DH, (pair + 1) * 2 * DH)
            both = two_heads(q_ref[0, mine, lanes] * LOW(0.125), first)
            grads = two_heads(g_ref[mine, lanes], first)
            scores = dot_nt(kp_ref[keys, lanes], both)
            if with_bias:
                scores = scores + t_ref[pair, shifted, :]
            scores = jnp.where(allowed, scores - lse_ref[0, pair, pl.ds(i, 1), :], -jnp.inf)
            probs = jnp.exp(scores)
            grad_probs = dot_nt(vp_ref[keys, lanes], grads)
            dv_acc[keys, lanes] += dot_nn(probs.astype(LOW), grads)
            inner = jnp.sum(probs * grad_probs, axis=0, keepdims=True)
            rounded = (probs * (grad_probs - inner)).astype(LOW)
            dk_acc[keys, lanes] += dot_nn(rounded, both)
            if with_bias:
                diag_ref[0, pair, shifted, :] += rounded.astype(F32)
            turned = dot_nn(kt_ref[lanes, keys], rounded)
            dq_ref[mine, lanes] = (joined_heads(turned) * 0.125).astype(LOW)

    visit_blocks(seg_ref, info[2], rows // QB, block)
    own = pl.ds(pl.multiple_of(info[2] * QB, QB), rows)
    dk_ref[...] = dk_acc[own, :].astype(LOW)
    dv_ref[...] = dv_acc[own, :].astype(LOW)
    if halo_count:
        far = pl.ds(pl.multiple_of(info[3] * QB, QB), halo_count)
        dh_ref[0] = dk_acc[far, :].astype(LOW)
        dh_ref[1] = dv_acc[far, :].astype(LOW)


def attend_back(info, segments, qkv, halo_kept, grad_context, bias, lse, previous):
    _, rows, width = qkv.shape
    width = width // 3
    span = min(HEAD_SPAN, width)
    groups = width // span
    pairs = span // (2 * DH)
    count = rows // QB
    blocks = segments.shape[0] // QB
    halo_count = 0 if halo_kept is None else halo_kept[0].shape[1]
    column, _ = head_specs(rows, span, groups, halo_count)
    plain = pl.BlockSpec((rows, span), lambda g, s, t: (0, g))
    in_specs = [
        pl.BlockSpec((blocks, QB), lambda g, s, t: (0, 0)),
        column(0),
        column(1),
        column(2),
        plain,
        pl.BlockSpec((1, pairs, count, 2 * QB), lambda g, s, t: (s[1], g, 0, 0)),
    ]
    inputs = [segments.reshape(blocks, QB), qkv, qkv, qkv, grad_context, lse]
    if bias is not None:
        in_specs.append(pl.BlockSpec((pairs,) + bias.shape[1:], lambda g, s, t: (g, 0, 0)))
        inputs.append(bias)
    outputs = [jax.ShapeDtypeStruct((3, rows, width), LOW)]
    out_specs = [pl.BlockSpec((3, rows, span), lambda g, s, t: (0, 0, g))]
    if bias is not None:
        outputs.append(slotted(bias.shape, F32))
        out_specs.append(pl.BlockSpec((1, pairs) + bias.shape[1:], lambda g, s, t: (s[1], g, 0, 0)))
    if halo_count:
        kept = pl.BlockSpec((1, halo_count, span), lambda g, s, t: (s[1], 0, g))
        in_specs += [kept, kept]
        inputs += list(halo_kept)
        outputs.append(jax.ShapeDtypeStruct((2, halo_count, width), LOW))
        out_specs.append(pl.BlockSpec((2, halo_count, span), lambda g, s, t: (0, 0, lax.rem(g + groups // 2, groups))))
    keep = None if previous is None else [None, previous] + [None] * (len(outputs) - 2)
    return call_with_slots(
        functools.partial(attend_back_kernel, halo_count, bias is not None),
        [info, segments],
        inputs,
        in_specs,
        outputs,
        out_specs,
        keep,
        (groups,),
        [
            pltpu.VMEM((blocks * QB, QB), jnp.int32),
            pltpu.VMEM((blocks * QB, span), LOW),
            pltpu.VMEM((blocks * QB, span), LOW),
            pltpu.VMEM((span, blocks * QB), LOW),
            pltpu.VMEM((blocks * QB, span), F32),
            pltpu.VMEM((blocks * QB, span), F32),
        ],
        "attend_back",
        26,
    )


def exchange_kernel(give_ref, get_ref, send_sem, recv_sem):
    peer = {"tensor": 1 - lax.axis_index("tensor")}
    barrier = pltpu.get_barrier_semaphore()
    pl.semaphore_signal(barrier, inc=1, device_id=peer, device_id_type=pl.DeviceIdType.MESH)
    pl.semaphore_wait(barrier, 1)
    copy = pltpu.make_async_remote_copy(
        src_ref=give_ref, dst_ref=get_ref, send_sem=send_sem, recv_sem=recv_sem,
        device_id=peer, device_id_type=pl.DeviceIdType.MESH,
    )
    copy.start()
    copy.wait()


def exchanged(value):
    return pl.pallas_call(
        exchange_kernel,
        in_specs=[pl.BlockSpec(memory_space=pl.ANY)],
        out_specs=pl.BlockSpec(memory_space=pl.ANY),
        out_shape=jax.ShapeDtypeStruct(value.shape, value.dtype),
        scratch_shapes=[pltpu.SemaphoreType.DMA, pltpu.SemaphoreType.DMA],
        compiler_params=pltpu.CompilerParams(collective_id=1, has_side_effects=True),
        cost_estimate=cost_of(3),
        name="exchange",
    )(value)


def mean_of(block):
    return jnp.mean(block, axis=-1, keepdims=True)


def rms_scale(block):
    return lax.rsqrt(mean_of(block * block) + 1e-06)


def sum_rows(block):
    return jnp.sum(block, axis=0, keepdims=True)


def gelu_parts(u):
    bell = jnp.exp(u * u * -0.5)
    below = 0.5 + 0.5 * lax.erf(u * 0.7071067811865476)
    return u * below, below + u * (bell * 0.3989422804014327)


def enter_kernel(lead, info, given_ref, gain_ref, shift_ref, own_ref, oth_ref, x_ref, e_ref, qkv_ref, halo_ref):
    m = pl.program_id(0)
    half = own_ref.shape[1]

    @pl.when(m == 0)
    def _():
        x_ref[0] = given_ref[0]
        if lead:
            e_ref[0] = given_ref[0]
        else:
            x = given_ref[0].astype(F32)
            e_ref[0] = (x * rms_scale(x) * gain_ref[...]).astype(LOW)

    e = e_ref[0]
    for part, weight in enumerate((own_ref, oth_ref)):
        lanes = slice(part * half, (part + 1) * half)
        block = (dot_nn(e, weight[...]) + shift_ref[:, lanes]).astype(LOW)
        qkv_ref[0, :, lanes] = block
    start = pl.ds(pl.multiple_of(info[4], QB), halo_ref.shape[1])
    halo_ref[0, :, :half] = qkv_ref[0, start, half:]
    halo_ref[0, :, half:] = qkv_ref[0, start, :half]


def enter(lead, info, given, at, gain, shift, own, oth, previous):
    _, rows, width = given.shape
    half = own.shape[1] // 3
    whole = pl.BlockSpec((1, rows, width), lambda m, s: (at, 0, 0))
    weight = pl.BlockSpec((width, half), lambda m, s: (0, m))
    kept = pl.BlockSpec((1, rows, width), lambda m, s: (s[1], 0, 0))
    keep = None if previous is None else list(previous) + [None]
    return call_with_slots(
        functools.partial(enter_kernel, lead),
        [info],
        [given, gain, shift, own, oth],
        [
            whole,
            pl.BlockSpec((1, width), lambda m, s: (0, 0)),
            pl.BlockSpec((1, 2 * half), lambda m, s: (0, m)),
            weight,
            weight,
        ],
        [
            slotted((rows, width), LOW),
            slotted((rows, width), LOW),
            slotted((rows, 6 * half), LOW),
            jax.ShapeDtypeStruct((2, REACH, 2 * half), LOW),
        ],
        [
            kept,
            kept,
            pl.BlockSpec((1, rows, 2 * half), lambda m, s: (s[1], 0, m)),
            pl.BlockSpec((1, REACH, 2 * half), lambda m, s: (jnp.maximum(m - 1, 0), 0, 0)),
        ],
        keep,
        (3,),
        [],
        "enter",
        9,
    )


def weight_stream(up, down, up_ref, down_ref, sem, steps):
    chunk = up_ref.shape[2]

    def copies(part, c, slot):
        at = pl.ds(pl.multiple_of(c * chunk, chunk), chunk)
        return [
            pltpu.make_async_copy(up[part].at[:, at], up_ref.at[slot], sem.at[slot, 0]),
            pltpu.make_async_copy(down[part].at[at, :], down_ref.at[slot], sem.at[slot, 1]),
        ]

    def start(j):
        slot = lax.rem(j, 2)
        for part in range(2):

            @pl.when((j >= part * (steps // 2)) & (j < (part + 1) * (steps // 2)))
            def _(part=part):
                for copy in copies(part, j - part * (steps // 2), slot):
                    copy.start()

    def wait(j):
        for copy in copies(0, 0, lax.rem(j, 2)):
            copy.wait()

    return start, wait


def feed_kernel(
    lead, info, x_ref, c_ref, wo_own, wo_oth, up_own, up_oth, down_own, down_oth, bias_ref, gain_ref, shift_ref,
    f_ref, slope_ref, n_ref, one_ref, two_ref, out_ref, acc_ref, carry_ref, up_ref, down_ref, sem
):
    j = pl.program_id(0)
    steps = 2 * up_own.shape[1] // up_ref.shape[2]
    half = wo_own.shape[0]
    rows = x_ref.shape[1]

    start, wait = weight_stream((up_own, up_oth), (down_own, down_oth), up_ref, down_ref, sem, steps)

    @pl.when(j == 0)
    def _():
        start(j)
        start(j + 1)
        joined = (
            dot_nn(c_ref[0, :, :half], wo_own[...])
            + dot_nn(c_ref[0, :, half:], wo_oth[...])
            + x_ref[0].astype(F32)
        )

        @when(lead)
        def _():
            before = joined + shift_ref[0:1, :]
            one_ref[0] = before.astype(LOW)
            center = before - mean_of(before)
            normed = center * lax.rsqrt(mean_of(center * center) + 1e-05) * gain_ref[0:1, :] + shift_ref[2:3, :]
            carry_ref[...] = normed
            n_ref[0] = normed.astype(LOW)

        @when(not lead)
        def _():
            one_ref[0] = joined.astype(LOW)
            carry_ref[...] = joined
            n_ref[0] = (joined * rms_scale(joined) * gain_ref[1:2, :]).astype(LOW)

        acc_ref[...] = jnp.zeros_like(acc_ref)

    wait(j)

    @pl.when((j > 0) & (j + 1 < steps))
    def _():
        start(j + 1)

    slot = lax.rem(j, 2)
    u = dot_nn(n_ref[0], up_ref[slot]) + bias_ref[...]
    f, slope = gelu_parts(u)
    f_ref[0] = f.astype(LOW)
    slope_ref[0] = slope.astype(LOW)
    acc_ref[...] += dot_nn(f_ref[0], down_ref[slot])

    @pl.when(j == steps - 1)
    def _():
        joined = carry_ref[...] + acc_ref[...]

        @when(lead)
        def _():
            before = joined + shift_ref[1:2, :]
            two_ref[0] = before.astype(LOW)
            center = before - mean_of(before)
            normed = center * lax.rsqrt(mean_of(center * center) + 1e-05) * gain_ref[1:2, :] + shift_ref[3:4, :]
            out_ref[...] = normed.astype(LOW)

        @when(not lead)
        def _():
            two_ref[0] = joined.astype(LOW)
            out_ref[...] = joined.astype(LOW)


def feed(lead, info, x, context, wo, up, down, bias, gains, shifts, previous):
    _, rows, width = x.shape
    hidden = up[0].shape[1]
    chunk = min(FEED_CHUNK, hidden)
    steps = 2 * hidden // chunk
    anywhere = pl.BlockSpec(memory_space=pl.ANY)
    kept = pl.BlockSpec((1, rows, width), lambda j, s: (s[1], 0, 0))
    fixed = lambda a: pl.BlockSpec(a.shape, lambda j, s: (0, 0))
    moving = pl.BlockSpec((1, rows, chunk), lambda j, s: (s[1], 0, j))
    keep = None if previous is None else list(previous) + [None]
    return call_with_slots(
        functools.partial(feed_kernel, lead),
        [info],
        [x, context, wo[0], wo[1], up[0], up[1], down[0], down[1], bias, gains, shifts],
        [
            kept,
            kept,
            fixed(wo[0]),
            fixed(wo[1]),
            anywhere,
            anywhere,
            anywhere,
            anywhere,
            pl.BlockSpec((1, chunk), lambda j, s: (0, j)),
            fixed(gains),
            fixed(shifts),
        ],
        [
            slotted((rows, 2 * hidden), LOW),
            slotted((rows, 2 * hidden), LOW),
            slotted((rows, width), LOW),
            slotted((rows, width), LOW),
            slotted((rows, width), LOW),
            jax.ShapeDtypeStruct((rows, width), LOW),
        ],
        [moving, moving, kept, kept, kept, pl.BlockSpec((rows, width), lambda j, s: (0, 0))],
        keep,
        (steps,),
        [
            pltpu.VMEM((rows, width), F32),
            pltpu.VMEM((rows, width), F32),
            pltpu.VMEM((2, width, chunk), LOW),
            pltpu.VMEM((2, chunk, width), LOW),
            pltpu.SemaphoreType.DMA((2, 2)),
        ],
        "feed",
        29,
    )


def layer_norm_back(before, grad, gain_row):
    center = before - mean_of(before)
    scale = lax.rsqrt(mean_of(center * center) + 1e-05)
    unit = center * scale
    inner = grad * gain_row
    back = scale * (inner - mean_of(inner) - unit * mean_of(inner * unit))
    return back, sum_rows(grad * unit)


def rms_norm_back(before, grad, gain_row):
    scale = rms_scale(before)
    unit = before * scale
    inner = grad * gain_row
    back = scale * (inner - unit * mean_of(inner * unit))
    return back, sum_rows(grad * unit)


def feed_back_kernel(
    lead, info, *refs
):
    refs = list(refs)
    got_refs = [refs.pop(0) for _ in range(2 - lead)]
    feed_back_steps(lead, got_refs, *refs)


def feed_back_steps(
    lead, got_refs, one_ref, two_ref, slope_ref, wo_own, wo_oth, up_own, up_oth, down_own, down_oth,
    gain_ref, dy_ref, du_ref, db_ref, stat_ref, bias_ref, dc_ref, acc_ref, carry_ref, up_ref, down_ref, wo_ref, sem, wo_sem
):
    j = pl.program_id(0)
    steps = 2 * up_own.shape[1] // up_ref.shape[2]
    start, wait = weight_stream((up_own, up_oth), (down_own, down_oth), up_ref, down_ref, sem, steps)
    wo_copies = [
        pltpu.make_async_copy(source, wo_ref.at[part], wo_sem.at[part]) for part, source in enumerate((wo_own, wo_oth))
    ]
    half = wo_own.shape[0]
    rows = dy_ref.shape[1]

    @pl.when(j == 0)
    def _():
        start(j)
        start(j + 1)
        for copy in wo_copies:
            copy.start()
        stat_ref[...] = jnp.zeros_like(stat_ref)
        acc_ref[...] = jnp.zeros_like(acc_ref)

        @when(lead)
        def _():
            grad = got_refs[0][0].astype(F32)
            back, gain = layer_norm_back(two_ref[0].astype(F32), grad, gain_ref[1:2, :])
            stat_ref[0, 1:2, :] = gain
            stat_ref[0, 5:6, :] = sum_rows(grad)
            stat_ref[0, 3:4, :] = sum_rows(back)
            carry_ref[...] = back
            dy_ref[0] = back.astype(LOW)

        @when(not lead)
        def _():
            grad = got_refs[0][0].astype(F32) + got_refs[1][0].astype(F32)
            carry_ref[...] = grad
            dy_ref[0] = grad.astype(LOW)

    wait(j)

    @pl.when((j > 0) & (j + 1 < steps))
    def _():
        start(j + 1)

    slot = lax.rem(j, 2)
    grad = dot_nt(dy_ref[0], down_ref[slot])
    du_ref[0] = (grad * slope_ref[0].astype(F32)).astype(LOW)
    acc_ref[...] += dot_nt(du_ref[0], up_ref[slot])
    bias_ref[0] = sum_rows(du_ref[0].astype(F32))

    @pl.when(j == steps - 1)
    def _():
        @when(lead)
        def _():
            grad = acc_ref[...] + carry_ref[...]
            back, gain = layer_norm_back(one_ref[0].astype(F32), grad, gain_ref[0:1, :])
            stat_ref[0, 0:1, :] = gain
            stat_ref[0, 4:5, :] = sum_rows(grad)
            stat_ref[0, 2:3, :] = sum_rows(back)
            db_ref[0] = back.astype(LOW)

        @when(not lead)
        def _():
            back, gain = rms_norm_back(one_ref[0].astype(F32), acc_ref[...], gain_ref[1:2, :])
            stat_ref[0, 1:2, :] = gain
            db_ref[0] = (carry_ref[...] + back).astype(LOW)

        for copy in wo_copies:
            copy.wait()
        low = db_ref[0]
        dc_ref[:, :half] = dot_nt(low, wo_ref[0]).astype(LOW)
        dc_ref[:, half:] = dot_nt(low, wo_ref[1]).astype(LOW)


def feed_back(lead, info, got, at, one, two, slope, wo, up, down, gains, previous):
    _, rows, width = one.shape
    hidden = up[0].shape[1]
    chunk = min(FEED_CHUNK, hidden)
    steps = 2 * hidden // chunk
    anywhere = pl.BlockSpec(memory_space=pl.ANY)
    kept = pl.BlockSpec((1, rows, width), lambda j, s: (s[1], 0, 0))
    fixed = lambda a: pl.BlockSpec(a.shape, lambda j, s: (0, 0))
    plain = pl.BlockSpec((rows, width), lambda j, s: (0, 0))
    moving = pl.BlockSpec((1, rows, chunk), lambda j, s: (s[1], 0, j))
    keep = None if previous is None else list(previous) + [None]
    return call_with_slots(
        functools.partial(feed_back_kernel, lead),
        [info],
        [*got, one, two, slope, wo[0], wo[1], up[0], up[1], down[0], down[1], gains],
        [pl.BlockSpec((1, rows, width), lambda j, s: (at, 0, 0))] * len(got)
        + [
            kept,
            kept,
            moving,
            anywhere,
            anywhere,
            anywhere,
            anywhere,
            anywhere,
            anywhere,
            fixed(gains),
        ],
        [
            slotted((rows, width), LOW),
            slotted((rows, 2 * hidden), LOW),
            slotted((rows, width), LOW),
            slotted((8, width), F32),
            slotted((1, 2 * hidden), F32),
            jax.ShapeDtypeStruct((rows, width), LOW),
        ],
        [
            kept,
            moving,
            kept,
            pl.BlockSpec((1, 8, width), lambda j, s: (s[1], 0, 0)),
            pl.BlockSpec((1, 1, chunk), lambda j, s: (s[1], 0, j)),
            plain,
        ],
        keep,
        (steps,),
        [
            pltpu.VMEM((rows, width), F32),
            pltpu.VMEM((rows, width), F32),
            pltpu.VMEM((2, width, chunk), LOW),
            pltpu.VMEM((2, chunk, width), LOW),
            pltpu.VMEM((2,) + wo[0].shape, LOW),
            pltpu.SemaphoreType.DMA((2, 2)),
            pltpu.SemaphoreType.DMA((2,)),
        ],
        "feed_back",
        27,
    )


def enter_back_kernel(lead, info, d3_ref, far_ref, db_ref, *refs):
    refs = list(refs)
    x_ref = None if lead else refs.pop(0)
    own_ref, oth_ref, gain_ref, d_ref, stat_ref, lower_ref, upper_ref, low_ref, acc_ref = refs
    m = pl.program_id(0)
    half = own_ref.shape[1]
    start = pl.ds(pl.multiple_of(info[4], QB), far_ref.shape[1])
    d_ref[0] = d3_ref[0]

    @pl.when(m == 0)
    def _():
        stat_ref[...] = jnp.zeros_like(stat_ref)
        acc_ref[...] = jnp.zeros_like(acc_ref)
        stat_ref[0, 0:1, :] = sum_rows(d_ref[0].astype(F32))

    @pl.when(m > 0)
    def _():
        d_ref[0, start, :] = (d3_ref[0, start, :].astype(F32) + far_ref[0].astype(F32)).astype(LOW)

    @pl.when(m == 2)
    def _():
        stat_ref[0, 1:2, :] = sum_rows(d_ref[0].astype(F32))

    acc_ref[...] += dot_nt(d_ref[0, :, :half], own_ref[...]) + dot_nt(d_ref[0, :, half:], oth_ref[...])

    @pl.when(m == 2)
    def _():
        split = lower_ref.shape[2]

        @when(lead)
        def _():
            total = db_ref[0].astype(F32) + acc_ref[...]
            low_ref[...] = total.astype(LOW)
            lower_ref[0] = total[:, :split]
            upper_ref[0] = total[:, split:].astype(LOW)

        @when(not lead)
        def _():
            back, gain = rms_norm_back(x_ref[0].astype(F32), acc_ref[...], gain_ref[...])
            stat_ref[0, 2:3, :] = gain
            total = db_ref[0].astype(F32) + back
            low_ref[...] = total.astype(LOW)
            lower_ref[0] = total[:, :split]
            upper_ref[0] = total[:, split:].astype(LOW)


def enter_back(lead, info, d3, far, db, x, own, oth, gain, previous):
    _, rows, width = x.shape
    half = own.shape[1] // 3
    plain = pl.BlockSpec((rows, width), lambda m, s: (0, 0))
    kept = pl.BlockSpec((1, rows, width), lambda m, s: (s[1], 0, 0))
    weight = pl.BlockSpec((width, half), lambda m, s: (0, m))
    keep = None if previous is None else list(previous) + [None]
    return call_with_slots(
        functools.partial(enter_back_kernel, lead),
        [info],
        [d3, far, db] + ([] if lead else [x]) + [own, oth, gain],
        [
            pl.BlockSpec((1, rows, width), lambda m, s: (m, 0, 0)),
            pl.BlockSpec((1,) + far.shape[1:], lambda m, s: (jnp.maximum(m - 1, 0), 0, 0)),
            kept,
        ]
        + ([] if lead else [kept])
        + [
            weight,
            weight,
            pl.BlockSpec((1, width), lambda m, s: (0, 0)),
        ],
        [
            slotted((rows, 6 * half), LOW),
            slotted((8, width), F32),
            slotted((rows, width // 2), F32),
            slotted((rows, width // 2), LOW),
            jax.ShapeDtypeStruct((rows, width), LOW),
        ],
        [
            pl.BlockSpec((1, rows, 2 * half), lambda m, s: (s[1], 0, m)),
            pl.BlockSpec((1, 8, width), lambda m, s: (s[1], 0, 0)),
            pl.BlockSpec((1, rows, width // 2), lambda m, s: (s[1], 0, 0)),
            pl.BlockSpec((1, rows, width // 2), lambda m, s: (s[1], 0, 0)),
            plain,
        ],
        keep,
        (3,),
        [pltpu.VMEM((rows, width), F32)],
        "enter_back",
        12,
    )


def passed_along(value, axis, steps):
    count = lax.axis_size(axis)
    initial, last = (max(0, -steps), min(count, count - steps))
    return lax.ppermute(value, axis, [(source, source + steps) for source in range(initial, last)])


def spread(block, axis, source):
    block = jnp.where(lax.axis_index(axis) == source, block, jnp.zeros_like(block))
    return lax.psum(block, axis)


def layer_norm(operand, gain_row, shift_row):
    center = operand - jnp.mean(operand, axis=-1, keepdims=True)
    variance = jnp.mean(center * center, axis=-1, keepdims=True)
    return center * lax.rsqrt(variance + 1e-05) * gain_row + shift_row


def rms_norm(operand, gain_row):
    return (
        operand * lax.rsqrt(jnp.mean(operand * operand, axis=-1, keepdims=True) + 1e-06) * gain_row
    )


def gelu_act(operand):
    return jax.nn.gelu(operand, approximate=False)


def gelu_slope(operand):
    return (
        0.5 * (1.0 + jax.scipy.special.erf(operand * 0.7071067811865476))
        + operand * jnp.exp(-0.5 * operand * operand) * 0.3989422804014327
    )


def entry_norm(residual, gain_rows, leading):
    return jnp.where(leading, residual, rms_norm(residual, gain_rows[0]))


def middle(residual, branch, gain_rows, shift_rows, leading):
    joined = residual + branch
    bert_rows = layer_norm(joined + shift_rows[0], gain_rows[0], shift_rows[2])
    carried = jnp.where(leading, bert_rows, joined)
    normed = jnp.where(leading, bert_rows, rms_norm(joined, gain_rows[1]))
    return (carried, normed)


def final(carried, second, gain_rows, shift_rows, leading):
    joined = carried + second
    return jnp.where(
        leading, layer_norm(joined + shift_rows[1], gain_rows[1], shift_rows[3]), joined
    )


def contract_rows(left, right):
    return lax.dot_general(
        left, right, (((0,), (0,)), ((), ())), preferred_element_type=jnp.float32
    )


def contract_cols(left, right):
    return lax.dot_general(
        left, right, (((1,), (1,)), ((), ())), preferred_element_type=jnp.float32
    )


def gather_rows(operand, weight):
    return (
        jnp.dot(
            lax.all_gather(operand, "tensor", axis=0, tiled=True),
            weight,
            preferred_element_type=jnp.float32,
        ),
        None,
    )


def collect(full_rows, weight):
    return lax.psum_scatter(
        jnp.dot(full_rows, weight, preferred_element_type=jnp.float32),
        "tensor",
        scatter_dimension=0,
        tiled=True,
    )


def scatter_back(grad_rows, weight):
    return lax.psum_scatter(
        contract_cols(grad_rows, weight).astype(jnp.bfloat16),
        "tensor",
        scatter_dimension=0,
        tiled=True,
    ).astype(jnp.float32)


def fold_back(grad_share, weight, activations):
    fragment = lax.all_gather(grad_share, "tensor", axis=0, tiled=True)
    product_rows = contract_cols(fragment, weight)
    return (product_rows, contract_rows(activations, fragment))


def weight_grad(operand, grad_rows):
    return contract_rows(lax.all_gather(operand, "tensor", axis=0, tiled=True), grad_rows)


DH = 64
QB = 128
NARROW = 3
WIDE = 5
VMEM = 56 * 1024 * 1024


def padded(segments):
    return jnp.pad(segments, (PAD * QB, PAD * QB), constant_values=-1)


def general_body(
    layer_input,
    segment_ids,
    buckets,
    attn_in,
    attn_out,
    ffn_in,
    ffn_out,
    norm_gain,
    bert_shift,
    head_bias,
    ffn_bias,
    position_bias,
    decoder_grads,
):
    micro_count = layer_input.shape[0]
    shard_rows = layer_input.shape[2]
    model_width = layer_input.shape[3]
    length = segment_ids.shape[2]
    leading = lax.axis_index("section") == 0
    weighting = jnp.where(leading, 1.0, 0.0)
    qkv_weight = attn_in[0].reshape(model_width, -1)
    out_weight = attn_out[0]
    ffn_up = ffn_in[0]
    ffn_down = ffn_out[0]
    gain_rows = jnp.where(leading, norm_gain[0], norm_gain[1])
    head_shift = head_bias * weighting
    qkv_shift = jnp.concatenate([head_shift[0], jnp.zeros_like(head_shift[0]), head_shift[1]])
    ffn_shift = ffn_bias * weighting
    bias_table = position_bias * (1.0 - weighting)
    bucket_hits = (buckets[None, :] == jnp.arange(bias_table.shape[1])[:, None]).astype(jnp.float32)
    offset_bias = jnp.dot(bias_table, bucket_hits, precision=lax.Precision.HIGHEST)
    near = length - 1 - 3 * QB
    bias = toeplitz(jnp.ones((1,), jnp.int32), offset_bias[:, near : near + 6 * QB])
    info = jnp.array([0, 0, PAD, 0, 0, 1], jnp.int32)
    segment_rows = segment_ids[:, 0]

    def middle_part(residual_in, branch_in, gain_in, shift_in):
        return middle(residual_in, branch_in, gain_in, shift_in, leading)

    def final_part(carried_in, second_in, gain_in, shift_in):
        return final(carried_in, second_in, gain_in, shift_in, leading)

    def entry_part(residual_in, gain_in):
        return entry_norm(residual_in, gain_in, leading)

    received = jnp.zeros((shard_rows, model_width), jnp.bfloat16)
    saved_steps = []
    encoded = []
    for moment in range(micro_count + 1):
        own_rows = layer_input[min(moment, micro_count - 1), 0]
        if moment >= micro_count:
            own_rows = jnp.zeros_like(own_rows)
        segment_row = jnp.where(
            leading, segment_rows[min(moment, micro_count - 1)], segment_rows[max(moment - 1, 0)]
        )
        forward_incoming = jnp.where(leading, own_rows, received)
        forward_residual = forward_incoming.astype(jnp.float32)
        forward_entered = entry_norm(forward_residual, gain_rows, leading).astype(jnp.bfloat16)
        projected, forward_gathered_in = gather_rows(forward_entered, qkv_weight)
        forward_qkv = (projected + qkv_shift).astype(jnp.bfloat16)
        forward_context, forward_log_totals = attend(
            info, padded(segment_row), forward_qkv[None], None, bias, None
        )
        forward_context = forward_context[0]
        forward_branch = collect(forward_context, out_weight)
        forward_carried, forward_normed = middle(
            forward_residual, forward_branch, gain_rows, bert_shift, leading
        )
        pre_full, forward_gathered_mid = gather_rows(forward_normed.astype(jnp.bfloat16), ffn_up)
        forward_pre_act = pre_full + ffn_shift
        forward_second = collect(gelu_act(forward_pre_act).astype(jnp.bfloat16), ffn_down)
        result = final(forward_carried, forward_second, gain_rows, bert_shift, leading).astype(
            jnp.bfloat16
        )
        result, saved = (
            result,
            (
                forward_incoming,
                segment_row,
                forward_branch,
                forward_second,
                forward_qkv,
                forward_context,
                forward_log_totals,
                forward_pre_act,
                forward_gathered_in,
                forward_gathered_mid,
            ),
        )
        saved_steps.append(saved)
        if moment >= 1:
            encoded.append(result)
        if moment < micro_count:
            received = passed_along(result, "section", 1)
    delivered = spread(jnp.stack(encoded), "section", 1)
    section_grads = lax.psum(
        decoder_grads[0, :, 0].astype(jnp.float32).astype(jnp.bfloat16), "section"
    ).astype(jnp.float32)
    grad_received = jnp.zeros((shard_rows, model_width), jnp.float32)
    running_terms = None
    input_rows = []
    for moment in range(micro_count + 1):
        own_grad = section_grads[min(moment, micro_count - 1)]
        if moment >= micro_count:
            own_grad = jnp.zeros_like(own_grad)
        earlier = saved_steps[max(moment - 1, 0)]
        later = saved_steps[min(moment + 1, micro_count)]
        chosen = jax.tree.map(
            lambda from_first, from_second: jnp.where(leading, from_first, from_second),
            earlier,
            later,
        )
        (
            incoming,
            backward_segment_row,
            branch,
            second,
            qkv,
            context,
            log_totals,
            pre_act,
            gathered_in,
            gathered_mid,
        ) = chosen
        residual = incoming.astype(jnp.float32)
        (carried, normed), pull_middle = jax.vjp(
            middle_part, residual, branch, gain_rows, bert_shift
        )
        finished, pull_final = jax.vjp(final_part, carried, second, gain_rows, bert_shift)
        grad_carried, grad_second, gain_end, shift_end = pull_final(
            jnp.where(leading, grad_received, own_grad)
        )
        hidden = gelu_act(pre_act).astype(jnp.bfloat16)
        grad_hidden, backward_grad_down = fold_back(
            grad_second.astype(jnp.bfloat16), ffn_down, hidden
        )
        grad_pre = (grad_hidden * gelu_slope(pre_act)).astype(jnp.bfloat16)
        grad_shift = jnp.sum(grad_pre.astype(jnp.float32), axis=0) * weighting
        backward_grad_up = weight_grad(normed.astype(jnp.bfloat16), grad_pre)
        grad_normed = scatter_back(grad_pre, ffn_up)
        grad_residual, grad_branch, gain_mid, shift_mid = pull_middle((grad_carried, grad_normed))
        grad_context, backward_grad_out_weight = fold_back(
            grad_branch.astype(jnp.bfloat16), out_weight, context
        )
        low_three, grad_table = attend_back(
            info, padded(backward_segment_row), qkv[None], None, grad_context.astype(jnp.bfloat16), bias, log_totals, None
        )
        low_q, low_k, low_v = low_three
        grad_table = grad_table[0]
        grad_head = (
            jnp.stack([jnp.sum(low.astype(jnp.float32), axis=0) for low in (low_q, low_v)]) * weighting
        )
        grad_rows = jnp.concatenate([low_q, low_k, low_v], axis=1)
        entered, pull_entry = jax.vjp(entry_part, residual, gain_rows)
        backward_grad_qkv = weight_grad(entered.astype(jnp.bfloat16), grad_rows)
        grad_entered = scatter_back(grad_rows, qkv_weight)
        grad_from_entry, gain_entry = pull_entry(grad_entered)
        grad_terms = (
            backward_grad_qkv,
            backward_grad_out_weight,
            backward_grad_up,
            backward_grad_down,
            gain_end + gain_mid + gain_entry,
            shift_end + shift_mid,
            grad_head,
            grad_shift,
            grad_table,
        )
        grad_input, grad_terms = (grad_residual + grad_from_entry, grad_terms)
        if running_terms is None:
            running_terms = grad_terms
        else:
            running_terms = jax.tree.map(jnp.add, running_terms, grad_terms)
        if moment >= 1:
            input_rows.append(grad_input)
        if moment < micro_count:
            grad_received = passed_along(grad_input.astype(jnp.bfloat16), "section", -1).astype(
                grad_input.dtype
            )
    input_all = jnp.stack(input_rows)
    half_width = model_width // 2
    upper_half = passed_along(
        input_all[:, :, half_width:].astype(jnp.bfloat16), "section", 1
    ).astype(jnp.float32)
    input_grad = jnp.where(leading, input_all[:, :, :half_width], upper_half)[:, None]
    (
        grad_qkv,
        grad_out_weight,
        grad_up,
        grad_down,
        gain_sum,
        shift_sum,
        head_sum,
        shift_ffn_sum,
        table_sum,
    ) = running_terms
    near_hits = bucket_hits[:, near : near + 6 * QB]
    table_sum = jnp.dot(diagonals(jnp.ones((1,), jnp.int32), table_sum[None], 1), near_hits.T, precision=lax.Precision.HIGHEST) * (
        1.0 - weighting
    )
    weights_out = (
        lax.psum_scatter(
            grad_qkv.reshape(1, model_width, 3, -1).astype(jnp.bfloat16),
            "dp",
            scatter_dimension=1,
            tiled=True,
        ).astype(jnp.float32),
        lax.psum_scatter(
            grad_out_weight[None].astype(jnp.bfloat16), "dp", scatter_dimension=2, tiled=True
        ).astype(jnp.float32),
        lax.psum_scatter(
            grad_up[None].astype(jnp.bfloat16), "dp", scatter_dimension=1, tiled=True
        ).astype(jnp.float32),
        lax.psum_scatter(
            grad_down[None].astype(jnp.bfloat16), "dp", scatter_dimension=2, tiled=True
        ).astype(jnp.float32),
    )
    gain_both = jnp.stack([gain_sum * weighting, gain_sum * (1.0 - weighting)])
    shared_out = lax.psum((gain_both, shift_sum), ("dp", "section", "tensor"))
    split_out = lax.psum((head_sum, shift_ffn_sum, table_sum), ("dp", "section"))
    return (
        delivered[None, :, None],
        input_grad,
        weights_out[0],
        weights_out[1],
        weights_out[2],
        weights_out[3],
        shared_out[0],
        shared_out[1],
        split_out[0],
        split_out[1],
        split_out[2],
    )


def grads_kernel(
    f_hbm, dy_hbm, c_hbm, db_hbm, n_hbm, du_hbm, e_hbm, dqkv_hbm, upper_hbm, packed_ref,
    down_ref, up_ref, row_ref, qkv_ref, summed_ref, upper_got,
    still, moving, turned, given, held, near_ref, y_ref, low_ref, high_ref, small_ref, small_got,
    still_sem, moving_sem, near_send, near_recv, y_send, y_recv, low_send, low_recv, high_send, high_recv,
    small_send, small_recv, upper_send, upper_recv
):
    dp = lax.axis_index("dp")
    core = lax.axis_index("tensor")
    section = lax.axis_index("section")
    y_side = lax.rem(dp, 2)
    low_side = lax.rem(dp // 2, 2)
    high_side = dp // 4

    def across(bit, side):
        return {"dp": dp + bit * (1 - 2 * side)}

    core_peer = {"tensor": 1 - core}
    y_peer = across(1, y_side)
    low_peer = across(2, low_side)
    high_peer = across(4, high_side)
    peers = [core_peer, y_peer, low_peer, high_peer, {"section": 1 - section}]
    mesh_id = pl.DeviceIdType.MESH
    total = held.shape[0]
    chunk = moving.shape[4]
    each = du_hbm.shape[2] // 2 // chunk

    barrier = pltpu.get_barrier_semaphore()
    for peer in peers:
        pl.semaphore_signal(barrier, inc=1, device_id=peer, device_id_type=mesh_id)
    pl.semaphore_wait(barrier, len(peers))

    def send(source, target, out_sem, in_sem, peer):
        return pltpu.make_async_remote_copy(
            src_ref=source, dst_ref=target, send_sem=out_sem, recv_sem=in_sem,
            device_id=peer, device_id_type=mesh_id,
        )

    def near_copy(k, slot):
        return send(given.at[slot], near_ref.at[k], near_send.at[slot], near_recv.at[k], core_peer)

    def y_copy(k):
        return send(held.at[k, :, :, 1 - y_side], y_ref.at[k], y_send.at[k], y_recv.at[k], y_peer)

    def low_copy(k):
        return send(y_ref.at[k, :, 1 - low_side], low_ref.at[k], low_send.at[k], low_recv.at[k], low_peer)

    def high_copy(k):
        return send(low_ref.at[k, 1 - high_side], high_ref.at[k], high_send.at[k], high_recv.at[k], high_peer)

    def small_copy(s):
        return send(small_ref.at[s], small_got.at[s], small_send.at[s], small_recv.at[s], peers[s])

    def added(a, b):
        return (a.astype(F32) + b.astype(F32)).astype(LOW)

    def near_stage(k):
        near_copy(k, 0).wait_recv()
        for hi in range(2):
            for lo in range(2):
                for side in range(2):
                    held[k, hi, lo, side] = added(held[k, hi, lo, side], near_ref[k, hi, lo, side])
        y_copy(k).start()

    def y_stage(k):
        y_copy(k).wait_recv()
        for hi in range(2):
            for lo in range(2):
                y_ref[k, hi, lo] = added(y_ref[k, hi, lo], held[k, hi, lo, y_side])
        low_copy(k).start()

    def low_stage(k):
        low_copy(k).wait_recv()
        for hi in range(2):
            low_ref[k, hi] = added(low_ref[k, hi], y_ref[k, hi, low_side])
        high_copy(k).start()

    def high_stage(k):
        high_copy(k).wait_recv()
        value = high_ref[k].astype(F32) + low_ref[k, high_side].astype(F32)

        def cut(ref, first):
            for q in range(chunk // QB):
                ref[pl.ds(first + q * QB, QB), :] = value[:, q * QB : (q + 1) * QB]

        def lay(ref, at):
            ref[:, pl.ds(pl.multiple_of(at * chunk, chunk), chunk)] = value

        pl.when(k < each)(lambda: cut(down_ref, pl.multiple_of(k * chunk, chunk)))
        pl.when((k >= each) & (k < 2 * each))(lambda: lay(up_ref, k - each))
        pl.when(k == 2 * each)(lambda: cut(row_ref, 0))
        pl.when(k > 2 * each)(lambda: lay(qkv_ref, k - 2 * each - 1))

    def small_stage(s):
        small_copy(s).wait_recv()
        small_ref[s + 1] = small_ref[s] + small_got[s]
        if s + 1 < len(peers):
            small_copy(s + 1).start()

    phases = [
        (False, dy_hbm, f_hbm, each, lambda c: c * chunk, lambda c: (each + c) * chunk),
        (True, n_hbm, du_hbm, each, lambda c: c * chunk, lambda c: (each + c) * chunk),
        (False, db_hbm, c_hbm, 1, lambda c: 0 * c, lambda c: 0 * c + chunk),
        (True, e_hbm, dqkv_hbm, 3, lambda c: 2 * c * chunk, lambda c: (2 * c + 1) * chunk),
    ]

    def still_copy(p):
        return pltpu.make_async_copy(phases[p][1].at[0:2], still.at[p % 2], still_sem.at[p % 2])

    def moving_copies(p, c, slot):
        _, _, source, _, own_at, oth_at = phases[p]
        return [
            pltpu.make_async_copy(
                source.at[0:2, :, pl.ds(pl.multiple_of(at(c), chunk), chunk)],
                moving.at[slot, part],
                moving_sem.at[slot, part],
            )
            for part, at in enumerate((own_at, oth_at))
        ]

    still_copy(0).start()
    for copy in moving_copies(0, 0, 0):
        copy.start()
    still_copy(1).start()
    upper_copy = send(upper_hbm.at[0:2], upper_got, upper_send, upper_recv, peers[4])
    upper_copy.start()
    small_ref[0] = packed_ref[...]
    small_copy(0).start()

    tokens = 2 * still.shape[2]
    base = 0
    for p, (wide, _, _, count, _, _) in enumerate(phases):
        still_copy(p).wait()
        stay = still.at[p % 2]
        if wide:
            for micro in range(2):
                turned[:, micro * tokens // 2 : (micro + 1) * tokens // 2] = stay[micro].T

        @pl.loop(0, count)
        def _(c, p=p, wide=wide, count=count, base=base, stay=stay):
            k = base + c
            slot = lax.rem(k, 2)
            for copy in moving_copies(p, c, slot):
                copy.wait()

            @pl.when(c + 1 < count)
            def _():
                for copy in moving_copies(p, c + 1, 1 - slot):
                    copy.start()

            if p + 1 < len(phases):

                @pl.when(c + 1 == count)
                def _():
                    for copy in moving_copies(p + 1, 0, 1 - slot):
                        copy.start()

            @pl.when(k >= 2)
            def _():
                near_copy(k, slot).wait_send()

            def product(part, store):
                block = moving[slot, part].reshape(tokens, chunk)
                if wide:
                    result = dot_nn(turned[...], block).astype(LOW)
                    for z in range(4):
                        for side in range(2):
                            at = (2 * z + side) * QB
                            store(z, side, slice(None), result[at : at + QB, :])
                else:
                    result = dot_nn(block.T, stay[...].reshape(tokens, -1)).astype(LOW)
                    for z in range(4):
                        for side in range(2):
                            at = (2 * z + side) * QB
                            for q in range(chunk // QB):
                                lanes = slice(q * QB, (q + 1) * QB)
                                store(z, side, lanes, result[lanes, at : at + QB])

            def to_given(z, side, lanes, value):
                given[slot, z // 2, z % 2, side, :, lanes] = value

            def to_held(z, side, lanes, value):
                held[k, z // 2, z % 2, side, :, lanes] = value

            product(1, to_given)
            near_copy(k, slot).start()
            product(0, to_held)

            @pl.when(k >= 1)
            def _():
                near_stage(k - 1)

            for s in range(len(peers)):

                @pl.when(k == 2 * s + 1)
                def _(s=s):
                    small_stage(s)

            @pl.when((k >= 5) & (lax.rem(k, 3) == 2))
            def _():
                y_stage((k - 5) // 3)

        if p + 2 < len(phases):
            still_copy(p + 2).start()
        base += count

    near_stage(total - 1)
    early = (total - 1 - 5) // 3 + 1
    @pl.loop(0, early)
    def _(k):
        low_stage(k)

    @pl.loop(0, early - 1)
    def _(k):
        high_stage(k)

    @pl.loop(early, total)
    def _(k):
        y_stage(k)
        high_stage(k - 1)
        low_stage(k)

    @pl.loop(total - 1, total)
    def _(k):
        high_stage(k)

    summed_ref[...] = small_ref[len(peers)]
    near_copy(total - 2, (total - 2) % 2).wait_send()
    near_copy(total - 1, (total - 1) % 2).wait_send()

    @pl.loop(0, total)
    def _(k):
        y_copy(k).wait_send()
        low_copy(k).wait_send()
        high_copy(k).wait_send()

    for s in range(len(peers)):
        small_copy(s).wait_send()
    upper_copy.wait()


def summed_grads(f, dy, context, db, n, du, e, dqkv, upper, packed):
    rows, width = dy.shape[1:]
    chunk = 512
    total = du.shape[2] // chunk + 4
    dma = pltpu.SemaphoreType.DMA
    anywhere = pl.BlockSpec(memory_space=pl.ANY)
    local = pl.BlockSpec(memory_space=pltpu.VMEM)
    return pl.pallas_call(
        grads_kernel,
        in_specs=[anywhere] * 9 + [local],
        out_specs=[local] * 5 + [anywhere],
        out_shape=[
            jax.ShapeDtypeStruct((du.shape[2] // 2, QB), F32),
            jax.ShapeDtypeStruct((QB, du.shape[2] // 2), F32),
            jax.ShapeDtypeStruct((width // 2, QB), F32),
            jax.ShapeDtypeStruct((QB, dqkv.shape[2] // 2), F32),
            jax.ShapeDtypeStruct(packed.shape, F32),
            jax.ShapeDtypeStruct((2,) + upper.shape[1:], LOW),
        ],
        scratch_shapes=[
            pltpu.VMEM((2, 2, rows, width), LOW),
            pltpu.VMEM((2, 2, 2, rows, chunk), LOW),
            pltpu.VMEM((width, 2 * rows), LOW),
            pltpu.VMEM((2, 2, 2, 2, QB, chunk), LOW),
            pltpu.VMEM((total, 2, 2, 2, QB, chunk), LOW),
            pltpu.VMEM((total, 2, 2, 2, QB, chunk), LOW),
            pltpu.VMEM((total, 2, 2, QB, chunk), LOW),
            pltpu.VMEM((total, 2, QB, chunk), LOW),
            pltpu.VMEM((total, QB, chunk), LOW),
            pltpu.VMEM((6,) + packed.shape, F32),
            pltpu.VMEM((5,) + packed.shape, F32),
            dma((2,)),
            dma((2, 2)),
            dma((2,)),
            dma((total,)),
            dma((total,)),
            dma((total,)),
            dma((total,)),
            dma((total,)),
            dma((total,)),
            dma((total,)),
            dma((5,)),
            dma((5,)),
            dma,
            dma,
        ],
        compiler_params=pltpu.CompilerParams(
            collective_id=0, has_side_effects=True, vmem_limit_bytes=TAIL_VMEM
        ),
        cost_estimate=cost_of(5000),
        name="summed_grads",
    )(f, dy, context, db, n, du, e, dqkv, upper, packed)


def swapped(value, axis, bit):
    pairs = [(at, at ^ bit) for at in range(lax.axis_size(axis))]
    return lax.ppermute(value, axis, pairs)


def paired_body(
    layer_input,
    segment_ids,
    buckets,
    attn_in,
    attn_out,
    ffn_in,
    ffn_out,
    norm_gain,
    bert_shift,
    head_bias,
    ffn_bias,
    position_bias,
    decoder_grads,
):
    micro_count, _, rows, width = layer_input.shape
    length = segment_ids.shape[2]
    heads, bucket_count = position_bias.shape
    section = lax.axis_index("section")
    core = lax.axis_index("tensor")
    leading = section == 0
    lead = jnp.where(leading, 1, 0).astype(jnp.int32)
    pieces = lax.axis_size("dp")

    own_grads = decoder_grads[0, :, 0]
    given_rows = layer_input[:, 0]
    qkv_own = jnp.concatenate([attn_in[0, :, part] for part in range(3)], axis=1)
    qkv_oth = swapped(qkv_own, "tensor", 1)
    wo = (attn_out[0], swapped(attn_out[0], "tensor", 1))
    up = (ffn_in[0], swapped(ffn_in[0], "tensor", 1))
    down = (ffn_out[0], swapped(ffn_out[0], "tensor", 1))
    small = jnp.concatenate([head_bias.reshape(-1), ffn_bias, position_bias.reshape(-1)])
    small_oth = swapped(small, "tensor", 1)
    near_heads = head_bias.size
    near_ffn = near_heads + ffn_bias.size
    both_small = jnp.stack([small, small_oth])
    head_both = both_small[:, :near_heads].reshape(2, 2, -1)
    ffn_both = jnp.where(leading, both_small[:, near_heads:near_ffn], 0.0).reshape(1, -1)
    table_both = jnp.where(leading, 0.0, both_small[:, near_ffn:]).reshape(2 * heads, bucket_count)
    q_shift = head_both[:, 0].reshape(1, -1)
    v_shift = head_both[:, 1].reshape(1, -1)
    qkv_shift = jnp.where(
        leading, jnp.concatenate([q_shift, jnp.zeros_like(q_shift), v_shift], axis=1), 0.0
    )
    gains = jnp.where(leading, norm_gain[0], norm_gain[1])
    entry_gain = gains[0:1]

    near = length - 1 - 3 * QB
    near_hits = (buckets[None, near : near + 6 * QB] == jnp.arange(bucket_count)[:, None]).astype(F32)
    trailing = jnp.reshape(1 - lead, (1,))
    bias = toeplitz(trailing, jnp.dot(table_both, near_hits, precision=lax.Precision.HIGHEST))

    window = rows + REACH
    base = core * (length - window)
    segments = jnp.pad(
        lax.dynamic_slice_in_dim(segment_ids[:, 0], base, window, axis=1),
        ((0, 0), (PAD * QB, PAD * QB)),
        constant_values=-1,
    )
    reach_blocks = REACH // QB
    own_block = PAD + core * reach_blocks
    halo_block = jnp.where(core == 0, PAD + rows // QB, PAD)
    edge = jnp.where(core == 0, rows - REACH, 0)

    def info_of(turn, micro):
        active = jnp.where(section == turn, 1, 0)
        slot = jnp.where(active == 1, micro, micro_count)
        return jnp.stack([lead, slot, own_block, halo_block, edge, active]).astype(jnp.int32)

    turns = [(turn, micro) for turn in range(2) for micro in range(micro_count)]
    received = [None] * micro_count
    entered = attended = fed = None
    results = []
    finished = []
    for turn, micro in turns:
        info = info_of(turn, micro)
        if turn + micro > 0:
            info, _ = lax.optimization_barrier((info, result))
        if turn == 1 and micro == 0:
            info, remote_grads = lax.optimization_barrier((info, remote_grads))
        lead_turn = turn == 0
        given, at = (given_rows, micro) if lead_turn else (received[micro][None], 0)
        *entered, halo = enter(
            lead_turn, info, given, at, entry_gain, qkv_shift, qkv_own, qkv_oth, entered
        )
        halo = exchanged(halo)
        if turn + micro == 0:
            later, _ = lax.optimization_barrier((own_grads, halo))
            remote_grads = lax.ppermute(later, "section", [(0, 1)])
        attended = attend(
            info, segments[micro], entered[2], halo, None if lead_turn else bias, attended
        )
        *fed, result = feed(
            lead_turn, info, entered[0], attended[0], wo, up, down, ffn_both, gains, bert_shift, fed
        )
        if turn == 0:
            received = list(received)
            received[micro] = lax.ppermute(result, "section", [(0, 1)])
        else:
            results.append(result)
            finished.append(lax.ppermute(result, "section", [(1, 0)]))
    x_saved, e_saved, qkv_saved = entered
    context, lse, *halo_saved = attended
    f_saved, slope_saved, n_saved, one_saved, two_saved = fed

    received = [None] * micro_count
    feed_kept = table_kept = entry_kept = None
    for step, (turn, micro) in enumerate([(1 - turn, micro) for turn, micro in turns]):
        info = info_of(turn, micro)
        if step > 0:
            info, _ = lax.optimization_barrier((info, low if step < 3 else entry_kept[1]))
        lead_turn = turn == 0
        got, at = ([received[micro][None]], 0) if lead_turn else ([own_grads, remote_grads], micro)
        *feed_kept, grad_context = feed_back(
            lead_turn, info, got, at, one_saved, two_saved, slope_saved, wo, up, down, gains, feed_kept
        )
        d3, *tables, far = attend_back(
            info, segments[micro], qkv_saved, halo_saved, grad_context, None if lead_turn else bias, lse,
            None if lead_turn else table_kept,
        )
        if not lead_turn:
            table_kept = tables[0]
        far = exchanged(far)
        if turn == 1 and micro == 0:
            info, *finished = lax.optimization_barrier((info, *finished))
        *entry_kept, low = enter_back(
            lead_turn, info, d3, far, feed_kept[2], x_saved, qkv_own, qkv_oth, entry_gain, entry_kept
        )
        if turn == 1:
            received = list(received)
            received[micro] = lax.ppermute(low, "section", [(1, 0)])
    dy_saved, du_saved, db_saved, stat_feed, stat_bias = feed_kept
    dqkv_saved, stat_entry, lower_kept, upper_kept = entry_kept

    near_table = jnp.dot(diagonals(trailing, table_kept, micro_count), near_hits.T, precision=lax.Precision.HIGHEST)

    def placed(pair):
        return jnp.where(core == 0, pair, pair[::-1])

    stat_feed = stat_feed[0] + stat_feed[1]
    stat_entry = stat_entry[0] + stat_entry[1]
    gain_first = jnp.where(leading, stat_feed[0:1], stat_entry[2:3])
    gain_rows = jnp.concatenate([gain_first, stat_feed[1:2]])
    nothing = jnp.zeros_like(gain_rows)
    gain_all = jnp.where(leading, jnp.concatenate([gain_rows, nothing]), jnp.concatenate([nothing, gain_rows]))
    shift_all = jnp.where(leading, stat_feed[2:6], 0.0)
    head_all = jnp.where(leading, stat_entry[0:2], 0.0).reshape(2, 2, -1)
    head_all = placed(jnp.moveaxis(head_all, 1, 0))
    bias_all = placed(jnp.where(leading, stat_bias[0] + stat_bias[1], 0.0).reshape(2, -1))
    table_all = placed(jnp.where(leading, 0.0, near_table).reshape(2, heads, bucket_count))
    parts = [gain_all, shift_all, head_all, bias_all, table_all]
    packed = jnp.concatenate([part.reshape(-1) for part in parts])
    packed_rows = 8 * (-(-packed.size // (8 * width)))
    packed = jnp.pad(packed, (0, packed_rows * width - packed.size)).reshape(packed_rows, width)
    down_sum, up_sum, out_sum, qkv_sum, packed, upper = summed_grads(
        f_saved, dy_saved, context, db_saved, n_saved, du_saved, e_saved, dqkv_saved, upper_kept, packed
    )
    packed = packed.reshape(-1)
    input_grad = jnp.where(leading, lower_kept[:micro_count], upper.astype(F32))[:, None]
    unpacked = []
    start = 0
    for part in parts:
        unpacked.append(packed[start : start + part.size].reshape(part.shape))
        start += part.size
    gain_all, shift_all, head_all, bias_all, table_all = unpacked
    mine = lambda value: lax.dynamic_index_in_dim(value, core, 0, keepdims=False)
    return (
        jnp.where(leading, jnp.stack(finished), jnp.stack(results))[None, :, None],
        input_grad,
        qkv_sum.reshape(1, width // pieces, 3, -1),
        out_sum[None],
        up_sum[None],
        down_sum[None],
        gain_all.reshape(norm_gain.shape),
        shift_all,
        mine(head_all),
        mine(bias_all),
        mine(table_all),
    )


def solution(mesh):
    placed = (
        P(None, "dp", "tensor", None),
        P(None, "dp", None),
        P(),
        P("section", None, None, "tensor"),
        P("section", "tensor", None),
        P("section", None, "tensor"),
        P("section", "tensor", None),
        P(),
        P(),
        P(None, "tensor"),
        P("tensor"),
        P("tensor", None),
        P("section", None, "dp", "tensor", None),
    )
    paired = mesh.shape["tensor"] == 2 and mesh.shape["dp"] == 8
    return jax.shard_map(
        paired_body if paired else general_body,
        mesh=mesh,
        in_specs=placed,
        out_specs=(
            P("section", None, "dp", "tensor", None),
            P(None, "dp", "tensor", "section"),
            P("section", "dp", None, "tensor"),
            P("section", "tensor", "dp"),
            P("section", "dp", "tensor"),
            P("section", "tensor", "dp"),
            P(),
            P(),
            P(None, "tensor"),
            P("tensor"),
            P("tensor", None),
        ),
        check_vma=False,
    )
```

```python
import functools

import jax
import jax.numpy as jnp
from jax import lax
from jax.experimental import pallas as pl
from jax.experimental.pallas import tpu as pltpu
from jax.sharding import PartitionSpec as P

DH = 64
QB = 128
PAD = 2
REACH = 256
STRIP = 64
HEAD_SPAN = 512
FEED_CHUNK = 1024
VMEM = 56 * 1024 * 1024
TAIL_VMEM = 60 * 1024 * 1024
LOW = jnp.bfloat16
F32 = jnp.float32


def dot_nt(left, right):
    return lax.dot_general(left, right, (((1,), (1,)), ((), ())), preferred_element_type=F32)


def dot_nn(left, right):
    return lax.dot_general(left, right, (((1,), (0,)), ((), ())), preferred_element_type=F32)


def params():
    return pltpu.CompilerParams(vmem_limit_bytes=VMEM)


def cost_of(micros):
    return pl.CostEstimate(flops=int(micros * 5e7), bytes_accessed=0, transcendentals=0)


def when(condition):
    return (lambda body: body()) if condition else (lambda body: None)


def slotted(shape, dtype):
    return jax.ShapeDtypeStruct((3,) + shape, dtype)


def call_with_slots(
    kernel, scalars, inputs, in_specs, outputs, out_specs, previous, grid, scratch, name, micros
):
    count = len(inputs)
    kept = [] if previous is None else [item for item in previous if item is not None]
    aliases = {}
    if previous is not None:
        at = len(scalars) + count
        for index, item in enumerate(previous):
            if item is not None:
                aliases[at] = index
                at += 1

    def gated(spec):
        if spec.index_map is None:
            return spec
        return pl.BlockSpec(spec.block_shape, lambda j, s, *rest: spec.index_map(j * s[5], s, *rest))

    in_specs = [gated(spec) for spec in in_specs]
    out_specs = [gated(spec) for spec in out_specs]

    def run(*refs):
        @pl.when(refs[0][5] == 1)
        def _():
            front = len(scalars) + count
            kernel(*refs[:front], *refs[front + len(kept) :])

    return pl.pallas_call(
        run,
        grid_spec=pltpu.PrefetchScalarGridSpec(
            num_scalar_prefetch=len(scalars),
            grid=grid,
            in_specs=list(in_specs) + [pl.BlockSpec(memory_space=pl.ANY)] * len(kept),
            out_specs=out_specs,
            scratch_shapes=scratch,
        ),
        out_shape=outputs,
        input_output_aliases=aliases,
        compiler_params=params(),
        cost_estimate=cost_of(micros),
        name=name,
    )(*scalars, *inputs, *kept)


def toeplitz_kernel(flag_ref, w_ref, t_ref):
    width = w_ref.shape[2]

    @pl.when(flag_ref[0] == 0)
    def _():
        t_ref[...] = jnp.zeros_like(t_ref)

    @pl.when(flag_ref[0] == 1)
    def _():
        half = []
        for head in range(2):
            rows = jnp.broadcast_to(w_ref[0, head : head + 1, :], (QB, width))
            rolled = pltpu.roll(rows, 0, 1, stride=1, stride_axis=0)
            half.append(rolled.T[QB:, :])
        t_ref[0] = jnp.concatenate(half, axis=1)


def toeplitz(flag, offset_bias):
    heads, width = offset_bias.shape
    pairs = heads // 2
    return pl.pallas_call(
        toeplitz_kernel,
        grid_spec=pltpu.PrefetchScalarGridSpec(
            num_scalar_prefetch=1,
            grid=(pairs,),
            in_specs=[pl.BlockSpec((1, 2, width), lambda p, s: (p, 0, 0))],
            out_specs=pl.BlockSpec((1, width - QB, 2 * QB), lambda p, s: (p, 0, 0)),
        ),
        out_shape=jax.ShapeDtypeStruct((pairs, width - QB, 2 * QB), F32),
        compiler_params=params(),
        cost_estimate=cost_of(6),
        name="toeplitz",
    )(flag, offset_bias.reshape(pairs, 2, width))


def diagonal_kernel(flag_ref, a_ref, s_ref):
    @pl.when(flag_ref[0] == 0)
    def _():
        s_ref[...] = jnp.zeros_like(s_ref)

    @pl.when(flag_ref[0] == 1)
    def _():
        sum_diagonals(a_ref, s_ref)


def sum_diagonals(a_ref, s_ref):
    total = a_ref[0, 0]
    for extra in range(1, a_ref.shape[0]):
        total = total + a_ref[extra, 0]
    total = jnp.concatenate([jnp.zeros((QB, 2 * QB), F32), total], axis=0)
    width = total.shape[0]
    row = lax.broadcasted_iota(jnp.int32, (QB, QB), 0)
    col = lax.broadcasted_iota(jnp.int32, (QB, QB), 1)
    mirror = jnp.where(row + col == QB - 1, 1.0, 0.0)
    for head in range(2):
        turned = lax.dot_general(
            mirror,
            total[:, head * QB : (head + 1) * QB],
            (((1,), (1,)), ((), ())),
            precision=lax.Precision.HIGHEST,
            preferred_element_type=F32,
        )
        aligned = pltpu.roll(turned, width - QB + 1, 1, stride=1, stride_axis=0)
        s_ref[0, head : head + 1, :] = jnp.sum(aligned, axis=0, keepdims=True)


def diagonals(flag, tables, steps):
    _, pairs, rows, _ = tables.shape
    width = rows + QB
    out = pl.pallas_call(
        diagonal_kernel,
        grid_spec=pltpu.PrefetchScalarGridSpec(
            num_scalar_prefetch=1,
            grid=(pairs,),
            in_specs=[pl.BlockSpec((steps, 1, rows, 2 * QB), lambda p, s: (0, p * s[0], 0, 0))],
            out_specs=pl.BlockSpec((1, 2, width), lambda p, s: (p, 0, 0)),
        ),
        out_shape=jax.ShapeDtypeStruct((pairs, 2, width), F32),
        compiler_params=params(),
        cost_estimate=cost_of(10),
        name="diagonals",
    )(flag, tables)
    return out.reshape(2 * pairs, width)


def two_heads(block, first):
    zero = jnp.zeros_like(block)
    return jnp.concatenate([jnp.where(first, block, zero), jnp.where(first, zero, block)], axis=0)


def joined_heads(turned):
    return jnp.concatenate([turned[:DH, :QB], turned[DH:, QB:]], axis=0).T


def fill_columns(segq_ref, segk_ref):
    for block in range(segq_ref.shape[0]):
        rows = jnp.broadcast_to(segq_ref[block : block + 1, :], (QB, QB))
        segk_ref[block * QB : (block + 1) * QB, :] = rows.T


def visit_blocks(seg_ref, origin, count, block):
    @pl.loop(0, count)
    def _(i):
        at = i + origin
        first = seg_ref[at * QB]
        last = seg_ref[at * QB + QB - 1]
        far = (seg_ref[(at - 1) * QB - 1] == first) | (seg_ref[(at + 2) * QB] == last)

        @pl.when(far)
        def _():
            block(i, at, 2)

        @pl.when(jnp.logical_not(far))
        def _():
            block(i, at, 1)


def placed_rows(info, source, halo, target, halo_count):
    edge = PAD * QB
    rows = source.shape[0]
    target[:edge, :] = jnp.zeros((edge, target.shape[1]), target.dtype)
    target[target.shape[0] - edge :, :] = jnp.zeros((edge, target.shape[1]), target.dtype)
    target[pl.ds(pl.multiple_of(info[2] * QB, QB), rows), :] = source[...]
    if halo_count:
        target[pl.ds(pl.multiple_of(info[3] * QB, QB), halo_count), :] = halo[...]


def turned_rows(info, source, halo, target, halo_count):
    edge = PAD * QB
    rows = source.shape[0]
    target[:, :edge] = jnp.zeros((target.shape[0], edge), target.dtype)
    target[:, target.shape[1] - edge :] = jnp.zeros((target.shape[0], edge), target.dtype)
    target[:, pl.ds(pl.multiple_of(info[2] * QB, QB), rows)] = source[...].T
    if halo_count:
        target[:, pl.ds(pl.multiple_of(info[3] * QB, QB), halo_count)] = halo[...].T


def attend_kernel(halo_count, with_bias, info, seg_ref, *refs):
    refs = list(refs)
    segq_ref, q_ref, k_ref, v_ref = refs[:4]
    t_ref = refs.pop(4) if with_bias else None
    kh_ref = vh_ref = None
    if halo_count:
        kh_ref, vh_ref = refs.pop(4).at[0], refs.pop(4).at[0]
    o_ref, lse_ref = refs[4:6]
    if halo_count:
        refs.pop(6)[0] = kh_ref[...]
        refs.pop(6)[0] = vh_ref[...]
    segk_ref, kp_ref, vt_ref, mask_ref, score_ref, prob_ref = refs[6:]
    rows = q_ref.shape[1]
    pairs = q_ref.shape[2] // (2 * DH)
    first = lax.broadcasted_iota(jnp.int32, (QB, 2 * DH), 1) < DH

    @pl.when(pl.program_id(0) == 0)
    def _():
        fill_columns(segq_ref, segk_ref)

    placed_rows(info, k_ref.at[0], kh_ref, kp_ref, halo_count)
    turned_rows(info, v_ref.at[0], vh_ref, vt_ref, halo_count)

    def block(i, at, reach):
        span = (2 * reach + 1) * QB
        keys = pl.ds(pl.multiple_of((at - reach) * QB, QB), span)
        mine = pl.ds(pl.multiple_of(i * QB, QB), QB)
        shifted = pl.ds((2 - reach) * QB, span)
        allowed = segk_ref[keys, :] == segq_ref[pl.ds(at, 1), :]
        mask_ref[:span, :] = jnp.where(allowed, 0.0, -jnp.inf)
        for pair in range(pairs):
            lanes = slice(pair * 2 * DH, (pair + 1) * 2 * DH)
            both = two_heads(q_ref[0, mine, lanes] * LOW(0.125), first)
            scores = dot_nt(kp_ref[keys, lanes], both)
            score_ref[pair, :span, :] = scores + t_ref[pair, shifted, :] if with_bias else scores
        for pair in range(pairs):
            lanes = slice(pair * 2 * DH, (pair + 1) * 2 * DH)
            stats = []
            for head in range(2):
                side = slice(head * QB, (head + 1) * QB)
                top = None
                for strip in range(0, span, STRIP):
                    piece = slice(strip, strip + STRIP)
                    masked = score_ref[pair, piece, side] + mask_ref[piece, :]
                    score_ref[pair, piece, side] = masked
                    peak = jnp.max(masked.reshape(STRIP // 8, 8, QB), axis=0)
                    top = peak if top is None else jnp.maximum(top, peak)
                highest = jnp.max(top, axis=0, keepdims=True)
                total = None
                for strip in range(0, span, STRIP):
                    piece = slice(strip, strip + STRIP)
                    weights = jnp.exp(score_ref[pair, piece, side] - highest)
                    score_ref[pair, piece, side] = weights
                    mass = jnp.sum(weights.reshape(STRIP // 8, 8, QB), axis=0)
                    total = mass if total is None else total + mass
                totals = jnp.sum(total, axis=0, keepdims=True)
                inverse = 1.0 / totals
                for strip in range(0, span, STRIP):
                    piece = slice(strip, strip + STRIP)
                    prob_ref[pair, piece, side] = (score_ref[pair, piece, side] * inverse).astype(LOW)
                stats.append(highest + jnp.log(totals))
            lse_ref[0, pair, pl.ds(i, 1), :] = jnp.concatenate(stats, axis=1)
        for pair in range(pairs):
            lanes = slice(pair * 2 * DH, (pair + 1) * 2 * DH)
            turned = dot_nn(vt_ref[lanes, keys], prob_ref[pair, :span, :])
            o_ref[0, mine, lanes] = joined_heads(turned).astype(LOW)

    visit_blocks(seg_ref, info[2], rows // QB, block)


def head_specs(rows, span, groups, halo_count):
    column = lambda part: pl.BlockSpec((1, rows, span), lambda g, s, t: (s[1], 0, g + part * groups))
    halo = lambda part: pl.BlockSpec((1, halo_count, span), lambda g, s, t: (part, 0, g))
    return column, halo


def attend(info, segments, qkv, halo, bias, previous):
    _, rows, width = qkv.shape
    width = width // 3
    span = min(HEAD_SPAN, width)
    groups = width // span
    pairs = span // (2 * DH)
    count = rows // QB
    blocks = segments.shape[0] // QB
    halo_count = 0 if halo is None else halo.shape[1]
    column, halo_spec = head_specs(rows, span, groups, halo_count)
    slot_pairs = pl.BlockSpec((1, pairs, count, 2 * QB), lambda g, s, t: (s[1], g, 0, 0))
    in_specs = [
        pl.BlockSpec((blocks, QB), lambda g, s, t: (0, 0)),
        column(0),
        column(1),
        column(2),
    ]
    inputs = [segments.reshape(blocks, QB), qkv, qkv, qkv]
    if bias is not None:
        in_specs.append(pl.BlockSpec((pairs,) + bias.shape[1:], lambda g, s, t: (g, 0, 0)))
        inputs.append(bias)
    outputs = [slotted((rows, width), LOW), slotted((groups * pairs, count, 2 * QB), F32)]
    out_specs = [column(0), slot_pairs]
    if halo_count:
        in_specs += [halo_spec(0), halo_spec(1)]
        inputs += [halo, halo]
        outputs += [slotted((halo_count, width), LOW)] * 2
        kept = pl.BlockSpec((1, halo_count, span), lambda g, s, t: (s[1], 0, g))
        out_specs += [kept, kept]
    return call_with_slots(
        functools.partial(attend_kernel, halo_count, bias is not None),
        [info, segments],
        inputs,
        in_specs,
        outputs,
        out_specs,
        previous,
        (groups,),
        [
            pltpu.VMEM((blocks * QB, QB), jnp.int32),
            pltpu.VMEM((blocks * QB, span), LOW),
            pltpu.VMEM((span, blocks * QB), LOW),
            pltpu.VMEM((5 * QB, QB), F32),
            pltpu.VMEM((pairs, 5 * QB, 2 * QB), F32),
            pltpu.VMEM((pairs, 5 * QB, 2 * QB), LOW),
        ],
        "attend",
        24,
    )


def attend_back_kernel(halo_count, with_bias, info, seg_ref, *refs):
    refs = list(refs)
    segq_ref, q_ref, k_ref, v_ref, g_ref, lse_ref = refs[:6]
    t_ref = refs.pop(6) if with_bias else None
    kh_ref = vh_ref = dh_ref = diag_ref = None
    if halo_count:
        kh_ref, vh_ref = refs.pop(6).at[0], refs.pop(6).at[0]
    dq_ref, dk_ref, dv_ref = [refs[6].at[part] for part in range(3)]
    if with_bias:
        diag_ref = refs.pop(7)
        diag_ref[...] = jnp.zeros_like(diag_ref)
    if halo_count:
        dh_ref = refs.pop(7)
    segk_ref, kp_ref, vp_ref, kt_ref, dk_acc, dv_acc = refs[7:]
    rows = q_ref.shape[1]
    pairs = q_ref.shape[2] // (2 * DH)
    first = lax.broadcasted_iota(jnp.int32, (QB, 2 * DH), 1) < DH

    @pl.when(pl.program_id(0) == 0)
    def _():
        fill_columns(segq_ref, segk_ref)

    placed_rows(info, k_ref.at[0], kh_ref, kp_ref, halo_count)
    placed_rows(info, v_ref.at[0], vh_ref, vp_ref, halo_count)
    turned_rows(info, k_ref.at[0], kh_ref, kt_ref, halo_count)
    dk_acc[...] = jnp.zeros_like(dk_acc)
    dv_acc[...] = jnp.zeros_like(dv_acc)

    def block(i, at, reach):
        span = (2 * reach + 1) * QB
        keys = pl.ds(pl.multiple_of((at - reach) * QB, QB), span)
        mine = pl.ds(pl.multiple_of(i * QB, QB), QB)
        shifted = pl.ds((2 - reach) * QB, span)
        allowed = segk_ref[keys, :] == segq_ref[pl.ds(at, 1), :]
        allowed = jnp.concatenate([allowed, allowed], axis=1)
        for pair in range(pairs):
            lanes = slice(pair * 2 * DH, (pair + 1) * 2 * DH)
            both = two_heads(q_ref[0, mine, lanes] * LOW(0.125), first)
            grads = two_heads(g_ref[mine, lanes], first)
            scores = dot_nt(kp_ref[keys, lanes], both)
            if with_bias:
                scores = scores + t_ref[pair, shifted, :]
            scores = jnp.where(allowed, scores - lse_ref[0, pair, pl.ds(i, 1), :], -jnp.inf)
            probs = jnp.exp(scores)
            grad_probs = dot_nt(vp_ref[keys, lanes], grads)
            dv_acc[keys, lanes] += dot_nn(probs.astype(LOW), grads)
            inner = jnp.sum(probs * grad_probs, axis=0, keepdims=True)
            rounded = (probs * (grad_probs - inner)).astype(LOW)
            dk_acc[keys, lanes] += dot_nn(rounded, both)
            if with_bias:
                diag_ref[0, pair, shifted, :] += rounded.astype(F32)
            turned = dot_nn(kt_ref[lanes, keys], rounded)
            dq_ref[mine, lanes] = (joined_heads(turned) * 0.125).astype(LOW)

    visit_blocks(seg_ref, info[2], rows // QB, block)
    own = pl.ds(pl.multiple_of(info[2] * QB, QB), rows)
    dk_ref[...] = dk_acc[own, :].astype(LOW)
    dv_ref[...] = dv_acc[own, :].astype(LOW)
    if halo_count:
        far = pl.ds(pl.multiple_of(info[3] * QB, QB), halo_count)
        dh_ref[0] = dk_acc[far, :].astype(LOW)
        dh_ref[1] = dv_acc[far, :].astype(LOW)


def attend_back(info, segments, qkv, halo_kept, grad_context, bias, lse, previous):
    _, rows, width = qkv.shape
    width = width // 3
    span = min(HEAD_SPAN, width)
    groups = width // span
    pairs = span // (2 * DH)
    count = rows // QB
    blocks = segments.shape[0] // QB
    halo_count = 0 if halo_kept is None else halo_kept[0].shape[1]
    column, _ = head_specs(rows, span, groups, halo_count)
    plain = pl.BlockSpec((rows, span), lambda g, s, t: (0, g))
    in_specs = [
        pl.BlockSpec((blocks, QB), lambda g, s, t: (0, 0)),
        column(0),
        column(1),
        column(2),
        plain,
        pl.BlockSpec((1, pairs, count, 2 * QB), lambda g, s, t: (s[1], g, 0, 0)),
    ]
    inputs = [segments.reshape(blocks, QB), qkv, qkv, qkv, grad_context, lse]
    if bias is not None:
        in_specs.append(pl.BlockSpec((pairs,) + bias.shape[1:], lambda g, s, t: (g, 0, 0)))
        inputs.append(bias)
    outputs = [jax.ShapeDtypeStruct((3, rows, width), LOW)]
    out_specs = [pl.BlockSpec((3, rows, span), lambda g, s, t: (0, 0, g))]
    if bias is not None:
        outputs.append(slotted(bias.shape, F32))
        out_specs.append(pl.BlockSpec((1, pairs) + bias.shape[1:], lambda g, s, t: (s[1], g, 0, 0)))
    if halo_count:
        kept = pl.BlockSpec((1, halo_count, span), lambda g, s, t: (s[1], 0, g))
        in_specs += [kept, kept]
        inputs += list(halo_kept)
        outputs.append(jax.ShapeDtypeStruct((2, halo_count, width), LOW))
        out_specs.append(pl.BlockSpec((2, halo_count, span), lambda g, s, t: (0, 0, lax.rem(g + groups // 2, groups))))
    keep = None if previous is None else [None, previous] + [None] * (len(outputs) - 2)
    return call_with_slots(
        functools.partial(attend_back_kernel, halo_count, bias is not None),
        [info, segments],
        inputs,
        in_specs,
        outputs,
        out_specs,
        keep,
        (groups,),
        [
            pltpu.VMEM((blocks * QB, QB), jnp.int32),
            pltpu.VMEM((blocks * QB, span), LOW),
            pltpu.VMEM((blocks * QB, span), LOW),
            pltpu.VMEM((span, blocks * QB), LOW),
            pltpu.VMEM((blocks * QB, span), F32),
            pltpu.VMEM((blocks * QB, span), F32),
        ],
        "attend_back",
        26,
    )


def exchange_kernel(give_ref, get_ref, send_sem, recv_sem):
    peer = {"tensor": 1 - lax.axis_index("tensor")}
    barrier = pltpu.get_barrier_semaphore()
    pl.semaphore_signal(barrier, inc=1, device_id=peer, device_id_type=pl.DeviceIdType.MESH)
    pl.semaphore_wait(barrier, 1)
    copy = pltpu.make_async_remote_copy(
        src_ref=give_ref, dst_ref=get_ref, send_sem=send_sem, recv_sem=recv_sem,
        device_id=peer, device_id_type=pl.DeviceIdType.MESH,
    )
    copy.start()
    copy.wait()


def exchanged(value):
    return pl.pallas_call(
        exchange_kernel,
        in_specs=[pl.BlockSpec(memory_space=pl.ANY)],
        out_specs=pl.BlockSpec(memory_space=pl.ANY),
        out_shape=jax.ShapeDtypeStruct(value.shape, value.dtype),
        scratch_shapes=[pltpu.SemaphoreType.DMA, pltpu.SemaphoreType.DMA],
        compiler_params=pltpu.CompilerParams(collective_id=1, has_side_effects=True),
        cost_estimate=cost_of(3),
        name="exchange",
    )(value)


def mean_of(block):
    return jnp.mean(block, axis=-1, keepdims=True)


def rms_scale(block):
    return lax.rsqrt(mean_of(block * block) + 1e-06)


def sum_rows(block):
    return jnp.sum(block, axis=0, keepdims=True)


def gelu_parts(u):
    bell = jnp.exp(u * u * -0.5)
    below = 0.5 + 0.5 * lax.erf(u * 0.7071067811865476)
    return u * below, below + u * (bell * 0.3989422804014327)


def enter_kernel(lead, info, given_ref, gain_ref, shift_ref, own_ref, oth_ref, x_ref, e_ref, qkv_ref, halo_ref):
    m = pl.program_id(0)
    half = own_ref.shape[1]

    @pl.when(m == 0)
    def _():
        x_ref[0] = given_ref[0]
        if lead:
            e_ref[0] = given_ref[0]
        else:
            x = given_ref[0].astype(F32)
            e_ref[0] = (x * rms_scale(x) * gain_ref[...]).astype(LOW)

    e = e_ref[0]
    for part, weight in enumerate((own_ref, oth_ref)):
        lanes = slice(part * half, (part + 1) * half)
        block = (dot_nn(e, weight[...]) + shift_ref[:, lanes]).astype(LOW)
        qkv_ref[0, :, lanes] = block
    start = pl.ds(pl.multiple_of(info[4], QB), halo_ref.shape[1])
    halo_ref[0, :, :half] = qkv_ref[0, start, half:]
    halo_ref[0, :, half:] = qkv_ref[0, start, :half]


def enter(lead, info, given, at, gain, shift, own, oth, previous):
    _, rows, width = given.shape
    half = own.shape[1] // 3
    whole = pl.BlockSpec((1, rows, width), lambda m, s: (at, 0, 0))
    weight = pl.BlockSpec((width, half), lambda m, s: (0, m))
    kept = pl.BlockSpec((1, rows, width), lambda m, s: (s[1], 0, 0))
    keep = None if previous is None else list(previous) + [None]
    return call_with_slots(
        functools.partial(enter_kernel, lead),
        [info],
        [given, gain, shift, own, oth],
        [
            whole,
            pl.BlockSpec((1, width), lambda m, s: (0, 0)),
            pl.BlockSpec((1, 2 * half), lambda m, s: (0, m)),
            weight,
            weight,
        ],
        [
            slotted((rows, width), LOW),
            slotted((rows, width), LOW),
            slotted((rows, 6 * half), LOW),
            jax.ShapeDtypeStruct((2, REACH, 2 * half), LOW),
        ],
        [
            kept,
            kept,
            pl.BlockSpec((1, rows, 2 * half), lambda m, s: (s[1], 0, m)),
            pl.BlockSpec((1, REACH, 2 * half), lambda m, s: (jnp.maximum(m - 1, 0), 0, 0)),
        ],
        keep,
        (3,),
        [],
        "enter",
        9,
    )


def weight_stream(up, down, up_ref, down_ref, sem, steps):
    chunk = up_ref.shape[2]

    def copies(part, c, slot):
        at = pl.ds(pl.multiple_of(c * chunk, chunk), chunk)
        return [
            pltpu.make_async_copy(up[part].at[:, at], up_ref.at[slot], sem.at[slot, 0]),
            pltpu.make_async_copy(down[part].at[at, :], down_ref.at[slot], sem.at[slot, 1]),
        ]

    def start(j):
        slot = lax.rem(j, 2)
        for part in range(2):

            @pl.when((j >= part * (steps // 2)) & (j < (part + 1) * (steps // 2)))
            def _(part=part):
                for copy in copies(part, j - part * (steps // 2), slot):
                    copy.start()

    def wait(j):
        for copy in copies(0, 0, lax.rem(j, 2)):
            copy.wait()

    return start, wait


def feed_kernel(
    lead, info, x_ref, c_ref, wo_own, wo_oth, up_own, up_oth, down_own, down_oth, bias_ref, gain_ref, shift_ref,
    f_ref, slope_ref, n_ref, one_ref, two_ref, out_ref, acc_ref, carry_ref, up_ref, down_ref, sem
):
    j = pl.program_id(0)
    steps = 2 * up_own.shape[1] // up_ref.shape[2]
    half = wo_own.shape[0]
    rows = x_ref.shape[1]

    start, wait = weight_stream((up_own, up_oth), (down_own, down_oth), up_ref, down_ref, sem, steps)

    @pl.when(j == 0)
    def _():
        start(j)
        start(j + 1)
        joined = (
            dot_nn(c_ref[0, :, :half], wo_own[...])
            + dot_nn(c_ref[0, :, half:], wo_oth[...])
            + x_ref[0].astype(F32)
        )

        @when(lead)
        def _():
            before = joined + shift_ref[0:1, :]
            one_ref[0] = before.astype(LOW)
            center = before - mean_of(before)
            normed = center * lax.rsqrt(mean_of(center * center) + 1e-05) * gain_ref[0:1, :] + shift_ref[2:3, :]
            carry_ref[...] = normed
            n_ref[0] = normed.astype(LOW)

        @when(not lead)
        def _():
            one_ref[0] = joined.astype(LOW)
            carry_ref[...] = joined
            n_ref[0] = (joined * rms_scale(joined) * gain_ref[1:2, :]).astype(LOW)

        acc_ref[...] = jnp.zeros_like(acc_ref)

    wait(j)

    @pl.when((j > 0) & (j + 1 < steps))
    def _():
        start(j + 1)

    slot = lax.rem(j, 2)
    u = dot_nn(n_ref[0], up_ref[slot]) + bias_ref[...]
    f, slope = gelu_parts(u)
    f_ref[0] = f.astype(LOW)
    slope_ref[0] = slope.astype(LOW)
    acc_ref[...] += dot_nn(f_ref[0], down_ref[slot])

    @pl.when(j == steps - 1)
    def _():
        joined = carry_ref[...] + acc_ref[...]

        @when(lead)
        def _():
            before = joined + shift_ref[1:2, :]
            two_ref[0] = before.astype(LOW)
            center = before - mean_of(before)
            normed = center * lax.rsqrt(mean_of(center * center) + 1e-05) * gain_ref[1:2, :] + shift_ref[3:4, :]
            out_ref[...] = normed.astype(LOW)

        @when(not lead)
        def _():
            two_ref[0] = joined.astype(LOW)
            out_ref[...] = joined.astype(LOW)


def feed(lead, info, x, context, wo, up, down, bias, gains, shifts, previous):
    _, rows, width = x.shape
    hidden = up[0].shape[1]
    chunk = min(FEED_CHUNK, hidden)
    steps = 2 * hidden // chunk
    anywhere = pl.BlockSpec(memory_space=pl.ANY)
    kept = pl.BlockSpec((1, rows, width), lambda j, s: (s[1], 0, 0))
    fixed = lambda a: pl.BlockSpec(a.shape, lambda j, s: (0, 0))
    moving = pl.BlockSpec((1, rows, chunk), lambda j, s: (s[1], 0, j))
    keep = None if previous is None else list(previous) + [None]
    return call_with_slots(
        functools.partial(feed_kernel, lead),
        [info],
        [x, context, wo[0], wo[1], up[0], up[1], down[0], down[1], bias, gains, shifts],
        [
            kept,
            kept,
            fixed(wo[0]),
            fixed(wo[1]),
            anywhere,
            anywhere,
            anywhere,
            anywhere,
            pl.BlockSpec((1, chunk), lambda j, s: (0, j)),
            fixed(gains),
            fixed(shifts),
        ],
        [
            slotted((rows, 2 * hidden), LOW),
            slotted((rows, 2 * hidden), LOW),
            slotted((rows, width), LOW),
            slotted((rows, width), LOW),
            slotted((rows, width), LOW),
            jax.ShapeDtypeStruct((rows, width), LOW),
        ],
        [moving, moving, kept, kept, kept, pl.BlockSpec((rows, width), lambda j, s: (0, 0))],
        keep,
        (steps,),
        [
            pltpu.VMEM((rows, width), F32),
            pltpu.VMEM((rows, width), F32),
            pltpu.VMEM((2, width, chunk), LOW),
            pltpu.VMEM((2, chunk, width), LOW),
            pltpu.SemaphoreType.DMA((2, 2)),
        ],
        "feed",
        29,
    )


def layer_norm_back(before, grad, gain_row):
    center = before - mean_of(before)
    scale = lax.rsqrt(mean_of(center * center) + 1e-05)
    unit = center * scale
    inner = grad * gain_row
    back = scale * (inner - mean_of(inner) - unit * mean_of(inner * unit))
    return back, sum_rows(grad * unit)


def rms_norm_back(before, grad, gain_row):
    scale = rms_scale(before)
    unit = before * scale
    inner = grad * gain_row
    back = scale * (inner - unit * mean_of(inner * unit))
    return back, sum_rows(grad * unit)


def feed_back_kernel(
    lead, info, *refs
):
    refs = list(refs)
    got_refs = [refs.pop(0) for _ in range(2 - lead)]
    feed_back_steps(lead, got_refs, *refs)


def feed_back_steps(
    lead, got_refs, one_ref, two_ref, slope_ref, wo_own, wo_oth, up_own, up_oth, down_own, down_oth,
    gain_ref, dy_ref, du_ref, db_ref, stat_ref, bias_ref, dc_ref, acc_ref, carry_ref, up_ref, down_ref, wo_ref, sem, wo_sem
):
    j = pl.program_id(0)
    steps = 2 * up_own.shape[1] // up_ref.shape[2]
    start, wait = weight_stream((up_own, up_oth), (down_own, down_oth), up_ref, down_ref, sem, steps)
    wo_copies = [
        pltpu.make_async_copy(source, wo_ref.at[part], wo_sem.at[part]) for part, source in enumerate((wo_own, wo_oth))
    ]
    half = wo_own.shape[0]
    rows = dy_ref.shape[1]

    @pl.when(j == 0)
    def _():
        start(j)
        start(j + 1)
        for copy in wo_copies:
            copy.start()
        stat_ref[...] = jnp.zeros_like(stat_ref)
        acc_ref[...] = jnp.zeros_like(acc_ref)

        @when(lead)
        def _():
            grad = got_refs[0][0].astype(F32)
            back, gain = layer_norm_back(two_ref[0].astype(F32), grad, gain_ref[1:2, :])
            stat_ref[0, 1:2, :] = gain
            stat_ref[0, 5:6, :] = sum_rows(grad)
            stat_ref[0, 3:4, :] = sum_rows(back)
            carry_ref[...] = back
            dy_ref[0] = back.astype(LOW)

        @when(not lead)
        def _():
            grad = got_refs[0][0].astype(F32) + got_refs[1][0].astype(F32)
            carry_ref[...] = grad
            dy_ref[0] = grad.astype(LOW)

    wait(j)

    @pl.when((j > 0) & (j + 1 < steps))
    def _():
        start(j + 1)

    slot = lax.rem(j, 2)
    grad = dot_nt(dy_ref[0], down_ref[slot])
    du_ref[0] = (grad * slope_ref[0].astype(F32)).astype(LOW)
    acc_ref[...] += dot_nt(du_ref[0], up_ref[slot])
    bias_ref[0] = sum_rows(du_ref[0].astype(F32))

    @pl.when(j == steps - 1)
    def _():
        @when(lead)
        def _():
            grad = acc_ref[...] + carry_ref[...]
            back, gain = layer_norm_back(one_ref[0].astype(F32), grad, gain_ref[0:1, :])
            stat_ref[0, 0:1, :] = gain
            stat_ref[0, 4:5, :] = sum_rows(grad)
            stat_ref[0, 2:3, :] = sum_rows(back)
            db_ref[0] = back.astype(LOW)

        @when(not lead)
        def _():
            back, gain = rms_norm_back(one_ref[0].astype(F32), acc_ref[...], gain_ref[1:2, :])
            stat_ref[0, 1:2, :] = gain
            db_ref[0] = (carry_ref[...] + back).astype(LOW)

        for copy in wo_copies:
            copy.wait()
        low = db_ref[0]
        dc_ref[:, :half] = dot_nt(low, wo_ref[0]).astype(LOW)
        dc_ref[:, half:] = dot_nt(low, wo_ref[1]).astype(LOW)


def feed_back(lead, info, got, at, one, two, slope, wo, up, down, gains, previous):
    _, rows, width = one.shape
    hidden = up[0].shape[1]
    chunk = min(FEED_CHUNK, hidden)
    steps = 2 * hidden // chunk
    anywhere = pl.BlockSpec(memory_space=pl.ANY)
    kept = pl.BlockSpec((1, rows, width), lambda j, s: (s[1], 0, 0))
    fixed = lambda a: pl.BlockSpec(a.shape, lambda j, s: (0, 0))
    plain = pl.BlockSpec((rows, width), lambda j, s: (0, 0))
    moving = pl.BlockSpec((1, rows, chunk), lambda j, s: (s[1], 0, j))
    keep = None if previous is None else list(previous) + [None]
    return call_with_slots(
        functools.partial(feed_back_kernel, lead),
        [info],
        [*got, one, two, slope, wo[0], wo[1], up[0], up[1], down[0], down[1], gains],
        [pl.BlockSpec((1, rows, width), lambda j, s: (at, 0, 0))] * len(got)
        + [
            kept,
            kept,
            moving,
            anywhere,
            anywhere,
            anywhere,
            anywhere,
            anywhere,
            anywhere,
            fixed(gains),
        ],
        [
            slotted((rows, width), LOW),
            slotted((rows, 2 * hidden), LOW),
            slotted((rows, width), LOW),
            slotted((8, width), F32),
            slotted((1, 2 * hidden), F32),
            jax.ShapeDtypeStruct((rows, width), LOW),
        ],
        [
            kept,
            moving,
            kept,
            pl.BlockSpec((1, 8, width), lambda j, s: (s[1], 0, 0)),
            pl.BlockSpec((1, 1, chunk), lambda j, s: (s[1], 0, j)),
            plain,
        ],
        keep,
        (steps,),
        [
            pltpu.VMEM((rows, width), F32),
            pltpu.VMEM((rows, width), F32),
            pltpu.VMEM((2, width, chunk), LOW),
            pltpu.VMEM((2, chunk, width), LOW),
            pltpu.VMEM((2,) + wo[0].shape, LOW),
            pltpu.SemaphoreType.DMA((2, 2)),
            pltpu.SemaphoreType.DMA((2,)),
        ],
        "feed_back",
        27,
    )


def enter_back_kernel(lead, info, d3_ref, far_ref, db_ref, *refs):
    refs = list(refs)
    x_ref = None if lead else refs.pop(0)
    own_ref, oth_ref, gain_ref, d_ref, stat_ref, lower_ref, upper_ref, low_ref, acc_ref = refs
    m = pl.program_id(0)
    half = own_ref.shape[1]
    start = pl.ds(pl.multiple_of(info[4], QB), far_ref.shape[1])
    d_ref[0] = d3_ref[0]

    @pl.when(m == 0)
    def _():
        stat_ref[...] = jnp.zeros_like(stat_ref)
        acc_ref[...] = jnp.zeros_like(acc_ref)
        stat_ref[0, 0:1, :] = sum_rows(d_ref[0].astype(F32))

    @pl.when(m > 0)
    def _():
        d_ref[0, start, :] = (d3_ref[0, start, :].astype(F32) + far_ref[0].astype(F32)).astype(LOW)

    @pl.when(m == 2)
    def _():
        stat_ref[0, 1:2, :] = sum_rows(d_ref[0].astype(F32))

    acc_ref[...] += dot_nt(d_ref[0, :, :half], own_ref[...]) + dot_nt(d_ref[0, :, half:], oth_ref[...])

    @pl.when(m == 2)
    def _():
        split = lower_ref.shape[2]

        @when(lead)
        def _():
            total = db_ref[0].astype(F32) + acc_ref[...]
            low_ref[...] = total.astype(LOW)
            lower_ref[0] = total[:, :split]
            upper_ref[0] = total[:, split:].astype(LOW)

        @when(not lead)
        def _():
            back, gain = rms_norm_back(x_ref[0].astype(F32), acc_ref[...], gain_ref[...])
            stat_ref[0, 2:3, :] = gain
            total = db_ref[0].astype(F32) + back
            low_ref[...] = total.astype(LOW)
            lower_ref[0] = total[:, :split]
            upper_ref[0] = total[:, split:].astype(LOW)


def enter_back(lead, info, d3, far, db, x, own, oth, gain, previous):
    _, rows, width = x.shape
    half = own.shape[1] // 3
    plain = pl.BlockSpec((rows, width), lambda m, s: (0, 0))
    kept = pl.BlockSpec((1, rows, width), lambda m, s: (s[1], 0, 0))
    weight = pl.BlockSpec((width, half), lambda m, s: (0, m))
    keep = None if previous is None else list(previous) + [None]
    return call_with_slots(
        functools.partial(enter_back_kernel, lead),
        [info],
        [d3, far, db] + ([] if lead else [x]) + [own, oth, gain],
        [
            pl.BlockSpec((1, rows, width), lambda m, s: (m, 0, 0)),
            pl.BlockSpec((1,) + far.shape[1:], lambda m, s: (jnp.maximum(m - 1, 0), 0, 0)),
            kept,
        ]
        + ([] if lead else [kept])
        + [
            weight,
            weight,
            pl.BlockSpec((1, width), lambda m, s: (0, 0)),
        ],
        [
            slotted((rows, 6 * half), LOW),
            slotted((8, width), F32),
            slotted((rows, width // 2), F32),
            slotted((rows, width // 2), LOW),
            jax.ShapeDtypeStruct((rows, width), LOW),
        ],
        [
            pl.BlockSpec((1, rows, 2 * half), lambda m, s: (s[1], 0, m)),
            pl.BlockSpec((1, 8, width), lambda m, s: (s[1], 0, 0)),
            pl.BlockSpec((1, rows, width // 2), lambda m, s: (s[1], 0, 0)),
            pl.BlockSpec((1, rows, width // 2), lambda m, s: (s[1], 0, 0)),
            plain,
        ],
        keep,
        (3,),
        [pltpu.VMEM((rows, width), F32)],
        "enter_back",
        12,
    )


def passed_along(value, axis, steps):
    count = lax.axis_size(axis)
    initial, last = (max(0, -steps), min(count, count - steps))
    return lax.ppermute(value, axis, [(source, source + steps) for source in range(initial, last)])


def spread(block, axis, source):
    block = jnp.where(lax.axis_index(axis) == source, block, jnp.zeros_like(block))
    return lax.psum(block, axis)


def layer_norm(operand, gain_row, shift_row):
    center = operand - jnp.mean(operand, axis=-1, keepdims=True)
    variance = jnp.mean(center * center, axis=-1, keepdims=True)
    return center * lax.rsqrt(variance + 1e-05) * gain_row + shift_row


def rms_norm(operand, gain_row):
    return (
        operand * lax.rsqrt(jnp.mean(operand * operand, axis=-1, keepdims=True) + 1e-06) * gain_row
    )


def gelu_act(operand):
    return jax.nn.gelu(operand, approximate=False)


def gelu_slope(operand):
    return (
        0.5 * (1.0 + jax.scipy.special.erf(operand * 0.7071067811865476))
        + operand * jnp.exp(-0.5 * operand * operand) * 0.3989422804014327
    )


def entry_norm(residual, gain_rows, leading):
    return jnp.where(leading, residual, rms_norm(residual, gain_rows[0]))


def middle(residual, branch, gain_rows, shift_rows, leading):
    joined = residual + branch
    bert_rows = layer_norm(joined + shift_rows[0], gain_rows[0], shift_rows[2])
    carried = jnp.where(leading, bert_rows, joined)
    normed = jnp.where(leading, bert_rows, rms_norm(joined, gain_rows[1]))
    return (carried, normed)


def final(carried, second, gain_rows, shift_rows, leading):
    joined = carried + second
    return jnp.where(
        leading, layer_norm(joined + shift_rows[1], gain_rows[1], shift_rows[3]), joined
    )


def contract_rows(left, right):
    return lax.dot_general(
        left, right, (((0,), (0,)), ((), ())), preferred_element_type=jnp.float32
    )


def contract_cols(left, right):
    return lax.dot_general(
        left, right, (((1,), (1,)), ((), ())), preferred_element_type=jnp.float32
    )


def gather_rows(operand, weight):
    return (
        jnp.dot(
            lax.all_gather(operand, "tensor", axis=0, tiled=True),
            weight,
            preferred_element_type=jnp.float32,
        ),
        None,
    )


def collect(full_rows, weight):
    return lax.psum_scatter(
        jnp.dot(full_rows, weight, preferred_element_type=jnp.float32),
        "tensor",
        scatter_dimension=0,
        tiled=True,
    )


def scatter_back(grad_rows, weight):
    return lax.psum_scatter(
        contract_cols(grad_rows, weight).astype(jnp.bfloat16),
        "tensor",
        scatter_dimension=0,
        tiled=True,
    ).astype(jnp.float32)


def fold_back(grad_share, weight, activations):
    fragment = lax.all_gather(grad_share, "tensor", axis=0, tiled=True)
    product_rows = contract_cols(fragment, weight)
    return (product_rows, contract_rows(activations, fragment))


def weight_grad(operand, grad_rows):
    return contract_rows(lax.all_gather(operand, "tensor", axis=0, tiled=True), grad_rows)


DH = 64
QB = 128
NARROW = 3
WIDE = 5
VMEM = 56 * 1024 * 1024


def padded(segments):
    return jnp.pad(segments, (PAD * QB, PAD * QB), constant_values=-1)


def general_body(
    layer_input,
    segment_ids,
    buckets,
    attn_in,
    attn_out,
    ffn_in,
    ffn_out,
    norm_gain,
    bert_shift,
    head_bias,
    ffn_bias,
    position_bias,
    decoder_grads,
):
    micro_count = layer_input.shape[0]
    shard_rows = layer_input.shape[2]
    model_width = layer_input.shape[3]
    length = segment_ids.shape[2]
    leading = lax.axis_index("section") == 0
    weighting = jnp.where(leading, 1.0, 0.0)
    qkv_weight = attn_in[0].reshape(model_width, -1)
    out_weight = attn_out[0]
    ffn_up = ffn_in[0]
    ffn_down = ffn_out[0]
    gain_rows = jnp.where(leading, norm_gain[0], norm_gain[1])
    head_shift = head_bias * weighting
    qkv_shift = jnp.concatenate([head_shift[0], jnp.zeros_like(head_shift[0]), head_shift[1]])
    ffn_shift = ffn_bias * weighting
    bias_table = position_bias * (1.0 - weighting)
    bucket_hits = (buckets[None, :] == jnp.arange(bias_table.shape[1])[:, None]).astype(jnp.float32)
    offset_bias = jnp.dot(bias_table, bucket_hits, precision=lax.Precision.HIGHEST)
    near = length - 1 - 3 * QB
    bias = toeplitz(jnp.ones((1,), jnp.int32), offset_bias[:, near : near + 6 * QB])
    info = jnp.array([0, 0, PAD, 0, 0, 1], jnp.int32)
    segment_rows = segment_ids[:, 0]

    def middle_part(residual_in, branch_in, gain_in, shift_in):
        return middle(residual_in, branch_in, gain_in, shift_in, leading)

    def final_part(carried_in, second_in, gain_in, shift_in):
        return final(carried_in, second_in, gain_in, shift_in, leading)

    def entry_part(residual_in, gain_in):
        return entry_norm(residual_in, gain_in, leading)

    received = jnp.zeros((shard_rows, model_width), jnp.bfloat16)
    saved_steps = []
    encoded = []
    for moment in range(micro_count + 1):
        own_rows = layer_input[min(moment, micro_count - 1), 0]
        if moment >= micro_count:
            own_rows = jnp.zeros_like(own_rows)
        segment_row = jnp.where(
            leading, segment_rows[min(moment, micro_count - 1)], segment_rows[max(moment - 1, 0)]
        )
        forward_incoming = jnp.where(leading, own_rows, received)
        forward_residual = forward_incoming.astype(jnp.float32)
        forward_entered = entry_norm(forward_residual, gain_rows, leading).astype(jnp.bfloat16)
        projected, forward_gathered_in = gather_rows(forward_entered, qkv_weight)
        forward_qkv = (projected + qkv_shift).astype(jnp.bfloat16)
        forward_context, forward_log_totals = attend(
            info, padded(segment_row), forward_qkv[None], None, bias, None
        )
        forward_context = forward_context[0]
        forward_branch = collect(forward_context, out_weight)
        forward_carried, forward_normed = middle(
            forward_residual, forward_branch, gain_rows, bert_shift, leading
        )
        pre_full, forward_gathered_mid = gather_rows(forward_normed.astype(jnp.bfloat16), ffn_up)
        forward_pre_act = pre_full + ffn_shift
        forward_second = collect(gelu_act(forward_pre_act).astype(jnp.bfloat16), ffn_down)
        result = final(forward_carried, forward_second, gain_rows, bert_shift, leading).astype(
            jnp.bfloat16
        )
        result, saved = (
            result,
            (
                forward_incoming,
                segment_row,
                forward_branch,
                forward_second,
                forward_qkv,
                forward_context,
                forward_log_totals,
                forward_pre_act,
                forward_gathered_in,
                forward_gathered_mid,
            ),
        )
        saved_steps.append(saved)
        if moment >= 1:
            encoded.append(result)
        if moment < micro_count:
            received = passed_along(result, "section", 1)
    delivered = spread(jnp.stack(encoded), "section", 1)
    section_grads = lax.psum(
        decoder_grads[0, :, 0].astype(jnp.float32).astype(jnp.bfloat16), "section"
    ).astype(jnp.float32)
    grad_received = jnp.zeros((shard_rows, model_width), jnp.float32)
    running_terms = None
    input_rows = []
    for moment in range(micro_count + 1):
        own_grad = section_grads[min(moment, micro_count - 1)]
        if moment >= micro_count:
            own_grad = jnp.zeros_like(own_grad)
        earlier = saved_steps[max(moment - 1, 0)]
        later = saved_steps[min(moment + 1, micro_count)]
        chosen = jax.tree.map(
            lambda from_first, from_second: jnp.where(leading, from_first, from_second),
            earlier,
            later,
        )
        (
            incoming,
            backward_segment_row,
            branch,
            second,
            qkv,
            context,
            log_totals,
            pre_act,
            gathered_in,
            gathered_mid,
        ) = chosen
        residual = incoming.astype(jnp.float32)
        (carried, normed), pull_middle = jax.vjp(
            middle_part, residual, branch, gain_rows, bert_shift
        )
        finished, pull_final = jax.vjp(final_part, carried, second, gain_rows, bert_shift)
        grad_carried, grad_second, gain_end, shift_end = pull_final(
            jnp.where(leading, grad_received, own_grad)
        )
        hidden = gelu_act(pre_act).astype(jnp.bfloat16)
        grad_hidden, backward_grad_down = fold_back(
            grad_second.astype(jnp.bfloat16), ffn_down, hidden
        )
        grad_pre = (grad_hidden * gelu_slope(pre_act)).astype(jnp.bfloat16)
        grad_shift = jnp.sum(grad_pre.astype(jnp.float32), axis=0) * weighting
        backward_grad_up = weight_grad(normed.astype(jnp.bfloat16), grad_pre)
        grad_normed = scatter_back(grad_pre, ffn_up)
        grad_residual, grad_branch, gain_mid, shift_mid = pull_middle((grad_carried, grad_normed))
        grad_context, backward_grad_out_weight = fold_back(
            grad_branch.astype(jnp.bfloat16), out_weight, context
        )
        low_three, grad_table = attend_back(
            info, padded(backward_segment_row), qkv[None], None, grad_context.astype(jnp.bfloat16), bias, log_totals, None
        )
        low_q, low_k, low_v = low_three
        grad_table = grad_table[0]
        grad_head = (
            jnp.stack([jnp.sum(low.astype(jnp.float32), axis=0) for low in (low_q, low_v)]) * weighting
        )
        grad_rows = jnp.concatenate([low_q, low_k, low_v], axis=1)
        entered, pull_entry = jax.vjp(entry_part, residual, gain_rows)
        backward_grad_qkv = weight_grad(entered.astype(jnp.bfloat16), grad_rows)
        grad_entered = scatter_back(grad_rows, qkv_weight)
        grad_from_entry, gain_entry = pull_entry(grad_entered)
        grad_terms = (
            backward_grad_qkv,
            backward_grad_out_weight,
            backward_grad_up,
            backward_grad_down,
            gain_end + gain_mid + gain_entry,
            shift_end + shift_mid,
            grad_head,
            grad_shift,
            grad_table,
        )
        grad_input, grad_terms = (grad_residual + grad_from_entry, grad_terms)
        if running_terms is None:
            running_terms = grad_terms
        else:
            running_terms = jax.tree.map(jnp.add, running_terms, grad_terms)
        if moment >= 1:
            input_rows.append(grad_input)
        if moment < micro_count:
            grad_received = passed_along(grad_input.astype(jnp.bfloat16), "section", -1).astype(
                grad_input.dtype
            )
    input_all = jnp.stack(input_rows)
    half_width = model_width // 2
    upper_half = passed_along(
        input_all[:, :, half_width:].astype(jnp.bfloat16), "section", 1
    ).astype(jnp.float32)
    input_grad = jnp.where(leading, input_all[:, :, :half_width], upper_half)[:, None]
    (
        grad_qkv,
        grad_out_weight,
        grad_up,
        grad_down,
        gain_sum,
        shift_sum,
        head_sum,
        shift_ffn_sum,
        table_sum,
    ) = running_terms
    near_hits = bucket_hits[:, near : near + 6 * QB]
    table_sum = jnp.dot(diagonals(jnp.ones((1,), jnp.int32), table_sum[None], 1), near_hits.T, precision=lax.Precision.HIGHEST) * (
        1.0 - weighting
    )
    weights_out = (
        lax.psum_scatter(
            grad_qkv.reshape(1, model_width, 3, -1).astype(jnp.bfloat16),
            "dp",
            scatter_dimension=1,
            tiled=True,
        ).astype(jnp.float32),
        lax.psum_scatter(
            grad_out_weight[None].astype(jnp.bfloat16), "dp", scatter_dimension=2, tiled=True
        ).astype(jnp.float32),
        lax.psum_scatter(
            grad_up[None].astype(jnp.bfloat16), "dp", scatter_dimension=1, tiled=True
        ).astype(jnp.float32),
        lax.psum_scatter(
            grad_down[None].astype(jnp.bfloat16), "dp", scatter_dimension=2, tiled=True
        ).astype(jnp.float32),
    )
    gain_both = jnp.stack([gain_sum * weighting, gain_sum * (1.0 - weighting)])
    shared_out = lax.psum((gain_both, shift_sum), ("dp", "section", "tensor"))
    split_out = lax.psum((head_sum, shift_ffn_sum, table_sum), ("dp", "section"))
    return (
        delivered[None, :, None],
        input_grad,
        weights_out[0],
        weights_out[1],
        weights_out[2],
        weights_out[3],
        shared_out[0],
        shared_out[1],
        split_out[0],
        split_out[1],
        split_out[2],
    )


def grads_kernel(
    f_hbm, dy_hbm, c_hbm, db_hbm, n_hbm, du_hbm, e_hbm, dqkv_hbm, upper_hbm, packed_ref,
    down_ref, up_ref, row_ref, qkv_ref, summed_ref, upper_got,
    still, moving, turned, given, held, near_ref, y_ref, low_ref, high_ref, small_ref, small_got,
    still_sem, moving_sem, near_send, near_recv, y_send, y_recv, low_send, low_recv, high_send, high_recv,
    small_send, small_recv, upper_send, upper_recv
):
    dp = lax.axis_index("dp")
    core = lax.axis_index("tensor")
    section = lax.axis_index("section")
    y_side = lax.rem(dp, 2)
    low_side = lax.rem(dp // 2, 2)
    high_side = dp // 4

    def across(bit, side):
        return {"dp": dp + bit * (1 - 2 * side)}

    core_peer = {"tensor": 1 - core}
    y_peer = across(1, y_side)
    low_peer = across(2, low_side)
    high_peer = across(4, high_side)
    peers = [core_peer, y_peer, low_peer, high_peer, {"section": 1 - section}]
    mesh_id = pl.DeviceIdType.MESH
    total = held.shape[0]
    chunk = moving.shape[4]
    each = du_hbm.shape[2] // 2 // chunk

    barrier = pltpu.get_barrier_semaphore()
    for peer in peers:
        pl.semaphore_signal(barrier, inc=1, device_id=peer, device_id_type=mesh_id)
    pl.semaphore_wait(barrier, len(peers))

    def send(source, target, out_sem, in_sem, peer):
        return pltpu.make_async_remote_copy(
            src_ref=source, dst_ref=target, send_sem=out_sem, recv_sem=in_sem,
            device_id=peer, device_id_type=mesh_id,
        )

    def near_copy(k, slot):
        return send(given.at[slot], near_ref.at[k], near_send.at[slot], near_recv.at[k], core_peer)

    def y_copy(k):
        return send(held.at[k, :, :, 1 - y_side], y_ref.at[k], y_send.at[k], y_recv.at[k], y_peer)

    def low_copy(k):
        return send(y_ref.at[k, :, 1 - low_side], low_ref.at[k], low_send.at[k], low_recv.at[k], low_peer)

    def high_copy(k):
        return send(low_ref.at[k, 1 - high_side], high_ref.at[k], high_send.at[k], high_recv.at[k], high_peer)

    def small_copy(s):
        return send(small_ref.at[s], small_got.at[s], small_send.at[s], small_recv.at[s], peers[s])

    def added(a, b):
        return (a.astype(F32) + b.astype(F32)).astype(LOW)

    def near_stage(k):
        near_copy(k, 0).wait_recv()
        for hi in range(2):
            for lo in range(2):
                for side in range(2):
                    held[k, hi, lo, side] = added(held[k, hi, lo, side], near_ref[k, hi, lo, side])
        y_copy(k).start()

    def y_stage(k):
        y_copy(k).wait_recv()
        for hi in range(2):
            for lo in range(2):
                y_ref[k, hi, lo] = added(y_ref[k, hi, lo], held[k, hi, lo, y_side])
        low_copy(k).start()

    def low_stage(k):
        low_copy(k).wait_recv()
        for hi in range(2):
            low_ref[k, hi] = added(low_ref[k, hi], y_ref[k, hi, low_side])
        high_copy(k).start()

    def high_stage(k):
        high_copy(k).wait_recv()
        value = high_ref[k].astype(F32) + low_ref[k, high_side].astype(F32)

        def cut(ref, first):
            for q in range(chunk // QB):
                ref[pl.ds(first + q * QB, QB), :] = value[:, q * QB : (q + 1) * QB]

        def lay(ref, at):
            ref[:, pl.ds(pl.multiple_of(at * chunk, chunk), chunk)] = value

        pl.when(k < each)(lambda: cut(down_ref, pl.multiple_of(k * chunk, chunk)))
        pl.when((k >= each) & (k < 2 * each))(lambda: lay(up_ref, k - each))
        pl.when(k == 2 * each)(lambda: cut(row_ref, 0))
        pl.when(k > 2 * each)(lambda: lay(qkv_ref, k - 2 * each - 1))

    def small_stage(s):
        small_copy(s).wait_recv()
        small_ref[s + 1] = small_ref[s] + small_got[s]
        if s + 1 < len(peers):
            small_copy(s + 1).start()

    phases = [
        (False, dy_hbm, f_hbm, each, lambda c: c * chunk, lambda c: (each + c) * chunk),
        (True, n_hbm, du_hbm, each, lambda c: c * chunk, lambda c: (each + c) * chunk),
        (False, db_hbm, c_hbm, 1, lambda c: 0 * c, lambda c: 0 * c + chunk),
        (True, e_hbm, dqkv_hbm, 3, lambda c: 2 * c * chunk, lambda c: (2 * c + 1) * chunk),
    ]

    def still_copy(p):
        return pltpu.make_async_copy(phases[p][1].at[0:2], still.at[p % 2], still_sem.at[p % 2])

    def moving_copies(p, c, slot):
        _, _, source, _, own_at, oth_at = phases[p]
        return [
            pltpu.make_async_copy(
                source.at[0:2, :, pl.ds(pl.multiple_of(at(c), chunk), chunk)],
                moving.at[slot, part],
                moving_sem.at[slot, part],
            )
            for part, at in enumerate((own_at, oth_at))
        ]

    still_copy(0).start()
    for copy in moving_copies(0, 0, 0):
        copy.start()
    still_copy(1).start()
    upper_copy = send(upper_hbm.at[0:2], upper_got, upper_send, upper_recv, peers[4])
    upper_copy.start()
    small_ref[0] = packed_ref[...]
    small_copy(0).start()

    tokens = 2 * still.shape[2]
    base = 0
    for p, (wide, _, _, count, _, _) in enumerate(phases):
        still_copy(p).wait()
        stay = still.at[p % 2]
        if wide:
            for micro in range(2):
                turned[:, micro * tokens // 2 : (micro + 1) * tokens // 2] = stay[micro].T

        @pl.loop(0, count)
        def _(c, p=p, wide=wide, count=count, base=base, stay=stay):
            k = base + c
            slot = lax.rem(k, 2)
            for copy in moving_copies(p, c, slot):
                copy.wait()

            @pl.when(c + 1 < count)
            def _():
                for copy in moving_copies(p, c + 1, 1 - slot):
                    copy.start()

            if p + 1 < len(phases):

                @pl.when(c + 1 == count)
                def _():
                    for copy in moving_copies(p + 1, 0, 1 - slot):
                        copy.start()

            @pl.when(k >= 2)
            def _():
                near_copy(k, slot).wait_send()

            def product(part, store):
                block = moving[slot, part].reshape(tokens, chunk)
                if wide:
                    result = dot_nn(turned[...], block).astype(LOW)
                    for z in range(4):
                        for side in range(2):
                            at = (2 * z + side) * QB
                            store(z, side, slice(None), result[at : at + QB, :])
                else:
                    result = dot_nn(block.T, stay[...].reshape(tokens, -1)).astype(LOW)
                    for z in range(4):
                        for side in range(2):
                            at = (2 * z + side) * QB
                            for q in range(chunk // QB):
                                lanes = slice(q * QB, (q + 1) * QB)
                                store(z, side, lanes, result[lanes, at : at + QB])

            def to_given(z, side, lanes, value):
                given[slot, z // 2, z % 2, side, :, lanes] = value

            def to_held(z, side, lanes, value):
                held[k, z // 2, z % 2, side, :, lanes] = value

            product(1, to_given)
            near_copy(k, slot).start()
            product(0, to_held)

            near_stage(k)

            for s in range(len(peers)):

                @pl.when(k == 2 * s + 1)
                def _(s=s):
                    small_stage(s)

            @pl.when((k >= 5) & (lax.rem(k, 3) == 2))
            def _():
                y_stage((k - 5) // 3)

        if p + 2 < len(phases):
            still_copy(p + 2).start()
        base += count

    early = (total - 1 - 5) // 3 + 1
    @pl.loop(0, early)
    def _(k):
        low_stage(k)

    @pl.loop(0, early - 1)
    def _(k):
        high_stage(k)

    @pl.loop(early, total)
    def _(k):
        y_stage(k)
        high_stage(k - 1)
        low_stage(k)

    @pl.loop(total - 1, total)
    def _(k):
        high_stage(k)

    summed_ref[...] = small_ref[len(peers)]
    near_copy(total - 2, (total - 2) % 2).wait_send()
    near_copy(total - 1, (total - 1) % 2).wait_send()

    @pl.loop(0, total)
    def _(k):
        y_copy(k).wait_send()
        low_copy(k).wait_send()
        high_copy(k).wait_send()

    for s in range(len(peers)):
        small_copy(s).wait_send()
    upper_copy.wait()


def summed_grads(f, dy, context, db, n, du, e, dqkv, upper, packed):
    rows, width = dy.shape[1:]
    chunk = 512
    total = du.shape[2] // chunk + 4
    dma = pltpu.SemaphoreType.DMA
    anywhere = pl.BlockSpec(memory_space=pl.ANY)
    local = pl.BlockSpec(memory_space=pltpu.VMEM)
    return pl.pallas_call(
        grads_kernel,
        in_specs=[anywhere] * 9 + [local],
        out_specs=[local] * 5 + [anywhere],
        out_shape=[
            jax.ShapeDtypeStruct((du.shape[2] // 2, QB), F32),
            jax.ShapeDtypeStruct((QB, du.shape[2] // 2), F32),
            jax.ShapeDtypeStruct((width // 2, QB), F32),
            jax.ShapeDtypeStruct((QB, dqkv.shape[2] // 2), F32),
            jax.ShapeDtypeStruct(packed.shape, F32),
            jax.ShapeDtypeStruct((2,) + upper.shape[1:], LOW),
        ],
        scratch_shapes=[
            pltpu.VMEM((2, 2, rows, width), LOW),
            pltpu.VMEM((2, 2, 2, rows, chunk), LOW),
            pltpu.VMEM((width, 2 * rows), LOW),
            pltpu.VMEM((2, 2, 2, 2, QB, chunk), LOW),
            pltpu.VMEM((total, 2, 2, 2, QB, chunk), LOW),
            pltpu.VMEM((total, 2, 2, 2, QB, chunk), LOW),
            pltpu.VMEM((total, 2, 2, QB, chunk), LOW),
            pltpu.VMEM((total, 2, QB, chunk), LOW),
            pltpu.VMEM((total, QB, chunk), LOW),
            pltpu.VMEM((6,) + packed.shape, F32),
            pltpu.VMEM((5,) + packed.shape, F32),
            dma((2,)),
            dma((2, 2)),
            dma((2,)),
            dma((total,)),
            dma((total,)),
            dma((total,)),
            dma((total,)),
            dma((total,)),
            dma((total,)),
            dma((total,)),
            dma((5,)),
            dma((5,)),
            dma,
            dma,
        ],
        compiler_params=pltpu.CompilerParams(
            collective_id=0, has_side_effects=True, vmem_limit_bytes=TAIL_VMEM
        ),
        cost_estimate=cost_of(5000),
        name="summed_grads",
    )(f, dy, context, db, n, du, e, dqkv, upper, packed)


def swapped(value, axis, bit):
    pairs = [(at, at ^ bit) for at in range(lax.axis_size(axis))]
    return lax.ppermute(value, axis, pairs)


def paired_body(
    layer_input,
    segment_ids,
    buckets,
    attn_in,
    attn_out,
    ffn_in,
    ffn_out,
    norm_gain,
    bert_shift,
    head_bias,
    ffn_bias,
    position_bias,
    decoder_grads,
):
    micro_count, _, rows, width = layer_input.shape
    length = segment_ids.shape[2]
    heads, bucket_count = position_bias.shape
    section = lax.axis_index("section")
    core = lax.axis_index("tensor")
    leading = section == 0
    lead = jnp.where(leading, 1, 0).astype(jnp.int32)
    pieces = lax.axis_size("dp")

    own_grads = decoder_grads[0, :, 0]
    given_rows = layer_input[:, 0]
    qkv_own = jnp.concatenate([attn_in[0, :, part] for part in range(3)], axis=1)
    qkv_oth = swapped(qkv_own, "tensor", 1)
    wo = (attn_out[0], swapped(attn_out[0], "tensor", 1))
    up = (ffn_in[0], swapped(ffn_in[0], "tensor", 1))
    down = (ffn_out[0], swapped(ffn_out[0], "tensor", 1))
    small = jnp.concatenate([head_bias.reshape(-1), ffn_bias, position_bias.reshape(-1)])
    small_oth = swapped(small, "tensor", 1)
    near_heads = head_bias.size
    near_ffn = near_heads + ffn_bias.size
    both_small = jnp.stack([small, small_oth])
    head_both = both_small[:, :near_heads].reshape(2, 2, -1)
    ffn_both = jnp.where(leading, both_small[:, near_heads:near_ffn], 0.0).reshape(1, -1)
    table_both = jnp.where(leading, 0.0, both_small[:, near_ffn:]).reshape(2 * heads, bucket_count)
    q_shift = head_both[:, 0].reshape(1, -1)
    v_shift = head_both[:, 1].reshape(1, -1)
    qkv_shift = jnp.where(
        leading, jnp.concatenate([q_shift, jnp.zeros_like(q_shift), v_shift], axis=1), 0.0
    )
    gains = jnp.where(leading, norm_gain[0], norm_gain[1])
    entry_gain = gains[0:1]

    near = length - 1 - 3 * QB
    near_hits = (buckets[None, near : near + 6 * QB] == jnp.arange(bucket_count)[:, None]).astype(F32)
    trailing = jnp.reshape(1 - lead, (1,))
    bias = toeplitz(trailing, jnp.dot(table_both, near_hits, precision=lax.Precision.HIGHEST))

    window = rows + REACH
    base = core * (length - window)
    segments = jnp.pad(
        lax.dynamic_slice_in_dim(segment_ids[:, 0], base, window, axis=1),
        ((0, 0), (PAD * QB, PAD * QB)),
        constant_values=-1,
    )
    reach_blocks = REACH // QB
    own_block = PAD + core * reach_blocks
    halo_block = jnp.where(core == 0, PAD + rows // QB, PAD)
    edge = jnp.where(core == 0, rows - REACH, 0)

    def info_of(turn, micro):
        active = jnp.where(section == turn, 1, 0)
        slot = jnp.where(active == 1, micro, micro_count)
        return jnp.stack([lead, slot, own_block, halo_block, edge, active]).astype(jnp.int32)

    turns = [(turn, micro) for turn in range(2) for micro in range(micro_count)]
    received = [None] * micro_count
    entered = attended = fed = None
    results = []
    finished = []
    for turn, micro in turns:
        info = info_of(turn, micro)
        if turn + micro > 0:
            info, _ = lax.optimization_barrier((info, result))
        if turn == 1 and micro == 0:
            info, remote_grads = lax.optimization_barrier((info, remote_grads))
        lead_turn = turn == 0
        given, at = (given_rows, micro) if lead_turn else (received[micro][None], 0)
        *entered, halo = enter(
            lead_turn, info, given, at, entry_gain, qkv_shift, qkv_own, qkv_oth, entered
        )
        halo = exchanged(halo)
        if turn + micro == 0:
            later, _ = lax.optimization_barrier((own_grads, halo))
            remote_grads = lax.ppermute(later, "section", [(0, 1)])
        attended = attend(
            info, segments[micro], entered[2], halo, None if lead_turn else bias, attended
        )
        *fed, result = feed(
            lead_turn, info, entered[0], attended[0], wo, up, down, ffn_both, gains, bert_shift, fed
        )
        if turn == 0:
            received = list(received)
            received[micro] = lax.ppermute(result, "section", [(0, 1)])
        else:
            results.append(result)
            finished.append(lax.ppermute(result, "section", [(1, 0)]))
    x_saved, e_saved, qkv_saved = entered
    context, lse, *halo_saved = attended
    f_saved, slope_saved, n_saved, one_saved, two_saved = fed

    received = [None] * micro_count
    feed_kept = table_kept = entry_kept = None
    for step, (turn, micro) in enumerate([(1 - turn, micro) for turn, micro in turns]):
        info = info_of(turn, micro)
        if step > 0:
            info, _ = lax.optimization_barrier((info, low if step < 3 else entry_kept[1]))
        lead_turn = turn == 0
        got, at = ([received[micro][None]], 0) if lead_turn else ([own_grads, remote_grads], micro)
        *feed_kept, grad_context = feed_back(
            lead_turn, info, got, at, one_saved, two_saved, slope_saved, wo, up, down, gains, feed_kept
        )
        d3, *tables, far = attend_back(
            info, segments[micro], qkv_saved, halo_saved, grad_context, None if lead_turn else bias, lse,
            None if lead_turn else table_kept,
        )
        if not lead_turn:
            table_kept = tables[0]
        far = exchanged(far)
        if turn == 1 and micro == 0:
            info, *finished = lax.optimization_barrier((info, *finished))
        *entry_kept, low = enter_back(
            lead_turn, info, d3, far, feed_kept[2], x_saved, qkv_own, qkv_oth, entry_gain, entry_kept
        )
        if turn == 1:
            received = list(received)
            received[micro] = lax.ppermute(low, "section", [(1, 0)])
    dy_saved, du_saved, db_saved, stat_feed, stat_bias = feed_kept
    dqkv_saved, stat_entry, lower_kept, upper_kept = entry_kept

    near_table = jnp.dot(diagonals(trailing, table_kept, micro_count), near_hits.T, precision=lax.Precision.HIGHEST)

    def placed(pair):
        return jnp.where(core == 0, pair, pair[::-1])

    stat_feed = stat_feed[0] + stat_feed[1]
    stat_entry = stat_entry[0] + stat_entry[1]
    gain_first = jnp.where(leading, stat_feed[0:1], stat_entry[2:3])
    gain_rows = jnp.concatenate([gain_first, stat_feed[1:2]])
    nothing = jnp.zeros_like(gain_rows)
    gain_all = jnp.where(leading, jnp.concatenate([gain_rows, nothing]), jnp.concatenate([nothing, gain_rows]))
    shift_all = jnp.where(leading, stat_feed[2:6], 0.0)
    head_all = jnp.where(leading, stat_entry[0:2], 0.0).reshape(2, 2, -1)
    head_all = placed(jnp.moveaxis(head_all, 1, 0))
    bias_all = placed(jnp.where(leading, stat_bias[0] + stat_bias[1], 0.0).reshape(2, -1))
    table_all = placed(jnp.where(leading, 0.0, near_table).reshape(2, heads, bucket_count))
    parts = [gain_all, shift_all, head_all, bias_all, table_all]
    packed = jnp.concatenate([part.reshape(-1) for part in parts])
    packed_rows = 8 * (-(-packed.size // (8 * width)))
    packed = jnp.pad(packed, (0, packed_rows * width - packed.size)).reshape(packed_rows, width)
    down_sum, up_sum, out_sum, qkv_sum, packed, upper = summed_grads(
        f_saved, dy_saved, context, db_saved, n_saved, du_saved, e_saved, dqkv_saved, upper_kept, packed
    )
    packed = packed.reshape(-1)
    input_grad = jnp.where(leading, lower_kept[:micro_count], upper.astype(F32))[:, None]
    unpacked = []
    start = 0
    for part in parts:
        unpacked.append(packed[start : start + part.size].reshape(part.shape))
        start += part.size
    gain_all, shift_all, head_all, bias_all, table_all = unpacked
    mine = lambda value: lax.dynamic_index_in_dim(value, core, 0, keepdims=False)
    return (
        jnp.where(leading, jnp.stack(finished), jnp.stack(results))[None, :, None],
        input_grad,
        qkv_sum.reshape(1, width // pieces, 3, -1),
        out_sum[None],
        up_sum[None],
        down_sum[None],
        gain_all.reshape(norm_gain.shape),
        shift_all,
        mine(head_all),
        mine(bias_all),
        mine(table_all),
    )


def solution(mesh):
    placed = (
        P(None, "dp", "tensor", None),
        P(None, "dp", None),
        P(),
        P("section", None, None, "tensor"),
        P("section", "tensor", None),
        P("section", None, "tensor"),
        P("section", "tensor", None),
        P(),
        P(),
        P(None, "tensor"),
        P("tensor"),
        P("tensor", None),
        P("section", None, "dp", "tensor", None),
    )
    paired = mesh.shape["tensor"] == 2 and mesh.shape["dp"] == 8
    return jax.shard_map(
        paired_body if paired else general_body,
        mesh=mesh,
        in_specs=placed,
        out_specs=(
            P("section", None, "dp", "tensor", None),
            P(None, "dp", "tensor", "section"),
            P("section", "dp", None, "tensor"),
            P("section", "tensor", "dp"),
            P("section", "dp", "tensor"),
            P("section", "tensor", "dp"),
            P(),
            P(),
            P(None, "tensor"),
            P("tensor"),
            P("tensor", None),
        ),
        check_vma=False,
    )
```
